32 devices in a mesh: seq: 8 (over z, y), head: 4 (over x, core).
Axes of the slice: x: 2, y: 2, z: 4, core: 2. Of those that a mesh axis runs over, the one named last changes fastest.
Arguments:
- queries: bfloat16 [4096, 4096], P('seq', 'head'), may hold values from -6 to 6
- keys: bfloat16 [4096, 4096], P('seq', 'head'), may hold values from -6 to 6
- values: bfloat16 [4096, 4096], P('seq', 'head'), may hold values from -6 to 6
- out_grad: bfloat16 [4096, 4096], P('seq', 'head'), may hold values from -6 to 6
- gain: float32 [4096], P('head'), may hold values from 0.3 to 3
Outputs:
- query_grad: bfloat16 [4096, 4096], P('seq', 'head')
- key_grad: bfloat16 [4096, 4096], P('seq', 'head')
- value_grad: bfloat16 [4096, 4096], P('seq', 'head')
The draws below stay inside these ranges and needn't reach their ends.
All inputs are finite; a program needn't handle non-finite values.
Results may differ from the reference program's by a relative error of at most 0.0058.
Values may be sent and summed in bfloat16 or wider, within the bound.
No kernel may reach another device: no remote copies, remote signals or barrier semaphores. Data moves between devices by JAX's collectives and lax.ppermute only.
A program may use at most 128 MiB of HBM per device.

```python
import math
import jax
import jax.numpy as jnp
from jax import lax

HEADS = 32
HEAD_DIM = 128
D = 4096
SPAN = 512
TOKENS = 4096


def block_scale(rng, shape, shards, low, top_value):
    level, own = 1.0, jax.random.fold_in(rng, 6)
    for position, shards_of in shards:
        heights = jnp.exp(jax.random.uniform(jax.random.fold_in(own, position), (shards_of,), jnp.float32, low / len(shards), top_value / len(shards)))
        level = level * jnp.repeat(heights, shape[position] // shards_of).reshape([-1 if axis == position else 1 for axis in range(len(shape))])
    return level


def normal_values(stream_key, extent, deviation, reach, cuts=(), held_as=jnp.bfloat16):
    result = deviation * jax.random.normal(stream_key, extent, jnp.float32)
    if cuts:
        result = result * block_scale(stream_key, extent, cuts, -0.22, 0.18)
    return jnp.clip(result, -reach, reach).astype(held_as)


def setup_inputs(seed: int = 0) -> dict:
    key_list = jax.random.split(jax.random.key(seed), 6)
    queries = normal_values(key_list[0], (TOKENS, D), 1.0, 6.0, ((0, 8), (1, 4)))
    keys = normal_values(key_list[1], (TOKENS, D), 1.0, 6.0, ((0, 8), (1, 4)))
    values = normal_values(key_list[2], (TOKENS, D), 1.0, 6.0, ((0, 8), (1, 4)))
    out_grad = normal_values(key_list[3], (TOKENS, D), 1.0, 6.0, ((0, 8), (1, 4)))
    gain = jnp.clip(jnp.exp(math.log(3.0) - 2.3025851 * jax.random.uniform(key_list[4], (D,), jnp.float32) ** block_scale(key_list[4], (D,), ((0, 4),), -0.2, 0.2)), 0.3, 3.0)
    return {"queries": queries, "keys": keys, "values": values, "out_grad": out_grad, "gain": gain}


def to_low(state):
    return lax.optimization_barrier(state.astype(jnp.bfloat16)).astype(jnp.float32)

def causal_table():
    rows = lax.broadcasted_iota(jnp.int32, (SPAN, SPAN), 0)
    cols = lax.broadcasted_iota(jnp.int32, (SPAN, SPAN), 1)
    return rows >= cols

def block_weights(query_block, key_block):
    scores = jnp.einsum('thd,shd->hts', query_block.astype(jnp.float32), key_block.astype(jnp.float32))
    return to_low(jnp.where(causal_table()[None], scores, 0.0))

def forward_block(items):
    query_block, key_block, value_block, grad_block, kv_state, gain_row = items
    weights = block_weights(query_block, key_block)
    attended = jnp.einsum('hts,she->the', weights, value_block.astype(jnp.float32))
    attended = attended + jnp.einsum('thd,hde->the', query_block.astype(jnp.float32), to_low(kv_state))
    attended = attended.reshape(SPAN, D)
    square_sum = lax.optimization_barrier(jnp.sum(attended * attended, axis=1))
    scaled = gain_row[None, :] * grad_block.reshape(SPAN, D).astype(jnp.float32)
    cross_sum = lax.optimization_barrier(jnp.sum(scaled * attended, axis=1))
    rms_rows = jnp.sqrt(square_sum / D + 1e-06)
    dout = scaled / rms_rows[:, None] - attended * (cross_sum / (D * rms_rows ** 3))[:, None]
    return dout.astype(jnp.bfloat16).reshape(SPAN, HEADS, HEAD_DIM)

def backward_block(items):
    query_block, key_block, value_block, dout, kv_state, grad_state = items
    q32 = query_block.astype(jnp.float32)
    k32 = key_block.astype(jnp.float32)
    v32 = value_block.astype(jnp.float32)
    d32 = dout.astype(jnp.float32)
    weights = block_weights(query_block, key_block)
    dscore = to_low(jnp.where(causal_table()[None], jnp.einsum('the,she->hts', d32, v32), 0.0))
    kv_low = to_low(kv_state)
    grad_low = to_low(grad_state)
    query_grad = jnp.einsum('hts,shd->thd', dscore, k32) + jnp.einsum('the,hde->thd', d32, kv_low)
    key_grad = jnp.einsum('hts,thd->shd', dscore, q32) + jnp.einsum('she,hde->shd', v32, grad_low)
    value_grad = jnp.einsum('hts,the->she', weights, d32) + jnp.einsum('shd,hde->she', k32, grad_low)
    return (query_grad.astype(jnp.bfloat16), key_grad.astype(jnp.bfloat16), value_grad.astype(jnp.bfloat16))

def reference(queries, keys, values, out_grad, gain):
    blocks = TOKENS // SPAN
    shape = (blocks, SPAN, HEADS, HEAD_DIM)
    query_all = queries.reshape(shape)
    key_all = keys.reshape(shape)
    value_all = values.reshape(shape)
    grad_all = out_grad.reshape(shape)
    own_kv = jnp.einsum('cthd,cthe->chde', key_all.astype(jnp.float32), value_all.astype(jnp.float32))
    kv_states = jnp.cumsum(own_kv, axis=0) - own_kv
    gains = jnp.broadcast_to(gain[None, :], (blocks, D))
    dout_all = lax.map(forward_block, (query_all, key_all, value_all, grad_all, kv_states, gains))
    own_grad = jnp.einsum('cthd,cthe->chde', query_all.astype(jnp.float32), dout_all.astype(jnp.float32))
    grad_states = lax.optimization_barrier(jnp.sum(own_grad, axis=0))[None] - jnp.cumsum(own_grad, axis=0)
    query_grad, key_grad, value_grad = lax.map(backward_block, (query_all, key_all, value_all, dout_all, kv_states, grad_states))
    return (query_grad.reshape(TOKENS, D), key_grad.reshape(TOKENS, D), value_grad.reshape(TOKENS, D))
```

```python
import jax
import jax.numpy as jnp
from jax import lax
from jax.sharding import PartitionSpec as P

HEAD_DIM = 128
D = 4096


def entering(part, axis, reverse):
    count = lax.axis_size(axis)
    heads, rows, cols = part.shape
    pieces = part.astype(jnp.bfloat16).reshape(count, heads * rows // count, cols)
    blocks = lax.all_to_all(pieces, axis, 0, 0).astype(jnp.float32)
    own = lax.broadcasted_iota(jnp.int32, (count, count), 0)
    other = lax.broadcasted_iota(jnp.int32, (count, count), 1)
    taken = other > own if reverse else other < own
    states = jnp.sum(jnp.where(taken[:, :, None, None], blocks[None], 0.0), axis=1)
    return lax.all_to_all(states.astype(jnp.bfloat16), axis, 0, 0).reshape(part.shape)


def shards(queries, keys, values, out_grad, gain):
    rows_local, width = queries.shape
    heads_local = width // HEAD_DIM
    shape = (rows_local, heads_local, HEAD_DIM)
    query_heads = queries.reshape(shape)
    key_heads = keys.reshape(shape)
    value_heads = values.reshape(shape)
    rows_index = lax.broadcasted_iota(jnp.int32, (rows_local, rows_local), 0)
    cols_index = lax.broadcasted_iota(jnp.int32, (rows_local, rows_local), 1)
    causal = (rows_index >= cols_index)[None]
    own_kv = jnp.einsum("thd,the->hde", key_heads, value_heads, preferred_element_type=jnp.float32)
    kv_low = entering(own_kv, "seq", False)
    scores = jnp.einsum("thd,shd->hts", query_heads, key_heads, preferred_element_type=jnp.float32)
    weights = jnp.where(causal, scores, 0.0).astype(jnp.bfloat16)
    attended = jnp.einsum("hts,she->the", weights, value_heads, preferred_element_type=jnp.float32)
    attended = attended + jnp.einsum(
        "thd,hde->the", query_heads, kv_low, preferred_element_type=jnp.float32
    )
    attended = attended.reshape(rows_local, width)
    scaled = gain[None, :] * out_grad.astype(jnp.float32)
    square_sum, cross_sum = lax.psum(
        (jnp.sum(attended * attended, axis=1), jnp.sum(scaled * attended, axis=1)), "head"
    )
    rms_rows = jnp.sqrt(square_sum / D + 1e-06)
    dout = scaled / rms_rows[:, None] - attended * (cross_sum / (D * rms_rows**3))[:, None]
    dout_heads = dout.astype(jnp.bfloat16).reshape(shape)
    own_grad = jnp.einsum(
        "thd,the->hde", query_heads, dout_heads, preferred_element_type=jnp.float32
    )
    grad_low = entering(own_grad, "seq", True)
    dscore = jnp.einsum("the,she->hts", dout_heads, value_heads, preferred_element_type=jnp.float32)
    dscore = jnp.where(causal, dscore, 0.0).astype(jnp.bfloat16)
    query_grad = jnp.einsum("hts,shd->thd", dscore, key_heads, preferred_element_type=jnp.float32)
    query_grad = query_grad + jnp.einsum(
        "the,hde->thd", dout_heads, kv_low, preferred_element_type=jnp.float32
    )
    key_grad = jnp.einsum("hts,thd->shd", dscore, query_heads, preferred_element_type=jnp.float32)
    key_grad = key_grad + jnp.einsum(
        "she,hde->shd", value_heads, grad_low, preferred_element_type=jnp.float32
    )
    value_grad = jnp.einsum("hts,the->she", weights, dout_heads, preferred_element_type=jnp.float32)
    value_grad = value_grad + jnp.einsum(
        "shd,hde->she", key_heads, grad_low, preferred_element_type=jnp.float32
    )
    return (
        query_grad.reshape(rows_local, width).astype(jnp.bfloat16),
        key_grad.reshape(rows_local, width).astype(jnp.bfloat16),
        value_grad.reshape(rows_local, width).astype(jnp.bfloat16),
    )


def solution(mesh):
    return jax.shard_map(
        shards,
        mesh=mesh,
        in_specs=(
            P("seq", "head"),
            P("seq", "head"),
            P("seq", "head"),
            P("seq", "head"),
            P("head"),
        ),
        out_specs=(P("seq", "head"), P("seq", "head"), P("seq", "head")),
        check_vma=False,
    )
```

```python
import jax
import jax.numpy as jnp
from jax import lax
from jax.sharding import PartitionSpec as P

HEAD_DIM = 128
D = 4096


def exchange(pieces, axis):
    count = lax.axis_size(axis)
    if count > 8:
        return lax.all_to_all(pieces, axis, 0, 0)
    got = [pieces[0]]
    for shift in range(1, count):
        pairs = [(place, (place + shift) % count) for place in range(count)]
        got.append(lax.ppermute(pieces[shift], axis, pairs))
    return jnp.stack(got)


def entering(part, axis, reverse):
    count = lax.axis_size(axis)
    place = lax.axis_index(axis)
    heads, rows, cols = part.shape
    pieces = part.astype(jnp.bfloat16).reshape(count, heads * rows // count, cols)
    lane = lax.broadcasted_iota(jnp.int32, (count, count), 0)
    other = lax.broadcasted_iota(jnp.int32, (count, count), 1)
    direct = count > 8
    if not direct:
        pieces = lax.dynamic_slice_in_dim(jnp.concatenate([pieces, pieces]), place, count, 0)
        lane = (place + lane) % count
        other = (place - other) % count
    blocks = exchange(pieces, axis).astype(jnp.float32)
    taken = other > lane if reverse else other < lane
    states = jnp.sum(jnp.where(taken[:, :, None, None], blocks[None], 0.0), axis=1)
    states = exchange(states.astype(jnp.bfloat16), axis)
    if not direct:
        states = jnp.flip(states, 0)
        states = lax.dynamic_slice_in_dim(jnp.concatenate([states, states]), count - 1 - place, count, 0)
    return states.reshape(part.shape)


def shards(queries, keys, values, out_grad, gain):
    rows_local, width = queries.shape
    heads_local = width // HEAD_DIM
    shape = (rows_local, heads_local, HEAD_DIM)
    query_heads = queries.reshape(shape)
    key_heads = keys.reshape(shape)
    value_heads = values.reshape(shape)
    rows_index = lax.broadcasted_iota(jnp.int32, (rows_local, rows_local), 0)
    cols_index = lax.broadcasted_iota(jnp.int32, (rows_local, rows_local), 1)
    causal = (rows_index >= cols_index)[None]
    own_kv = jnp.einsum("thd,the->hde", key_heads, value_heads, preferred_element_type=jnp.float32)
    kv_low = entering(own_kv, "seq", False)
    scores = jnp.einsum("thd,shd->hts", query_heads, key_heads, preferred_element_type=jnp.float32)
    weights = jnp.where(causal, scores, 0.0).astype(jnp.bfloat16)
    attended = jnp.einsum("hts,she->the", weights, value_heads, preferred_element_type=jnp.float32)
    attended = attended + jnp.einsum(
        "thd,hde->the", query_heads, kv_low, preferred_element_type=jnp.float32
    )
    attended = attended.reshape(rows_local, width)
    scaled = gain[None, :] * out_grad.astype(jnp.float32)
    square_sum, cross_sum = lax.psum(
        (jnp.sum(attended * attended, axis=1), jnp.sum(scaled * attended, axis=1)), "head"
    )
    rms_rows = jnp.sqrt(square_sum / D + 1e-06)
    dout = scaled / rms_rows[:, None] - attended * (cross_sum / (D * rms_rows**3))[:, None]
    dout_heads = dout.astype(jnp.bfloat16).reshape(shape)
    own_grad = jnp.einsum(
        "thd,the->hde", query_heads, dout_heads, preferred_element_type=jnp.float32
    )
    grad_low = entering(own_grad, "seq", True)
    dscore = jnp.einsum("the,she->hts", dout_heads, value_heads, preferred_element_type=jnp.float32)
    dscore = jnp.where(causal, dscore, 0.0).astype(jnp.bfloat16)
    query_grad = jnp.einsum("hts,shd->thd", dscore, key_heads, preferred_element_type=jnp.float32)
    query_grad = query_grad + jnp.einsum(
        "the,hde->thd", dout_heads, kv_low, preferred_element_type=jnp.float32
    )
    key_grad = jnp.einsum("hts,thd->shd", dscore, query_heads, preferred_element_type=jnp.float32)
    key_grad = key_grad + jnp.einsum(
        "she,hde->shd", value_heads, grad_low, preferred_element_type=jnp.float32
    )
    value_grad = jnp.einsum("hts,the->she", weights, dout_heads, preferred_element_type=jnp.float32)
    value_grad = value_grad + jnp.einsum(
        "shd,hde->she", key_heads, grad_low, preferred_element_type=jnp.float32
    )
    return (
        query_grad.reshape(rows_local, width).astype(jnp.bfloat16),
        key_grad.reshape(rows_local, width).astype(jnp.bfloat16),
        value_grad.reshape(rows_local, width).astype(jnp.bfloat16),
    )


def solution(mesh):
    return jax.shard_map(
        shards,
        mesh=mesh,
        in_specs=(
            P("seq", "head"),
            P("seq", "head"),
            P("seq", "head"),
            P("seq", "head"),
            P("head"),
        ),
        out_specs=(P("seq", "head"), P("seq", "head"), P("seq", "head")),
        check_vma=False,
    )
```

```python
import functools

import jax
import jax.numpy as jnp
from jax import lax
from jax.experimental import pallas as pl
from jax.experimental.pallas import tpu as pltpu
from jax.sharding import PartitionSpec as P

HEAD_DIM = 128
BLOCK = 256
EPSILON = 1e-06
MIB = 1 << 20


def mm(a, b):
    return lax.dot_general(a, b, (((1,), (0,)), ((), ())), preferred_element_type=jnp.float32)


def mm_nt(a, b):
    return lax.dot_general(a, b, (((1,), (1,)), ((), ())), preferred_element_type=jnp.float32)


def mm_tn(a, b):
    return lax.dot_general(a, b, (((0,), (0,)), ((), ())), preferred_element_type=jnp.float32)


def head_columns(ref):
    return [slice(at, at + HEAD_DIM) for at in range(0, ref.shape[1], HEAD_DIM)]


def masked(scores, row_start, col_start, rows_first):
    rows = row_start + lax.broadcasted_iota(jnp.int32, scores.shape, 0)
    cols = col_start + lax.broadcasted_iota(jnp.int32, scores.shape, 1)
    keep = rows >= cols if rows_first else cols >= rows
    return jnp.where(keep, scores, 0.0).astype(jnp.bfloat16)


def states_body(key_ref, value_ref, state_ref):
    for cols in head_columns(key_ref):
        state_ref[cols, :] = mm_tn(key_ref[:, cols], value_ref[:, cols]).astype(jnp.bfloat16)


def local_body(query_ref, key_ref, value_ref, local_ref):
    rows = query_ref.shape[0]
    for cols in head_columns(query_ref):
        for start in range(0, rows, BLOCK):
            end = start + BLOCK
            scores = mm_nt(query_ref[start:end, cols], key_ref[:end, cols])
            weights = masked(scores, start, 0, True)
            local_ref[start:end, cols] = mm(weights, value_ref[:end, cols])


def scan_body(reverse, block_ref, state_ref):
    count = block_ref.shape[0]
    total = jnp.zeros(block_ref.shape[1:], jnp.float32)
    order = range(count - 1, -1, -1) if reverse else range(count)
    for place in order:
        state_ref[place] = total.astype(jnp.bfloat16)
        total = total + block_ref[place].astype(jnp.float32)


def sums_body(query_ref, grad_ref, gain_ref, local_ref, state_ref, sums_ref, square, cross):
    step = pl.program_id(0)

    @pl.when(step == 0)
    def _():
        square[...] = jnp.zeros_like(square)
        cross[...] = jnp.zeros_like(cross)

    for cols in head_columns(query_ref):
        attended = local_ref[:, cols] + mm(query_ref[:, cols], state_ref[cols, :])
        scaled = gain_ref[:, cols] * grad_ref[:, cols].astype(jnp.float32)
        square[...] += attended * attended
        cross[...] += scaled * attended

    @pl.when(step == pl.num_programs(0) - 1)
    def _():
        sums_ref[0:1, :] = jnp.sum(square[...].T, axis=0, keepdims=True)
        sums_ref[1:2, :] = jnp.sum(cross[...].T, axis=0, keepdims=True)


def dout_body(width, query_ref, grad_ref, gain_ref, local_ref, state_ref, sums_ref, dout_ref, own_ref, factors):
    @pl.when(pl.program_id(0) == 0)
    def _():
        inverse = 1.0 / jnp.sqrt(sums_ref[0:1, :] / width + EPSILON)
        drop = sums_ref[1:2, :] * (inverse * inverse * inverse) / width
        both = jnp.concatenate([inverse, drop] + [jnp.zeros_like(drop)] * 6, axis=0)
        factors[...] = both.T

    inverse = factors[:, 0:1]
    drop = factors[:, 1:2]
    for cols in head_columns(query_ref):
        query = query_ref[:, cols]
        attended = local_ref[:, cols] + mm(query, state_ref[cols, :])
        scaled = gain_ref[:, cols] * grad_ref[:, cols].astype(jnp.float32)
        dout = (scaled * inverse - attended * drop).astype(jnp.bfloat16)
        dout_ref[:, cols] = dout
        own_ref[cols, :] = mm_tn(query, dout).astype(jnp.bfloat16)


def query_body(key_ref, value_ref, dout_ref, state_ref, out_ref):
    rows = dout_ref.shape[0]
    for cols in head_columns(dout_ref):
        for start in range(0, rows, BLOCK):
            end = start + BLOCK
            dout = dout_ref[start:end, cols]
            dscore = masked(mm_nt(dout, value_ref[:end, cols]), start, 0, True)
            grad = mm(dscore, key_ref[:end, cols]) + mm_nt(dout, state_ref[cols, :])
            out_ref[start:end, cols] = grad.astype(jnp.bfloat16)


def inner_body(query_ref, key_ref, value_ref, dout_ref, key_out, value_out):
    rows = dout_ref.shape[0]
    for cols in head_columns(dout_ref):
        for start in range(0, rows, BLOCK):
            end = start + BLOCK
            query = query_ref[start:, cols]
            dout = dout_ref[start:, cols]
            dscore = masked(mm_nt(value_ref[start:end, cols], dout), 0, 0, False)
            key_out[start:end, cols] = mm(dscore, query)
            weights = masked(mm_nt(key_ref[start:end, cols], query), 0, 0, False)
            value_out[start:end, cols] = mm(weights, dout)


def final_body(key_ref, value_ref, key_part, value_part, state_ref, key_out, value_out):
    for cols in head_columns(key_ref):
        state = state_ref[cols, :]
        key_grad = key_part[:, cols] + mm_nt(value_ref[:, cols], state)
        key_out[:, cols] = key_grad.astype(jnp.bfloat16)
        value_grad = value_part[:, cols] + mm(key_ref[:, cols], state)
        value_out[:, cols] = value_grad.astype(jnp.bfloat16)


def by_heads(body, args, kinds, outs, heads_step, flops, scratch=()):
    rows, width = args[0].shape
    step_cols = heads_step * HEAD_DIM
    specs = {
        "tokens": pl.BlockSpec((rows, step_cols), lambda step: (0, step)),
        "gain": pl.BlockSpec((1, step_cols), lambda step: (0, step)),
        "state": pl.BlockSpec((step_cols, HEAD_DIM), lambda step: (step, 0)),
        "sums": pl.BlockSpec((2, rows), lambda step: (0, 0)),
    }
    shapes = {"tokens": (rows, width), "state": (width, HEAD_DIM), "sums": (2, rows)}
    out_shape = [jax.ShapeDtypeStruct(shapes[kind], dtype) for kind, dtype in outs]
    moved = sum(a.size * a.dtype.itemsize for a in args)
    moved += sum(o.size * o.dtype.itemsize for o in out_shape)
    result = pl.pallas_call(
        body,
        grid=(width // step_cols,),
        in_specs=[specs[kind] for kind in kinds],
        out_specs=[specs[kind] for kind, _ in outs],
        out_shape=out_shape,
        scratch_shapes=scratch,
        compiler_params=pltpu.CompilerParams(vmem_limit_bytes=24 * MIB),
        cost_estimate=pl.CostEstimate(flops=flops, bytes_accessed=moved, transcendentals=0),
    )(*args)
    return result


def scan_blocks(blocks, reverse):
    return pl.pallas_call(
        functools.partial(scan_body, reverse),
        out_shape=jax.ShapeDtypeStruct(blocks.shape, blocks.dtype),
        compiler_params=pltpu.CompilerParams(vmem_limit_bytes=8 * MIB),
        cost_estimate=pl.CostEstimate(
            flops=blocks.size, bytes_accessed=4 * blocks.size, transcendentals=0
        ),
    )(blocks)


def entering(state, axis, reverse):
    count = lax.axis_size(axis)
    rows, cols = state.shape
    pieces = state.reshape(count, rows // count, cols)
    blocks = lax.all_to_all(pieces, axis, 0, 0)
    states = scan_blocks(blocks, reverse)
    return lax.all_to_all(states, axis, 0, 0).reshape(rows, cols)


def shards(queries, keys, values, out_grad, gain):
    rows, width = queries.shape
    total_width = width * lax.axis_size("head")
    bf16, f32 = jnp.bfloat16, jnp.float32
    small = 2 * rows * width * HEAD_DIM
    large = 2 * rows * rows * width * 3 // 4
    gain_row = gain.reshape(1, width)

    (own_kv,) = by_heads(states_body, (keys, values), ("tokens",) * 2, [("state", bf16)], 2, small)
    kv_low = entering(own_kv, "seq", False)
    (local,) = by_heads(
        local_body, (queries, keys, values), ("tokens",) * 3, [("tokens", f32)], 2, 2 * large
    )
    shared = (queries, out_grad, gain_row, local, kv_low)
    shared_kinds = ("tokens", "tokens", "gain", "tokens", "state")
    (sums,) = by_heads(
        sums_body,
        shared,
        shared_kinds,
        [("sums", f32)],
        2,
        small,
        [pltpu.VMEM((rows, HEAD_DIM), f32)] * 2,
    )
    sums = lax.psum(sums, "head")
    dout, own_grad = by_heads(
        functools.partial(dout_body, total_width),
        shared + (sums,),
        shared_kinds + ("sums",),
        [("tokens", bf16), ("state", bf16)],
        2,
        2 * small,
        [pltpu.VMEM((rows, 8), f32)],
    )
    grad_low = entering(own_grad, "seq", True)
    (query_grad,) = by_heads(
        query_body,
        (keys, values, dout, kv_low),
        ("tokens",) * 3 + ("state",),
        [("tokens", bf16)],
        2,
        2 * large + small,
    )
    key_part, value_part = by_heads(
        inner_body,
        (queries, keys, values, dout),
        ("tokens",) * 4,
        [("tokens", f32)] * 2,
        2,
        4 * large,
    )
    key_grad, value_grad = by_heads(
        final_body,
        (keys, values, key_part, value_part, grad_low),
        ("tokens",) * 4 + ("state",),
        [("tokens", bf16)] * 2,
        2,
        2 * small,
    )
    return query_grad, key_grad, value_grad


def solution(mesh):
    return jax.shard_map(
        shards,
        mesh=mesh,
        in_specs=(
            P("seq", "head"),
            P("seq", "head"),
            P("seq", "head"),
            P("seq", "head"),
            P("head"),
        ),
        out_specs=(P("seq", "head"), P("seq", "head"), P("seq", "head")),
        check_vma=False,
    )
```

```python
import functools

import jax
import jax.numpy as jnp
from jax import lax
from jax.experimental import pallas as pl
from jax.experimental.pallas import tpu as pltpu
from jax.sharding import PartitionSpec as P

HEAD_DIM = 128
BLOCK = 256
EPSILON = 1e-06
MIB = 1 << 20


def mm(a, b):
    return lax.dot_general(a, b, (((1,), (0,)), ((), ())), preferred_element_type=jnp.float32)


def mm_nt(a, b):
    return lax.dot_general(a, b, (((1,), (1,)), ((), ())), preferred_element_type=jnp.float32)


def mm_tn(a, b):
    return lax.dot_general(a, b, (((0,), (0,)), ((), ())), preferred_element_type=jnp.float32)


def head_columns(ref):
    return [slice(at, at + HEAD_DIM) for at in range(0, ref.shape[1], HEAD_DIM)]


def masked(scores, row_start, col_start, rows_first):
    rows = row_start + lax.broadcasted_iota(jnp.int32, scores.shape, 0)
    cols = col_start + lax.broadcasted_iota(jnp.int32, scores.shape, 1)
    keep = rows >= cols if rows_first else cols >= rows
    return jnp.where(keep, scores, 0.0).astype(jnp.bfloat16)


def states_body(key_ref, value_ref, state_ref):
    for cols in head_columns(key_ref):
        state_ref[cols, :] = mm_tn(key_ref[:, cols], value_ref[:, cols]).astype(jnp.bfloat16)


def local_body(query_ref, key_ref, value_ref, local_ref):
    rows = query_ref.shape[0]
    for cols in head_columns(query_ref):
        for start in range(0, rows, BLOCK):
            end = start + BLOCK
            scores = mm_nt(query_ref[start:end, cols], key_ref[:end, cols])
            weights = masked(scores, start, 0, True)
            local_ref[start:end, cols] = mm(weights, value_ref[:end, cols])


def scan_body(reverse, block_ref, state_ref):
    count = block_ref.shape[0]
    total = jnp.zeros(block_ref.shape[1:], jnp.float32)
    order = range(count - 1, -1, -1) if reverse else range(count)
    for place in order:
        state_ref[place] = total.astype(jnp.bfloat16)
        total = total + block_ref[place].astype(jnp.float32)


def sums_body(query_ref, grad_ref, gain_ref, local_ref, state_ref, sums_ref, square, cross):
    step = pl.program_id(0)

    @pl.when(step == 0)
    def _():
        square[...] = jnp.zeros_like(square)
        cross[...] = jnp.zeros_like(cross)

    for cols in head_columns(query_ref):
        attended = local_ref[:, cols] + mm(query_ref[:, cols], state_ref[cols, :])
        scaled = gain_ref[:, cols] * grad_ref[:, cols].astype(jnp.float32)
        square[...] += attended * attended
        cross[...] += scaled * attended

    @pl.when(step == pl.num_programs(0) - 1)
    def _():
        sums_ref[0:1, :] = jnp.sum(square[...].T, axis=0, keepdims=True)
        sums_ref[1:2, :] = jnp.sum(cross[...].T, axis=0, keepdims=True)


def dout_body(width, query_ref, grad_ref, gain_ref, local_ref, state_ref, sums_ref, dout_ref, own_ref, factors):
    @pl.when(pl.program_id(0) == 0)
    def _():
        inverse = 1.0 / jnp.sqrt(sums_ref[0:1, :] / width + EPSILON)
        drop = sums_ref[1:2, :] * (inverse * inverse * inverse) / width
        both = jnp.concatenate([inverse, drop] + [jnp.zeros_like(drop)] * 6, axis=0)
        factors[...] = both.T

    inverse = factors[:, 0:1]
    drop = factors[:, 1:2]
    for cols in head_columns(query_ref):
        query = query_ref[:, cols]
        attended = local_ref[:, cols] + mm(query, state_ref[cols, :])
        scaled = gain_ref[:, cols] * grad_ref[:, cols].astype(jnp.float32)
        dout = (scaled * inverse - attended * drop).astype(jnp.bfloat16)
        dout_ref[:, cols] = dout
        own_ref[cols, :] = mm_tn(query, dout).astype(jnp.bfloat16)


def query_body(key_ref, value_ref, dout_ref, state_ref, out_ref):
    rows = dout_ref.shape[0]
    for cols in head_columns(dout_ref):
        for start in range(0, rows, BLOCK):
            end = start + BLOCK
            dout = dout_ref[start:end, cols]
            dscore = masked(mm_nt(dout, value_ref[:end, cols]), start, 0, True)
            grad = mm(dscore, key_ref[:end, cols]) + mm_nt(dout, state_ref[cols, :])
            out_ref[start:end, cols] = grad.astype(jnp.bfloat16)


def inner_body(query_ref, key_ref, value_ref, dout_ref, key_out, value_out):
    rows = dout_ref.shape[0]
    for cols in head_columns(dout_ref):
        for start in range(0, rows, BLOCK):
            end = start + BLOCK
            query = query_ref[start:, cols]
            dout = dout_ref[start:, cols]
            dscore = masked(mm_nt(value_ref[start:end, cols], dout), 0, 0, False)
            key_out[start:end, cols] = mm(dscore, query).astype(jnp.bfloat16)
            weights = masked(mm_nt(key_ref[start:end, cols], query), 0, 0, False)
            value_out[start:end, cols] = mm(weights, dout).astype(jnp.bfloat16)


def final_body(key_ref, value_ref, key_part, value_part, state_ref, key_out, value_out):
    for cols in head_columns(key_ref):
        state = state_ref[cols, :]
        key_grad = key_part[:, cols].astype(jnp.float32) + mm_nt(value_ref[:, cols], state)
        key_out[:, cols] = key_grad.astype(jnp.bfloat16)
        value_grad = value_part[:, cols].astype(jnp.float32) + mm(key_ref[:, cols], state)
        value_out[:, cols] = value_grad.astype(jnp.bfloat16)


def by_heads(body, args, kinds, outs, heads_step, flops, scratch=()):
    rows, width = args[0].shape
    step_cols = heads_step * HEAD_DIM
    specs = {
        "tokens": pl.BlockSpec((rows, step_cols), lambda step: (0, step)),
        "gain": pl.BlockSpec((1, step_cols), lambda step: (0, step)),
        "state": pl.BlockSpec((step_cols, HEAD_DIM), lambda step: (step, 0)),
        "sums": pl.BlockSpec((2, rows), lambda step: (0, 0)),
    }
    shapes = {"tokens": (rows, width), "state": (width, HEAD_DIM), "sums": (2, rows)}
    out_shape = [jax.ShapeDtypeStruct(shapes[kind], dtype) for kind, dtype in outs]
    moved = sum(a.size * a.dtype.itemsize for a in args)
    moved += sum(o.size * o.dtype.itemsize for o in out_shape)
    result = pl.pallas_call(
        body,
        grid=(width // step_cols,),
        in_specs=[specs[kind] for kind in kinds],
        out_specs=[specs[kind] for kind, _ in outs],
        out_shape=out_shape,
        scratch_shapes=scratch,
        compiler_params=pltpu.CompilerParams(vmem_limit_bytes=60 * MIB),
        cost_estimate=pl.CostEstimate(flops=flops, bytes_accessed=moved, transcendentals=0),
    )(*args)
    return result


def scan_blocks(blocks, reverse):
    return pl.pallas_call(
        functools.partial(scan_body, reverse),
        out_shape=jax.ShapeDtypeStruct(blocks.shape, blocks.dtype),
        compiler_params=pltpu.CompilerParams(vmem_limit_bytes=60 * MIB),
        cost_estimate=pl.CostEstimate(
            flops=blocks.size, bytes_accessed=4 * blocks.size, transcendentals=0
        ),
    )(blocks)


def exchange(pieces, axis):
    return lax.all_to_all(pieces, axis, 0, 0)


def in_pieces(state, axis):
    count = lax.axis_size(axis)
    rows, cols = state.shape
    return state.reshape(count, rows // count, cols)


def shards(queries, keys, values, out_grad, gain):
    rows, width = queries.shape
    total_width = width * lax.axis_size("head")
    bf16, f32 = jnp.bfloat16, jnp.float32
    small = 2 * rows * width * HEAD_DIM
    large = 2 * rows * rows * width * 3 // 4
    gain_row = gain.reshape(1, width)

    (own_kv,) = by_heads(states_body, (keys, values), ("tokens",) * 2, [("state", bf16)], 2, small)
    kv_blocks = exchange(in_pieces(own_kv, "seq"), "seq")
    kv_low = exchange(scan_blocks(kv_blocks, False), "seq").reshape(own_kv.shape)
    (local,) = by_heads(
        local_body, (queries, keys, values), ("tokens",) * 3, [("tokens", f32)], 2, 2 * large
    )
    shared = (queries, out_grad, gain_row, local, kv_low)
    shared_kinds = ("tokens", "tokens", "gain", "tokens", "state")
    (sums,) = by_heads(
        sums_body,
        shared,
        shared_kinds,
        [("sums", f32)],
        2,
        small,
        [pltpu.VMEM((rows, HEAD_DIM), f32)] * 2,
    )
    sums = lax.psum(sums, "head")
    dout, own_grad = by_heads(
        functools.partial(dout_body, total_width),
        shared + (sums,),
        shared_kinds + ("sums",),
        [("tokens", bf16), ("state", bf16)],
        2,
        2 * small,
        [pltpu.VMEM((rows, 8), f32)],
    )
    grad_blocks = exchange(in_pieces(own_grad, "seq"), "seq")
    (query_grad,) = by_heads(
        query_body,
        (keys, values, dout, kv_low),
        ("tokens",) * 3 + ("state",),
        [("tokens", bf16)],
        2,
        2 * large + small,
    )
    grad_blocks, query_grad = lax.optimization_barrier((grad_blocks, query_grad))
    grad_low = exchange(scan_blocks(grad_blocks, True), "seq").reshape(own_grad.shape)
    key_part, value_part = by_heads(
        inner_body,
        (queries, keys, values, dout),
        ("tokens",) * 4,
        [("tokens", bf16)] * 2,
        2,
        4 * large,
    )
    key_grad, value_grad = by_heads(
        final_body,
        (keys, values, key_part, value_part, grad_low),
        ("tokens",) * 4 + ("state",),
        [("tokens", bf16)] * 2,
        2,
        2 * small,
    )
    return query_grad, key_grad, value_grad


def solution(mesh):
    return jax.shard_map(
        shards,
        mesh=mesh,
        in_specs=(
            P("seq", "head"),
            P("seq", "head"),
            P("seq", "head"),
            P("seq", "head"),
            P("head"),
        ),
        out_specs=(P("seq", "head"), P("seq", "head"), P("seq", "head")),
        check_vma=False,
    )
```

```python
import functools

import jax
import jax.numpy as jnp
from jax import lax
from jax.experimental import pallas as pl
from jax.experimental.pallas import tpu as pltpu
from jax.sharding import PartitionSpec as P

HEAD_DIM = 128
BLOCK = 256
COPY_COLS = 256
EPSILON = 1e-06
MIB = 1 << 20


def mm(a, b):
    return lax.dot_general(a, b, (((1,), (0,)), ((), ())), preferred_element_type=jnp.float32)


def mm_nt(a, b):
    return lax.dot_general(a, b, (((1,), (1,)), ((), ())), preferred_element_type=jnp.float32)


def mm_tn(a, b):
    return lax.dot_general(a, b, (((0,), (0,)), ((), ())), preferred_element_type=jnp.float32)


def pieces_of(ref, size):
    return [slice(at, at + size) for at in range(0, ref.shape[1], size)]


def head_columns(ref):
    return pieces_of(ref, HEAD_DIM)


def masked(scores, row_start, col_start, rows_first):
    rows = row_start + lax.broadcasted_iota(jnp.int32, scores.shape, 0)
    cols = col_start + lax.broadcasted_iota(jnp.int32, scores.shape, 1)
    keep = rows >= cols if rows_first else cols >= rows
    return jnp.where(keep, scores, 0.0).astype(jnp.bfloat16)


def column_copies(source, target, sems):
    copies = []
    for index, cols in enumerate(pieces_of(source, COPY_COLS)):
        copies.append(pltpu.make_async_copy(source.at[:, cols], target.at[:, cols], sems.at[index]))
    return copies


def states_body(key_hbm, value_hbm, key_ref, value_ref, state_ref, key_sems, value_sems):
    key_copies = column_copies(key_hbm, key_ref, key_sems)
    value_copies = column_copies(value_hbm, value_ref, value_sems)
    for key_copy, value_copy in zip(key_copies, value_copies):
        key_copy.start()
        value_copy.start()
    for index, cols in enumerate(pieces_of(key_ref, COPY_COLS)):
        key_copies[index].wait()
        value_copies[index].wait()
        for start in range(cols.start, cols.stop, HEAD_DIM):
            head = slice(start, start + HEAD_DIM)
            state_ref[head, :] = mm_tn(key_ref[:, head], value_ref[:, head]).astype(jnp.bfloat16)


def local_body(query_hbm, grad_hbm, gain_ref, key_ref, value_ref, query_ref, flipped_ref, scaled_ref, local_ref, grad_ref, query_sems, grad_sems):
    rows = query_ref.shape[0]
    query_copies = column_copies(query_hbm, query_ref, query_sems)
    grad_copies = column_copies(grad_hbm, grad_ref, grad_sems)
    for copy in query_copies + grad_copies:
        copy.start()
    for copy in query_copies + grad_copies:
        copy.wait()

    @pl.loop(0, query_ref.shape[1] // HEAD_DIM)
    def _(head):
        cols = pl.ds(pl.multiple_of(head * HEAD_DIM, HEAD_DIM), HEAD_DIM)
        scaled_ref[:, cols] = gain_ref[:, cols] * grad_ref[:, cols].astype(jnp.float32)
        flipped_ref[cols, :] = query_ref[:, cols].T
        for start in range(0, rows, BLOCK):
            end = start + BLOCK
            scores = mm_nt(query_ref[start:end, cols], key_ref[:end, cols])
            weights = masked(scores, start, 0, True)
            local_ref[start:end, cols] = mm(weights, value_ref[:end, cols])


def scan_body(reverse, block_ref, state_ref):
    count = block_ref.shape[0]
    total = jnp.zeros(block_ref.shape[1:], jnp.float32)
    order = range(count - 1, -1, -1) if reverse else range(count)
    for place in order:
        state_ref[place] = total.astype(jnp.bfloat16)
        total = total + block_ref[place].astype(jnp.float32)


def sums_body(query_ref, scaled_ref, local_ref, state_ref, attended_ref, sums_ref):
    for start in range(0, query_ref.shape[0], BLOCK):
        rows = slice(start, start + BLOCK)
        square = jnp.zeros((BLOCK, HEAD_DIM), jnp.float32)
        cross = jnp.zeros((BLOCK, HEAD_DIM), jnp.float32)
        for cols in head_columns(query_ref):
            attended = local_ref[rows, cols] + mm(query_ref[rows, cols], state_ref[cols, :])
            attended_ref[rows, cols] = attended
            square += attended * attended
            cross += scaled_ref[rows, cols] * attended
        sums_ref[0:1, rows] = jnp.sum(square.T, axis=0, keepdims=True)
        sums_ref[1:2, rows] = jnp.sum(cross.T, axis=0, keepdims=True)


def dout_body(width, flipped_ref, scaled_ref, attended_ref, sums_ref, dout_ref, own_ref):
    inverse = 1.0 / jnp.sqrt(sums_ref[0:1, :] / width + EPSILON)
    drop = sums_ref[1:2, :] * (inverse * inverse * inverse) / width
    factors = jnp.concatenate([inverse, drop] + [jnp.zeros_like(drop)] * 6, axis=0).T
    shape = (factors.shape[0], HEAD_DIM)
    inverse = jnp.broadcast_to(factors[:, 0:1], shape)
    drop = jnp.broadcast_to(factors[:, 1:2], shape)
    for cols in head_columns(dout_ref):
        dout = scaled_ref[:, cols] * inverse - attended_ref[:, cols] * drop
        dout = dout.astype(jnp.bfloat16)
        dout_ref[:, cols] = dout
        own_ref[cols, :] = mm(flipped_ref[cols, :], dout).astype(jnp.bfloat16)


def query_body(key_ref, value_ref, dout_ref, state_ref, out_hbm, out_ref, sems):
    rows = dout_ref.shape[0]
    copies = column_copies(out_ref, out_hbm, sems)
    for index, step in enumerate(pieces_of(out_ref, COPY_COLS)):
        for left in range(step.start, step.stop, HEAD_DIM):
            cols = slice(left, left + HEAD_DIM)
            for start in range(0, rows, BLOCK):
                end = start + BLOCK
                dout = dout_ref[start:end, cols]
                dscore = masked(mm_nt(dout, value_ref[:end, cols]), start, 0, True)
                grad = mm(dscore, key_ref[:end, cols]) + mm_nt(dout, state_ref[cols, :])
                out_ref[start:end, cols] = grad.astype(jnp.bfloat16)
        copies[index].start()
    for copy in copies:
        copy.wait()


def inner_body(query_ref, key_ref, value_ref, dout_ref, key_out, value_out):
    rows = dout_ref.shape[0]

    @pl.loop(0, dout_ref.shape[1] // HEAD_DIM)
    def _(head):
        cols = pl.ds(pl.multiple_of(head * HEAD_DIM, HEAD_DIM), HEAD_DIM)
        for start in range(0, rows, BLOCK):
            end = start + BLOCK
            query = query_ref[start:, cols]
            dout = dout_ref[start:, cols]
            dscore = masked(mm_nt(value_ref[start:end, cols], dout), 0, 0, False)
            key_out[start:end, cols] = mm(dscore, query)
            weights = masked(mm_nt(key_ref[start:end, cols], query), 0, 0, False)
            value_out[start:end, cols] = mm(weights, dout)


def final_body(key_ref, value_ref, key_part, value_part, state_ref, key_hbm, value_hbm, key_out, value_out, key_sems, value_sems):
    key_copies = column_copies(key_out, key_hbm, key_sems)
    value_copies = column_copies(value_out, value_hbm, value_sems)
    for index, step in enumerate(pieces_of(key_out, COPY_COLS)):
        for left in range(step.start, step.stop, HEAD_DIM):
            cols = slice(left, left + HEAD_DIM)
            state = state_ref[cols, :]
            key_grad = key_part[:, cols] + mm_nt(value_ref[:, cols], state)
            key_out[:, cols] = key_grad.astype(jnp.bfloat16)
            value_grad = value_part[:, cols] + mm(key_ref[:, cols], state)
            value_out[:, cols] = value_grad.astype(jnp.bfloat16)
        key_copies[index].start()
        value_copies[index].start()
    for copy in key_copies + value_copies:
        copy.wait()


def in_vmem(shape, dtype):
    return pltpu.VMEM(shape, dtype)


def local_call(body, in_args, outs, flops, hbm_args=(), scratch=(), aliases=None):
    args = [pltpu.with_memory_space_constraint(a, pltpu.HBM) for a in hbm_args]
    args += [pltpu.with_memory_space_constraint(a, pltpu.VMEM) for a in in_args]
    specs = [pl.BlockSpec(memory_space=pltpu.HBM)] * len(hbm_args)
    specs += [pl.BlockSpec(memory_space=pltpu.VMEM)] * len(in_args)
    out_specs = []
    for out in outs:
        space = pltpu.HBM if isinstance(out, jax.ShapeDtypeStruct) else pltpu.VMEM
        out_specs.append(pl.BlockSpec(memory_space=space))
    moved = sum(a.size * a.dtype.itemsize for a in args)
    return pl.pallas_call(
        body,
        in_specs=specs,
        out_specs=out_specs,
        out_shape=outs,
        scratch_shapes=scratch,
        input_output_aliases=aliases or {},
        compiler_params=pltpu.CompilerParams(vmem_limit_bytes=16 * MIB),
        cost_estimate=pl.CostEstimate(flops=flops, bytes_accessed=moved, transcendentals=0),
    )(*args)


def scan_blocks(blocks, reverse):
    (states,) = local_call(
        functools.partial(scan_body, reverse),
        [blocks],
        [in_vmem(blocks.shape, blocks.dtype)],
        blocks.size,
    )
    return states


def exchange(pieces, axis):
    return lax.all_to_all(pieces, axis, 0, 0)


def in_pieces(state, axis):
    count = lax.axis_size(axis)
    rows, cols = state.shape
    return state.reshape(count, rows // count, cols)


def shards(queries, keys, values, out_grad, gain):
    rows, width = queries.shape
    total_width = width * lax.axis_size("head")
    bf16, f32 = jnp.bfloat16, jnp.float32
    tokens, state = (rows, width), (width, HEAD_DIM)
    small = 2 * rows * width * HEAD_DIM
    large = 2 * rows * rows * width * 3 // 4
    gain_row = gain.reshape(1, width)
    copy_sems = [pltpu.SemaphoreType.DMA((width // COPY_COLS,))]
    kept, result = in_vmem(tokens, bf16), jax.ShapeDtypeStruct(tokens, bf16)

    key_vm, value_vm, own_kv = local_call(
        states_body,
        [],
        [kept, kept, in_vmem(state, bf16)],
        small,
        [keys, values],
        copy_sems * 2,
    )
    kv_blocks = exchange(in_pieces(own_kv, "seq"), "seq")
    kv_low = exchange(scan_blocks(kv_blocks, False), "seq").reshape(state)
    query_vm, flipped, scaled, local = local_call(
        local_body,
        [gain_row, key_vm, value_vm],
        [kept, in_vmem((width, rows), bf16), in_vmem(tokens, f32), in_vmem(tokens, f32)],
        2 * large,
        [queries, out_grad],
        [pltpu.VMEM(tokens, bf16)] + copy_sems * 2,
    )
    attended, sums = local_call(
        sums_body,
        [query_vm, scaled, local, kv_low],
        [in_vmem(tokens, f32), in_vmem((2, rows), f32)],
        small,
        aliases={2: 0},
    )
    sums = lax.psum(sums, "head")
    dout, own_grad = local_call(
        functools.partial(dout_body, total_width),
        [flipped, scaled, attended, sums],
        [kept, in_vmem(state, bf16)],
        small,
    )
    grad_blocks = exchange(in_pieces(own_grad, "seq"), "seq")
    (query_grad,) = local_call(
        query_body,
        [key_vm, value_vm, dout, kv_low],
        [result],
        2 * large + small,
        scratch=[pltpu.VMEM(tokens, bf16)] + copy_sems,
    )
    grad_blocks, query_grad = lax.optimization_barrier((grad_blocks, query_grad))
    grad_low = exchange(scan_blocks(grad_blocks, True), "seq").reshape(state)
    key_part, value_part = local_call(
        inner_body,
        [query_vm, key_vm, value_vm, dout],
        [in_vmem(tokens, f32)] * 2,
        4 * large,
    )
    key_grad, value_grad = local_call(
        final_body,
        [key_vm, value_vm, key_part, value_part, grad_low],
        [result] * 2,
        2 * small,
        scratch=[pltpu.VMEM(tokens, bf16)] * 2 + copy_sems * 2,
    )
    return query_grad, key_grad, value_grad


def solution(mesh):
    return jax.shard_map(
        shards,
        mesh=mesh,
        in_specs=(
            P("seq", "head"),
            P("seq", "head"),
            P("seq", "head"),
            P("seq", "head"),
            P("head"),
        ),
        out_specs=(P("seq", "head"), P("seq", "head"), P("seq", "head")),
        check_vma=False,
    )
```

```python
import functools

import jax
import jax.numpy as jnp
from jax import lax
from jax.experimental import pallas as pl
from jax.experimental.pallas import tpu as pltpu
from jax.sharding import PartitionSpec as P

HEAD_DIM = 128
BLOCK = 256
COPY_COLS = 256
EPSILON = 1e-06
MIB = 1 << 20


def mm(a, b):
    return lax.dot_general(a, b, (((1,), (0,)), ((), ())), preferred_element_type=jnp.float32)


def mm_nt(a, b):
    return lax.dot_general(a, b, (((1,), (1,)), ((), ())), preferred_element_type=jnp.float32)


def mm_tn(a, b):
    return lax.dot_general(a, b, (((0,), (0,)), ((), ())), preferred_element_type=jnp.float32)


def pieces_of(ref, size):
    return [slice(at, at + size) for at in range(0, ref.shape[1], size)]


def masked(scores, row_start, col_start, rows_first):
    rows = row_start + lax.broadcasted_iota(jnp.int32, scores.shape, 0)
    cols = col_start + lax.broadcasted_iota(jnp.int32, scores.shape, 1)
    keep = rows >= cols if rows_first else cols >= rows
    return jnp.where(keep, scores, 0.0).astype(jnp.bfloat16)


def column_copies(source, target, sems):
    copies = []
    for index, cols in enumerate(pieces_of(source, COPY_COLS)):
        copies.append(pltpu.make_async_copy(source.at[:, cols], target.at[:, cols], sems.at[index]))
    return copies


def start_all(*groups):
    for parts in zip(*groups):
        for part in parts:
            part.start()


def wait_all(*groups):
    for group in groups:
        for part in group:
            part.wait()


def whole_copy(source, target, sem):
    return pltpu.make_async_copy(source, target, sem)


def states_body(key_hbm, value_hbm, state_ref, key_ref, value_ref, key_sems, value_sems):
    key_copies = column_copies(key_hbm, key_ref, key_sems)
    value_copies = column_copies(value_hbm, value_ref, value_sems)
    start_all(key_copies, value_copies)
    for index, cols in enumerate(pieces_of(key_ref, COPY_COLS)):
        key_copies[index].wait()
        value_copies[index].wait()
        for start in range(cols.start, cols.stop, HEAD_DIM):
            head = slice(start, start + HEAD_DIM)
            state_ref[head, :] = mm_tn(key_ref[:, head], value_ref[:, head]).astype(jnp.bfloat16)


def local_body(
    query_hbm, key_hbm, value_hbm, grad_hbm,
    flipped_hbm, grad_flipped_hbm, flipped_ref, local_ref,
    query_ref, key_ref, value_ref, grad_ref, rest_ref, grad_flipped_ref, in_sems, out_sems,
):
    rows = query_ref.shape[0]
    sources = (query_hbm, key_hbm, value_hbm, grad_hbm)
    targets = (query_ref, key_ref, value_ref, grad_ref)
    loads = [whole_copy(a, b, in_sems.at[i]) for i, (a, b) in enumerate(zip(sources, targets))]
    start_all(loads)
    wait_all(loads)

    def one(head, target, row):
        cols = pl.ds(pl.multiple_of(head * HEAD_DIM, HEAD_DIM), HEAD_DIM)
        target[pl.ds(pl.multiple_of(row, HEAD_DIM), HEAD_DIM), :] = query_ref[:, cols].T
        grad_flipped_ref[cols, :] = grad_ref[:, cols].T
        value_flipped = value_ref[:, cols].T
        for start in range(0, rows, BLOCK):
            end = start + BLOCK
            scores = mm_nt(query_ref[start:end, cols], key_ref[:end, cols])
            weights = masked(scores, start, 0, True)
            local_ref[cols, start:end] = mm_nt(value_flipped[:, :end], weights)

    kept = flipped_ref.shape[0]

    @pl.loop(0, kept // HEAD_DIM)
    def _(head):
        one(head, flipped_ref, head * HEAD_DIM)

    @pl.loop(kept // HEAD_DIM, query_ref.shape[1] // HEAD_DIM)
    def _(head):
        one(head, rest_ref, head * HEAD_DIM - kept)

    stores = [
        whole_copy(flipped_ref, flipped_hbm.at[:kept, :], out_sems.at[0]),
        whole_copy(rest_ref, flipped_hbm.at[kept:, :], out_sems.at[1]),
        whole_copy(grad_flipped_ref, grad_flipped_hbm, out_sems.at[2]),
    ]
    start_all(stores)
    wait_all(stores)


def scan_body(reverse, block_ref, state_ref):
    count = block_ref.shape[0]
    total = jnp.zeros(block_ref.shape[1:], jnp.float32)
    order = range(count - 1, -1, -1) if reverse else range(count)
    for place in order:
        state_ref[place] = total.astype(jnp.bfloat16)
        total = total + block_ref[place].astype(jnp.float32)


def heads_of(ref):
    return [slice(at, at + HEAD_DIM) for at in range(0, ref.shape[0], HEAD_DIM)]


def scaled_grad(gain_ref, grad_ref, head):
    gain = jnp.broadcast_to(gain_ref[:, head], (HEAD_DIM, HEAD_DIM)).T
    gain = jnp.concatenate([gain] * (grad_ref.shape[1] // HEAD_DIM), axis=1)
    return gain * grad_ref[head, :].astype(jnp.float32)


def fold(values):
    parts = [values[at : at + 8, :] for at in range(0, values.shape[0], 8)]
    while len(parts) > 1:
        parts = [sum(parts[at + 1 : at + 2], parts[at]) for at in range(0, len(parts), 2)]
    return parts[0]


def sums_body(
    flipped_hbm, grad_hbm, gain_ref, flipped_ref, local_ref, state_ref,
    attended_ref, grad_ref, sums_ref, rest_ref, sems,
):
    kept = flipped_ref.shape[0]
    rest = whole_copy(flipped_hbm.at[kept:, :], rest_ref, sems.at[0])
    grad = whole_copy(grad_hbm, grad_ref, sems.at[1])
    rest.start()
    grad.start()
    square = cross = jnp.zeros((8, local_ref.shape[1]), jnp.float32)
    for head in heads_of(local_ref):
        if head.start == kept:
            rest.wait()
        if head.start < kept:
            flipped = flipped_ref[head, :]
        else:
            flipped = rest_ref[head.start - kept : head.stop - kept, :]
        attended = local_ref[head, :] + mm_tn(state_ref[head, :], flipped)
        attended_ref[head, :] = attended
        square += fold(attended * attended)
    grad.wait()
    for head in heads_of(local_ref):
        cross += fold(scaled_grad(gain_ref, grad_ref, head) * attended_ref[head, :])
    sums_ref[0:1, :] = jnp.sum(square, axis=0, keepdims=True)
    sums_ref[1:2, :] = jnp.sum(cross, axis=0, keepdims=True)


def dout_body(
    width, flipped_hbm, gain_ref, grad_ref, attended_ref, sums_ref, dout_ref, own_ref, flipped_ref, sems
):
    half = flipped_ref.shape[0] // 2
    halves = (slice(0, half), slice(half, 2 * half))
    loads = [
        whole_copy(flipped_hbm.at[part, :], flipped_ref.at[part, :], sems.at[index])
        for index, part in enumerate(halves)
    ]
    start_all(loads)
    inverse = 1.0 / jnp.sqrt(sums_ref[0:1, :] / width + EPSILON)
    drop = sums_ref[1:2, :] * (inverse * inverse * inverse) / width
    for head in heads_of(dout_ref):
        dout = scaled_grad(gain_ref, grad_ref, head) * inverse - attended_ref[head, :] * drop
        dout_ref[head, :] = dout.astype(jnp.bfloat16)
    for index, part in enumerate(halves):
        loads[index].wait()
        for start in range(part.start, part.stop, HEAD_DIM):
            head = slice(start, start + HEAD_DIM)
            own_ref[head, :] = mm_nt(flipped_ref[head, :], dout_ref[head, :]).astype(jnp.bfloat16)


def query_body(
    key_hbm, value_hbm, flipped_ref, state_ref, out_hbm, dout_ref, key_ref, value_ref, out_ref, in_sems, sems
):
    rows = dout_ref.shape[0]
    loads = [
        whole_copy(key_hbm, key_ref, in_sems.at[0]),
        whole_copy(value_hbm, value_ref, in_sems.at[1]),
    ]
    start_all(loads)
    for head in heads_of(flipped_ref):
        dout_ref[:, head] = flipped_ref[head, :].T
    wait_all(loads)

    @pl.loop(0, dout_ref.shape[1] // HEAD_DIM)
    def _(head):
        cols = pl.ds(pl.multiple_of(head * HEAD_DIM, HEAD_DIM), HEAD_DIM)
        for start in range(0, rows, BLOCK):
            end = start + BLOCK
            dout = dout_ref[start:end, cols]
            dscore = masked(mm_nt(dout, value_ref[:end, cols]), start, 0, True)
            grad = mm(dscore, key_ref[:end, cols]) + mm_nt(dout, state_ref[cols, :])
            out_ref[start:end, cols] = grad.astype(jnp.bfloat16)

    stores = column_copies(out_ref, out_hbm, sems)
    start_all(stores)
    wait_all(stores)


def inner_body(
    query_hbm, key_hbm, value_hbm, dout_ref, key_out, value_out, kept_ref, query_ref, key_ref, value_ref, sems
):
    rows = dout_ref.shape[0]
    loads = [
        whole_copy(query_hbm, query_ref, sems.at[0]),
        whole_copy(key_hbm, key_ref, sems.at[1]),
        whole_copy(value_hbm, value_ref, sems.at[2]),
        whole_copy(value_hbm.at[:, : kept_ref.shape[1]], kept_ref, sems.at[3]),
    ]
    start_all(loads)
    wait_all(loads)

    @pl.loop(0, dout_ref.shape[1] // HEAD_DIM)
    def _(head):
        cols = pl.ds(pl.multiple_of(head * HEAD_DIM, HEAD_DIM), HEAD_DIM)
        for start in range(0, rows, BLOCK):
            end = start + BLOCK
            query = query_ref[start:, cols]
            dout = dout_ref[start:, cols]
            dscore = masked(mm_nt(value_ref[start:end, cols], dout), 0, 0, False)
            key_out[start:end, cols] = mm(dscore, query).astype(jnp.bfloat16)
            weights = masked(mm_nt(key_ref[start:end, cols], query), 0, 0, False)
            value_out[start:end, cols] = mm(weights, dout).astype(jnp.bfloat16)


def final_body(
    key_hbm, value_hbm, kept_ref, key_part, value_part, state_ref, key_out_hbm, value_out_hbm,
    key_ref, rest_ref, key_out, value_out, key_sems, value_sems, in_sems,
):
    kept = kept_ref.shape[1]
    rest = whole_copy(value_hbm.at[:, kept:], rest_ref, in_sems.at[0])
    keys = column_copies(key_hbm, key_ref, in_sems.at[1:])
    rest.start()
    start_all(keys)
    key_stores = column_copies(key_out, key_out_hbm, key_sems)
    value_stores = column_copies(value_out, value_out_hbm, value_sems)
    for index, step in enumerate(pieces_of(key_out, COPY_COLS)):
        if step.start == kept:
            rest.wait()
        for left in range(step.start, step.stop, HEAD_DIM):
            cols = slice(left, left + HEAD_DIM)
            if left < kept:
                value = kept_ref[:, cols]
            else:
                value = rest_ref[:, left - kept : left - kept + HEAD_DIM]
            grad = key_part[:, cols].astype(jnp.float32) + mm_nt(value, state_ref[cols, :])
            key_out[:, cols] = grad.astype(jnp.bfloat16)
        key_stores[index].start()
    for index, step in enumerate(pieces_of(value_out, COPY_COLS)):
        keys[index].wait()
        for left in range(step.start, step.stop, HEAD_DIM):
            cols = slice(left, left + HEAD_DIM)
            grad = value_part[:, cols].astype(jnp.float32) + mm(key_ref[:, cols], state_ref[cols, :])
            value_out[:, cols] = grad.astype(jnp.bfloat16)
        value_stores[index].start()
    wait_all(key_stores, value_stores)


def local_call(body, in_args, outs, flops, hbm_args=(), scratch=(), aliases=None):
    args = [pltpu.with_memory_space_constraint(a, pltpu.HBM) for a in hbm_args]
    args += [pltpu.with_memory_space_constraint(a, pltpu.VMEM) for a in in_args]
    specs = [pl.BlockSpec(memory_space=pltpu.HBM)] * len(hbm_args)
    specs += [pl.BlockSpec(memory_space=pltpu.VMEM)] * len(in_args)
    out_specs = []
    for out in outs:
        out_specs.append(pl.BlockSpec(memory_space=out.memory_space))
    moved = sum(a.size * a.dtype.itemsize for a in args)
    return pl.pallas_call(
        body,
        in_specs=specs,
        out_specs=out_specs,
        out_shape=outs,
        scratch_shapes=scratch,
        input_output_aliases=aliases or {},
        compiler_params=pltpu.CompilerParams(vmem_limit_bytes=16 * MIB),
        cost_estimate=pl.CostEstimate(flops=flops, bytes_accessed=moved, transcendentals=0),
    )(*args)


def scan_blocks(blocks, reverse):
    (states,) = local_call(
        functools.partial(scan_body, reverse),
        [blocks],
        [pltpu.VMEM(blocks.shape, blocks.dtype)],
        blocks.size,
    )
    return states


def exchange(pieces, axis):
    return lax.all_to_all(pieces, axis, 0, 0)


def in_pieces(state, axis):
    count = lax.axis_size(axis)
    rows, cols = state.shape
    return state.reshape(count, rows // count, cols)


def shards(queries, keys, values, out_grad, gain):
    rows, width = queries.shape
    total_width = width * lax.axis_size("head")
    bf16, f32 = jnp.bfloat16, jnp.float32
    tokens, state = (rows, width), (width, HEAD_DIM)
    small = 2 * rows * width * HEAD_DIM
    large = 2 * rows * rows * width * 3 // 4
    gain_row = gain.reshape(1, width)
    flat = (width, rows)
    dma = pltpu.SemaphoreType.DMA
    chunks = width // COPY_COLS
    kept = width * 3 // 4 // HEAD_DIM * HEAD_DIM
    half = width // 2 // COPY_COLS * COPY_COLS
    vm, hbm = pltpu.VMEM, pltpu.HBM

    (own_kv,) = local_call(
        states_body,
        [],
        [vm(state, bf16)],
        small,
        [keys, values],
        [vm(tokens, bf16)] * 2 + [dma((chunks,))] * 2,
    )
    kv_blocks = exchange(in_pieces(own_kv, "seq"), "seq")
    kv_low = exchange(scan_blocks(kv_blocks, False), "seq").reshape(state)
    flipped, grad_flipped, flipped_vm, local = local_call(
        local_body,
        [],
        [hbm(flat, bf16), hbm(flat, bf16), vm((kept, rows), bf16), vm(flat, f32)],
        2 * large,
        [queries, keys, values, out_grad],
        [vm(tokens, bf16)] * 4
        + [vm((width - kept, rows), bf16), vm(flat, bf16), dma((4,)), dma((3,))],
    )
    attended, grad_vm, sums = local_call(
        sums_body,
        [gain_row, flipped_vm, local, kv_low],
        [vm(flat, f32), vm(flat, bf16), vm((2, rows), f32)],
        small,
        [flipped, grad_flipped],
        [vm((width - kept, rows), bf16), dma((2,))],
        {4: 0},
    )
    sums = lax.psum(sums, "head")
    dout_flipped, own_grad = local_call(
        functools.partial(dout_body, total_width),
        [gain_row, grad_vm, attended, sums],
        [vm(flat, bf16), vm(state, bf16)],
        small,
        [flipped],
        [vm(flat, bf16), dma((2,))],
    )
    grad_blocks = exchange(in_pieces(own_grad, "seq"), "seq")
    query_grad, dout = local_call(
        query_body,
        [dout_flipped, kv_low],
        [hbm(tokens, bf16), vm(tokens, bf16)],
        2 * large + small,
        [keys, values],
        [vm(tokens, bf16)] * 3 + [dma((2,)), dma((chunks,))],
    )
    grad_blocks, query_grad, dout = lax.optimization_barrier((grad_blocks, query_grad, dout))
    grad_low = exchange(scan_blocks(grad_blocks, True), "seq").reshape(state)
    key_part, value_part, value_kept = local_call(
        inner_body,
        [dout],
        [vm(tokens, bf16), vm(tokens, bf16), vm((rows, half), bf16)],
        4 * large,
        [queries, keys, values],
        [vm(tokens, bf16)] * 3 + [dma((4,))],
    )
    key_grad, value_grad = local_call(
        final_body,
        [value_kept, key_part, value_part, grad_low],
        [hbm(tokens, bf16)] * 2,
        2 * small,
        [keys, values],
        [vm(tokens, bf16), vm((rows, width - half), bf16), vm(tokens, bf16), vm(tokens, bf16)]
        + [dma((chunks,))] * 2
        + [dma((chunks + 1,))],
    )
    return query_grad, key_grad, value_grad


def solution(mesh):
    return jax.shard_map(
        shards,
        mesh=mesh,
        in_specs=(
            P("seq", "head"),
            P("seq", "head"),
            P("seq", "head"),
            P("seq", "head"),
            P("head"),
        ),
        out_specs=(P("seq", "head"), P("seq", "head"), P("seq", "head")),
        check_vma=False,
    )
```

```python
import functools

import jax
import jax.numpy as jnp
from jax import lax
from jax.experimental import pallas as pl
from jax.experimental.pallas import tpu as pltpu
from jax.sharding import PartitionSpec as P

HEAD_DIM = 128
BLOCK = 256
COPY_COLS = 256
EPSILON = 1e-06
MIB = 1 << 20


def mm(a, b):
    return lax.dot_general(a, b, (((1,), (0,)), ((), ())), preferred_element_type=jnp.float32)


def mm_nt(a, b):
    return lax.dot_general(a, b, (((1,), (1,)), ((), ())), preferred_element_type=jnp.float32)


def mm_tn(a, b):
    return lax.dot_general(a, b, (((0,), (0,)), ((), ())), preferred_element_type=jnp.float32)


def pieces_of(ref, size):
    return [slice(at, at + size) for at in range(0, ref.shape[1], size)]


def masked(scores, row_start, col_start, rows_first):
    rows = row_start + lax.broadcasted_iota(jnp.int32, scores.shape, 0)
    cols = col_start + lax.broadcasted_iota(jnp.int32, scores.shape, 1)
    keep = rows >= cols if rows_first else cols >= rows
    return jnp.where(keep, scores, 0.0).astype(jnp.bfloat16)


def column_copies(source, target, sems):
    copies = []
    for index, cols in enumerate(pieces_of(source, COPY_COLS)):
        copies.append(pltpu.make_async_copy(source.at[:, cols], target.at[:, cols], sems.at[index]))
    return copies


def start_all(*groups):
    for parts in zip(*groups):
        for part in parts:
            part.start()


def wait_all(*groups):
    for group in groups:
        for part in group:
            part.wait()


def states_body(key_hbm, value_hbm, state_ref, key_ref, value_ref, key_sems, value_sems):
    key_copies = column_copies(key_hbm, key_ref, key_sems)
    value_copies = column_copies(value_hbm, value_ref, value_sems)
    start_all(key_copies, value_copies)
    for index, cols in enumerate(pieces_of(key_ref, COPY_COLS)):
        key_copies[index].wait()
        value_copies[index].wait()
        for start in range(cols.start, cols.stop, HEAD_DIM):
            head = slice(start, start + HEAD_DIM)
            state_ref[head, :] = mm_tn(key_ref[:, head], value_ref[:, head]).astype(jnp.bfloat16)


def flip_body(query_hbm, grad_hbm, flipped_ref, grad_flipped_ref, query_ref, grad_ref, query_sems, grad_sems):
    loads = (
        (query_ref, flipped_ref, column_copies(query_hbm, query_ref, query_sems)),
        (grad_ref, grad_flipped_ref, column_copies(grad_hbm, grad_ref, grad_sems)),
    )
    start_all(loads[0][2])
    start_all(loads[1][2])
    for source, target, copies in loads:
        for copy, cols in zip(copies, pieces_of(source, COPY_COLS)):
            copy.wait()
            target[cols, :] = source[:, cols].T


def local_body(key_hbm, value_hbm, flipped_ref, local_ref, key_ref, value_ref, key_sems, value_sems):
    rows = key_ref.shape[0]
    key_copies = column_copies(key_hbm, key_ref, key_sems)
    value_copies = column_copies(value_hbm, value_ref, value_sems)
    start_all(key_copies, value_copies)
    for index, step in enumerate(pieces_of(key_ref, COPY_COLS)):
        key_copies[index].wait()
        value_copies[index].wait()
        for left in range(step.start, step.stop, HEAD_DIM):
            cols = slice(left, left + HEAD_DIM)
            for start in range(0, rows, BLOCK):
                end = start + BLOCK
                scores = mm(key_ref[:end, cols], flipped_ref[cols, start:end])
                weights = masked(scores, 0, start, False)
                local = mm_tn(value_ref[:end, cols], weights)
                local_ref[cols, start:end] = local.astype(jnp.bfloat16)


def scan_body(reverse, block_ref, state_ref):
    count = block_ref.shape[0]
    total = jnp.zeros(block_ref.shape[1:], jnp.float32)
    order = range(count - 1, -1, -1) if reverse else range(count)
    for place in order:
        state_ref[place] = total.astype(jnp.bfloat16)
        total = total + block_ref[place].astype(jnp.float32)


def heads_of(ref):
    return [slice(at, at + HEAD_DIM) for at in range(0, ref.shape[0], HEAD_DIM)]


def scaled_grad(gain_ref, grad_ref, head):
    gain = jnp.broadcast_to(gain_ref[:, head], (HEAD_DIM, HEAD_DIM)).T
    gain = jnp.concatenate([gain] * (grad_ref.shape[1] // HEAD_DIM), axis=1)
    return gain * grad_ref[head, :].astype(jnp.float32)


def fold(values):
    parts = [values[at : at + 8, :] for at in range(0, values.shape[0], 8)]
    while len(parts) > 1:
        parts = [sum(parts[at + 1 : at + 2], parts[at]) for at in range(0, len(parts), 2)]
    return parts[0]


def sums_body(gain_ref, flipped_ref, grad_ref, local_ref, state_ref, attended_ref, sums_ref):
    square = cross = jnp.zeros((8, local_ref.shape[1]), jnp.float32)
    for head in heads_of(local_ref):
        attended = mm_tn(state_ref[head, :], flipped_ref[head, :])
        attended = attended + attended_ref[head, :].astype(jnp.float32)
        attended_ref[head, :] = attended.astype(jnp.bfloat16)
        square += fold(attended * attended)
        cross += fold(scaled_grad(gain_ref, grad_ref, head) * attended)
    sums_ref[0:1, :] = jnp.sum(square, axis=0, keepdims=True)
    sums_ref[1:2, :] = jnp.sum(cross, axis=0, keepdims=True)


def dout_body(width, gain_ref, flipped_ref, grad_ref, attended_ref, sums_ref, dout_ref, own_ref):
    inverse = 1.0 / jnp.sqrt(sums_ref[0:1, :] / width + EPSILON)
    drop = sums_ref[1:2, :] * (inverse * inverse * inverse) / width
    for head in heads_of(dout_ref):
        attended = dout_ref[head, :].astype(jnp.float32)
        dout = scaled_grad(gain_ref, grad_ref, head) * inverse - attended * drop
        dout = dout.astype(jnp.bfloat16)
        dout_ref[head, :] = dout
        own_ref[head, :] = mm_nt(flipped_ref[head, :], dout).astype(jnp.bfloat16)


def query_body(
    key_hbm, value_hbm, flipped_ref, state_ref, out_hbm, dout_ref,
    key_ref, value_ref, out_ref, key_sems, value_sems, out_sems,
):
    rows = dout_ref.shape[0]
    key_copies = column_copies(key_hbm, key_ref, key_sems)
    value_copies = column_copies(value_hbm, value_ref, value_sems)
    start_all(key_copies, value_copies)
    for head in heads_of(flipped_ref):
        dout_ref[:, head] = flipped_ref[head, :].T
    stores = column_copies(out_ref, out_hbm, out_sems)
    for index, step in enumerate(pieces_of(out_ref, COPY_COLS)):
        key_copies[index].wait()
        value_copies[index].wait()
        for left in range(step.start, step.stop, HEAD_DIM):
            cols = slice(left, left + HEAD_DIM)
            for start in range(0, rows, BLOCK):
                end = start + BLOCK
                dout = dout_ref[start:end, cols]
                dscore = masked(mm_nt(dout, value_ref[:end, cols]), start, 0, True)
                grad = mm(dscore, key_ref[:end, cols]) + mm_nt(dout, state_ref[cols, :])
                out_ref[start:end, cols] = grad.astype(jnp.bfloat16)
        stores[index].start()
    wait_all(stores)


def inner_body(
    query_hbm, key_hbm, value_hbm, dout_ref, key_out, value_out, value_ref,
    query_ref, key_ref, query_sems, key_sems, value_sems,
):
    rows = value_out.shape[0]
    loads = (
        column_copies(query_hbm, query_ref, query_sems),
        column_copies(key_hbm, key_ref, key_sems),
        column_copies(value_hbm, value_ref, value_sems),
    )
    start_all(*loads)
    for index, step in enumerate(pieces_of(key_out, COPY_COLS)):
        for load in loads:
            load[index].wait()
        for left in range(step.start, step.stop, HEAD_DIM):
            cols = slice(left, left + HEAD_DIM)
            dout_all = value_out[:, cols]
            for start in range(0, rows, BLOCK):
                end = start + BLOCK
                query = query_ref[start:, cols]
                dout = dout_all[start:, :]
                dscore = masked(mm_nt(value_ref[start:end, cols], dout), 0, 0, False)
                key_out[start:end, cols] = mm(dscore, query).astype(jnp.bfloat16)
                weights = masked(mm_nt(key_ref[start:end, cols], query), 0, 0, False)
                value_out[start:end, cols] = mm(weights, dout).astype(jnp.bfloat16)


def final_body(
    key_hbm, value_ref, key_part, value_part, state_ref, key_out_hbm, value_out_hbm,
    key_ref, key_out, value_out, in_sems, key_sems, value_sems,
):
    keys = column_copies(key_hbm, key_ref, in_sems)
    start_all(keys)
    key_stores = column_copies(key_out, key_out_hbm, key_sems)
    value_stores = column_copies(value_out, value_out_hbm, value_sems)
    for index, step in enumerate(pieces_of(key_out, COPY_COLS)):
        for left in range(step.start, step.stop, HEAD_DIM):
            cols = slice(left, left + HEAD_DIM)
            grad = key_part[:, cols].astype(jnp.float32) + mm_nt(value_ref[:, cols], state_ref[cols, :])
            key_out[:, cols] = grad.astype(jnp.bfloat16)
        key_stores[index].start()
    for index, step in enumerate(pieces_of(value_out, COPY_COLS)):
        keys[index].wait()
        for left in range(step.start, step.stop, HEAD_DIM):
            cols = slice(left, left + HEAD_DIM)
            grad = value_part[:, cols].astype(jnp.float32) + mm(key_ref[:, cols], state_ref[cols, :])
            value_out[:, cols] = grad.astype(jnp.bfloat16)
        value_stores[index].start()
    wait_all(key_stores, value_stores)


def local_call(body, in_args, outs, flops, hbm_args=(), scratch=(), aliases=None):
    args = [pltpu.with_memory_space_constraint(a, pltpu.HBM) for a in hbm_args]
    args += [pltpu.with_memory_space_constraint(a, pltpu.VMEM) for a in in_args]
    specs = [pl.BlockSpec(memory_space=pltpu.HBM)] * len(hbm_args)
    specs += [pl.BlockSpec(memory_space=pltpu.VMEM)] * len(in_args)
    out_specs = []
    for out in outs:
        out_specs.append(pl.BlockSpec(memory_space=out.memory_space))
    moved = sum(a.size * a.dtype.itemsize for a in args)
    return pl.pallas_call(
        body,
        in_specs=specs,
        out_specs=out_specs,
        out_shape=outs,
        scratch_shapes=scratch,
        input_output_aliases=aliases or {},
        compiler_params=pltpu.CompilerParams(vmem_limit_bytes=16 * MIB),
        cost_estimate=pl.CostEstimate(flops=flops, bytes_accessed=moved, transcendentals=0),
    )(*args)


def scan_blocks(blocks, reverse):
    (states,) = local_call(
        functools.partial(scan_body, reverse),
        [blocks],
        [pltpu.VMEM(blocks.shape, blocks.dtype)],
        blocks.size,
    )
    return states


def exchange(pieces, axis):
    return lax.all_to_all(pieces, axis, 0, 0)


def in_pieces(state, axis):
    count = lax.axis_size(axis)
    rows, cols = state.shape
    return state.reshape(count, rows // count, cols)


def shards(queries, keys, values, out_grad, gain):
    rows, width = queries.shape
    total_width = width * lax.axis_size("head")
    bf16, f32 = jnp.bfloat16, jnp.float32
    tokens, state = (rows, width), (width, HEAD_DIM)
    small = 2 * rows * width * HEAD_DIM
    large = 2 * rows * rows * width * 3 // 4
    gain_row = gain.reshape(1, width)
    flat = (width, rows)
    chunks = pltpu.SemaphoreType.DMA((width // COPY_COLS,))
    vm, hbm = pltpu.VMEM, pltpu.HBM
    rows_vm, flat_vm, state_vm = vm(tokens, bf16), vm(flat, bf16), vm(state, bf16)

    (own_kv,) = local_call(
        states_body, [], [state_vm], small, [keys, values], [rows_vm] * 2 + [chunks] * 2
    )
    kv_blocks = exchange(in_pieces(own_kv, "seq"), "seq")
    flipped, grad_flipped = local_call(
        flip_body, [], [flat_vm] * 2, large, [queries, out_grad], [rows_vm] * 2 + [chunks] * 2
    )
    kv_blocks, flipped, grad_flipped = lax.optimization_barrier((kv_blocks, flipped, grad_flipped))
    kv_low = exchange(scan_blocks(kv_blocks, False), "seq").reshape(state)
    (local,) = local_call(
        local_body, [flipped], [flat_vm], 2 * large, [keys, values], [rows_vm] * 2 + [chunks] * 2
    )
    attended, sums = local_call(
        sums_body,
        [gain_row, flipped, grad_flipped, local, kv_low],
        [flat_vm, vm((2, rows), f32)],
        small,
        aliases={3: 0},
    )
    sums = lax.psum(sums, "head")
    dout_flipped, own_grad = local_call(
        functools.partial(dout_body, total_width),
        [gain_row, flipped, grad_flipped, attended, sums],
        [flat_vm, state_vm],
        small,
        aliases={3: 0},
    )
    grad_blocks = exchange(in_pieces(own_grad, "seq"), "seq")
    query_grad, dout = local_call(
        query_body,
        [dout_flipped, kv_low],
        [hbm(tokens, bf16), rows_vm],
        2 * large + small,
        [keys, values],
        [rows_vm] * 3 + [chunks] * 3,
    )
    grad_blocks, query_grad, dout = lax.optimization_barrier((grad_blocks, query_grad, dout))
    grad_low = exchange(scan_blocks(grad_blocks, True), "seq").reshape(state)
    key_part, value_part, value_kept = local_call(
        inner_body,
        [dout],
        [rows_vm] * 3,
        4 * large,
        [queries, keys, values],
        [rows_vm] * 2 + [chunks] * 3,
        {3: 1},
    )
    key_grad, value_grad = local_call(
        final_body,
        [value_kept, key_part, value_part, grad_low],
        [hbm(tokens, bf16)] * 2,
        2 * small,
        [keys],
        [rows_vm] * 3 + [chunks] * 3,
    )
    return query_grad, key_grad, value_grad


def solution(mesh):
    return jax.shard_map(
        shards,
        mesh=mesh,
        in_specs=(
            P("seq", "head"),
            P("seq", "head"),
            P("seq", "head"),
            P("seq", "head"),
            P("head"),
        ),
        out_specs=(P("seq", "head"), P("seq", "head"), P("seq", "head")),
        check_vma=False,
    )
```

```python
import functools

import jax
import jax.numpy as jnp
from jax import lax
from jax.experimental import pallas as pl
from jax.experimental.pallas import tpu as pltpu
from jax.sharding import PartitionSpec as P

HEAD_DIM = 128
BLOCK = 256
COPY_COLS = 256
EPSILON = 1e-06
MIB = 1 << 20


def mm(a, b):
    return lax.dot_general(a, b, (((1,), (0,)), ((), ())), preferred_element_type=jnp.float32)


def mm_nt(a, b):
    return lax.dot_general(a, b, (((1,), (1,)), ((), ())), preferred_element_type=jnp.float32)


def mm_tn(a, b):
    return lax.dot_general(a, b, (((0,), (0,)), ((), ())), preferred_element_type=jnp.float32)


def pieces_of(ref, size):
    return [slice(at, at + size) for at in range(0, ref.shape[1], size)]


def masked(scores, row_start, col_start, rows_first):
    rows = row_start + lax.broadcasted_iota(jnp.int32, scores.shape, 0)
    cols = col_start + lax.broadcasted_iota(jnp.int32, scores.shape, 1)
    keep = rows >= cols if rows_first else cols >= rows
    return jnp.where(keep, scores, 0.0).astype(jnp.bfloat16)


def column_copies(source, target, sems):
    copies = []
    for index, cols in enumerate(pieces_of(source, COPY_COLS)):
        copies.append(pltpu.make_async_copy(source.at[:, cols], target.at[:, cols], sems.at[index]))
    return copies


def start_all(*groups):
    for parts in zip(*groups):
        for part in parts:
            part.start()


def wait_all(*groups):
    for group in groups:
        for part in group:
            part.wait()


def states_body(key_hbm, value_hbm, state_ref, key_ref, value_ref, key_sems, value_sems):
    key_copies = column_copies(key_hbm, key_ref, key_sems)
    value_copies = column_copies(value_hbm, value_ref, value_sems)
    start_all(key_copies, value_copies)
    for index, cols in enumerate(pieces_of(key_ref, COPY_COLS)):
        key_copies[index].wait()
        value_copies[index].wait()
        for start in range(cols.start, cols.stop, HEAD_DIM):
            head = slice(start, start + HEAD_DIM)
            state_ref[head, :] = mm_tn(key_ref[:, head], value_ref[:, head]).astype(jnp.bfloat16)


def flip_body(query_hbm, grad_hbm, flipped_ref, grad_flipped_ref, query_ref, grad_ref, query_sems, grad_sems):
    loads = (
        (query_ref, flipped_ref, column_copies(query_hbm, query_ref, query_sems)),
        (grad_ref, grad_flipped_ref, column_copies(grad_hbm, grad_ref, grad_sems)),
    )
    start_all(loads[0][2])
    start_all(loads[1][2])
    for source, target, copies in loads:
        for copy, cols in zip(copies, pieces_of(source, COPY_COLS)):
            copy.wait()
            target[cols, :] = source[:, cols].T


def local_body(key_hbm, value_hbm, flipped_ref, local_ref, key_ref, value_ref, key_sems, value_sems):
    rows = key_ref.shape[0]
    key_copies = column_copies(key_hbm, key_ref, key_sems)
    value_copies = column_copies(value_hbm, value_ref, value_sems)
    start_all(key_copies, value_copies)
    for index, step in enumerate(pieces_of(key_ref, COPY_COLS)):
        key_copies[index].wait()
        value_copies[index].wait()
        for left in range(step.start, step.stop, HEAD_DIM):
            cols = slice(left, left + HEAD_DIM)
            for start in range(0, rows, BLOCK):
                end = start + BLOCK
                scores = mm(key_ref[:end, cols], flipped_ref[cols, start:end])
                weights = masked(scores, 0, start, False)
                local = mm_tn(value_ref[:end, cols], weights)
                local_ref[cols, start:end] = local.astype(jnp.bfloat16)


def scan_body(reverse, block_ref, state_ref):
    count = block_ref.shape[0]
    total = jnp.zeros(block_ref.shape[1:], jnp.float32)
    order = range(count - 1, -1, -1) if reverse else range(count)
    for place in order:
        state_ref[place] = total.astype(jnp.bfloat16)
        total = total + block_ref[place].astype(jnp.float32)


def heads_of(ref):
    return [slice(at, at + HEAD_DIM) for at in range(0, ref.shape[0], HEAD_DIM)]


def scaled_grad(gain_ref, grad_ref, head):
    gain = jnp.broadcast_to(gain_ref[:, head], (HEAD_DIM, HEAD_DIM)).T
    gain = jnp.concatenate([gain] * (grad_ref.shape[1] // HEAD_DIM), axis=1)
    return gain * grad_ref[head, :].astype(jnp.float32)


def fold(values):
    parts = [values[at : at + 8, :] for at in range(0, values.shape[0], 8)]
    while len(parts) > 1:
        parts = [sum(parts[at + 1 : at + 2], parts[at]) for at in range(0, len(parts), 2)]
    return parts[0]


def sums_body(
    gain_ref, flipped_ref, grad_ref, local_ref, state_ref, attended_ref, sums_ref, state_hbm, sem
):
    copy = pltpu.make_async_copy(state_ref, state_hbm, sem.at[0])
    copy.start()
    square = cross = jnp.zeros((8, local_ref.shape[1]), jnp.float32)
    for head in heads_of(local_ref):
        attended = mm_tn(state_ref[head, :], flipped_ref[head, :])
        attended = attended + attended_ref[head, :].astype(jnp.float32)
        attended_ref[head, :] = attended.astype(jnp.bfloat16)
        square += fold(attended * attended)
        cross += fold(scaled_grad(gain_ref, grad_ref, head) * attended)
    square = jnp.sum(square, axis=0, keepdims=True)
    cross = jnp.sum(cross, axis=0, keepdims=True)
    for group in range(sums_ref.shape[0]):
        sums_ref[group, 0:1, :] = square
        sums_ref[group, 1:2, :] = cross
    copy.wait()


def dout_body(width, gain_ref, flipped_ref, grad_ref, attended_ref, sums_ref, dout_ref, own_ref):
    sums = sum(sums_ref[group] for group in range(sums_ref.shape[0]))
    inverse = 1.0 / jnp.sqrt(sums[0:1, :] / width + EPSILON)
    drop = sums[1:2, :] * (inverse * inverse * inverse) / width
    for head in heads_of(dout_ref):
        attended = dout_ref[head, :].astype(jnp.float32)
        dout = scaled_grad(gain_ref, grad_ref, head) * inverse - attended * drop
        dout = dout.astype(jnp.bfloat16)
        dout_ref[head, :] = dout
        own_ref[head, :] = mm_nt(flipped_ref[head, :], dout).astype(jnp.bfloat16)


def query_body(
    key_hbm, value_hbm, state_hbm, flipped_ref, out_hbm, dout_ref,
    key_ref, value_ref, state_ref, out_ref, key_sems, value_sems, out_sems, state_sem,
):
    rows = dout_ref.shape[0]
    key_copies = column_copies(key_hbm, key_ref, key_sems)
    value_copies = column_copies(value_hbm, value_ref, value_sems)
    state_copy = pltpu.make_async_copy(state_hbm, state_ref, state_sem.at[0])
    state_copy.start()
    start_all(key_copies, value_copies)
    for head in heads_of(flipped_ref):
        dout_ref[:, head] = flipped_ref[head, :].T
    state_copy.wait()
    stores = column_copies(out_ref, out_hbm, out_sems)
    for index, step in enumerate(pieces_of(out_ref, COPY_COLS)):
        key_copies[index].wait()
        value_copies[index].wait()
        for left in range(step.start, step.stop, HEAD_DIM):
            cols = slice(left, left + HEAD_DIM)
            for start in range(0, rows, BLOCK):
                end = start + BLOCK
                dout = dout_ref[start:end, cols]
                dscore = masked(mm_nt(dout, value_ref[:end, cols]), start, 0, True)
                grad = mm(dscore, key_ref[:end, cols]) + mm_nt(dout, state_ref[cols, :])
                out_ref[start:end, cols] = grad.astype(jnp.bfloat16)
        stores[index].start()
    wait_all(stores)


def inner_body(
    query_hbm, key_hbm, value_hbm, dout_ref, key_out, value_out, value_ref,
    query_ref, key_ref, query_sems, key_sems, value_sems,
):
    rows = value_out.shape[0]
    loads = (
        column_copies(query_hbm, query_ref, query_sems),
        column_copies(key_hbm, key_ref, key_sems),
        column_copies(value_hbm, value_ref, value_sems),
    )
    start_all(*loads)
    for index, step in enumerate(pieces_of(key_out, COPY_COLS)):
        for load in loads:
            load[index].wait()
        for left in range(step.start, step.stop, HEAD_DIM):
            cols = slice(left, left + HEAD_DIM)
            dout_all = value_out[:, cols]
            for start in range(0, rows, BLOCK):
                end = start + BLOCK
                query = query_ref[start:, cols]
                dout = dout_all[start:, :]
                dscore = masked(mm_nt(value_ref[start:end, cols], dout), 0, 0, False)
                key_out[start:end, cols] = mm(dscore, query).astype(jnp.bfloat16)
                weights = masked(mm_nt(key_ref[start:end, cols], query), 0, 0, False)
                value_out[start:end, cols] = mm(weights, dout).astype(jnp.bfloat16)


def final_body(
    key_hbm, value_ref, key_part, value_part, state_ref, key_out_hbm, value_out_hbm,
    key_ref, key_out, value_out, in_sems, key_sems, value_sems,
):
    keys = column_copies(key_hbm, key_ref, in_sems)
    start_all(keys)
    key_stores = column_copies(key_out, key_out_hbm, key_sems)
    value_stores = column_copies(value_out, value_out_hbm, value_sems)
    for index, step in enumerate(pieces_of(key_out, COPY_COLS)):
        for left in range(step.start, step.stop, HEAD_DIM):
            cols = slice(left, left + HEAD_DIM)
            grad = key_part[:, cols].astype(jnp.float32) + mm_nt(value_ref[:, cols], state_ref[cols, :])
            key_out[:, cols] = grad.astype(jnp.bfloat16)
        key_stores[index].start()
    for index, step in enumerate(pieces_of(value_out, COPY_COLS)):
        keys[index].wait()
        for left in range(step.start, step.stop, HEAD_DIM):
            cols = slice(left, left + HEAD_DIM)
            grad = value_part[:, cols].astype(jnp.float32) + mm(key_ref[:, cols], state_ref[cols, :])
            value_out[:, cols] = grad.astype(jnp.bfloat16)
        value_stores[index].start()
    wait_all(key_stores, value_stores)


def local_call(body, in_args, outs, flops, hbm_args=(), scratch=(), aliases=None):
    args = [pltpu.with_memory_space_constraint(a, pltpu.HBM) for a in hbm_args]
    args += [pltpu.with_memory_space_constraint(a, pltpu.VMEM) for a in in_args]
    specs = [pl.BlockSpec(memory_space=pltpu.HBM)] * len(hbm_args)
    specs += [pl.BlockSpec(memory_space=pltpu.VMEM)] * len(in_args)
    out_specs = []
    for out in outs:
        out_specs.append(pl.BlockSpec(memory_space=out.memory_space))
    moved = sum(a.size * a.dtype.itemsize for a in args)
    return pl.pallas_call(
        body,
        in_specs=specs,
        out_specs=out_specs,
        out_shape=outs,
        scratch_shapes=scratch,
        input_output_aliases=aliases or {},
        compiler_params=pltpu.CompilerParams(vmem_limit_bytes=16 * MIB),
        cost_estimate=pl.CostEstimate(flops=flops, bytes_accessed=moved, transcendentals=0),
    )(*args)


def scan_blocks(blocks, reverse):
    (states,) = local_call(
        functools.partial(scan_body, reverse),
        [blocks],
        [pltpu.VMEM(blocks.shape, blocks.dtype)],
        blocks.size,
    )
    return states


def exchange(pieces, axis):
    return lax.all_to_all(pieces, axis, 0, 0)


def in_pieces(state, axis):
    count = lax.axis_size(axis)
    rows, cols = state.shape
    return state.reshape(count, rows // count, cols)


def shards(queries, keys, values, out_grad, gain):
    rows, width = queries.shape
    total_width = width * lax.axis_size("head")
    bf16, f32 = jnp.bfloat16, jnp.float32
    tokens, state = (rows, width), (width, HEAD_DIM)
    small = 2 * rows * width * HEAD_DIM
    large = 2 * rows * rows * width * 3 // 4
    gain_row = gain.reshape(1, width)
    flat = (width, rows)
    chunks = pltpu.SemaphoreType.DMA((width // COPY_COLS,))
    one_sem = pltpu.SemaphoreType.DMA((1,))
    vm, hbm = pltpu.VMEM, pltpu.HBM
    rows_vm, flat_vm, state_vm = vm(tokens, bf16), vm(flat, bf16), vm(state, bf16)

    (own_kv,) = local_call(
        states_body, [], [state_vm], small, [keys, values], [rows_vm] * 2 + [chunks] * 2
    )
    kv_blocks = exchange(in_pieces(own_kv, "seq"), "seq")
    flipped, grad_flipped = local_call(
        flip_body, [], [flat_vm] * 2, large, [queries, out_grad], [rows_vm] * 2 + [chunks] * 2
    )
    kv_blocks, flipped, grad_flipped = lax.optimization_barrier((kv_blocks, flipped, grad_flipped))
    kv_low = exchange(scan_blocks(kv_blocks, False), "seq").reshape(state)
    (local,) = local_call(
        local_body, [flipped], [flat_vm], 2 * large, [keys, values], [rows_vm] * 2 + [chunks] * 2
    )
    groups = lax.axis_size("head")
    attended, sums, kv_copy = local_call(
        sums_body,
        [gain_row, flipped, grad_flipped, local, kv_low],
        [flat_vm, vm((groups, 2, rows), f32), hbm(state, bf16)],
        small,
        scratch=[one_sem],
        aliases={3: 0},
    )
    sums = exchange(sums, "head")
    dout_flipped, own_grad = local_call(
        functools.partial(dout_body, total_width),
        [gain_row, flipped, grad_flipped, attended, sums],
        [flat_vm, state_vm],
        small,
        aliases={3: 0},
    )
    grad_blocks = exchange(in_pieces(own_grad, "seq"), "seq")
    query_grad, dout = local_call(
        query_body,
        [dout_flipped],
        [hbm(tokens, bf16), rows_vm],
        2 * large + small,
        [keys, values, kv_copy],
        [rows_vm] * 2 + [state_vm, rows_vm] + [chunks] * 3 + [one_sem],
    )
    grad_blocks, query_grad, dout = lax.optimization_barrier((grad_blocks, query_grad, dout))
    grad_low = exchange(scan_blocks(grad_blocks, True), "seq").reshape(state)
    key_part, value_part, value_kept = local_call(
        inner_body,
        [dout],
        [rows_vm] * 3,
        4 * large,
        [queries, keys, values],
        [rows_vm] * 2 + [chunks] * 3,
        {3: 1},
    )
    key_grad, value_grad = local_call(
        final_body,
        [value_kept, key_part, value_part, grad_low],
        [hbm(tokens, bf16)] * 2,
        2 * small,
        [keys],
        [rows_vm] * 3 + [chunks] * 3,
    )
    return query_grad, key_grad, value_grad


def solution(mesh):
    return jax.shard_map(
        shards,
        mesh=mesh,
        in_specs=(
            P("seq", "head"),
            P("seq", "head"),
            P("seq", "head"),
            P("seq", "head"),
            P("head"),
        ),
        out_specs=(P("seq", "head"), P("seq", "head"), P("seq", "head")),
        check_vma=False,
    )
```

```python
import functools

import jax
import jax.numpy as jnp
from jax import lax
from jax.experimental import pallas as pl
from jax.experimental.pallas import tpu as pltpu
from jax.sharding import PartitionSpec as P

HEAD_DIM = 128
BLOCK = 256
COPY_COLS = 256
EPSILON = 1e-06
MIB = 1 << 20


def mm(a, b):
    return lax.dot_general(a, b, (((1,), (0,)), ((), ())), preferred_element_type=jnp.float32)


def mm_nt(a, b):
    return lax.dot_general(a, b, (((1,), (1,)), ((), ())), preferred_element_type=jnp.float32)


def mm_tn(a, b):
    return lax.dot_general(a, b, (((0,), (0,)), ((), ())), preferred_element_type=jnp.float32)


def pieces_of(ref, size):
    return [slice(at, at + size) for at in range(0, ref.shape[1], size)]


def masked(scores, row_start, col_start, rows_first):
    rows = row_start + lax.broadcasted_iota(jnp.int32, scores.shape, 0)
    cols = col_start + lax.broadcasted_iota(jnp.int32, scores.shape, 1)
    keep = rows >= cols if rows_first else cols >= rows
    return jnp.where(keep, scores, 0.0).astype(jnp.bfloat16)


def column_copies(source, target, sems):
    copies = []
    for index, cols in enumerate(pieces_of(source, COPY_COLS)):
        copies.append(pltpu.make_async_copy(source.at[:, cols], target.at[:, cols], sems.at[index]))
    return copies


def start_all(*groups):
    for parts in zip(*groups):
        for part in parts:
            part.start()


def wait_all(*groups):
    for group in groups:
        for part in group:
            part.wait()


def states_body(key_hbm, value_hbm, state_ref, key_ref, value_ref, key_sems, value_sems):
    key_copies = column_copies(key_hbm, key_ref, key_sems)
    value_copies = column_copies(value_hbm, value_ref, value_sems)
    start_all(key_copies, value_copies)
    for index, cols in enumerate(pieces_of(key_ref, COPY_COLS)):
        key_copies[index].wait()
        value_copies[index].wait()
        for start in range(cols.start, cols.stop, HEAD_DIM):
            head = slice(start, start + HEAD_DIM)
            state_ref[head, :] = mm_tn(key_ref[:, head], value_ref[:, head]).astype(jnp.bfloat16)


def flip_body(query_hbm, grad_hbm, flipped_ref, grad_flipped_ref, query_ref, grad_ref, query_sems, grad_sems):
    loads = (
        (query_ref, flipped_ref, column_copies(query_hbm, query_ref, query_sems)),
        (grad_ref, grad_flipped_ref, column_copies(grad_hbm, grad_ref, grad_sems)),
    )
    start_all(loads[0][2])
    start_all(loads[1][2])
    for source, target, copies in loads:
        for copy, cols in zip(copies, pieces_of(source, COPY_COLS)):
            copy.wait()
            target[cols, :] = source[:, cols].T


def local_body(key_hbm, value_hbm, flipped_ref, local_ref, key_ref, value_ref, key_sems, value_sems):
    rows = key_ref.shape[0]
    key_copies = column_copies(key_hbm, key_ref, key_sems)
    value_copies = column_copies(value_hbm, value_ref, value_sems)
    start_all(key_copies, value_copies)
    for index, step in enumerate(pieces_of(key_ref, COPY_COLS)):
        key_copies[index].wait()
        value_copies[index].wait()
        for left in range(step.start, step.stop, HEAD_DIM):
            cols = slice(left, left + HEAD_DIM)
            for start in range(0, rows, BLOCK):
                end = start + BLOCK
                scores = mm(key_ref[:end, cols], flipped_ref[cols, start:end])
                weights = masked(scores, 0, start, False)
                local = mm_tn(value_ref[:end, cols], weights)
                local_ref[cols, start:end] = local.astype(jnp.bfloat16)


def scan_body(reverse, block_ref, state_ref):
    count = block_ref.shape[0]
    total = jnp.zeros(block_ref.shape[1:], jnp.float32)
    places = places_in_order(count)
    for place in range(count - 1, -1, -1) if reverse else range(count):
        rank = places.index(place)
        state_ref[rank] = total.astype(jnp.bfloat16)
        total = total + block_ref[rank].astype(jnp.float32)


def heads_of(ref):
    return [slice(at, at + HEAD_DIM) for at in range(0, ref.shape[0], HEAD_DIM)]


def scaled_grad(gain_ref, grad_ref, head):
    gain = jnp.broadcast_to(gain_ref[:, head], (HEAD_DIM, HEAD_DIM)).T
    gain = jnp.concatenate([gain] * (grad_ref.shape[1] // HEAD_DIM), axis=1)
    return gain * grad_ref[head, :].astype(jnp.float32)


def fold(values):
    parts = [values[at : at + 8, :] for at in range(0, values.shape[0], 8)]
    while len(parts) > 1:
        parts = [sum(parts[at + 1 : at + 2], parts[at]) for at in range(0, len(parts), 2)]
    return parts[0]


def sums_body(
    gain_ref, flipped_ref, grad_ref, local_ref, state_ref, attended_ref, sums_ref, state_hbm, sem
):
    copy = pltpu.make_async_copy(state_ref, state_hbm, sem.at[0])
    copy.start()
    square = cross = jnp.zeros((8, local_ref.shape[1]), jnp.float32)
    for head in heads_of(local_ref):
        attended = mm_tn(state_ref[head, :], flipped_ref[head, :])
        attended = attended + attended_ref[head, :].astype(jnp.float32)
        attended_ref[head, :] = attended.astype(jnp.bfloat16)
        square += fold(attended * attended)
        cross += fold(scaled_grad(gain_ref, grad_ref, head) * attended)
    square = jnp.sum(square, axis=0, keepdims=True)
    cross = jnp.sum(cross, axis=0, keepdims=True)
    sums_ref[0:1, :] = square
    sums_ref[1:2, :] = cross
    copy.wait()


def dout_body(width, gain_ref, flipped_ref, grad_ref, attended_ref, sums_ref, dout_ref, own_ref):
    inverse = 1.0 / jnp.sqrt(sums_ref[0:1, :] / width + EPSILON)
    drop = sums_ref[1:2, :] * (inverse * inverse * inverse) / width
    for head in heads_of(dout_ref):
        attended = dout_ref[head, :].astype(jnp.float32)
        dout = scaled_grad(gain_ref, grad_ref, head) * inverse - attended * drop
        dout = dout.astype(jnp.bfloat16)
        dout_ref[head, :] = dout
        own_ref[head, :] = mm_nt(flipped_ref[head, :], dout).astype(jnp.bfloat16)


def query_body(
    key_hbm, value_hbm, state_hbm, flipped_ref, out_hbm, dout_ref,
    key_ref, value_ref, state_ref, out_ref, key_sems, value_sems, out_sems, state_sem,
):
    rows = dout_ref.shape[0]
    key_copies = column_copies(key_hbm, key_ref, key_sems)
    value_copies = column_copies(value_hbm, value_ref, value_sems)
    state_copy = pltpu.make_async_copy(state_hbm, state_ref, state_sem.at[0])
    state_copy.start()
    start_all(key_copies, value_copies)
    for head in heads_of(flipped_ref):
        dout_ref[:, head] = flipped_ref[head, :].T
    state_copy.wait()
    stores = column_copies(out_ref, out_hbm, out_sems)
    for index, step in enumerate(pieces_of(out_ref, COPY_COLS)):
        key_copies[index].wait()
        value_copies[index].wait()
        for left in range(step.start, step.stop, HEAD_DIM):
            cols = slice(left, left + HEAD_DIM)
            for start in range(0, rows, BLOCK):
                end = start + BLOCK
                dout = dout_ref[start:end, cols]
                dscore = masked(mm_nt(dout, value_ref[:end, cols]), start, 0, True)
                grad = mm(dscore, key_ref[:end, cols]) + mm_nt(dout, state_ref[cols, :])
                out_ref[start:end, cols] = grad.astype(jnp.bfloat16)
        stores[index].start()
    wait_all(stores)


def inner_body(
    query_hbm, key_hbm, value_hbm, dout_ref, key_out, value_out, value_ref,
    query_ref, key_ref, query_sems, key_sems, value_sems,
):
    rows = value_out.shape[0]
    loads = (
        column_copies(query_hbm, query_ref, query_sems),
        column_copies(key_hbm, key_ref, key_sems),
        column_copies(value_hbm, value_ref, value_sems),
    )
    start_all(*loads)
    for index, step in enumerate(pieces_of(key_out, COPY_COLS)):
        for load in loads:
            load[index].wait()
        for left in range(step.start, step.stop, HEAD_DIM):
            cols = slice(left, left + HEAD_DIM)
            dout_all = value_out[:, cols]
            for start in range(0, rows, BLOCK):
                end = start + BLOCK
                query = query_ref[start:, cols]
                dout = dout_all[start:, :]
                dscore = masked(mm_nt(value_ref[start:end, cols], dout), 0, 0, False)
                key_out[start:end, cols] = mm(dscore, query).astype(jnp.bfloat16)
                weights = masked(mm_nt(key_ref[start:end, cols], query), 0, 0, False)
                value_out[start:end, cols] = mm(weights, dout).astype(jnp.bfloat16)


def final_body(
    key_hbm, value_ref, key_part, value_part, state_ref, key_out_hbm, value_out_hbm,
    key_ref, key_out, value_out, in_sems, key_sems, value_sems,
):
    keys = column_copies(key_hbm, key_ref, in_sems)
    start_all(keys)
    key_stores = column_copies(key_out, key_out_hbm, key_sems)
    value_stores = column_copies(value_out, value_out_hbm, value_sems)
    for index, step in enumerate(pieces_of(key_out, COPY_COLS)):
        for left in range(step.start, step.stop, HEAD_DIM):
            cols = slice(left, left + HEAD_DIM)
            grad = key_part[:, cols].astype(jnp.float32) + mm_nt(value_ref[:, cols], state_ref[cols, :])
            key_out[:, cols] = grad.astype(jnp.bfloat16)
        key_stores[index].start()
    for index, step in enumerate(pieces_of(value_out, COPY_COLS)):
        keys[index].wait()
        for left in range(step.start, step.stop, HEAD_DIM):
            cols = slice(left, left + HEAD_DIM)
            grad = value_part[:, cols].astype(jnp.float32) + mm(key_ref[:, cols], state_ref[cols, :])
            value_out[:, cols] = grad.astype(jnp.bfloat16)
        value_stores[index].start()
    wait_all(key_stores, value_stores)


def local_call(body, in_args, outs, flops, hbm_args=(), scratch=(), aliases=None):
    args = [pltpu.with_memory_space_constraint(a, pltpu.HBM) for a in hbm_args]
    args += [pltpu.with_memory_space_constraint(a, pltpu.VMEM) for a in in_args]
    specs = [pl.BlockSpec(memory_space=pltpu.HBM)] * len(hbm_args)
    specs += [pl.BlockSpec(memory_space=pltpu.VMEM)] * len(in_args)
    out_specs = []
    for out in outs:
        out_specs.append(pl.BlockSpec(memory_space=out.memory_space))
    moved = sum(a.size * a.dtype.itemsize for a in args)
    return pl.pallas_call(
        body,
        in_specs=specs,
        out_specs=out_specs,
        out_shape=outs,
        scratch_shapes=scratch,
        input_output_aliases=aliases or {},
        compiler_params=pltpu.CompilerParams(vmem_limit_bytes=16 * MIB),
        cost_estimate=pl.CostEstimate(flops=flops, bytes_accessed=moved, transcendentals=0),
    )(*args)


def scan_blocks(blocks, reverse):
    (states,) = local_call(
        functools.partial(scan_body, reverse),
        [blocks],
        [pltpu.VMEM(blocks.shape, blocks.dtype)],
        blocks.size,
    )
    return states


def places_in_order(count):
    places = list(range(count))
    return places[count // 4 : count * 3 // 4] + places[: count // 4] + places[count * 3 // 4 :]


def exchange(pieces, axis):
    groups = [places_in_order(lax.axis_size(axis))]
    return lax.all_to_all(pieces, axis, 0, 0, axis_index_groups=groups)


def in_pieces(state, axis):
    count = lax.axis_size(axis)
    rows, cols = state.shape
    return state.reshape(count, rows // count, cols)


def shards(queries, keys, values, out_grad, gain):
    rows, width = queries.shape
    total_width = width * lax.axis_size("head")
    bf16, f32 = jnp.bfloat16, jnp.float32
    tokens, state = (rows, width), (width, HEAD_DIM)
    small = 2 * rows * width * HEAD_DIM
    large = 2 * rows * rows * width * 3 // 4
    gain_row = gain.reshape(1, width)
    flat = (width, rows)
    chunks = pltpu.SemaphoreType.DMA((width // COPY_COLS,))
    one_sem = pltpu.SemaphoreType.DMA((1,))
    vm, hbm = pltpu.VMEM, pltpu.HBM
    rows_vm, flat_vm, state_vm = vm(tokens, bf16), vm(flat, bf16), vm(state, bf16)

    (own_kv,) = local_call(
        states_body, [], [state_vm], small, [keys, values], [rows_vm] * 2 + [chunks] * 2
    )
    kv_blocks = exchange(in_pieces(own_kv, "seq"), "seq")
    flipped, grad_flipped = local_call(
        flip_body, [], [flat_vm] * 2, large, [queries, out_grad], [rows_vm] * 2 + [chunks] * 2
    )
    kv_blocks, flipped, grad_flipped = lax.optimization_barrier((kv_blocks, flipped, grad_flipped))
    kv_low = exchange(scan_blocks(kv_blocks, False), "seq").reshape(state)
    (local,) = local_call(
        local_body, [flipped], [flat_vm], 2 * large, [keys, values], [rows_vm] * 2 + [chunks] * 2
    )
    attended, sums, kv_copy = local_call(
        sums_body,
        [gain_row, flipped, grad_flipped, local, kv_low],
        [flat_vm, vm((2, rows), f32), hbm(state, bf16)],
        small,
        scratch=[one_sem],
        aliases={3: 0},
    )
    sums = lax.psum(sums, "head")
    dout_flipped, own_grad = local_call(
        functools.partial(dout_body, total_width),
        [gain_row, flipped, grad_flipped, attended, sums],
        [flat_vm, state_vm],
        small,
        aliases={3: 0},
    )
    grad_blocks = exchange(in_pieces(own_grad, "seq"), "seq")
    query_grad, dout = local_call(
        query_body,
        [dout_flipped],
        [hbm(tokens, bf16), rows_vm],
        2 * large + small,
        [keys, values, kv_copy],
        [rows_vm] * 2 + [state_vm, rows_vm] + [chunks] * 3 + [one_sem],
    )
    grad_blocks, query_grad, dout = lax.optimization_barrier((grad_blocks, query_grad, dout))
    grad_low = exchange(scan_blocks(grad_blocks, True), "seq").reshape(state)
    key_part, value_part, value_kept = local_call(
        inner_body,
        [dout],
        [rows_vm] * 3,
        4 * large,
        [queries, keys, values],
        [rows_vm] * 2 + [chunks] * 3,
        {3: 1},
    )
    key_grad, value_grad = local_call(
        final_body,
        [value_kept, key_part, value_part, grad_low],
        [hbm(tokens, bf16)] * 2,
        2 * small,
        [keys],
        [rows_vm] * 3 + [chunks] * 3,
    )
    return query_grad, key_grad, value_grad


def solution(mesh):
    return jax.shard_map(
        shards,
        mesh=mesh,
        in_specs=(
            P("seq", "head"),
            P("seq", "head"),
            P("seq", "head"),
            P("seq", "head"),
            P("head"),
        ),
        out_specs=(P("seq", "head"), P("seq", "head"), P("seq", "head")),
        check_vma=False,
    )
```

```python
import functools

import jax
import jax.numpy as jnp
from jax import lax
from jax.experimental import pallas as pl
from jax.experimental.pallas import tpu as pltpu
from jax.sharding import PartitionSpec as P

HEAD_DIM = 128
BLOCK = 256
COPY_COLS = 256
EPSILON = 1e-06
MIB = 1 << 20


def mm(a, b):
    return lax.dot_general(a, b, (((1,), (0,)), ((), ())), preferred_element_type=jnp.float32)


def mm_nt(a, b):
    return lax.dot_general(a, b, (((1,), (1,)), ((), ())), preferred_element_type=jnp.float32)


def mm_tn(a, b):
    return lax.dot_general(a, b, (((0,), (0,)), ((), ())), preferred_element_type=jnp.float32)


def pieces_of(ref, size):
    return [slice(at, at + size) for at in range(0, ref.shape[1], size)]


def masked(scores, row_start, col_start, rows_first):
    rows = row_start + lax.broadcasted_iota(jnp.int32, scores.shape, 0)
    cols = col_start + lax.broadcasted_iota(jnp.int32, scores.shape, 1)
    keep = rows >= cols if rows_first else cols >= rows
    return jnp.where(keep, scores, 0.0).astype(jnp.bfloat16)


def column_copies(source, target, sems):
    copies = []
    for index, cols in enumerate(pieces_of(source, COPY_COLS)):
        copies.append(pltpu.make_async_copy(source.at[:, cols], target.at[:, cols], sems.at[index]))
    return copies


def row_copies(source, target, sems):
    copies = []
    for index in range(source.shape[0] // COPY_COLS):
        part = slice(index * COPY_COLS, (index + 1) * COPY_COLS)
        copies.append(pltpu.make_async_copy(source.at[part, :], target.at[part, :], sems.at[index]))
    return copies


def start_all(*groups):
    for parts in zip(*groups):
        for part in parts:
            part.start()


def wait_all(*groups):
    for group in groups:
        for part in group:
            part.wait()


def states_body(
    key_hbm, value_hbm, state_hbm, key_ref, value_ref, state_ref, key_sems, value_sems, state_sems
):
    stores = row_copies(state_ref, state_hbm, state_sems)
    key_copies = column_copies(key_hbm, key_ref, key_sems)
    value_copies = column_copies(value_hbm, value_ref, value_sems)
    start_all(key_copies, value_copies)
    for index, cols in enumerate(pieces_of(key_ref, COPY_COLS)):
        key_copies[index].wait()
        value_copies[index].wait()
        for start in range(cols.start, cols.stop, HEAD_DIM):
            head = slice(start, start + HEAD_DIM)
            state_ref[head, :] = mm_tn(key_ref[:, head], value_ref[:, head]).astype(jnp.bfloat16)
        stores[index].start()
    wait_all(stores)


def flip_body(query_hbm, grad_hbm, flipped_ref, grad_flipped_ref, query_ref, grad_ref, query_sems, grad_sems):
    loads = (
        (query_ref, flipped_ref, column_copies(query_hbm, query_ref, query_sems)),
        (grad_ref, grad_flipped_ref, column_copies(grad_hbm, grad_ref, grad_sems)),
    )
    start_all(loads[0][2])
    start_all(loads[1][2])
    for source, target, copies in loads:
        for copy, cols in zip(copies, pieces_of(source, COPY_COLS)):
            copy.wait()
            target[cols, :] = source[:, cols].T


def local_body(key_hbm, value_hbm, flipped_ref, local_ref, key_ref, value_ref, key_sems, value_sems):
    rows = key_ref.shape[0]
    key_copies = column_copies(key_hbm, key_ref, key_sems)
    value_copies = column_copies(value_hbm, value_ref, value_sems)
    start_all(key_copies, value_copies)
    for index, step in enumerate(pieces_of(key_ref, COPY_COLS)):
        key_copies[index].wait()
        value_copies[index].wait()
        for left in range(step.start, step.stop, HEAD_DIM):
            cols = slice(left, left + HEAD_DIM)
            for start in range(0, rows, BLOCK):
                end = start + BLOCK
                scores = mm(key_ref[:end, cols], flipped_ref[cols, start:end])
                weights = masked(scores, 0, start, False)
                local = mm_tn(value_ref[:end, cols], weights)
                local_ref[cols, start:end] = local.astype(jnp.bfloat16)


def scan_body(reverse, block_ref, state_hbm, state_ref, sems):
    count = block_ref.shape[0]
    total = jnp.zeros(block_ref.shape[1:], jnp.float32)
    places = places_in_order(count)
    stores = []
    for place in range(count - 1, -1, -1) if reverse else range(count):
        rank = places.index(place)
        state_ref[rank] = total.astype(jnp.bfloat16)
        total = total + block_ref[rank].astype(jnp.float32)
        stores.append(pltpu.make_async_copy(state_ref.at[rank], state_hbm.at[rank], sems.at[rank]))
        stores[-1].start()
    wait_all(stores)


def heads_of(ref):
    return [slice(at, at + HEAD_DIM) for at in range(0, ref.shape[0], HEAD_DIM)]


def scaled_grad(gain_ref, grad_ref, head):
    gain = jnp.broadcast_to(gain_ref[:, head], (HEAD_DIM, HEAD_DIM)).T
    gain = jnp.concatenate([gain] * (grad_ref.shape[1] // HEAD_DIM), axis=1)
    return gain * grad_ref[head, :].astype(jnp.float32)


def fold(values):
    parts = [values[at : at + 8, :] for at in range(0, values.shape[0], 8)]
    while len(parts) > 1:
        parts = [sum(parts[at + 1 : at + 2], parts[at]) for at in range(0, len(parts), 2)]
    return parts[0]


def sums_body(gain_ref, flipped_ref, grad_ref, local_ref, state_ref, attended_ref, sums_ref):
    square = cross = jnp.zeros((8, local_ref.shape[1]), jnp.float32)
    for head in heads_of(local_ref):
        attended = mm_tn(state_ref[head, :], flipped_ref[head, :])
        attended = attended + attended_ref[head, :].astype(jnp.float32)
        attended_ref[head, :] = attended.astype(jnp.bfloat16)
        square += fold(attended * attended)
        cross += fold(scaled_grad(gain_ref, grad_ref, head) * attended)
    square = jnp.sum(square, axis=0, keepdims=True)
    cross = jnp.sum(cross, axis=0, keepdims=True)
    sums_ref[0:1, :] = square
    sums_ref[1:2, :] = cross


def dout_body(
    width, gain_ref, flipped_ref, grad_ref, attended_ref, sums_ref, dout_ref, own_hbm, own_ref, sems
):
    stores = row_copies(own_ref, own_hbm, sems)
    inverse = 1.0 / jnp.sqrt(sums_ref[0:1, :] / width + EPSILON)
    drop = sums_ref[1:2, :] * (inverse * inverse * inverse) / width
    for head in heads_of(dout_ref):
        attended = dout_ref[head, :].astype(jnp.float32)
        dout = scaled_grad(gain_ref, grad_ref, head) * inverse - attended * drop
        dout = dout.astype(jnp.bfloat16)
        dout_ref[head, :] = dout
        own_ref[head, :] = mm_nt(flipped_ref[head, :], dout).astype(jnp.bfloat16)
        if head.stop % COPY_COLS == 0:
            stores[head.stop // COPY_COLS - 1].start()
    wait_all(stores)


def query_body(
    key_hbm, value_hbm, flipped_ref, state_ref, out_hbm, dout_ref,
    key_ref, value_ref, out_ref, key_sems, value_sems, out_sems,
):
    rows = dout_ref.shape[0]
    key_copies = column_copies(key_hbm, key_ref, key_sems)
    value_copies = column_copies(value_hbm, value_ref, value_sems)
    start_all(key_copies, value_copies)
    for head in heads_of(flipped_ref):
        dout_ref[:, head] = flipped_ref[head, :].T
    stores = column_copies(out_ref, out_hbm, out_sems)
    for index, step in enumerate(pieces_of(out_ref, COPY_COLS)):
        key_copies[index].wait()
        value_copies[index].wait()
        for left in range(step.start, step.stop, HEAD_DIM):
            cols = slice(left, left + HEAD_DIM)
            for start in range(0, rows, BLOCK):
                end = start + BLOCK
                dout = dout_ref[start:end, cols]
                dscore = masked(mm_nt(dout, value_ref[:end, cols]), start, 0, True)
                grad = mm(dscore, key_ref[:end, cols]) + mm_nt(dout, state_ref[cols, :])
                out_ref[start:end, cols] = grad.astype(jnp.bfloat16)
        stores[index].start()
    wait_all(stores)


def inner_body(
    query_hbm, key_hbm, value_hbm, dout_ref, key_out, value_out, value_ref,
    query_ref, key_ref, query_sems, key_sems, value_sems,
):
    rows = value_out.shape[0]
    loads = (
        column_copies(query_hbm, query_ref, query_sems),
        column_copies(key_hbm, key_ref, key_sems),
        column_copies(value_hbm, value_ref, value_sems),
    )
    start_all(*loads)
    for index, step in enumerate(pieces_of(key_out, COPY_COLS)):
        for load in loads:
            load[index].wait()
        for left in range(step.start, step.stop, HEAD_DIM):
            cols = slice(left, left + HEAD_DIM)
            dout_all = value_out[:, cols]
            for start in range(0, rows, BLOCK):
                end = start + BLOCK
                query = query_ref[start:, cols]
                dout = dout_all[start:, :]
                dscore = masked(mm_nt(value_ref[start:end, cols], dout), 0, 0, False)
                key_out[start:end, cols] = mm(dscore, query).astype(jnp.bfloat16)
                weights = masked(mm_nt(key_ref[start:end, cols], query), 0, 0, False)
                value_out[start:end, cols] = mm(weights, dout).astype(jnp.bfloat16)


def final_body(
    key_hbm, value_ref, key_part, value_part, state_ref, key_out_hbm, value_out_hbm,
    key_ref, key_out, value_out, in_sems, key_sems, value_sems,
):
    keys = column_copies(key_hbm, key_ref, in_sems)
    start_all(keys)
    key_stores = column_copies(key_out, key_out_hbm, key_sems)
    value_stores = column_copies(value_out, value_out_hbm, value_sems)
    for index, step in enumerate(pieces_of(key_out, COPY_COLS)):
        for left in range(step.start, step.stop, HEAD_DIM):
            cols = slice(left, left + HEAD_DIM)
            grad = key_part[:, cols].astype(jnp.float32) + mm_nt(value_ref[:, cols], state_ref[cols, :])
            key_out[:, cols] = grad.astype(jnp.bfloat16)
        key_stores[index].start()
    for index, step in enumerate(pieces_of(value_out, COPY_COLS)):
        keys[index].wait()
        for left in range(step.start, step.stop, HEAD_DIM):
            cols = slice(left, left + HEAD_DIM)
            grad = value_part[:, cols].astype(jnp.float32) + mm(key_ref[:, cols], state_ref[cols, :])
            value_out[:, cols] = grad.astype(jnp.bfloat16)
        value_stores[index].start()
    wait_all(key_stores, value_stores)


def local_call(body, in_args, outs, flops, hbm_args=(), scratch=(), aliases=None):
    args = [pltpu.with_memory_space_constraint(a, pltpu.HBM) for a in hbm_args]
    args += [pltpu.with_memory_space_constraint(a, pltpu.VMEM) for a in in_args]
    specs = [pl.BlockSpec(memory_space=pltpu.HBM)] * len(hbm_args)
    specs += [pl.BlockSpec(memory_space=pltpu.VMEM)] * len(in_args)
    out_specs = []
    for out in outs:
        out_specs.append(pl.BlockSpec(memory_space=out.memory_space))
    moved = sum(a.size * a.dtype.itemsize for a in args)
    return pl.pallas_call(
        body,
        in_specs=specs,
        out_specs=out_specs,
        out_shape=outs,
        scratch_shapes=scratch,
        input_output_aliases=aliases or {},
        compiler_params=pltpu.CompilerParams(vmem_limit_bytes=16 * MIB),
        cost_estimate=pl.CostEstimate(flops=flops, bytes_accessed=moved, transcendentals=0),
    )(*args)


def scan_blocks(blocks, reverse):
    (states,) = local_call(
        functools.partial(scan_body, reverse),
        [blocks],
        [pltpu.HBM(blocks.shape, blocks.dtype)],
        blocks.size,
        scratch=[
            pltpu.VMEM(blocks.shape, blocks.dtype),
            pltpu.SemaphoreType.DMA((blocks.shape[0],)),
        ],
    )
    return states


def places_in_order(count):
    quarter = count // 4
    first, second, third, fourth = (list(range(at, at + quarter)) for at in range(0, count, quarter))
    half = quarter // 2
    return second + first[:half] + third[:half] + first[half:] + third[half:] + fourth


def exchange(pieces, axis):
    groups = [places_in_order(lax.axis_size(axis))]
    return lax.all_to_all(pieces, axis, 0, 0, axis_index_groups=groups)


def in_pieces(state, axis):
    count = lax.axis_size(axis)
    rows, cols = state.shape
    return state.reshape(count, rows // count, cols)


def shards(queries, keys, values, out_grad, gain):
    rows, width = queries.shape
    total_width = width * lax.axis_size("head")
    bf16, f32 = jnp.bfloat16, jnp.float32
    tokens, state = (rows, width), (width, HEAD_DIM)
    small = 2 * rows * width * HEAD_DIM
    large = 2 * rows * rows * width * 3 // 4
    gain_row = gain.reshape(1, width)
    flat = (width, rows)
    chunks = pltpu.SemaphoreType.DMA((width // COPY_COLS,))
    vm, hbm = pltpu.VMEM, pltpu.HBM
    rows_vm, flat_vm, state_vm = vm(tokens, bf16), vm(flat, bf16), vm(state, bf16)

    (own_kv,) = local_call(
        states_body,
        [],
        [hbm(state, bf16)],
        small,
        [keys, values],
        [rows_vm] * 2 + [state_vm] + [chunks] * 3,
    )
    kv_blocks = exchange(in_pieces(own_kv, "seq"), "seq")
    flipped, grad_flipped = local_call(
        flip_body, [], [flat_vm] * 2, large, [queries, out_grad], [rows_vm] * 2 + [chunks] * 2
    )
    kv_blocks, flipped, grad_flipped = lax.optimization_barrier((kv_blocks, flipped, grad_flipped))
    kv_low = exchange(scan_blocks(kv_blocks, False), "seq").reshape(state)
    (local,) = local_call(
        local_body, [flipped], [flat_vm], 2 * large, [keys, values], [rows_vm] * 2 + [chunks] * 2
    )
    attended, sums = local_call(
        sums_body,
        [gain_row, flipped, grad_flipped, local, kv_low],
        [flat_vm, vm((2, rows), f32)],
        small,
        aliases={3: 0},
    )
    sums = lax.psum(sums, "head")
    dout_flipped, own_grad = local_call(
        functools.partial(dout_body, total_width),
        [gain_row, flipped, grad_flipped, attended, sums],
        [flat_vm, hbm(state, bf16)],
        small,
        scratch=[state_vm, chunks],
        aliases={3: 0},
    )
    grad_blocks = exchange(in_pieces(own_grad, "seq"), "seq")
    query_grad, dout = local_call(
        query_body,
        [dout_flipped, kv_low],
        [hbm(tokens, bf16), rows_vm],
        2 * large + small,
        [keys, values],
        [rows_vm] * 3 + [chunks] * 3,
    )
    grad_blocks, query_grad, dout = lax.optimization_barrier((grad_blocks, query_grad, dout))
    grad_low = exchange(scan_blocks(grad_blocks, True), "seq").reshape(state)
    key_part, value_part, value_kept = local_call(
        inner_body,
        [dout],
        [rows_vm] * 3,
        4 * large,
        [queries, keys, values],
        [rows_vm] * 2 + [chunks] * 3,
        {3: 1},
    )
    key_grad, value_grad = local_call(
        final_body,
        [value_kept, key_part, value_part, grad_low],
        [hbm(tokens, bf16)] * 2,
        2 * small,
        [keys],
        [rows_vm] * 3 + [chunks] * 3,
    )
    return query_grad, key_grad, value_grad


def solution(mesh):
    return jax.shard_map(
        shards,
        mesh=mesh,
        in_specs=(
            P("seq", "head"),
            P("seq", "head"),
            P("seq", "head"),
            P("seq", "head"),
            P("head"),
        ),
        out_specs=(P("seq", "head"), P("seq", "head"), P("seq", "head")),
        check_vma=False,
    )
```

```python
import functools

import jax
import jax.numpy as jnp
from jax import lax
from jax.experimental import pallas as pl
from jax.experimental.pallas import tpu as pltpu
from jax.sharding import PartitionSpec as P

HEAD_DIM = 128
BLOCK = 256
COPY_COLS = 256
EPSILON = 1e-06
MIB = 1 << 20


def mm(a, b):
    return lax.dot_general(a, b, (((1,), (0,)), ((), ())), preferred_element_type=jnp.float32)


def mm_nt(a, b):
    return lax.dot_general(a, b, (((1,), (1,)), ((), ())), preferred_element_type=jnp.float32)


def mm_tn(a, b):
    return lax.dot_general(a, b, (((0,), (0,)), ((), ())), preferred_element_type=jnp.float32)


def pieces_of(ref, size):
    return [slice(at, at + size) for at in range(0, ref.shape[1], size)]


def masked(scores, row_start, col_start, rows_first):
    rows = row_start + lax.broadcasted_iota(jnp.int32, scores.shape, 0)
    cols = col_start + lax.broadcasted_iota(jnp.int32, scores.shape, 1)
    keep = rows >= cols if rows_first else cols >= rows
    return jnp.where(keep, scores, 0.0).astype(jnp.bfloat16)


def column_copies(source, target, sems):
    copies = []
    for index, cols in enumerate(pieces_of(source, COPY_COLS)):
        copies.append(pltpu.make_async_copy(source.at[:, cols], target.at[:, cols], sems.at[index]))
    return copies


def row_copies(source, target, sems):
    copies = []
    for index in range(source.shape[0] // COPY_COLS):
        part = slice(index * COPY_COLS, (index + 1) * COPY_COLS)
        copies.append(pltpu.make_async_copy(source.at[part, :], target.at[part, :], sems.at[index]))
    return copies


def start_all(*groups):
    for parts in zip(*groups):
        for part in parts:
            part.start()


def wait_all(*groups):
    for group in groups:
        for part in group:
            part.wait()


def states_body(
    key_hbm, value_hbm, state_hbm, key_ref, value_ref, state_ref, key_sems, value_sems, state_sems
):
    stores = row_copies(state_ref, state_hbm, state_sems)
    key_copies = column_copies(key_hbm, key_ref, key_sems)
    value_copies = column_copies(value_hbm, value_ref, value_sems)
    start_all(key_copies, value_copies)
    for index, cols in enumerate(pieces_of(key_ref, COPY_COLS)):
        key_copies[index].wait()
        value_copies[index].wait()
        for start in range(cols.start, cols.stop, HEAD_DIM):
            head = slice(start, start + HEAD_DIM)
            state_ref[head, :] = mm_tn(key_ref[:, head], value_ref[:, head]).astype(jnp.bfloat16)
        stores[index].start()
    wait_all(stores)


def flip_body(query_hbm, grad_hbm, flipped_ref, grad_flipped_ref, query_ref, grad_ref, query_sems, grad_sems):
    loads = (
        (query_ref, flipped_ref, column_copies(query_hbm, query_ref, query_sems)),
        (grad_ref, grad_flipped_ref, column_copies(grad_hbm, grad_ref, grad_sems)),
    )
    start_all(loads[0][2])
    start_all(loads[1][2])
    for source, target, copies in loads:
        for copy, cols in zip(copies, pieces_of(source, COPY_COLS)):
            copy.wait()
            target[cols, :] = source[:, cols].T


def local_body(key_hbm, value_hbm, flipped_ref, local_ref, key_ref, value_ref, key_sems, value_sems):
    rows = key_ref.shape[0]
    key_copies = column_copies(key_hbm, key_ref, key_sems)
    value_copies = column_copies(value_hbm, value_ref, value_sems)
    start_all(key_copies, value_copies)
    for index, step in enumerate(pieces_of(key_ref, COPY_COLS)):
        key_copies[index].wait()
        value_copies[index].wait()
        for left in range(step.start, step.stop, HEAD_DIM):
            cols = slice(left, left + HEAD_DIM)
            for start in range(0, rows, BLOCK):
                end = start + BLOCK
                scores = mm(key_ref[:end, cols], flipped_ref[cols, start:end])
                weights = masked(scores, 0, start, False)
                local = mm_tn(value_ref[:end, cols], weights)
                local_ref[cols, start:end] = local.astype(jnp.bfloat16)


def scan_body(reverse, block_ref, state_hbm, state_ref, sems):
    count = block_ref.shape[0]
    total = jnp.zeros(block_ref.shape[1:], jnp.float32)
    places = places_in_order(count)
    stores = []
    for place in range(count - 1, -1, -1) if reverse else range(count):
        rank = places.index(place)
        state_ref[rank] = total.astype(jnp.bfloat16)
        total = total + block_ref[rank].astype(jnp.float32)
        stores.append(pltpu.make_async_copy(state_ref.at[rank], state_hbm.at[rank], sems.at[rank]))
        stores[-1].start()
    wait_all(stores)


def heads_of(ref):
    return [slice(at, at + HEAD_DIM) for at in range(0, ref.shape[0], HEAD_DIM)]


def scaled_grad(gain_ref, grad_ref, head):
    gain = jnp.broadcast_to(gain_ref[:, head], (HEAD_DIM, HEAD_DIM)).T
    gain = jnp.concatenate([gain] * (grad_ref.shape[1] // HEAD_DIM), axis=1)
    return gain * grad_ref[head, :].astype(jnp.float32)


def fold(values):
    parts = [values[at : at + 8, :] for at in range(0, values.shape[0], 8)]
    while len(parts) > 1:
        parts = [sum(parts[at + 1 : at + 2], parts[at]) for at in range(0, len(parts), 2)]
    return parts[0]


def sums_body(gain_ref, flipped_ref, grad_ref, local_ref, state_ref, attended_ref, sums_ref):
    square = cross = jnp.zeros((8, local_ref.shape[1]), jnp.float32)
    for head in heads_of(local_ref):
        attended = mm_tn(state_ref[head, :], flipped_ref[head, :])
        attended = attended + attended_ref[head, :].astype(jnp.float32)
        attended_ref[head, :] = attended.astype(jnp.bfloat16)
        square += fold(attended * attended)
        cross += fold(scaled_grad(gain_ref, grad_ref, head) * attended)
    square = jnp.sum(square, axis=0, keepdims=True)
    cross = jnp.sum(cross, axis=0, keepdims=True)
    sums_ref[0:1, :] = square
    sums_ref[1:2, :] = cross


def dout_body(
    width, gain_ref, flipped_ref, grad_ref, attended_ref, sums_ref, dout_ref, own_hbm, own_ref, sems
):
    stores = row_copies(own_ref, own_hbm, sems)
    inverse = 1.0 / jnp.sqrt(sums_ref[0:1, :] / width + EPSILON)
    drop = sums_ref[1:2, :] * (inverse * inverse * inverse) / width
    for head in heads_of(dout_ref):
        attended = dout_ref[head, :].astype(jnp.float32)
        dout = scaled_grad(gain_ref, grad_ref, head) * inverse - attended * drop
        dout = dout.astype(jnp.bfloat16)
        dout_ref[head, :] = dout
        own_ref[head, :] = mm_nt(flipped_ref[head, :], dout).astype(jnp.bfloat16)
        if head.stop % COPY_COLS == 0:
            stores[head.stop // COPY_COLS - 1].start()
    wait_all(stores)


def value_local(query_ref, key_ref, dout, cols, target):
    rows = key_ref.shape[0]
    for start in range(0, rows, BLOCK):
        end = start + BLOCK
        weights = masked(mm_nt(key_ref[start:end, cols], query_ref[start:, cols]), 0, 0, False)
        target[start:end, :] = mm(weights, dout[start:, :]).astype(jnp.bfloat16)


def query_body(
    query_hbm, key_hbm, value_hbm, flipped_ref, state_ref, out_hbm, dout_ref, value_out,
    query_ref, key_ref, value_ref, out_ref, query_sems, key_sems, value_sems, out_sems,
):
    rows = dout_ref.shape[0]
    early = value_out.shape[1]
    query_copies = column_copies(query_hbm.at[:, :early], query_ref, query_sems)
    key_copies = column_copies(key_hbm, key_ref, key_sems)
    value_copies = column_copies(value_hbm, value_ref, value_sems)
    start_all(key_copies, value_copies)
    start_all(query_copies)
    for head in heads_of(flipped_ref):
        dout_ref[:, head] = flipped_ref[head, :].T
    stores = column_copies(out_ref, out_hbm, out_sems)
    for index, step in enumerate(pieces_of(out_ref, COPY_COLS)):
        key_copies[index].wait()
        value_copies[index].wait()
        for left in range(step.start, step.stop, HEAD_DIM):
            cols = slice(left, left + HEAD_DIM)
            for start in range(0, rows, BLOCK):
                end = start + BLOCK
                dout = dout_ref[start:end, cols]
                dscore = masked(mm_nt(dout, value_ref[:end, cols]), start, 0, True)
                grad = mm(dscore, key_ref[:end, cols]) + mm_nt(dout, state_ref[cols, :])
                out_ref[start:end, cols] = grad.astype(jnp.bfloat16)
        stores[index].start()
    wait_all(query_copies)
    for cols in pieces_of(value_out, HEAD_DIM):
        value_local(query_ref, key_ref, dout_ref[:, cols], cols, value_out.at[:, cols])
    wait_all(stores)


def inner_body(
    query_hbm, key_hbm, value_hbm, dout_ref, key_out, value_out, value_ref,
    query_ref, key_ref, query_sems, key_sems, value_sems,
):
    rows, width = key_out.shape
    early = width - value_out.shape[1]
    loads = (
        column_copies(query_hbm, query_ref, query_sems),
        column_copies(value_hbm, value_ref, value_sems),
        column_copies(key_hbm.at[:, early:], key_ref, key_sems),
    )
    start_all(*loads[:2])
    start_all(loads[2])
    for index, step in enumerate(pieces_of(key_out, COPY_COLS)):
        loads[0][index].wait()
        loads[1][index].wait()
        if step.start == early:
            wait_all(loads[2])
        for left in range(step.start, step.stop, HEAD_DIM):
            cols = slice(left, left + HEAD_DIM)
            dout = key_out[:, cols]
            for start in range(0, rows, BLOCK):
                end = start + BLOCK
                scores = mm_nt(value_ref[start:end, cols], dout[start:, :])
                key_out[start:end, cols] = mm(masked(scores, 0, 0, False), query_ref[start:, cols]).astype(jnp.bfloat16)
            if left >= early:
                late = slice(left - early, left - early + HEAD_DIM)
                value_local(query_ref.at[:, early:], key_ref, dout, late, value_out.at[:, late])


def final_body(
    key_hbm, value_ref, key_part, early_part, late_part, state_ref, key_out_hbm, value_out_hbm,
    key_ref, key_out, value_out, in_sems, key_sems, value_sems,
):
    keys = column_copies(key_hbm, key_ref, in_sems)
    start_all(keys)
    key_stores = column_copies(key_out, key_out_hbm, key_sems)
    value_stores = column_copies(value_out, value_out_hbm, value_sems)
    for index, step in enumerate(pieces_of(key_out, COPY_COLS)):
        for left in range(step.start, step.stop, HEAD_DIM):
            cols = slice(left, left + HEAD_DIM)
            grad = key_part[:, cols].astype(jnp.float32) + mm_nt(value_ref[:, cols], state_ref[cols, :])
            key_out[:, cols] = grad.astype(jnp.bfloat16)
        key_stores[index].start()
    for index, step in enumerate(pieces_of(value_out, COPY_COLS)):
        keys[index].wait()
        for left in range(step.start, step.stop, HEAD_DIM):
            cols = slice(left, left + HEAD_DIM)
            early = early_part.shape[1]
            if left < early:
                part = early_part[:, cols]
            else:
                part = late_part[:, left - early : left - early + HEAD_DIM]
            grad = part.astype(jnp.float32) + mm(key_ref[:, cols], state_ref[cols, :])
            value_out[:, cols] = grad.astype(jnp.bfloat16)
        value_stores[index].start()
    wait_all(key_stores, value_stores)


def local_call(body, in_args, outs, flops, hbm_args=(), scratch=(), aliases=None):
    args = [pltpu.with_memory_space_constraint(a, pltpu.HBM) for a in hbm_args]
    args += [pltpu.with_memory_space_constraint(a, pltpu.VMEM) for a in in_args]
    specs = [pl.BlockSpec(memory_space=pltpu.HBM)] * len(hbm_args)
    specs += [pl.BlockSpec(memory_space=pltpu.VMEM)] * len(in_args)
    out_specs = []
    for out in outs:
        out_specs.append(pl.BlockSpec(memory_space=out.memory_space))
    moved = sum(a.size * a.dtype.itemsize for a in args)
    return pl.pallas_call(
        body,
        in_specs=specs,
        out_specs=out_specs,
        out_shape=outs,
        scratch_shapes=scratch,
        input_output_aliases=aliases or {},
        compiler_params=pltpu.CompilerParams(vmem_limit_bytes=16 * MIB),
        cost_estimate=pl.CostEstimate(flops=flops, bytes_accessed=moved, transcendentals=0),
    )(*args)


def scan_blocks(blocks, reverse):
    (states,) = local_call(
        functools.partial(scan_body, reverse),
        [blocks],
        [pltpu.HBM(blocks.shape, blocks.dtype)],
        blocks.size,
        scratch=[
            pltpu.VMEM(blocks.shape, blocks.dtype),
            pltpu.SemaphoreType.DMA((blocks.shape[0],)),
        ],
    )
    return states


def places_in_order(count):
    quarter = count // 4
    first, second, third, fourth = (list(range(at, at + quarter)) for at in range(0, count, quarter))
    return second + fourth + first[::-1] + third


def exchange(pieces, axis):
    groups = [places_in_order(lax.axis_size(axis))]
    return lax.all_to_all(pieces, axis, 0, 0, axis_index_groups=groups)


def in_pieces(state, axis):
    count = lax.axis_size(axis)
    rows, cols = state.shape
    return state.reshape(count, rows // count, cols)


def shards(queries, keys, values, out_grad, gain):
    rows, width = queries.shape
    total_width = width * lax.axis_size("head")
    bf16, f32 = jnp.bfloat16, jnp.float32
    tokens, state = (rows, width), (width, HEAD_DIM)
    small = 2 * rows * width * HEAD_DIM
    large = 2 * rows * rows * width * 3 // 4
    gain_row = gain.reshape(1, width)
    flat = (width, rows)
    chunks = pltpu.SemaphoreType.DMA((width // COPY_COLS,))
    vm, hbm = pltpu.VMEM, pltpu.HBM
    rows_vm, flat_vm, state_vm = vm(tokens, bf16), vm(flat, bf16), vm(state, bf16)

    (own_kv,) = local_call(
        states_body,
        [],
        [hbm(state, bf16)],
        small,
        [keys, values],
        [rows_vm] * 2 + [state_vm] + [chunks] * 3,
    )
    kv_blocks = exchange(in_pieces(own_kv, "seq"), "seq")
    flipped, grad_flipped = local_call(
        flip_body, [], [flat_vm] * 2, large, [queries, out_grad], [rows_vm] * 2 + [chunks] * 2
    )
    kv_blocks, flipped, grad_flipped = lax.optimization_barrier((kv_blocks, flipped, grad_flipped))
    kv_low = exchange(scan_blocks(kv_blocks, False), "seq").reshape(state)
    (local,) = local_call(
        local_body, [flipped], [flat_vm], 2 * large, [keys, values], [rows_vm] * 2 + [chunks] * 2
    )
    attended, sums = local_call(
        sums_body,
        [gain_row, flipped, grad_flipped, local, kv_low],
        [flat_vm, vm((2, rows), f32)],
        small,
        aliases={3: 0},
    )
    sums = lax.psum(sums, "head")
    dout_flipped, own_grad = local_call(
        functools.partial(dout_body, total_width),
        [gain_row, flipped, grad_flipped, attended, sums],
        [flat_vm, hbm(state, bf16)],
        small,
        scratch=[state_vm, chunks],
        aliases={3: 0},
    )
    grad_blocks = exchange(in_pieces(own_grad, "seq"), "seq")
    early = width // 2 // COPY_COLS * COPY_COLS
    early_vm, late_vm = vm((rows, early), bf16), vm((rows, width - early), bf16)
    query_grad, dout, early_part = local_call(
        query_body,
        [dout_flipped, kv_low],
        [hbm(tokens, bf16), rows_vm, early_vm],
        2 * large + small,
        [queries, keys, values],
        [early_vm] + [rows_vm] * 3 + [chunks] * 4,
    )
    grad_blocks, query_grad, dout, early_part = lax.optimization_barrier(
        (grad_blocks, query_grad, dout, early_part)
    )
    grad_low = exchange(scan_blocks(grad_blocks, True), "seq").reshape(state)
    key_part, late_part, value_kept = local_call(
        inner_body,
        [dout],
        [rows_vm, late_vm, rows_vm],
        3 * large,
        [queries, keys, values],
        [rows_vm, late_vm] + [chunks] * 3,
        {3: 0},
    )
    key_grad, value_grad = local_call(
        final_body,
        [value_kept, key_part, early_part, late_part, grad_low],
        [hbm(tokens, bf16)] * 2,
        2 * small,
        [keys],
        [rows_vm] * 3 + [chunks] * 3,
    )
    return query_grad, key_grad, value_grad


def solution(mesh):
    return jax.shard_map(
        shards,
        mesh=mesh,
        in_specs=(
            P("seq", "head"),
            P("seq", "head"),
            P("seq", "head"),
            P("seq", "head"),
            P("head"),
        ),
        out_specs=(P("seq", "head"), P("seq", "head"), P("seq", "head")),
        check_vma=False,
    )
```

```python
import functools

import jax
import jax.numpy as jnp
from jax import lax
from jax.experimental import pallas as pl
from jax.experimental.pallas import tpu as pltpu
from jax.sharding import PartitionSpec as P

HEAD_DIM = 128
BLOCK = 256
COPY_COLS = 256
EPSILON = 1e-06
MIB = 1 << 20


def mm(a, b):
    return lax.dot_general(a, b, (((1,), (0,)), ((), ())), preferred_element_type=jnp.float32)


def mm_nt(a, b):
    return lax.dot_general(a, b, (((1,), (1,)), ((), ())), preferred_element_type=jnp.float32)


def mm_tn(a, b):
    return lax.dot_general(a, b, (((0,), (0,)), ((), ())), preferred_element_type=jnp.float32)


def pieces_of(ref, size):
    return [slice(at, at + size) for at in range(0, ref.shape[1], size)]


def masked(scores, row_start, col_start, rows_first):
    rows = row_start + lax.broadcasted_iota(jnp.int32, scores.shape, 0)
    cols = col_start + lax.broadcasted_iota(jnp.int32, scores.shape, 1)
    keep = rows >= cols if rows_first else cols >= rows
    return jnp.where(keep, scores, 0.0).astype(jnp.bfloat16)


def column_copies(source, target, sems):
    copies = []
    for index, cols in enumerate(pieces_of(source, COPY_COLS)):
        copies.append(pltpu.make_async_copy(source.at[:, cols], target.at[:, cols], sems.at[index]))
    return copies


def row_copies(source, target, sems):
    copies = []
    for index in range(source.shape[0] // COPY_COLS):
        part = slice(index * COPY_COLS, (index + 1) * COPY_COLS)
        copies.append(pltpu.make_async_copy(source.at[part, :], target.at[part, :], sems.at[index]))
    return copies


def start_all(*groups):
    for index, parts in enumerate(zip(*groups)):
        for other, part in enumerate(parts):
            part.start(priority=(index + other) % 2)


def wait_all(*groups):
    for group in groups:
        for part in group:
            part.wait()


def states_body(
    key_hbm, value_hbm, state_hbm, key_ref, value_ref, state_ref, key_sems, value_sems, state_sems
):
    stores = row_copies(state_ref, state_hbm, state_sems)
    key_copies = column_copies(key_hbm, key_ref, key_sems)
    value_copies = column_copies(value_hbm, value_ref, value_sems)
    start_all(key_copies, value_copies)
    for index, cols in enumerate(pieces_of(key_ref, COPY_COLS)):
        key_copies[index].wait()
        value_copies[index].wait()
        for start in range(cols.start, cols.stop, HEAD_DIM):
            head = slice(start, start + HEAD_DIM)
            state_ref[head, :] = mm_tn(key_ref[:, head], value_ref[:, head]).astype(jnp.bfloat16)
        stores[index].start(priority=index % 2)
    wait_all(stores)


def flip_body(query_hbm, grad_hbm, flipped_ref, grad_flipped_ref, query_ref, grad_ref, query_sems, grad_sems):
    loads = (
        (query_ref, flipped_ref, column_copies(query_hbm, query_ref, query_sems)),
        (grad_ref, grad_flipped_ref, column_copies(grad_hbm, grad_ref, grad_sems)),
    )
    start_all(loads[0][2])
    start_all(loads[1][2])
    for source, target, copies in loads:
        for copy, cols in zip(copies, pieces_of(source, COPY_COLS)):
            copy.wait()
            target[cols, :] = source[:, cols].T


def local_body(key_hbm, value_hbm, flipped_ref, local_ref, key_ref, value_ref, key_sems, value_sems):
    rows = key_ref.shape[0]
    key_copies = column_copies(key_hbm, key_ref, key_sems)
    value_copies = column_copies(value_hbm, value_ref, value_sems)
    start_all(key_copies, value_copies)
    for index, step in enumerate(pieces_of(key_ref, COPY_COLS)):
        key_copies[index].wait()
        value_copies[index].wait()
        for left in range(step.start, step.stop, HEAD_DIM):
            cols = slice(left, left + HEAD_DIM)
            for start in range(0, rows, BLOCK):
                end = start + BLOCK
                scores = mm(key_ref[:end, cols], flipped_ref[cols, start:end])
                weights = masked(scores, 0, start, False)
                local = mm_tn(value_ref[:end, cols], weights)
                local_ref[cols, start:end] = local.astype(jnp.bfloat16)


def scan_body(reverse, block_ref, state_hbm, state_ref, sems):
    count = block_ref.shape[0]
    total = jnp.zeros(block_ref.shape[1:], jnp.float32)
    places = places_in_order(count)
    stores = []
    for place in range(count - 1, -1, -1) if reverse else range(count):
        rank = places.index(place)
        state_ref[rank] = total.astype(jnp.bfloat16)
        total = total + block_ref[rank].astype(jnp.float32)
        stores.append(pltpu.make_async_copy(state_ref.at[rank], state_hbm.at[rank], sems.at[rank]))
        stores[-1].start()
    wait_all(stores)


def heads_of(ref):
    return [slice(at, at + HEAD_DIM) for at in range(0, ref.shape[0], HEAD_DIM)]


def scaled_grad(gain_ref, grad_ref, head):
    gain = jnp.broadcast_to(gain_ref[:, head], (HEAD_DIM, HEAD_DIM)).T
    gain = jnp.concatenate([gain] * (grad_ref.shape[1] // HEAD_DIM), axis=1)
    return gain * grad_ref[head, :].astype(jnp.float32)


def fold(values):
    parts = [values[at : at + 8, :] for at in range(0, values.shape[0], 8)]
    while len(parts) > 1:
        parts = [sum(parts[at + 1 : at + 2], parts[at]) for at in range(0, len(parts), 2)]
    return parts[0]


def sums_body(gain_ref, flipped_ref, grad_ref, local_ref, state_ref, attended_ref, sums_ref):
    square = cross = jnp.zeros((8, local_ref.shape[1]), jnp.float32)
    for head in heads_of(local_ref):
        attended = mm_tn(state_ref[head, :], flipped_ref[head, :])
        attended = attended + attended_ref[head, :].astype(jnp.float32)
        attended_ref[head, :] = attended.astype(jnp.bfloat16)
        square += fold(attended * attended)
        cross += fold(scaled_grad(gain_ref, grad_ref, head) * attended)
    square = jnp.sum(square, axis=0, keepdims=True)
    cross = jnp.sum(cross, axis=0, keepdims=True)
    sums_ref[0:1, :] = square
    sums_ref[1:2, :] = cross


def dout_body(
    width, gain_ref, flipped_ref, grad_ref, attended_ref, sums_ref, dout_ref, own_hbm, own_ref, sems
):
    stores = row_copies(own_ref, own_hbm, sems)
    inverse = 1.0 / jnp.sqrt(sums_ref[0:1, :] / width + EPSILON)
    drop = sums_ref[1:2, :] * (inverse * inverse * inverse) / width
    for head in heads_of(dout_ref):
        attended = dout_ref[head, :].astype(jnp.float32)
        dout = scaled_grad(gain_ref, grad_ref, head) * inverse - attended * drop
        dout = dout.astype(jnp.bfloat16)
        dout_ref[head, :] = dout
        own_ref[head, :] = mm_nt(flipped_ref[head, :], dout).astype(jnp.bfloat16)
        if head.stop % COPY_COLS == 0:
            stores[head.stop // COPY_COLS - 1].start()
    wait_all(stores)


def value_local(query_ref, key_ref, dout, cols, target):
    rows = key_ref.shape[0]
    for start in range(0, rows, BLOCK):
        end = start + BLOCK
        weights = masked(mm_nt(key_ref[start:end, cols], query_ref[start:, cols]), 0, 0, False)
        target[start:end, :] = mm(weights, dout[start:, :]).astype(jnp.bfloat16)


def query_body(
    query_hbm, key_hbm, value_hbm, flipped_ref, state_ref, out_hbm, dout_ref, value_out,
    query_ref, key_ref, value_ref, out_ref, query_sems, key_sems, value_sems, out_sems,
):
    rows = dout_ref.shape[0]
    early = value_out.shape[1]
    query_copies = column_copies(query_hbm.at[:, :early], query_ref, query_sems)
    key_copies = column_copies(key_hbm, key_ref, key_sems)
    value_copies = column_copies(value_hbm, value_ref, value_sems)
    start_all(key_copies, value_copies)
    start_all(query_copies)
    for head in heads_of(flipped_ref):
        dout_ref[:, head] = flipped_ref[head, :].T
    stores = column_copies(out_ref, out_hbm, out_sems)
    for index, step in enumerate(pieces_of(out_ref, COPY_COLS)):
        key_copies[index].wait()
        value_copies[index].wait()
        for left in range(step.start, step.stop, HEAD_DIM):
            cols = slice(left, left + HEAD_DIM)
            for start in range(0, rows, BLOCK):
                end = start + BLOCK
                dout = dout_ref[start:end, cols]
                dscore = masked(mm_nt(dout, value_ref[:end, cols]), start, 0, True)
                grad = mm(dscore, key_ref[:end, cols]) + mm_nt(dout, state_ref[cols, :])
                out_ref[start:end, cols] = grad.astype(jnp.bfloat16)
        stores[index].start(priority=index % 2)
    wait_all(query_copies)
    for cols in pieces_of(value_out, HEAD_DIM):
        value_local(query_ref, key_ref, dout_ref[:, cols], cols, value_out.at[:, cols])
    wait_all(stores)


def inner_body(
    query_hbm, key_hbm, value_hbm, dout_ref, key_out, value_out, value_ref,
    query_ref, key_ref, query_sems, key_sems, value_sems,
):
    rows, width = key_out.shape
    early = width - value_out.shape[1]
    loads = (
        column_copies(query_hbm, query_ref, query_sems),
        column_copies(value_hbm, value_ref, value_sems),
        column_copies(key_hbm.at[:, early:], key_ref, key_sems),
    )
    start_all(*loads[:2])
    start_all(loads[2])
    for index, step in enumerate(pieces_of(key_out, COPY_COLS)):
        loads[0][index].wait()
        loads[1][index].wait()
        if step.start == early:
            wait_all(loads[2])
        for left in range(step.start, step.stop, HEAD_DIM):
            cols = slice(left, left + HEAD_DIM)
            dout = key_out[:, cols]
            for start in range(0, rows, BLOCK):
                end = start + BLOCK
                scores = mm_nt(value_ref[start:end, cols], dout[start:, :])
                key_out[start:end, cols] = mm(masked(scores, 0, 0, False), query_ref[start:, cols]).astype(jnp.bfloat16)
            if left >= early:
                late = slice(left - early, left - early + HEAD_DIM)
                value_local(query_ref.at[:, early:], key_ref, dout, late, value_out.at[:, late])


def final_body(
    key_hbm, value_ref, key_part, early_part, late_part, state_ref, key_out_hbm, value_out_hbm,
    key_ref, key_out, value_out, in_sems, key_sems, value_sems,
):
    keys = column_copies(key_hbm, key_ref, in_sems)
    start_all(keys)
    key_stores = column_copies(key_out, key_out_hbm, key_sems)
    value_stores = column_copies(value_out, value_out_hbm, value_sems)
    for index, step in enumerate(pieces_of(key_out, COPY_COLS)):
        for left in range(step.start, step.stop, HEAD_DIM):
            cols = slice(left, left + HEAD_DIM)
            grad = key_part[:, cols].astype(jnp.float32) + mm_nt(value_ref[:, cols], state_ref[cols, :])
            key_out[:, cols] = grad.astype(jnp.bfloat16)
        key_stores[index].start(priority=index % 2)
    for index, step in enumerate(pieces_of(value_out, COPY_COLS)):
        keys[index].wait()
        for left in range(step.start, step.stop, HEAD_DIM):
            cols = slice(left, left + HEAD_DIM)
            early = early_part.shape[1]
            if left < early:
                part = early_part[:, cols]
            else:
                part = late_part[:, left - early : left - early + HEAD_DIM]
            grad = part.astype(jnp.float32) + mm(key_ref[:, cols], state_ref[cols, :])
            value_out[:, cols] = grad.astype(jnp.bfloat16)
        value_stores[index].start(priority=index % 2)
    wait_all(key_stores, value_stores)


def local_call(body, in_args, outs, flops, hbm_args=(), scratch=(), aliases=None):
    args = [pltpu.with_memory_space_constraint(a, pltpu.HBM) for a in hbm_args]
    args += [pltpu.with_memory_space_constraint(a, pltpu.VMEM) for a in in_args]
    specs = [pl.BlockSpec(memory_space=pltpu.HBM)] * len(hbm_args)
    specs += [pl.BlockSpec(memory_space=pltpu.VMEM)] * len(in_args)
    out_specs = []
    for out in outs:
        out_specs.append(pl.BlockSpec(memory_space=out.memory_space))
    moved = sum(a.size * a.dtype.itemsize for a in args)
    return pl.pallas_call(
        body,
        in_specs=specs,
        out_specs=out_specs,
        out_shape=outs,
        scratch_shapes=scratch,
        input_output_aliases=aliases or {},
        compiler_params=pltpu.CompilerParams(vmem_limit_bytes=16 * MIB),
        cost_estimate=pl.CostEstimate(flops=flops, bytes_accessed=moved, transcendentals=0),
    )(*args)


def scan_blocks(blocks, reverse):
    (states,) = local_call(
        functools.partial(scan_body, reverse),
        [blocks],
        [pltpu.HBM(blocks.shape, blocks.dtype)],
        blocks.size,
        scratch=[
            pltpu.VMEM(blocks.shape, blocks.dtype),
            pltpu.SemaphoreType.DMA((blocks.shape[0],)),
        ],
    )
    return states


def places_in_order(count):
    quarter = count // 4
    first, second, third, fourth = (list(range(at, at + quarter)) for at in range(0, count, quarter))
    half = quarter // 2
    return second + first[:half] + third[:half] + first[half:] + third[half:] + fourth


def exchange(pieces, axis):
    groups = [places_in_order(lax.axis_size(axis))]
    return lax.all_to_all(pieces, axis, 0, 0, axis_index_groups=groups)


def in_pieces(state, axis):
    count = lax.axis_size(axis)
    rows, cols = state.shape
    return state.reshape(count, rows // count, cols)


def shards(queries, keys, values, out_grad, gain):
    rows, width = queries.shape
    total_width = width * lax.axis_size("head")
    bf16, f32 = jnp.bfloat16, jnp.float32
    tokens, state = (rows, width), (width, HEAD_DIM)
    small = 2 * rows * width * HEAD_DIM
    large = 2 * rows * rows * width * 3 // 4
    gain_row = gain.reshape(1, width)
    flat = (width, rows)
    chunks = pltpu.SemaphoreType.DMA((width // COPY_COLS,))
    vm, hbm = pltpu.VMEM, pltpu.HBM
    rows_vm, flat_vm, state_vm = vm(tokens, bf16), vm(flat, bf16), vm(state, bf16)

    (own_kv,) = local_call(
        states_body,
        [],
        [hbm(state, bf16)],
        small,
        [keys, values],
        [rows_vm] * 2 + [state_vm] + [chunks] * 3,
    )
    kv_blocks = exchange(in_pieces(own_kv, "seq"), "seq")
    flipped, grad_flipped = local_call(
        flip_body, [], [flat_vm] * 2, large, [queries, out_grad], [rows_vm] * 2 + [chunks] * 2
    )
    kv_blocks, flipped, grad_flipped = lax.optimization_barrier((kv_blocks, flipped, grad_flipped))
    kv_low = exchange(scan_blocks(kv_blocks, False), "seq").reshape(state)
    (local,) = local_call(
        local_body, [flipped], [flat_vm], 2 * large, [keys, values], [rows_vm] * 2 + [chunks] * 2
    )
    attended, sums = local_call(
        sums_body,
        [gain_row, flipped, grad_flipped, local, kv_low],
        [flat_vm, vm((2, rows), f32)],
        small,
        aliases={3: 0},
    )
    sums = lax.psum(sums, "head")
    dout_flipped, own_grad = local_call(
        functools.partial(dout_body, total_width),
        [gain_row, flipped, grad_flipped, attended, sums],
        [flat_vm, hbm(state, bf16)],
        small,
        scratch=[state_vm, chunks],
        aliases={3: 0},
    )
    grad_blocks = exchange(in_pieces(own_grad, "seq"), "seq")
    early = width // 2 // COPY_COLS * COPY_COLS
    early_vm, late_vm = vm((rows, early), bf16), vm((rows, width - early), bf16)
    query_grad, dout, early_part = local_call(
        query_body,
        [dout_flipped, kv_low],
        [hbm(tokens, bf16), rows_vm, early_vm],
        2 * large + small,
        [queries, keys, values],
        [early_vm] + [rows_vm] * 3 + [chunks] * 4,
    )
    grad_blocks, query_grad, dout, early_part = lax.optimization_barrier(
        (grad_blocks, query_grad, dout, early_part)
    )
    grad_low = exchange(scan_blocks(grad_blocks, True), "seq").reshape(state)
    key_part, late_part, value_kept = local_call(
        inner_body,
        [dout],
        [rows_vm, late_vm, rows_vm],
        3 * large,
        [queries, keys, values],
        [rows_vm, late_vm] + [chunks] * 3,
        {3: 0},
    )
    key_grad, value_grad = local_call(
        final_body,
        [value_kept, key_part, early_part, late_part, grad_low],
        [hbm(tokens, bf16)] * 2,
        2 * small,
        [keys],
        [rows_vm] * 3 + [chunks] * 3,
    )
    return query_grad, key_grad, value_grad


def solution(mesh):
    return jax.shard_map(
        shards,
        mesh=mesh,
        in_specs=(
            P("seq", "head"),
            P("seq", "head"),
            P("seq", "head"),
            P("seq", "head"),
            P("head"),
        ),
        out_specs=(P("seq", "head"), P("seq", "head"), P("seq", "head")),
        check_vma=False,
    )
```

```python
import functools

import jax
import jax.numpy as jnp
from jax import lax
from jax.experimental import pallas as pl
from jax.experimental.pallas import tpu as pltpu
from jax.sharding import PartitionSpec as P

HEAD_DIM = 128
BLOCK = 256
COPY_COLS = 256
EPSILON = 1e-06
MIB = 1 << 20


def mm(a, b):
    return lax.dot_general(a, b, (((1,), (0,)), ((), ())), preferred_element_type=jnp.float32)


def mm_nt(a, b):
    return lax.dot_general(a, b, (((1,), (1,)), ((), ())), preferred_element_type=jnp.float32)


def mm_tn(a, b):
    return lax.dot_general(a, b, (((0,), (0,)), ((), ())), preferred_element_type=jnp.float32)


def pieces_of(ref, size):
    return [slice(at, at + size) for at in range(0, ref.shape[1], size)]


def masked(scores, row_start, col_start, rows_first):
    rows = row_start + lax.broadcasted_iota(jnp.int32, scores.shape, 0)
    cols = col_start + lax.broadcasted_iota(jnp.int32, scores.shape, 1)
    keep = rows >= cols if rows_first else cols >= rows
    return jnp.where(keep, scores, 0.0).astype(jnp.bfloat16)


def column_copies(source, target, sems):
    copies = []
    for index, cols in enumerate(pieces_of(source, COPY_COLS)):
        copies.append(pltpu.make_async_copy(source.at[:, cols], target.at[:, cols], sems.at[index]))
    return copies


def row_copies(source, target, sems):
    copies = []
    for index in range(source.shape[0] // COPY_COLS):
        part = slice(index * COPY_COLS, (index + 1) * COPY_COLS)
        copies.append(pltpu.make_async_copy(source.at[part, :], target.at[part, :], sems.at[index]))
    return copies


def start_all(*groups):
    for parts in zip(*groups):
        for part in parts:
            part.start()


def wait_all(*groups):
    for group in groups:
        for part in group:
            part.wait()


def states_body(
    key_hbm, value_hbm, state_hbm, key_ref, value_ref, state_ref, key_sems, value_sems, state_sems
):
    stores = row_copies(state_ref, state_hbm, state_sems)
    key_copies = column_copies(key_hbm, key_ref, key_sems)
    value_copies = column_copies(value_hbm, value_ref, value_sems)
    start_all(key_copies, value_copies)
    for index, cols in enumerate(pieces_of(key_ref, COPY_COLS)):
        key_copies[index].wait()
        value_copies[index].wait()
        for start in range(cols.start, cols.stop, HEAD_DIM):
            head = slice(start, start + HEAD_DIM)
            state_ref[head, :] = mm_tn(key_ref[:, head], value_ref[:, head]).astype(jnp.bfloat16)
        stores[index].start()
    wait_all(stores)


def flip_body(query_hbm, grad_hbm, flipped_ref, grad_flipped_ref, query_ref, grad_ref, query_sems, grad_sems):
    loads = (
        (query_ref, flipped_ref, column_copies(query_hbm, query_ref, query_sems)),
        (grad_ref, grad_flipped_ref, column_copies(grad_hbm, grad_ref, grad_sems)),
    )
    start_all(loads[0][2])
    start_all(loads[1][2])
    for source, target, copies in loads:
        for copy, cols in zip(copies, pieces_of(source, COPY_COLS)):
            copy.wait()
            target[cols, :] = source[:, cols].T


def local_body(key_hbm, value_hbm, flipped_ref, local_ref, key_ref, value_ref, key_sems, value_sems):
    rows = key_ref.shape[0]
    key_copies = column_copies(key_hbm, key_ref, key_sems)
    value_copies = column_copies(value_hbm, value_ref, value_sems)
    start_all(key_copies, value_copies)
    for index, step in enumerate(pieces_of(key_ref, COPY_COLS)):
        key_copies[index].wait()
        value_copies[index].wait()
        for left in range(step.start, step.stop, HEAD_DIM):
            cols = slice(left, left + HEAD_DIM)
            for start in range(0, rows, BLOCK):
                end = start + BLOCK
                scores = mm(key_ref[:end, cols], flipped_ref[cols, start:end])
                weights = masked(scores, 0, start, False)
                local = mm_tn(value_ref[:end, cols], weights)
                local_ref[cols, start:end] = local.astype(jnp.bfloat16)


def scan_body(reverse, block_ref, state_hbm, state_ref, sems):
    count = block_ref.shape[0]
    total = jnp.zeros(block_ref.shape[1:], jnp.float32)
    places = places_in_order(count)
    stores = []
    for place in range(count - 1, -1, -1) if reverse else range(count):
        rank = places.index(place)
        state_ref[rank] = total.astype(jnp.bfloat16)
        total = total + block_ref[rank].astype(jnp.float32)
        stores.append(pltpu.make_async_copy(state_ref.at[rank], state_hbm.at[rank], sems.at[rank]))
        stores[-1].start()
    wait_all(stores)


def heads_of(ref):
    return [slice(at, at + HEAD_DIM) for at in range(0, ref.shape[0], HEAD_DIM)]


def scaled_grad(gain_ref, grad_ref, head):
    gain = jnp.broadcast_to(gain_ref[:, head], (HEAD_DIM, HEAD_DIM)).T
    gain = jnp.concatenate([gain] * (grad_ref.shape[1] // HEAD_DIM), axis=1)
    return gain * grad_ref[head, :].astype(jnp.float32)


def fold(values):
    parts = [values[at : at + 8, :] for at in range(0, values.shape[0], 8)]
    while len(parts) > 1:
        parts = [sum(parts[at + 1 : at + 2], parts[at]) for at in range(0, len(parts), 2)]
    return parts[0]


def sums_body(gain_ref, flipped_ref, grad_ref, local_ref, state_ref, attended_ref, sums_ref):
    square = cross = jnp.zeros((8, local_ref.shape[1]), jnp.float32)
    for head in heads_of(local_ref):
        attended = mm_tn(state_ref[head, :], flipped_ref[head, :])
        attended = attended + attended_ref[head, :].astype(jnp.float32)
        attended_ref[head, :] = attended.astype(jnp.bfloat16)
        square += fold(attended * attended)
        cross += fold(scaled_grad(gain_ref, grad_ref, head) * attended)
    square = jnp.sum(square, axis=0, keepdims=True)
    cross = jnp.sum(cross, axis=0, keepdims=True)
    sums_ref[0:1, :] = square
    sums_ref[1:2, :] = cross


def dout_body(
    width, gain_ref, flipped_ref, grad_ref, attended_ref, sums_ref, dout_ref, own_hbm, own_ref, sems
):
    stores = row_copies(own_ref, own_hbm, sems)
    inverse = 1.0 / jnp.sqrt(sums_ref[0:1, :] / width + EPSILON)
    drop = sums_ref[1:2, :] * (inverse * inverse * inverse) / width
    for head in heads_of(dout_ref):
        attended = dout_ref[head, :].astype(jnp.float32)
        dout = scaled_grad(gain_ref, grad_ref, head) * inverse - attended * drop
        dout = dout.astype(jnp.bfloat16)
        dout_ref[head, :] = dout
        own_ref[head, :] = mm_nt(flipped_ref[head, :], dout).astype(jnp.bfloat16)
        if head.stop % COPY_COLS == 0:
            stores[head.stop // COPY_COLS - 1].start()
    wait_all(stores)


def value_local(query_ref, key_ref, dout, cols, target):
    rows = key_ref.shape[0]
    for start in range(0, rows, BLOCK):
        end = start + BLOCK
        weights = masked(mm_nt(key_ref[start:end, cols], query_ref[start:, cols]), 0, 0, False)
        target[start:end, :] = mm(weights, dout[start:, :]).astype(jnp.bfloat16)


def query_body(
    query_hbm, key_hbm, value_hbm, flipped_ref, state_ref, out_hbm, dout_ref, value_out,
    query_ref, key_ref, value_ref, out_ref, query_sems, key_sems, value_sems, out_sems,
):
    rows = dout_ref.shape[0]
    early = value_out.shape[1]
    query_copies = column_copies(query_hbm.at[:, :early], query_ref, query_sems)
    key_copies = column_copies(key_hbm, key_ref, key_sems)
    value_copies = column_copies(value_hbm, value_ref, value_sems)
    start_all(key_copies, value_copies)
    start_all(query_copies)
    for head in heads_of(flipped_ref):
        dout_ref[:, head] = flipped_ref[head, :].T
    stores = column_copies(out_ref, out_hbm, out_sems)
    for index, step in enumerate(pieces_of(out_ref, COPY_COLS)):
        key_copies[index].wait()
        value_copies[index].wait()
        for left in range(step.start, step.stop, HEAD_DIM):
            cols = slice(left, left + HEAD_DIM)
            for start in range(0, rows, BLOCK):
                end = start + BLOCK
                dout = dout_ref[start:end, cols]
                dscore = masked(mm_nt(dout, value_ref[:end, cols]), start, 0, True)
                grad = mm(dscore, key_ref[:end, cols]) + mm_nt(dout, state_ref[cols, :])
                out_ref[start:end, cols] = grad.astype(jnp.bfloat16)
        stores[index].start()
    wait_all(query_copies)
    for cols in pieces_of(value_out, HEAD_DIM):
        value_local(query_ref, key_ref, dout_ref[:, cols], cols, value_out.at[:, cols])
    wait_all(stores)


def inner_body(
    query_hbm, key_hbm, value_hbm, dout_ref, key_out, value_out, value_ref,
    query_ref, key_ref, query_sems, key_sems, value_sems,
):
    rows, width = key_out.shape
    early = width - value_out.shape[1]
    loads = (
        column_copies(query_hbm, query_ref, query_sems),
        column_copies(value_hbm, value_ref, value_sems),
        column_copies(key_hbm.at[:, early:], key_ref, key_sems),
    )
    start_all(*loads[:2])
    start_all(loads[2])
    for index, step in enumerate(pieces_of(key_out, COPY_COLS)):
        loads[0][index].wait()
        loads[1][index].wait()
        if step.start == early:
            wait_all(loads[2])
        for left in range(step.start, step.stop, HEAD_DIM):
            cols = slice(left, left + HEAD_DIM)
            dout = key_out[:, cols]
            for start in range(0, rows, BLOCK):
                end = start + BLOCK
                scores = mm_nt(value_ref[start:end, cols], dout[start:, :])
                key_out[start:end, cols] = mm(masked(scores, 0, 0, False), query_ref[start:, cols]).astype(jnp.bfloat16)
            if left >= early:
                late = slice(left - early, left - early + HEAD_DIM)
                value_local(query_ref.at[:, early:], key_ref, dout, late, value_out.at[:, late])


def final_body(
    key_hbm, value_ref, key_part, early_part, late_part, state_ref, key_out_hbm, value_out_hbm,
    key_ref, key_out, value_out, in_sems, key_sems, value_sems,
):
    keys = column_copies(key_hbm, key_ref, in_sems)
    start_all(keys)
    key_stores = column_copies(key_out, key_out_hbm, key_sems)
    value_stores = column_copies(value_out, value_out_hbm, value_sems)
    for index, step in enumerate(pieces_of(key_out, COPY_COLS)):
        for left in range(step.start, step.stop, HEAD_DIM):
            cols = slice(left, left + HEAD_DIM)
            grad = key_part[:, cols].astype(jnp.float32) + mm_nt(value_ref[:, cols], state_ref[cols, :])
            key_out[:, cols] = grad.astype(jnp.bfloat16)
        key_stores[index].start()
    for index, step in enumerate(pieces_of(value_out, COPY_COLS)):
        keys[index].wait()
        for left in range(step.start, step.stop, HEAD_DIM):
            cols = slice(left, left + HEAD_DIM)
            early = early_part.shape[1]
            if left < early:
                part = early_part[:, cols]
            else:
                part = late_part[:, left - early : left - early + HEAD_DIM]
            grad = part.astype(jnp.float32) + mm(key_ref[:, cols], state_ref[cols, :])
            value_out[:, cols] = grad.astype(jnp.bfloat16)
        value_stores[index].start()
    wait_all(key_stores, value_stores)


def local_call(body, in_args, outs, flops, hbm_args=(), scratch=(), aliases=None):
    args = [pltpu.with_memory_space_constraint(a, pltpu.HBM) for a in hbm_args]
    args += [pltpu.with_memory_space_constraint(a, pltpu.VMEM) for a in in_args]
    specs = [pl.BlockSpec(memory_space=pltpu.HBM)] * len(hbm_args)
    specs += [pl.BlockSpec(memory_space=pltpu.VMEM)] * len(in_args)
    out_specs = []
    for out in outs:
        out_specs.append(pl.BlockSpec(memory_space=out.memory_space))
    moved = sum(a.size * a.dtype.itemsize for a in args)
    return pl.pallas_call(
        body,
        in_specs=specs,
        out_specs=out_specs,
        out_shape=outs,
        scratch_shapes=scratch,
        input_output_aliases=aliases or {},
        compiler_params=pltpu.CompilerParams(vmem_limit_bytes=16 * MIB),
        cost_estimate=pl.CostEstimate(flops=flops, bytes_accessed=moved, transcendentals=0),
    )(*args)


def scan_blocks(blocks, reverse):
    (states,) = local_call(
        functools.partial(scan_body, reverse),
        [blocks],
        [pltpu.HBM(blocks.shape, blocks.dtype)],
        blocks.size,
        scratch=[
            pltpu.VMEM(blocks.shape, blocks.dtype),
            pltpu.SemaphoreType.DMA((blocks.shape[0],)),
        ],
    )
    return states


def places_in_order(count):
    quarter = count // 4
    first, second, third, fourth = (list(range(at, at + quarter)) for at in range(0, count, quarter))
    half = quarter // 2
    order = second + first[:half] + third[:half] + first[half:] + third[half:] + fourth
    return [count - 1 - place for place in order]


def exchange(pieces, axis):
    groups = [places_in_order(lax.axis_size(axis))]
    return lax.all_to_all(pieces, axis, 0, 0, axis_index_groups=groups)


def in_pieces(state, axis):
    count = lax.axis_size(axis)
    rows, cols = state.shape
    return state.reshape(count, rows // count, cols)


def shards(queries, keys, values, out_grad, gain):
    rows, width = queries.shape
    total_width = width * lax.axis_size("head")
    bf16, f32 = jnp.bfloat16, jnp.float32
    tokens, state = (rows, width), (width, HEAD_DIM)
    small = 2 * rows * width * HEAD_DIM
    large = 2 * rows * rows * width * 3 // 4
    gain_row = gain.reshape(1, width)
    flat = (width, rows)
    chunks = pltpu.SemaphoreType.DMA((width // COPY_COLS,))
    vm, hbm = pltpu.VMEM, pltpu.HBM
    rows_vm, flat_vm, state_vm = vm(tokens, bf16), vm(flat, bf16), vm(state, bf16)

    (own_kv,) = local_call(
        states_body,
        [],
        [hbm(state, bf16)],
        small,
        [keys, values],
        [rows_vm] * 2 + [state_vm] + [chunks] * 3,
    )
    kv_blocks = exchange(in_pieces(own_kv, "seq"), "seq")
    flipped, grad_flipped = local_call(
        flip_body, [], [flat_vm] * 2, large, [queries, out_grad], [rows_vm] * 2 + [chunks] * 2
    )
    kv_blocks, flipped, grad_flipped = lax.optimization_barrier((kv_blocks, flipped, grad_flipped))
    kv_low = exchange(scan_blocks(kv_blocks, False), "seq").reshape(state)
    (local,) = local_call(
        local_body, [flipped], [flat_vm], 2 * large, [keys, values], [rows_vm] * 2 + [chunks] * 2
    )
    attended, sums = local_call(
        sums_body,
        [gain_row, flipped, grad_flipped, local, kv_low],
        [flat_vm, vm((2, rows), f32)],
        small,
        aliases={3: 0},
    )
    sums = lax.psum(sums, "head")
    dout_flipped, own_grad = local_call(
        functools.partial(dout_body, total_width),
        [gain_row, flipped, grad_flipped, attended, sums],
        [flat_vm, hbm(state, bf16)],
        small,
        scratch=[state_vm, chunks],
        aliases={3: 0},
    )
    grad_blocks = exchange(in_pieces(own_grad, "seq"), "seq")
    early = width // 2 // COPY_COLS * COPY_COLS
    early_vm, late_vm = vm((rows, early), bf16), vm((rows, width - early), bf16)
    query_grad, dout, early_part = local_call(
        query_body,
        [dout_flipped, kv_low],
        [hbm(tokens, bf16), rows_vm, early_vm],
        2 * large + small,
        [queries, keys, values],
        [early_vm] + [rows_vm] * 3 + [chunks] * 4,
    )
    grad_blocks, query_grad, dout, early_part = lax.optimization_barrier(
        (grad_blocks, query_grad, dout, early_part)
    )
    grad_low = exchange(scan_blocks(grad_blocks, True), "seq").reshape(state)
    key_part, late_part, value_kept = local_call(
        inner_body,
        [dout],
        [rows_vm, late_vm, rows_vm],
        3 * large,
        [queries, keys, values],
        [rows_vm, late_vm] + [chunks] * 3,
        {3: 0},
    )
    key_grad, value_grad = local_call(
        final_body,
        [value_kept, key_part, early_part, late_part, grad_low],
        [hbm(tokens, bf16)] * 2,
        2 * small,
        [keys],
        [rows_vm] * 3 + [chunks] * 3,
    )
    return query_grad, key_grad, value_grad


def solution(mesh):
    return jax.shard_map(
        shards,
        mesh=mesh,
        in_specs=(
            P("seq", "head"),
            P("seq", "head"),
            P("seq", "head"),
            P("seq", "head"),
            P("head"),
        ),
        out_specs=(P("seq", "head"), P("seq", "head"), P("seq", "head")),
        check_vma=False,
    )
```

```python
import functools

import jax
import jax.numpy as jnp
from jax import lax
from jax.experimental import pallas as pl
from jax.experimental.pallas import tpu as pltpu
from jax.sharding import PartitionSpec as P

HEAD_DIM = 128
BLOCK = 256
COPY_COLS = 256
EPSILON = 1e-06
MIB = 1 << 20


def mm(a, b):
    return lax.dot_general(a, b, (((1,), (0,)), ((), ())), preferred_element_type=jnp.float32)


def mm_nt(a, b):
    return lax.dot_general(a, b, (((1,), (1,)), ((), ())), preferred_element_type=jnp.float32)


def mm_tn(a, b):
    return lax.dot_general(a, b, (((0,), (0,)), ((), ())), preferred_element_type=jnp.float32)


def pieces_of(ref, size):
    return [slice(at, at + size) for at in range(0, ref.shape[1], size)]


def masked(scores, diagonal, rows_first):
    shape = (BLOCK, BLOCK)
    rows = lax.broadcasted_iota(jnp.int32, shape, 0)
    cols = lax.broadcasted_iota(jnp.int32, shape, 1)
    keep = rows >= cols if rows_first else cols >= rows
    inside = slice(diagonal, diagonal + BLOCK)
    kept = jnp.where(keep, scores[:, inside], 0.0).astype(jnp.bfloat16)
    before = scores[:, :diagonal].astype(jnp.bfloat16)
    after = scores[:, inside.stop :].astype(jnp.bfloat16)
    parts = [part for part in (before, kept, after) if part.shape[1]]
    return jnp.concatenate(parts, axis=1) if len(parts) > 1 else kept


def column_copies(source, target, sems):
    copies = []
    for index, cols in enumerate(pieces_of(source, COPY_COLS)):
        copies.append(pltpu.make_async_copy(source.at[:, cols], target.at[:, cols], sems.at[index]))
    return copies


def row_copies(source, target, sems):
    copies = []
    for index in range(source.shape[0] // COPY_COLS):
        part = slice(index * COPY_COLS, (index + 1) * COPY_COLS)
        copies.append(pltpu.make_async_copy(source.at[part, :], target.at[part, :], sems.at[index]))
    return copies


def start_all(*groups):
    for parts in zip(*groups):
        for part in parts:
            part.start()


def wait_all(*groups):
    for group in groups:
        for part in group:
            part.wait()


def states_body(
    key_hbm, value_hbm, state_hbm, key_ref, value_ref, state_ref, key_sems, value_sems, state_sems
):
    stores = row_copies(state_ref, state_hbm, state_sems)
    key_copies = column_copies(key_hbm, key_ref, key_sems)
    value_copies = column_copies(value_hbm, value_ref, value_sems)
    start_all(key_copies, value_copies)
    for index, cols in enumerate(pieces_of(key_ref, COPY_COLS)):
        key_copies[index].wait()
        value_copies[index].wait()
        for start in range(cols.start, cols.stop, HEAD_DIM):
            head = slice(start, start + HEAD_DIM)
            state_ref[head, :] = mm_tn(key_ref[:, head], value_ref[:, head]).astype(jnp.bfloat16)
        stores[index].start()
    wait_all(stores)


def flip_body(query_hbm, grad_hbm, flipped_ref, grad_flipped_ref, query_ref, grad_ref, query_sems, grad_sems):
    loads = (
        (query_ref, flipped_ref, column_copies(query_hbm, query_ref, query_sems)),
        (grad_ref, grad_flipped_ref, column_copies(grad_hbm, grad_ref, grad_sems)),
    )
    start_all(loads[0][2])
    start_all(loads[1][2])
    for source, target, copies in loads:
        for copy, cols in zip(copies, pieces_of(source, COPY_COLS)):
            copy.wait()
            target[cols, :] = source[:, cols].T


def local_body(key_hbm, value_hbm, flipped_ref, local_ref, key_ref, value_ref, key_sems, value_sems):
    rows = key_ref.shape[0]
    key_copies = column_copies(key_hbm, key_ref, key_sems)
    value_copies = column_copies(value_hbm, value_ref, value_sems)
    start_all(key_copies, value_copies)
    for index, step in enumerate(pieces_of(key_ref, COPY_COLS)):
        key_copies[index].wait()
        value_copies[index].wait()
        for left in range(step.start, step.stop, HEAD_DIM):
            cols = slice(left, left + HEAD_DIM)
            for start in range(0, rows, BLOCK):
                end = start + BLOCK
                parts = []
                for row in range(0, end, BLOCK):
                    key = key_ref[row : row + BLOCK, cols]
                    scores = mm(key, flipped_ref[cols, start:end])
                    below = row == start
                    parts.append(masked(scores, 0, False) if below else scores.astype(jnp.bfloat16))
                weights = jnp.concatenate(parts, axis=0) if len(parts) > 1 else parts[0]
                local = mm_tn(value_ref[:end, cols], weights)
                local_ref[cols, start:end] = local.astype(jnp.bfloat16)


def scan_body(reverse, block_ref, state_hbm, state_ref, sems):
    count = block_ref.shape[0]
    total = jnp.zeros(block_ref.shape[1:], jnp.float32)
    places = places_in_order(count)
    stores = []
    for place in range(count - 1, -1, -1) if reverse else range(count):
        rank = places.index(place)
        state_ref[rank] = total.astype(jnp.bfloat16)
        total = total + block_ref[rank].astype(jnp.float32)
        stores.append(pltpu.make_async_copy(state_ref.at[rank], state_hbm.at[rank], sems.at[rank]))
        stores[-1].start()
    wait_all(stores)


def heads_of(ref):
    return [slice(at, at + HEAD_DIM) for at in range(0, ref.shape[0], HEAD_DIM)]


def scaled_grad(gain_ref, grad_ref, head):
    gain = jnp.broadcast_to(gain_ref[:, head], (HEAD_DIM, HEAD_DIM)).T
    gain = jnp.concatenate([gain] * (grad_ref.shape[1] // HEAD_DIM), axis=1)
    return gain * grad_ref[head, :].astype(jnp.float32)


def fold(values):
    parts = [values[at : at + 8, :] for at in range(0, values.shape[0], 8)]
    while len(parts) > 1:
        parts = [sum(parts[at + 1 : at + 2], parts[at]) for at in range(0, len(parts), 2)]
    return parts[0]


def sums_body(gain_ref, flipped_ref, grad_ref, local_ref, state_ref, attended_ref, sums_ref):
    square = cross = jnp.zeros((8, local_ref.shape[1]), jnp.float32)
    for head in heads_of(local_ref):
        attended = mm_tn(state_ref[head, :], flipped_ref[head, :])
        attended = attended + attended_ref[head, :].astype(jnp.float32)
        attended_ref[head, :] = attended.astype(jnp.bfloat16)
        square += fold(attended * attended)
        cross += fold(scaled_grad(gain_ref, grad_ref, head) * attended)
    square = jnp.sum(square, axis=0, keepdims=True)
    cross = jnp.sum(cross, axis=0, keepdims=True)
    for group in range(sums_ref.shape[0]):
        sums_ref[group, 0:1, :] = square
        sums_ref[group, 1:2, :] = cross


def dout_body(
    width, gain_ref, flipped_ref, grad_ref, attended_ref, sums_ref, dout_ref, own_hbm, own_ref, sems
):
    stores = row_copies(own_ref, own_hbm, sems)
    sums = sum(sums_ref[group] for group in range(sums_ref.shape[0]))
    inverse = 1.0 / jnp.sqrt(sums[0:1, :] / width + EPSILON)
    drop = sums[1:2, :] * (inverse * inverse * inverse) / width
    for head in heads_of(dout_ref):
        attended = dout_ref[head, :].astype(jnp.float32)
        dout = scaled_grad(gain_ref, grad_ref, head) * inverse - attended * drop
        dout = dout.astype(jnp.bfloat16)
        dout_ref[head, :] = dout
        own_ref[head, :] = mm_nt(flipped_ref[head, :], dout).astype(jnp.bfloat16)
        if head.stop % COPY_COLS == 0:
            stores[head.stop // COPY_COLS - 1].start()
    wait_all(stores)


def value_local(query_ref, key_ref, dout, cols, target):
    rows = key_ref.shape[0]
    for start in range(0, rows, BLOCK):
        end = start + BLOCK
        weights = masked(mm_nt(key_ref[start:end, cols], query_ref[start:, cols]), 0, False)
        target[start:end, :] = mm(weights, dout[start:, :]).astype(jnp.bfloat16)


def query_body(
    query_hbm, key_hbm, value_hbm, flipped_ref, state_ref, out_hbm, dout_ref, value_out,
    query_ref, key_ref, value_ref, out_ref, query_sems, key_sems, value_sems, out_sems,
):
    rows = dout_ref.shape[0]
    early = value_out.shape[1]
    query_copies = column_copies(query_hbm.at[:, :early], query_ref, query_sems)
    key_copies = column_copies(key_hbm, key_ref, key_sems)
    value_copies = column_copies(value_hbm, value_ref, value_sems)
    start_all(key_copies, value_copies)
    start_all(query_copies)
    for head in heads_of(flipped_ref):
        dout_ref[:, head] = flipped_ref[head, :].T
    stores = column_copies(out_ref, out_hbm, out_sems)
    for index, step in enumerate(pieces_of(out_ref, COPY_COLS)):
        key_copies[index].wait()
        value_copies[index].wait()
        for left in range(step.start, step.stop, HEAD_DIM):
            cols = slice(left, left + HEAD_DIM)
            for start in range(0, rows, BLOCK):
                end = start + BLOCK
                dout = dout_ref[start:end, cols]
                dscore = masked(mm_nt(dout, value_ref[:end, cols]), start, True)
                grad = mm(dscore, key_ref[:end, cols]) + mm_nt(dout, state_ref[cols, :])
                out_ref[start:end, cols] = grad.astype(jnp.bfloat16)
        stores[index].start()
    wait_all(query_copies)
    for cols in pieces_of(value_out, HEAD_DIM):
        value_local(query_ref, key_ref, dout_ref[:, cols], cols, value_out.at[:, cols])
    wait_all(stores)


def inner_body(
    query_hbm, key_hbm, value_hbm, dout_ref, key_out, value_out, value_ref,
    query_ref, key_ref, query_sems, key_sems, value_sems,
):
    rows, width = key_out.shape
    early = width - value_out.shape[1]
    loads = (
        column_copies(query_hbm, query_ref, query_sems),
        column_copies(value_hbm, value_ref, value_sems),
        column_copies(key_hbm.at[:, early:], key_ref, key_sems),
    )
    start_all(*loads[:2])
    start_all(loads[2])
    for index, step in enumerate(pieces_of(key_out, COPY_COLS)):
        loads[0][index].wait()
        loads[1][index].wait()
        if step.start == early:
            wait_all(loads[2])
        for left in range(step.start, step.stop, HEAD_DIM):
            cols = slice(left, left + HEAD_DIM)
            dout = key_out[:, cols]
            for start in range(0, rows, BLOCK):
                end = start + BLOCK
                scores = mm_nt(value_ref[start:end, cols], dout[start:, :])
                grad = mm(masked(scores, 0, False), query_ref[start:, cols])
                key_out[start:end, cols] = grad.astype(jnp.bfloat16)
            if left >= early:
                late = slice(left - early, left - early + HEAD_DIM)
                value_local(query_ref.at[:, early:], key_ref, dout, late, value_out.at[:, late])


def final_body(
    key_hbm, value_ref, key_part, early_part, late_part, state_ref, key_out_hbm, value_out_hbm,
    key_ref, key_out, value_out, in_sems, key_sems, value_sems,
):
    keys = column_copies(key_hbm, key_ref, in_sems)
    start_all(keys)
    key_stores = column_copies(key_out, key_out_hbm, key_sems)
    value_stores = column_copies(value_out, value_out_hbm, value_sems)
    for index, step in enumerate(pieces_of(key_out, COPY_COLS)):
        for left in range(step.start, step.stop, HEAD_DIM):
            cols = slice(left, left + HEAD_DIM)
            grad = key_part[:, cols].astype(jnp.float32) + mm_nt(value_ref[:, cols], state_ref[cols, :])
            key_out[:, cols] = grad.astype(jnp.bfloat16)
        key_stores[index].start()
    for index, step in enumerate(pieces_of(value_out, COPY_COLS)):
        keys[index].wait()
        for left in range(step.start, step.stop, HEAD_DIM):
            cols = slice(left, left + HEAD_DIM)
            early = early_part.shape[1]
            if left < early:
                part = early_part[:, cols]
            else:
                part = late_part[:, left - early : left - early + HEAD_DIM]
            grad = part.astype(jnp.float32) + mm(key_ref[:, cols], state_ref[cols, :])
            value_out[:, cols] = grad.astype(jnp.bfloat16)
        value_stores[index].start()
    wait_all(key_stores, value_stores)


def local_call(body, in_args, outs, flops, hbm_args=(), scratch=(), aliases=None):
    args = [pltpu.with_memory_space_constraint(a, pltpu.HBM) for a in hbm_args]
    args += [pltpu.with_memory_space_constraint(a, pltpu.VMEM) for a in in_args]
    specs = [pl.BlockSpec(memory_space=pltpu.HBM)] * len(hbm_args)
    specs += [pl.BlockSpec(memory_space=pltpu.VMEM)] * len(in_args)
    out_specs = []
    for out in outs:
        out_specs.append(pl.BlockSpec(memory_space=out.memory_space))
    moved = sum(a.size * a.dtype.itemsize for a in args)
    return pl.pallas_call(
        body,
        in_specs=specs,
        out_specs=out_specs,
        out_shape=outs,
        scratch_shapes=scratch,
        input_output_aliases=aliases or {},
        compiler_params=pltpu.CompilerParams(vmem_limit_bytes=16 * MIB),
        cost_estimate=pl.CostEstimate(flops=flops, bytes_accessed=moved, transcendentals=0),
    )(*args)


def scan_blocks(blocks, reverse):
    (states,) = local_call(
        functools.partial(scan_body, reverse),
        [blocks],
        [pltpu.HBM(blocks.shape, blocks.dtype)],
        blocks.size,
        scratch=[
            pltpu.VMEM(blocks.shape, blocks.dtype),
            pltpu.SemaphoreType.DMA((blocks.shape[0],)),
        ],
    )
    return states


def places_in_order(count):
    quarter = count // 4
    first, second, third, fourth = (list(range(at, at + quarter)) for at in range(0, count, quarter))
    half = quarter // 2
    order = second + first[:half] + third[:half] + first[half:] + third[half:] + fourth
    return [count - 1 - place for place in order]


def odd_first(count):
    return list(range(1, count, 2)) + list(range(0, count, 2))


def exchange(pieces, axis):
    groups = [places_in_order(lax.axis_size(axis))]
    return lax.all_to_all(pieces, axis, 0, 0, axis_index_groups=groups)


def in_pieces(state, axis):
    count = lax.axis_size(axis)
    rows, cols = state.shape
    return state.reshape(count, rows // count, cols)


def shards(queries, keys, values, out_grad, gain):
    rows, width = queries.shape
    total_width = width * lax.axis_size("head")
    bf16, f32 = jnp.bfloat16, jnp.float32
    tokens, state = (rows, width), (width, HEAD_DIM)
    small = 2 * rows * width * HEAD_DIM
    large = 2 * rows * rows * width * 3 // 4
    gain_row = gain.reshape(1, width)
    flat = (width, rows)
    chunks = pltpu.SemaphoreType.DMA((width // COPY_COLS,))
    vm, hbm = pltpu.VMEM, pltpu.HBM
    rows_vm, flat_vm, state_vm = vm(tokens, bf16), vm(flat, bf16), vm(state, bf16)

    (own_kv,) = local_call(
        states_body,
        [],
        [hbm(state, bf16)],
        small,
        [keys, values],
        [rows_vm] * 2 + [state_vm] + [chunks] * 3,
    )
    kv_blocks = exchange(in_pieces(own_kv, "seq"), "seq")
    flipped, grad_flipped = local_call(
        flip_body, [], [flat_vm] * 2, large, [queries, out_grad], [rows_vm] * 2 + [chunks] * 2
    )
    kv_blocks, flipped, grad_flipped = lax.optimization_barrier((kv_blocks, flipped, grad_flipped))
    kv_low = exchange(scan_blocks(kv_blocks, False), "seq").reshape(state)
    (local,) = local_call(
        local_body, [flipped], [flat_vm], 2 * large, [keys, values], [rows_vm] * 2 + [chunks] * 2
    )
    groups = lax.axis_size("head")
    attended, sums = local_call(
        sums_body,
        [gain_row, flipped, grad_flipped, local, kv_low],
        [flat_vm, vm((groups, 2, rows), f32)],
        small,
        aliases={3: 0},
    )
    sums = lax.all_to_all(sums, "head", 0, 0, axis_index_groups=[odd_first(groups)])
    dout_flipped, own_grad = local_call(
        functools.partial(dout_body, total_width),
        [gain_row, flipped, grad_flipped, attended, sums],
        [flat_vm, hbm(state, bf16)],
        small,
        scratch=[state_vm, chunks],
        aliases={3: 0},
    )
    grad_blocks = exchange(in_pieces(own_grad, "seq"), "seq")
    early = width * 3 // 4 // COPY_COLS * COPY_COLS
    early_vm, late_vm = vm((rows, early), bf16), vm((rows, width - early), bf16)
    query_grad, dout, early_part = local_call(
        query_body,
        [dout_flipped, kv_low],
        [hbm(tokens, bf16), rows_vm, early_vm],
        2 * large + small,
        [queries, keys, values],
        [early_vm] + [rows_vm] * 3 + [chunks] * 4,
    )
    grad_blocks, query_grad, dout, early_part = lax.optimization_barrier(
        (grad_blocks, query_grad, dout, early_part)
    )
    grad_low = exchange(scan_blocks(grad_blocks, True), "seq").reshape(state)
    key_part, late_part, value_kept = local_call(
        inner_body,
        [dout],
        [rows_vm, late_vm, rows_vm],
        3 * large,
        [queries, keys, values],
        [rows_vm, late_vm] + [chunks] * 3,
        {3: 0},
    )
    key_grad, value_grad = local_call(
        final_body,
        [value_kept, key_part, early_part, late_part, grad_low],
        [hbm(tokens, bf16)] * 2,
        2 * small,
        [keys],
        [rows_vm] * 3 + [chunks] * 3,
    )
    return query_grad, key_grad, value_grad


def solution(mesh):
    return jax.shard_map(
        shards,
        mesh=mesh,
        in_specs=(
            P("seq", "head"),
            P("seq", "head"),
            P("seq", "head"),
            P("seq", "head"),
            P("head"),
        ),
        out_specs=(P("seq", "head"), P("seq", "head"), P("seq", "head")),
        check_vma=False,
    )
```

```python
import functools

import jax
import jax.numpy as jnp
from jax import lax
from jax.experimental import pallas as pl
from jax.experimental.pallas import tpu as pltpu
from jax.sharding import PartitionSpec as P

HEAD_DIM = 128
BLOCK = 256
COPY_COLS = 256
EPSILON = 1e-06
MIB = 1 << 20


def mm(a, b):
    return lax.dot_general(a, b, (((1,), (0,)), ((), ())), preferred_element_type=jnp.float32)


def mm_nt(a, b):
    return lax.dot_general(a, b, (((1,), (1,)), ((), ())), preferred_element_type=jnp.float32)


def mm_tn(a, b):
    return lax.dot_general(a, b, (((0,), (0,)), ((), ())), preferred_element_type=jnp.float32)


def pieces_of(ref, size):
    return [slice(at, at + size) for at in range(0, ref.shape[1], size)]


def masked(scores, diagonal, rows_first):
    shape = (BLOCK, BLOCK)
    rows = lax.broadcasted_iota(jnp.int32, shape, 0)
    cols = lax.broadcasted_iota(jnp.int32, shape, 1)
    keep = rows >= cols if rows_first else cols >= rows
    inside = slice(diagonal, diagonal + BLOCK)
    kept = jnp.where(keep, scores[:, inside], 0.0).astype(jnp.bfloat16)
    before = scores[:, :diagonal].astype(jnp.bfloat16)
    after = scores[:, inside.stop :].astype(jnp.bfloat16)
    parts = [part for part in (before, kept, after) if part.shape[1]]
    return jnp.concatenate(parts, axis=1) if len(parts) > 1 else kept


def column_copies(source, target, sems):
    copies = []
    for index, cols in enumerate(pieces_of(source, COPY_COLS)):
        copies.append(pltpu.make_async_copy(source.at[:, cols], target.at[:, cols], sems.at[index]))
    return copies


def row_copies(source, target, sems):
    copies = []
    for index in range(source.shape[0] // COPY_COLS):
        part = slice(index * COPY_COLS, (index + 1) * COPY_COLS)
        copies.append(pltpu.make_async_copy(source.at[part, :], target.at[part, :], sems.at[index]))
    return copies


def start_all(*groups):
    for parts in zip(*groups):
        for part in parts:
            part.start()


def wait_all(*groups):
    for group in groups:
        for part in group:
            part.wait()


def states_body(
    key_hbm, value_hbm, state_hbm, key_ref, value_ref, state_ref, key_sems, value_sems, state_sems
):
    stores = row_copies(state_ref, state_hbm, state_sems)
    key_copies = column_copies(key_hbm, key_ref, key_sems)
    value_copies = column_copies(value_hbm, value_ref, value_sems)
    start_all(key_copies, value_copies)
    for index, cols in enumerate(pieces_of(key_ref, COPY_COLS)):
        key_copies[index].wait()
        value_copies[index].wait()
        for start in range(cols.start, cols.stop, HEAD_DIM):
            head = slice(start, start + HEAD_DIM)
            state_ref[head, :] = mm_tn(key_ref[:, head], value_ref[:, head]).astype(jnp.bfloat16)
        stores[index].start()
    wait_all(stores)


def flip_body(query_hbm, grad_hbm, flipped_ref, grad_flipped_ref, query_ref, grad_ref, query_sems, grad_sems):
    loads = (
        (query_ref, flipped_ref, column_copies(query_hbm, query_ref, query_sems)),
        (grad_ref, grad_flipped_ref, column_copies(grad_hbm, grad_ref, grad_sems)),
    )
    start_all(loads[0][2])
    start_all(loads[1][2])
    for source, target, copies in loads:
        for copy, cols in zip(copies, pieces_of(source, COPY_COLS)):
            copy.wait()
            target[cols, :] = source[:, cols].T


def local_body(key_hbm, value_hbm, flipped_ref, local_ref, key_ref, value_ref, key_sems, value_sems):
    rows = key_ref.shape[0]
    key_copies = column_copies(key_hbm, key_ref, key_sems)
    value_copies = column_copies(value_hbm, value_ref, value_sems)
    start_all(key_copies, value_copies)
    for index, step in enumerate(pieces_of(key_ref, COPY_COLS)):
        key_copies[index].wait()
        value_copies[index].wait()
        for left in range(step.start, step.stop, HEAD_DIM):
            cols = slice(left, left + HEAD_DIM)
            for start in range(0, rows, BLOCK):
                end = start + BLOCK
                parts = []
                for row in range(0, end, BLOCK):
                    key = key_ref[row : row + BLOCK, cols]
                    scores = mm(key, flipped_ref[cols, start:end])
                    below = row == start
                    parts.append(masked(scores, 0, False) if below else scores.astype(jnp.bfloat16))
                weights = jnp.concatenate(parts, axis=0) if len(parts) > 1 else parts[0]
                local = mm_tn(value_ref[:end, cols], weights)
                local_ref[cols, start:end] = local.astype(jnp.bfloat16)


def scan_body(reverse, block_ref, state_hbm, state_ref, sems):
    count = block_ref.shape[0]
    total = jnp.zeros(block_ref.shape[1:], jnp.float32)
    places = places_in_order(count)
    stores = []
    for place in range(count - 1, -1, -1) if reverse else range(count):
        rank = places.index(place)
        state_ref[rank] = total.astype(jnp.bfloat16)
        total = total + block_ref[rank].astype(jnp.float32)
        stores.append(pltpu.make_async_copy(state_ref.at[rank], state_hbm.at[rank], sems.at[rank]))
        stores[-1].start()
    wait_all(stores)


def heads_of(ref):
    return [slice(at, at + HEAD_DIM) for at in range(0, ref.shape[0], HEAD_DIM)]


def scaled_grad(gain_ref, grad_ref, head):
    gain = jnp.broadcast_to(gain_ref[:, head], (HEAD_DIM, HEAD_DIM)).T
    gain = jnp.concatenate([gain] * (grad_ref.shape[1] // HEAD_DIM), axis=1)
    return gain * grad_ref[head, :].astype(jnp.float32)


def fold(values):
    parts = [values[at : at + 8, :] for at in range(0, values.shape[0], 8)]
    while len(parts) > 1:
        parts = [sum(parts[at + 1 : at + 2], parts[at]) for at in range(0, len(parts), 2)]
    return parts[0]


def sums_body(gain_ref, flipped_ref, grad_ref, local_ref, state_ref, attended_ref, sums_ref):
    square = cross = jnp.zeros((8, local_ref.shape[1]), jnp.float32)
    for head in heads_of(local_ref):
        attended = mm_tn(state_ref[head, :], flipped_ref[head, :])
        attended = attended + attended_ref[head, :].astype(jnp.float32)
        attended_ref[head, :] = attended.astype(jnp.bfloat16)
        square += fold(attended * attended)
        cross += fold(scaled_grad(gain_ref, grad_ref, head) * attended)
    square = jnp.sum(square, axis=0, keepdims=True)
    cross = jnp.sum(cross, axis=0, keepdims=True)
    for group in range(sums_ref.shape[0]):
        sums_ref[group, 0:1, :] = square
        sums_ref[group, 1:2, :] = cross


def dout_body(
    width, gain_ref, flipped_ref, grad_ref, attended_ref, sums_ref, dout_ref, own_hbm, own_ref, sems
):
    stores = row_copies(own_ref, own_hbm, sems)
    sums = sum(sums_ref[group] for group in range(sums_ref.shape[0]))
    inverse = 1.0 / jnp.sqrt(sums[0:1, :] / width + EPSILON)
    drop = sums[1:2, :] * (inverse * inverse * inverse) / width
    for head in heads_of(dout_ref):
        attended = dout_ref[head, :].astype(jnp.float32)
        dout = scaled_grad(gain_ref, grad_ref, head) * inverse - attended * drop
        dout = dout.astype(jnp.bfloat16)
        dout_ref[head, :] = dout
        own_ref[head, :] = mm_nt(flipped_ref[head, :], dout).astype(jnp.bfloat16)
        if head.stop % COPY_COLS == 0:
            stores[head.stop // COPY_COLS - 1].start()
    wait_all(stores)


def value_local(query_ref, key_ref, dout, cols, target):
    rows = key_ref.shape[0]
    for start in range(0, rows, BLOCK):
        end = start + BLOCK
        weights = masked(mm_nt(key_ref[start:end, cols], query_ref[start:, cols]), 0, False)
        target[start:end, :] = mm(weights, dout[start:, :]).astype(jnp.bfloat16)


def query_body(
    query_hbm, key_hbm, value_hbm, flipped_ref, state_ref, out_hbm, dout_ref, value_out,
    query_ref, key_ref, value_ref, out_ref, query_sems, key_sems, value_sems, out_sems,
):
    rows = dout_ref.shape[0]
    early = value_out.shape[1]
    query_copies = column_copies(query_hbm.at[:, :early], query_ref, query_sems)
    key_copies = column_copies(key_hbm, key_ref, key_sems)
    value_copies = column_copies(value_hbm, value_ref, value_sems)
    start_all(key_copies, value_copies)
    start_all(query_copies)
    for head in heads_of(flipped_ref):
        dout_ref[:, head] = flipped_ref[head, :].T
    stores = column_copies(out_ref, out_hbm, out_sems)
    for index, step in enumerate(pieces_of(out_ref, COPY_COLS)):
        key_copies[index].wait()
        value_copies[index].wait()
        for left in range(step.start, step.stop, HEAD_DIM):
            cols = slice(left, left + HEAD_DIM)
            for start in range(0, rows, BLOCK):
                end = start + BLOCK
                dout = dout_ref[start:end, cols]
                dscore = masked(mm_nt(dout, value_ref[:end, cols]), start, True)
                grad = mm(dscore, key_ref[:end, cols]) + mm_nt(dout, state_ref[cols, :])
                out_ref[start:end, cols] = grad.astype(jnp.bfloat16)
        stores[index].start()
    wait_all(query_copies)
    for cols in pieces_of(value_out, HEAD_DIM):
        value_local(query_ref, key_ref, dout_ref[:, cols], cols, value_out.at[:, cols])
    wait_all(stores)


def inner_body(
    query_hbm, key_hbm, value_hbm, dout_ref, key_out, value_out, value_ref,
    query_ref, key_ref, query_sems, key_sems, value_sems,
):
    rows, width = key_out.shape
    early = width - value_out.shape[1]
    loads = (
        column_copies(query_hbm, query_ref, query_sems),
        column_copies(value_hbm, value_ref, value_sems),
        column_copies(key_hbm.at[:, early:], key_ref, key_sems),
    )
    start_all(*loads[:2])
    start_all(loads[2])
    for index, step in enumerate(pieces_of(key_out, COPY_COLS)):
        loads[0][index].wait()
        loads[1][index].wait()
        if step.start == early:
            wait_all(loads[2])
        for left in range(step.start, step.stop, HEAD_DIM):
            cols = slice(left, left + HEAD_DIM)
            dout = key_out[:, cols]
            for start in range(0, rows, BLOCK):
                end = start + BLOCK
                scores = mm_nt(value_ref[start:end, cols], dout[start:, :])
                grad = mm(masked(scores, 0, False), query_ref[start:, cols])
                key_out[start:end, cols] = grad.astype(jnp.bfloat16)
            if left >= early:
                late = slice(left - early, left - early + HEAD_DIM)
                value_local(query_ref.at[:, early:], key_ref, dout, late, value_out.at[:, late])


def final_body(
    key_hbm, value_ref, key_part, early_part, late_part, state_ref, key_out_hbm, value_out_hbm,
    key_ref, key_out, value_out, in_sems, key_sems, value_sems,
):
    keys = column_copies(key_hbm, key_ref, in_sems)
    start_all(keys)
    key_stores = column_copies(key_out, key_out_hbm, key_sems)
    value_stores = column_copies(value_out, value_out_hbm, value_sems)
    for index, step in enumerate(pieces_of(key_out, COPY_COLS)):
        for left in range(step.start, step.stop, HEAD_DIM):
            cols = slice(left, left + HEAD_DIM)
            grad = key_part[:, cols].astype(jnp.float32) + mm_nt(value_ref[:, cols], state_ref[cols, :])
            key_out[:, cols] = grad.astype(jnp.bfloat16)
        key_stores[index].start()
    for index, step in enumerate(pieces_of(value_out, COPY_COLS)):
        keys[index].wait()
        for left in range(step.start, step.stop, HEAD_DIM):
            cols = slice(left, left + HEAD_DIM)
            early = early_part.shape[1]
            if left < early:
                part = early_part[:, cols]
            else:
                part = late_part[:, left - early : left - early + HEAD_DIM]
            grad = part.astype(jnp.float32) + mm(key_ref[:, cols], state_ref[cols, :])
            value_out[:, cols] = grad.astype(jnp.bfloat16)
        value_stores[index].start()
    wait_all(key_stores, value_stores)


def local_call(body, in_args, outs, flops, hbm_args=(), scratch=(), aliases=None):
    args = [pltpu.with_memory_space_constraint(a, pltpu.HBM) for a in hbm_args]
    args += [pltpu.with_memory_space_constraint(a, pltpu.VMEM) for a in in_args]
    specs = [pl.BlockSpec(memory_space=pltpu.HBM)] * len(hbm_args)
    specs += [pl.BlockSpec(memory_space=pltpu.VMEM)] * len(in_args)
    out_specs = []
    for out in outs:
        out_specs.append(pl.BlockSpec(memory_space=out.memory_space))
    moved = sum(a.size * a.dtype.itemsize for a in args)
    return pl.pallas_call(
        body,
        in_specs=specs,
        out_specs=out_specs,
        out_shape=outs,
        scratch_shapes=scratch,
        input_output_aliases=aliases or {},
        compiler_params=pltpu.CompilerParams(vmem_limit_bytes=16 * MIB),
        cost_estimate=pl.CostEstimate(flops=flops, bytes_accessed=moved, transcendentals=0),
    )(*args)


def scan_blocks(blocks, reverse):
    (states,) = local_call(
        functools.partial(scan_body, reverse),
        [blocks],
        [pltpu.HBM(blocks.shape, blocks.dtype)],
        blocks.size,
        scratch=[
            pltpu.VMEM(blocks.shape, blocks.dtype),
            pltpu.SemaphoreType.DMA((blocks.shape[0],)),
        ],
    )
    return states


def places_in_order(count):
    quarter = count // 4
    first, second, third, fourth = (list(range(at, at + quarter)) for at in range(0, count, quarter))
    half = quarter // 2
    order = second + first[:half] + third[:half] + first[half:] + third[half:] + fourth
    return [count - 1 - place for place in order]


def last_first(count):
    return list(range(count - 1, -1, -1))


def exchange(pieces, axis):
    groups = [places_in_order(lax.axis_size(axis))]
    return lax.all_to_all(pieces, axis, 0, 0, axis_index_groups=groups)


def in_pieces(state, axis):
    count = lax.axis_size(axis)
    rows, cols = state.shape
    return state.reshape(count, rows // count, cols)


def shards(queries, keys, values, out_grad, gain):
    rows, width = queries.shape
    total_width = width * lax.axis_size("head")
    bf16, f32 = jnp.bfloat16, jnp.float32
    tokens, state = (rows, width), (width, HEAD_DIM)
    small = 2 * rows * width * HEAD_DIM
    large = 2 * rows * rows * width * 3 // 4
    gain_row = gain.reshape(1, width)
    flat = (width, rows)
    chunks = pltpu.SemaphoreType.DMA((width // COPY_COLS,))
    vm, hbm = pltpu.VMEM, pltpu.HBM
    rows_vm, flat_vm, state_vm = vm(tokens, bf16), vm(flat, bf16), vm(state, bf16)

    (own_kv,) = local_call(
        states_body,
        [],
        [hbm(state, bf16)],
        small,
        [keys, values],
        [rows_vm] * 2 + [state_vm] + [chunks] * 3,
    )
    kv_blocks = exchange(in_pieces(own_kv, "seq"), "seq")
    flipped, grad_flipped = local_call(
        flip_body, [], [flat_vm] * 2, large, [queries, out_grad], [rows_vm] * 2 + [chunks] * 2
    )
    kv_blocks, flipped, grad_flipped = lax.optimization_barrier((kv_blocks, flipped, grad_flipped))
    kv_low = exchange(scan_blocks(kv_blocks, False), "seq").reshape(state)
    (local,) = local_call(
        local_body, [flipped], [flat_vm], 2 * large, [keys, values], [rows_vm] * 2 + [chunks] * 2
    )
    groups = lax.axis_size("head")
    attended, sums = local_call(
        sums_body,
        [gain_row, flipped, grad_flipped, local, kv_low],
        [flat_vm, vm((groups, 2, rows), f32)],
        small,
        aliases={3: 0},
    )
    sums = lax.all_to_all(sums, "head", 0, 0, axis_index_groups=[last_first(groups)])
    dout_flipped, own_grad = local_call(
        functools.partial(dout_body, total_width),
        [gain_row, flipped, grad_flipped, attended, sums],
        [flat_vm, hbm(state, bf16)],
        small,
        scratch=[state_vm, chunks],
        aliases={3: 0},
    )
    grad_blocks = exchange(in_pieces(own_grad, "seq"), "seq")
    early = width * 3 // 4 // COPY_COLS * COPY_COLS
    early_vm, late_vm = vm((rows, early), bf16), vm((rows, width - early), bf16)
    query_grad, dout, early_part = local_call(
        query_body,
        [dout_flipped, kv_low],
        [hbm(tokens, bf16), rows_vm, early_vm],
        2 * large + small,
        [queries, keys, values],
        [early_vm] + [rows_vm] * 3 + [chunks] * 4,
    )
    grad_blocks, query_grad, dout, early_part = lax.optimization_barrier(
        (grad_blocks, query_grad, dout, early_part)
    )
    grad_low = exchange(scan_blocks(grad_blocks, True), "seq").reshape(state)
    key_part, late_part, value_kept = local_call(
        inner_body,
        [dout],
        [rows_vm, late_vm, rows_vm],
        3 * large,
        [queries, keys, values],
        [rows_vm, late_vm] + [chunks] * 3,
        {3: 0},
    )
    key_grad, value_grad = local_call(
        final_body,
        [value_kept, key_part, early_part, late_part, grad_low],
        [hbm(tokens, bf16)] * 2,
        2 * small,
        [keys],
        [rows_vm] * 3 + [chunks] * 3,
    )
    return query_grad, key_grad, value_grad


def solution(mesh):
    return jax.shard_map(
        shards,
        mesh=mesh,
        in_specs=(
            P("seq", "head"),
            P("seq", "head"),
            P("seq", "head"),
            P("seq", "head"),
            P("head"),
        ),
        out_specs=(P("seq", "head"), P("seq", "head"), P("seq", "head")),
        check_vma=False,
    )
```

```python
import functools

import jax
import jax.numpy as jnp
from jax import lax
from jax.experimental import pallas as pl
from jax.experimental.pallas import tpu as pltpu
from jax.sharding import PartitionSpec as P

HEAD_DIM = 128
BLOCK = 256
COPY_COLS = 256
EPSILON = 1e-06
MIB = 1 << 20


def mm(a, b):
    return lax.dot_general(a, b, (((1,), (0,)), ((), ())), preferred_element_type=jnp.float32)


def mm_nt(a, b):
    return lax.dot_general(a, b, (((1,), (1,)), ((), ())), preferred_element_type=jnp.float32)


def mm_tn(a, b):
    return lax.dot_general(a, b, (((0,), (0,)), ((), ())), preferred_element_type=jnp.float32)


def pieces_of(ref, size):
    return [slice(at, at + size) for at in range(0, ref.shape[1], size)]


def masked(scores, diagonal, rows_first):
    shape = (BLOCK, BLOCK)
    rows = lax.broadcasted_iota(jnp.int32, shape, 0)
    cols = lax.broadcasted_iota(jnp.int32, shape, 1)
    keep = rows >= cols if rows_first else cols >= rows
    inside = slice(diagonal, diagonal + BLOCK)
    kept = jnp.where(keep, scores[:, inside], 0.0).astype(jnp.bfloat16)
    before = scores[:, :diagonal].astype(jnp.bfloat16)
    after = scores[:, inside.stop :].astype(jnp.bfloat16)
    parts = [part for part in (before, kept, after) if part.shape[1]]
    return jnp.concatenate(parts, axis=1) if len(parts) > 1 else kept


def column_copies(source, target, sems):
    copies = []
    for index, cols in enumerate(pieces_of(source, COPY_COLS)):
        copies.append(pltpu.make_async_copy(source.at[:, cols], target.at[:, cols], sems.at[index]))
    return copies


def row_copies(source, target, sems):
    copies = []
    for index in range(source.shape[0] // COPY_COLS):
        part = slice(index * COPY_COLS, (index + 1) * COPY_COLS)
        copies.append(pltpu.make_async_copy(source.at[part, :], target.at[part, :], sems.at[index]))
    return copies


def start_all(*groups):
    for parts in zip(*groups):
        for part in parts:
            part.start()


def wait_all(*groups):
    for group in groups:
        for part in group:
            part.wait()


def states_body(
    key_hbm, value_hbm, state_hbm, key_ref, value_ref, state_ref, key_sems, value_sems, state_sems
):
    stores = row_copies(state_ref, state_hbm, state_sems)
    key_copies = column_copies(key_hbm, key_ref, key_sems)
    value_copies = column_copies(value_hbm, value_ref, value_sems)
    start_all(key_copies, value_copies)
    for index, cols in enumerate(pieces_of(key_ref, COPY_COLS)):
        key_copies[index].wait()
        value_copies[index].wait()
        for start in range(cols.start, cols.stop, HEAD_DIM):
            head = slice(start, start + HEAD_DIM)
            state_ref[head, :] = mm_tn(key_ref[:, head], value_ref[:, head]).astype(jnp.bfloat16)
        stores[index].start()
    wait_all(stores)


def weight_rows(rows):
    blocks = rows // BLOCK
    return blocks * (blocks + 1) // 2 * BLOCK


def local_part(key_ref, value_ref, own, flipped_ref, head, local_ref, weight_ref, row):
    for start in range(0, key_ref.shape[0], BLOCK):
        end = start + BLOCK
        parts = []
        for first in range(0, end, BLOCK):
            scores = mm(key_ref[first : first + BLOCK, own], flipped_ref[head, start:end])
            part = masked(scores, 0, False) if first == start else scores.astype(jnp.bfloat16)
            weight_ref[row : row + BLOCK, :] = part
            parts.append(part)
            row += BLOCK
        weights = jnp.concatenate(parts, axis=0) if len(parts) > 1 else parts[0]
        local = mm_tn(value_ref[:end, own], weights)
        local_ref[head, start:end] = local.astype(jnp.bfloat16)


def local_heads(first, key_ref, value_ref, loads, flipped_ref, local_ref, weight_ref, weight_hbm, sems):
    size = weight_rows(key_ref.shape[0])
    stores = []
    for index, step in enumerate(pieces_of(key_ref, COPY_COLS)):
        for load in loads:
            load[index].wait()
        for left in range(step.start, step.stop, HEAD_DIM):
            own = slice(left, left + HEAD_DIM)
            head = slice(first + left, first + left + HEAD_DIM)
            number = left // HEAD_DIM
            part = slice(number * size, (number + 1) * size)
            local_part(key_ref, value_ref, own, flipped_ref, head, local_ref, weight_ref, part.start)
            store = pltpu.make_async_copy(weight_ref.at[part, :], weight_hbm.at[part, :], sems.at[number])
            store.start()
            stores.append(store)
    return stores


def flip_body(
    query_hbm, key_hbm, value_hbm, grad_hbm, flipped_ref, grad_flipped_ref, local_ref, weight_hbm,
    query_ref, key_ref, value_ref, grad_ref, weight_ref,
    query_sems, key_sems, value_sems, grad_sems, weight_sems,
):
    part = slice(0, key_ref.shape[1])
    query_loads = column_copies(query_hbm, query_ref, query_sems)
    key_loads = column_copies(key_hbm.at[:, part], key_ref, key_sems)
    value_loads = column_copies(value_hbm.at[:, part], value_ref, value_sems)
    grad_loads = column_copies(grad_hbm, grad_ref, grad_sems)
    start_all(query_loads)
    start_all(key_loads, value_loads)
    start_all(grad_loads)
    for load, cols in zip(query_loads, pieces_of(query_ref, COPY_COLS)):
        load.wait()
        flipped_ref[cols, :] = query_ref[:, cols].T
    stores = local_heads(
        0, key_ref, value_ref, (key_loads, value_loads), flipped_ref, local_ref, weight_ref, weight_hbm, weight_sems
    )
    for load, cols in zip(grad_loads, pieces_of(grad_ref, COPY_COLS)):
        load.wait()
        grad_flipped_ref[cols, :] = grad_ref[:, cols].T
    wait_all(stores)


def local_body(
    key_hbm, value_hbm, flipped_ref, given_ref, local_ref, weight_hbm,
    key_ref, value_ref, weight_ref, key_sems, value_sems, weight_sems,
):
    first = local_ref.shape[0] - key_ref.shape[1]
    key_loads = column_copies(key_hbm.at[:, first:], key_ref, key_sems)
    value_loads = column_copies(value_hbm.at[:, first:], value_ref, value_sems)
    start_all(key_loads, value_loads)
    stores = local_heads(
        first, key_ref, value_ref, (key_loads, value_loads), flipped_ref, local_ref, weight_ref, weight_hbm, weight_sems
    )
    wait_all(stores)


def scan_body(reverse, block_ref, state_hbm, state_ref, sems):
    count = block_ref.shape[0]
    total = jnp.zeros(block_ref.shape[1:], jnp.float32)
    places = places_in_order(count)
    stores = []
    for place in range(count - 1, -1, -1) if reverse else range(count):
        rank = places.index(place)
        state_ref[rank] = total.astype(jnp.bfloat16)
        total = total + block_ref[rank].astype(jnp.float32)
        stores.append(pltpu.make_async_copy(state_ref.at[rank], state_hbm.at[rank], sems.at[rank]))
        stores[-1].start()
    wait_all(stores)


def heads_of(ref):
    return [slice(at, at + HEAD_DIM) for at in range(0, ref.shape[0], HEAD_DIM)]


def scaled_grad(gain_ref, grad_ref, head):
    gain = jnp.broadcast_to(gain_ref[:, head], (HEAD_DIM, HEAD_DIM)).T
    gain = jnp.concatenate([gain] * (grad_ref.shape[1] // HEAD_DIM), axis=1)
    return gain * grad_ref[head, :].astype(jnp.float32)


def fold(values):
    parts = [values[at : at + 8, :] for at in range(0, values.shape[0], 8)]
    while len(parts) > 1:
        parts = [sum(parts[at + 1 : at + 2], parts[at]) for at in range(0, len(parts), 2)]
    return parts[0]


def sums_body(gain_ref, flipped_ref, grad_ref, local_ref, state_ref, attended_ref, sums_ref):
    square = cross = jnp.zeros((8, local_ref.shape[1]), jnp.float32)
    for head in heads_of(local_ref):
        attended = mm_tn(state_ref[head, :], flipped_ref[head, :])
        attended = attended + attended_ref[head, :].astype(jnp.float32)
        attended_ref[head, :] = attended.astype(jnp.bfloat16)
        square += fold(attended * attended)
        cross += fold(scaled_grad(gain_ref, grad_ref, head) * attended)
    square = jnp.sum(square, axis=0, keepdims=True)
    cross = jnp.sum(cross, axis=0, keepdims=True)
    for group in range(sums_ref.shape[0]):
        sums_ref[group, 0:1, :] = square
        sums_ref[group, 1:2, :] = cross


def dout_body(
    width, gain_ref, flipped_ref, grad_ref, attended_ref, sums_ref, dout_ref, own_hbm, own_ref, sems
):
    stores = row_copies(own_ref, own_hbm, sems)
    sums = sum(sums_ref[group] for group in range(sums_ref.shape[0]))
    inverse = 1.0 / jnp.sqrt(sums[0:1, :] / width + EPSILON)
    drop = sums[1:2, :] * (inverse * inverse * inverse) / width
    for head in heads_of(dout_ref):
        attended = dout_ref[head, :].astype(jnp.float32)
        dout = scaled_grad(gain_ref, grad_ref, head) * inverse - attended * drop
        dout = dout.astype(jnp.bfloat16)
        dout_ref[head, :] = dout
        own_ref[head, :] = mm_nt(flipped_ref[head, :], dout).astype(jnp.bfloat16)
        if head.stop % COPY_COLS == 0:
            stores[head.stop // COPY_COLS - 1].start()
    wait_all(stores)


def value_local(weight_ref, row, dout, target):
    blocks = dout.shape[0] // BLOCK
    for own in range(blocks):
        parts = []
        for other in range(own, blocks):
            start = row + (other * (other + 1) // 2 + own) * BLOCK
            parts.append(weight_ref[start : start + BLOCK, :])
        weights = jnp.concatenate(parts, axis=1) if len(parts) > 1 else parts[0]
        at = own * BLOCK
        target[at : at + BLOCK, :] = mm(weights, dout[at:, :]).astype(jnp.bfloat16)


def query_body(
    key_hbm, value_hbm, first_hbm, second_hbm, flipped_ref, state_ref, out_hbm, dout_ref, value_out,
    key_ref, value_ref, out_ref, weight_ref, key_sems, value_sems, out_sems, weight_sems,
):
    rows = dout_ref.shape[0]
    size = weight_rows(rows)
    key_copies = column_copies(key_hbm, key_ref, key_sems)
    value_copies = column_copies(value_hbm, value_ref, value_sems)
    there = first_hbm.shape[0]
    rest = weight_ref.shape[0] - there
    weight_copies = [
        pltpu.make_async_copy(first_hbm, weight_ref.at[:there, :], weight_sems.at[0]),
        pltpu.make_async_copy(second_hbm.at[:rest, :], weight_ref.at[there:, :], weight_sems.at[1]),
    ]
    start_all(key_copies, value_copies)
    start_all(weight_copies)
    for head in heads_of(flipped_ref):
        dout_ref[:, head] = flipped_ref[head, :].T
    stores = column_copies(out_ref, out_hbm, out_sems)
    for index, step in enumerate(pieces_of(out_ref, COPY_COLS)):
        key_copies[index].wait()
        value_copies[index].wait()
        for left in range(step.start, step.stop, HEAD_DIM):
            cols = slice(left, left + HEAD_DIM)
            for start in range(0, rows, BLOCK):
                end = start + BLOCK
                dout = dout_ref[start:end, cols]
                dscore = masked(mm_nt(dout, value_ref[:end, cols]), start, True)
                grad = mm(dscore, key_ref[:end, cols]) + mm_nt(dout, state_ref[cols, :])
                out_ref[start:end, cols] = grad.astype(jnp.bfloat16)
        stores[index].start()
    wait_all(weight_copies)
    for number, cols in enumerate(pieces_of(value_out, HEAD_DIM)):
        value_local(weight_ref, number * size, dout_ref[:, cols], value_out.at[:, cols])
    wait_all(stores)


def inner_body(
    query_hbm, value_hbm, weight_hbm, dout_ref, key_out, value_out, value_ref,
    query_ref, weight_ref, query_sems, value_sems, weight_sem,
):
    rows, width = key_out.shape
    size = weight_rows(rows)
    early = width - value_out.shape[1]
    query_copies = column_copies(query_hbm, query_ref, query_sems)
    value_copies = column_copies(value_hbm, value_ref, value_sems)
    skipped = weight_hbm.shape[0] - weight_ref.shape[0]
    weight_copy = pltpu.make_async_copy(weight_hbm.at[skipped:, :], weight_ref, weight_sem.at[0])
    start_all(query_copies, value_copies)
    weight_copy.start()
    for index, step in enumerate(pieces_of(key_out, COPY_COLS)):
        query_copies[index].wait()
        value_copies[index].wait()
        if step.start == early:
            weight_copy.wait()
        for left in range(step.start, step.stop, HEAD_DIM):
            cols = slice(left, left + HEAD_DIM)
            dout = key_out[:, cols]
            for start in range(0, rows, BLOCK):
                end = start + BLOCK
                scores = mm_nt(value_ref[start:end, cols], dout[start:, :])
                grad = mm(masked(scores, 0, False), query_ref[start:, cols])
                key_out[start:end, cols] = grad.astype(jnp.bfloat16)
            if left >= early:
                late = slice(left - early, left - early + HEAD_DIM)
                value_local(weight_ref, late.start // HEAD_DIM * size, dout, value_out.at[:, late])


def final_body(
    key_hbm, value_ref, key_part, early_part, late_part, state_ref, key_out_hbm, value_out_hbm,
    key_ref, key_out, value_out, in_sems, key_sems, value_sems,
):
    keys = column_copies(key_hbm, key_ref, in_sems)
    start_all(keys)
    key_stores = column_copies(key_out, key_out_hbm, key_sems)
    value_stores = column_copies(value_out, value_out_hbm, value_sems)
    for index, step in enumerate(pieces_of(key_out, COPY_COLS)):
        for left in range(step.start, step.stop, HEAD_DIM):
            cols = slice(left, left + HEAD_DIM)
            grad = key_part[:, cols].astype(jnp.float32) + mm_nt(value_ref[:, cols], state_ref[cols, :])
            key_out[:, cols] = grad.astype(jnp.bfloat16)
        key_stores[index].start()
    for index, step in enumerate(pieces_of(value_out, COPY_COLS)):
        keys[index].wait()
        for left in range(step.start, step.stop, HEAD_DIM):
            cols = slice(left, left + HEAD_DIM)
            early = early_part.shape[1]
            if left < early:
                part = early_part[:, cols]
            else:
                part = late_part[:, left - early : left - early + HEAD_DIM]
            grad = part.astype(jnp.float32) + mm(key_ref[:, cols], state_ref[cols, :])
            value_out[:, cols] = grad.astype(jnp.bfloat16)
        value_stores[index].start()
    wait_all(key_stores, value_stores)


def local_call(body, in_args, outs, flops, hbm_args=(), scratch=(), aliases=None):
    args = [pltpu.with_memory_space_constraint(a, pltpu.HBM) for a in hbm_args]
    args += [pltpu.with_memory_space_constraint(a, pltpu.VMEM) for a in in_args]
    specs = [pl.BlockSpec(memory_space=pltpu.HBM)] * len(hbm_args)
    specs += [pl.BlockSpec(memory_space=pltpu.VMEM)] * len(in_args)
    out_specs = []
    for out in outs:
        out_specs.append(pl.BlockSpec(memory_space=out.memory_space))
    moved = sum(a.size * a.dtype.itemsize for a in args)
    return pl.pallas_call(
        body,
        in_specs=specs,
        out_specs=out_specs,
        out_shape=outs,
        scratch_shapes=scratch,
        input_output_aliases=aliases or {},
        compiler_params=pltpu.CompilerParams(vmem_limit_bytes=16 * MIB),
        cost_estimate=pl.CostEstimate(flops=flops, bytes_accessed=moved, transcendentals=0),
    )(*args)


def scan_blocks(blocks, reverse):
    (states,) = local_call(
        functools.partial(scan_body, reverse),
        [blocks],
        [pltpu.HBM(blocks.shape, blocks.dtype)],
        blocks.size,
        scratch=[
            pltpu.VMEM(blocks.shape, blocks.dtype),
            pltpu.SemaphoreType.DMA((blocks.shape[0],)),
        ],
    )
    return states


def places_in_order(count):
    quarter = count // 4
    first, second, third, fourth = (list(range(at, at + quarter)) for at in range(0, count, quarter))
    half = quarter // 2
    order = second + first[:half] + third[:half] + first[half:] + third[half:] + fourth
    return [count - 1 - place for place in order]


def last_first(count):
    return list(range(count - 1, -1, -1))


def exchange(pieces, axis):
    groups = [places_in_order(lax.axis_size(axis))]
    return lax.all_to_all(pieces, axis, 0, 0, axis_index_groups=groups)


def in_pieces(state, axis):
    count = lax.axis_size(axis)
    rows, cols = state.shape
    return state.reshape(count, rows // count, cols)


def shards(queries, keys, values, out_grad, gain):
    rows, width = queries.shape
    total_width = width * lax.axis_size("head")
    bf16, f32 = jnp.bfloat16, jnp.float32
    tokens, state = (rows, width), (width, HEAD_DIM)
    small = 2 * rows * width * HEAD_DIM
    large = 2 * rows * rows * width * 3 // 4
    gain_row = gain.reshape(1, width)
    flat = (width, rows)
    chunks = pltpu.SemaphoreType.DMA((width // COPY_COLS,))
    vm, hbm = pltpu.VMEM, pltpu.HBM
    rows_vm, flat_vm, state_vm = vm(tokens, bf16), vm(flat, bf16), vm(state, bf16)

    (own_kv,) = local_call(
        states_body,
        [],
        [hbm(state, bf16)],
        small,
        [keys, values],
        [rows_vm] * 2 + [state_vm] + [chunks] * 3,
    )
    kv_blocks = exchange(in_pieces(own_kv, "seq"), "seq")
    half = width // 2 // COPY_COLS * COPY_COLS
    early = width * 3 // 4 // COPY_COLS * COPY_COLS
    dma = pltpu.SemaphoreType.DMA

    def weights_of(cols):
        return (cols // HEAD_DIM * weight_rows(rows), BLOCK)

    half_vm, half_chunks = vm((rows, half), bf16), dma((half // COPY_COLS,))
    flipped, grad_flipped, local, first_weights = local_call(
        flip_body,
        [],
        [flat_vm] * 3 + [hbm(weights_of(half), bf16)],
        2 * large,
        [queries, keys, values, out_grad],
        [rows_vm, half_vm, half_vm, rows_vm, vm(weights_of(half), bf16)]
        + [chunks, half_chunks, half_chunks, chunks, dma((half // HEAD_DIM,))],
    )
    kv_blocks, flipped, grad_flipped, local, first_weights = lax.optimization_barrier(
        (kv_blocks, flipped, grad_flipped, local, first_weights)
    )
    kv_low = exchange(scan_blocks(kv_blocks, False), "seq").reshape(state)
    other = width - half
    other_vm, other_chunks = vm((rows, other), bf16), dma((other // COPY_COLS,))
    local, second_weights = local_call(
        local_body,
        [flipped, local],
        [flat_vm, hbm(weights_of(other), bf16)],
        large,
        [keys, values],
        [other_vm, other_vm, vm(weights_of(other), bf16)]
        + [other_chunks, other_chunks, dma((other // HEAD_DIM,))],
        {3: 0},
    )
    groups = lax.axis_size("head")
    attended, sums = local_call(
        sums_body,
        [gain_row, flipped, grad_flipped, local, kv_low],
        [flat_vm, vm((groups, 2, rows), f32)],
        small,
        aliases={3: 0},
    )
    sums = lax.all_to_all(sums, "head", 0, 0, axis_index_groups=[last_first(groups)])
    dout_flipped, own_grad = local_call(
        functools.partial(dout_body, total_width),
        [gain_row, flipped, grad_flipped, attended, sums],
        [flat_vm, hbm(state, bf16)],
        small,
        scratch=[state_vm, chunks],
        aliases={3: 0},
    )
    grad_blocks = exchange(in_pieces(own_grad, "seq"), "seq")
    early_vm, late_vm = vm((rows, early), bf16), vm((rows, width - early), bf16)
    query_grad, dout, early_part = local_call(
        query_body,
        [dout_flipped, kv_low],
        [hbm(tokens, bf16), rows_vm, early_vm],
        2 * large + small,
        [keys, values, first_weights, second_weights],
        [rows_vm] * 3 + [vm(weights_of(early), bf16)] + [chunks] * 3 + [dma((2,))],
    )
    grad_blocks, query_grad, dout, early_part = lax.optimization_barrier(
        (grad_blocks, query_grad, dout, early_part)
    )
    grad_low = exchange(scan_blocks(grad_blocks, True), "seq").reshape(state)
    key_part, late_part, value_kept = local_call(
        inner_body,
        [dout],
        [rows_vm, late_vm, rows_vm],
        3 * large,
        [queries, values, second_weights],
        [rows_vm, vm(weights_of(width - early), bf16)] + [chunks] * 2 + [dma((1,))],
        {3: 0},
    )
    key_grad, value_grad = local_call(
        final_body,
        [value_kept, key_part, early_part, late_part, grad_low],
        [hbm(tokens, bf16)] * 2,
        2 * small,
        [keys],
        [rows_vm] * 3 + [chunks] * 3,
    )
    return query_grad, key_grad, value_grad


def solution(mesh):
    return jax.shard_map(
        shards,
        mesh=mesh,
        in_specs=(
            P("seq", "head"),
            P("seq", "head"),
            P("seq", "head"),
            P("seq", "head"),
            P("head"),
        ),
        out_specs=(P("seq", "head"), P("seq", "head"), P("seq", "head")),
        check_vma=False,
    )
```

```python
import functools

import jax
import jax.numpy as jnp
from jax import lax
from jax.experimental import pallas as pl
from jax.experimental.pallas import tpu as pltpu
from jax.sharding import PartitionSpec as P

HEAD_DIM = 128
BLOCK = 256
COPY_COLS = 128
EPSILON = 1e-06
MIB = 1 << 20


def mm(a, b):
    return lax.dot_general(a, b, (((1,), (0,)), ((), ())), preferred_element_type=jnp.float32)


def mm_nt(a, b):
    return lax.dot_general(a, b, (((1,), (1,)), ((), ())), preferred_element_type=jnp.float32)


def mm_tn(a, b):
    return lax.dot_general(a, b, (((0,), (0,)), ((), ())), preferred_element_type=jnp.float32)


def pieces_of(ref, size):
    return [slice(at, at + size) for at in range(0, ref.shape[1], size)]


def masked(scores, diagonal, rows_first):
    shape = (BLOCK, BLOCK)
    rows = lax.broadcasted_iota(jnp.int32, shape, 0)
    cols = lax.broadcasted_iota(jnp.int32, shape, 1)
    keep = rows >= cols if rows_first else cols >= rows
    inside = slice(diagonal, diagonal + BLOCK)
    kept = jnp.where(keep, scores[:, inside], 0.0).astype(jnp.bfloat16)
    before = scores[:, :diagonal].astype(jnp.bfloat16)
    after = scores[:, inside.stop :].astype(jnp.bfloat16)
    parts = [part for part in (before, kept, after) if part.shape[1]]
    return jnp.concatenate(parts, axis=1) if len(parts) > 1 else kept


def column_copies(source, target, sems):
    copies = []
    for index, cols in enumerate(pieces_of(source, COPY_COLS)):
        copies.append(pltpu.make_async_copy(source.at[:, cols], target.at[:, cols], sems.at[index]))
    return copies


def row_copies(source, target, sems):
    copies = []
    for index in range(source.shape[0] // COPY_COLS):
        part = slice(index * COPY_COLS, (index + 1) * COPY_COLS)
        copies.append(pltpu.make_async_copy(source.at[part, :], target.at[part, :], sems.at[index]))
    return copies


def start_all(*groups):
    for parts in zip(*groups):
        for part in parts:
            part.start()


def wait_all(*groups):
    for group in groups:
        for part in group:
            part.wait()


def states_body(
    key_hbm, value_hbm, state_hbm, key_ref, value_ref, state_ref, key_sems, value_sems, state_sems
):
    stores = row_copies(state_ref, state_hbm, state_sems)
    key_copies = column_copies(key_hbm, key_ref, key_sems)
    value_copies = column_copies(value_hbm, value_ref, value_sems)
    start_all(key_copies, value_copies)
    for index, cols in enumerate(pieces_of(key_ref, COPY_COLS)):
        key_copies[index].wait()
        value_copies[index].wait()
        for start in range(cols.start, cols.stop, HEAD_DIM):
            head = slice(start, start + HEAD_DIM)
            state_ref[head, :] = mm_tn(key_ref[:, head], value_ref[:, head]).astype(jnp.bfloat16)
        stores[index].start()
    wait_all(stores)


def weight_rows(rows):
    blocks = rows // BLOCK
    return blocks * (blocks + 1) // 2 * BLOCK


def local_part(key_ref, value_ref, own, flipped_ref, head, local_ref, weight_ref, row):
    for start in range(0, key_ref.shape[0], BLOCK):
        end = start + BLOCK
        parts = []
        for first in range(0, end, BLOCK):
            scores = mm(key_ref[first : first + BLOCK, own], flipped_ref[head, start:end])
            part = masked(scores, 0, False) if first == start else scores.astype(jnp.bfloat16)
            weight_ref[row : row + BLOCK, :] = part
            parts.append(part)
            row += BLOCK
        weights = jnp.concatenate(parts, axis=0) if len(parts) > 1 else parts[0]
        local = mm_tn(value_ref[:end, own], weights)
        local_ref[head, start:end] = local.astype(jnp.bfloat16)


def local_heads(first, key_ref, value_ref, loads, flipped_ref, local_ref, weight_ref, weight_hbm, sems):
    size = weight_rows(key_ref.shape[0])
    stores = []
    for index, step in enumerate(pieces_of(key_ref, COPY_COLS)):
        for load in loads:
            load[index].wait()
        for left in range(step.start, step.stop, HEAD_DIM):
            own = slice(left, left + HEAD_DIM)
            head = slice(first + left, first + left + HEAD_DIM)
            number = left // HEAD_DIM
            part = slice(number * size, (number + 1) * size)
            local_part(key_ref, value_ref, own, flipped_ref, head, local_ref, weight_ref, part.start)
            store = pltpu.make_async_copy(weight_ref.at[part, :], weight_hbm.at[part, :], sems.at[number])
            store.start()
            stores.append(store)
    return stores


def flip_body(
    query_hbm, key_hbm, value_hbm, grad_hbm, flipped_ref, grad_flipped_ref, local_ref, weight_hbm,
    query_ref, key_ref, value_ref, grad_ref, weight_ref,
    query_sems, key_sems, value_sems, grad_sems, weight_sems,
):
    part = slice(0, key_ref.shape[1])
    query_loads = column_copies(query_hbm, query_ref, query_sems)
    key_loads = column_copies(key_hbm.at[:, part], key_ref, key_sems)
    value_loads = column_copies(value_hbm.at[:, part], value_ref, value_sems)
    grad_loads = column_copies(grad_hbm, grad_ref, grad_sems)
    start_all(query_loads)
    start_all(key_loads, value_loads)
    start_all(grad_loads)
    for load, cols in zip(query_loads, pieces_of(query_ref, COPY_COLS)):
        load.wait()
        flipped_ref[cols, :] = query_ref[:, cols].T
    stores = local_heads(
        0, key_ref, value_ref, (key_loads, value_loads), flipped_ref, local_ref, weight_ref, weight_hbm, weight_sems
    )
    for load, cols in zip(grad_loads, pieces_of(grad_ref, COPY_COLS)):
        load.wait()
        grad_flipped_ref[cols, :] = grad_ref[:, cols].T
    wait_all(stores)


def local_body(
    key_hbm, value_hbm, flipped_ref, given_ref, local_ref, weight_hbm,
    key_ref, value_ref, weight_ref, key_sems, value_sems, weight_sems,
):
    first = local_ref.shape[0] - key_ref.shape[1]
    key_loads = column_copies(key_hbm.at[:, first:], key_ref, key_sems)
    value_loads = column_copies(value_hbm.at[:, first:], value_ref, value_sems)
    start_all(key_loads, value_loads)
    stores = local_heads(
        first, key_ref, value_ref, (key_loads, value_loads), flipped_ref, local_ref, weight_ref, weight_hbm, weight_sems
    )
    wait_all(stores)


def scan_body(reverse, block_ref, state_hbm, state_ref, sems):
    count = block_ref.shape[0]
    total = jnp.zeros(block_ref.shape[1:], jnp.float32)
    places = places_in_order(count)
    stores = []
    for place in range(count - 1, -1, -1) if reverse else range(count):
        rank = places.index(place)
        state_ref[rank] = total.astype(jnp.bfloat16)
        total = total + block_ref[rank].astype(jnp.float32)
        stores.append(pltpu.make_async_copy(state_ref.at[rank], state_hbm.at[rank], sems.at[rank]))
        stores[-1].start()
    wait_all(stores)


def heads_of(ref):
    return [slice(at, at + HEAD_DIM) for at in range(0, ref.shape[0], HEAD_DIM)]


def scaled_grad(gain_ref, grad_ref, head):
    gain = jnp.broadcast_to(gain_ref[:, head], (HEAD_DIM, HEAD_DIM)).T
    gain = jnp.concatenate([gain] * (grad_ref.shape[1] // HEAD_DIM), axis=1)
    return gain * grad_ref[head, :].astype(jnp.float32)


def fold(values):
    parts = [values[at : at + 8, :] for at in range(0, values.shape[0], 8)]
    while len(parts) > 1:
        parts = [sum(parts[at + 1 : at + 2], parts[at]) for at in range(0, len(parts), 2)]
    return parts[0]


def sums_body(gain_ref, flipped_ref, grad_ref, local_ref, state_ref, attended_ref, sums_ref):
    square = cross = jnp.zeros((8, local_ref.shape[1]), jnp.float32)
    for head in heads_of(local_ref):
        attended = mm_tn(state_ref[head, :], flipped_ref[head, :])
        attended = attended + attended_ref[head, :].astype(jnp.float32)
        attended_ref[head, :] = attended.astype(jnp.bfloat16)
        square += fold(attended * attended)
        cross += fold(scaled_grad(gain_ref, grad_ref, head) * attended)
    square = jnp.sum(square, axis=0, keepdims=True)
    cross = jnp.sum(cross, axis=0, keepdims=True)
    for group in range(sums_ref.shape[0]):
        sums_ref[group, 0:1, :] = square
        sums_ref[group, 1:2, :] = cross


def dout_body(
    width, gain_ref, flipped_ref, grad_ref, attended_ref, sums_ref, dout_ref, own_hbm, own_ref, sems
):
    stores = row_copies(own_ref, own_hbm, sems)
    sums = sum(sums_ref[group] for group in range(sums_ref.shape[0]))
    inverse = 1.0 / jnp.sqrt(sums[0:1, :] / width + EPSILON)
    drop = sums[1:2, :] * (inverse * inverse * inverse) / width
    for head in heads_of(dout_ref):
        attended = dout_ref[head, :].astype(jnp.float32)
        dout = scaled_grad(gain_ref, grad_ref, head) * inverse - attended * drop
        dout = dout.astype(jnp.bfloat16)
        dout_ref[head, :] = dout
        own_ref[head, :] = mm_nt(flipped_ref[head, :], dout).astype(jnp.bfloat16)
        if head.stop % COPY_COLS == 0:
            stores[head.stop // COPY_COLS - 1].start()
    wait_all(stores)


def value_local(weight_ref, row, dout, target):
    blocks = dout.shape[0] // BLOCK
    for own in range(blocks):
        parts = []
        for other in range(own, blocks):
            start = row + (other * (other + 1) // 2 + own) * BLOCK
            parts.append(weight_ref[start : start + BLOCK, :])
        weights = jnp.concatenate(parts, axis=1) if len(parts) > 1 else parts[0]
        at = own * BLOCK
        target[at : at + BLOCK, :] = mm(weights, dout[at:, :]).astype(jnp.bfloat16)


def query_body(
    key_hbm, value_hbm, first_hbm, second_hbm, flipped_ref, state_ref, out_hbm, dout_ref, value_out,
    key_ref, value_ref, out_ref, weight_ref, key_sems, value_sems, out_sems, weight_sems,
):
    rows = dout_ref.shape[0]
    size = weight_rows(rows)
    key_copies = column_copies(key_hbm, key_ref, key_sems)
    value_copies = column_copies(value_hbm, value_ref, value_sems)
    there = first_hbm.shape[0]
    rest = weight_ref.shape[0] - there
    weight_copies = [
        pltpu.make_async_copy(first_hbm, weight_ref.at[:there, :], weight_sems.at[0]),
        pltpu.make_async_copy(second_hbm.at[:rest, :], weight_ref.at[there:, :], weight_sems.at[1]),
    ]
    start_all(key_copies, value_copies)
    start_all(weight_copies)
    for head in heads_of(flipped_ref):
        dout_ref[:, head] = flipped_ref[head, :].T
    stores = column_copies(out_ref, out_hbm, out_sems)
    for index, step in enumerate(pieces_of(out_ref, COPY_COLS)):
        key_copies[index].wait()
        value_copies[index].wait()
        for left in range(step.start, step.stop, HEAD_DIM):
            cols = slice(left, left + HEAD_DIM)
            for start in range(0, rows, BLOCK):
                end = start + BLOCK
                dout = dout_ref[start:end, cols]
                dscore = masked(mm_nt(dout, value_ref[:end, cols]), start, True)
                grad = mm(dscore, key_ref[:end, cols]) + mm_nt(dout, state_ref[cols, :])
                out_ref[start:end, cols] = grad.astype(jnp.bfloat16)
        stores[index].start()
    wait_all(weight_copies)
    for number, cols in enumerate(pieces_of(value_out, HEAD_DIM)):
        value_local(weight_ref, number * size, dout_ref[:, cols], value_out.at[:, cols])
    wait_all(stores)


def inner_body(
    query_hbm, value_hbm, weight_hbm, dout_ref, key_out, value_out, value_ref,
    query_ref, weight_ref, query_sems, value_sems, weight_sem,
):
    rows, width = key_out.shape
    size = weight_rows(rows)
    early = width - value_out.shape[1]
    query_copies = column_copies(query_hbm, query_ref, query_sems)
    value_copies = column_copies(value_hbm, value_ref, value_sems)
    skipped = weight_hbm.shape[0] - weight_ref.shape[0]
    weight_copy = pltpu.make_async_copy(weight_hbm.at[skipped:, :], weight_ref, weight_sem.at[0])
    start_all(query_copies, value_copies)
    weight_copy.start()
    for index, step in enumerate(pieces_of(key_out, COPY_COLS)):
        query_copies[index].wait()
        value_copies[index].wait()
        if step.start == early:
            weight_copy.wait()
        for left in range(step.start, step.stop, HEAD_DIM):
            cols = slice(left, left + HEAD_DIM)
            dout = key_out[:, cols]
            for start in range(0, rows, BLOCK):
                end = start + BLOCK
                scores = mm_nt(value_ref[start:end, cols], dout[start:, :])
                grad = mm(masked(scores, 0, False), query_ref[start:, cols])
                key_out[start:end, cols] = grad.astype(jnp.bfloat16)
            if left >= early:
                late = slice(left - early, left - early + HEAD_DIM)
                value_local(weight_ref, late.start // HEAD_DIM * size, dout, value_out.at[:, late])


def final_body(
    key_hbm, value_ref, key_part, early_part, late_part, state_ref, key_out_hbm, value_out_hbm,
    key_ref, key_out, value_out, in_sems, key_sems, value_sems,
):
    keys = column_copies(key_hbm, key_ref, in_sems)
    start_all(keys)
    key_stores = column_copies(key_out, key_out_hbm, key_sems)
    value_stores = column_copies(value_out, value_out_hbm, value_sems)
    for index, step in enumerate(pieces_of(key_out, COPY_COLS)):
        for left in range(step.start, step.stop, HEAD_DIM):
            cols = slice(left, left + HEAD_DIM)
            grad = key_part[:, cols].astype(jnp.float32) + mm_nt(value_ref[:, cols], state_ref[cols, :])
            key_out[:, cols] = grad.astype(jnp.bfloat16)
        key_stores[index].start()
    for index, step in enumerate(pieces_of(value_out, COPY_COLS)):
        keys[index].wait()
        for left in range(step.start, step.stop, HEAD_DIM):
            cols = slice(left, left + HEAD_DIM)
            early = early_part.shape[1]
            if left < early:
                part = early_part[:, cols]
            else:
                part = late_part[:, left - early : left - early + HEAD_DIM]
            grad = part.astype(jnp.float32) + mm(key_ref[:, cols], state_ref[cols, :])
            value_out[:, cols] = grad.astype(jnp.bfloat16)
        value_stores[index].start()
    wait_all(key_stores, value_stores)


def local_call(body, in_args, outs, flops, hbm_args=(), scratch=(), aliases=None):
    args = [pltpu.with_memory_space_constraint(a, pltpu.HBM) for a in hbm_args]
    args += [pltpu.with_memory_space_constraint(a, pltpu.VMEM) for a in in_args]
    specs = [pl.BlockSpec(memory_space=pltpu.HBM)] * len(hbm_args)
    specs += [pl.BlockSpec(memory_space=pltpu.VMEM)] * len(in_args)
    out_specs = []
    for out in outs:
        out_specs.append(pl.BlockSpec(memory_space=out.memory_space))
    moved = sum(a.size * a.dtype.itemsize for a in args)
    return pl.pallas_call(
        body,
        in_specs=specs,
        out_specs=out_specs,
        out_shape=outs,
        scratch_shapes=scratch,
        input_output_aliases=aliases or {},
        compiler_params=pltpu.CompilerParams(vmem_limit_bytes=16 * MIB),
        cost_estimate=pl.CostEstimate(flops=flops, bytes_accessed=moved, transcendentals=0),
    )(*args)


def scan_blocks(blocks, reverse):
    (states,) = local_call(
        functools.partial(scan_body, reverse),
        [blocks],
        [pltpu.HBM(blocks.shape, blocks.dtype)],
        blocks.size,
        scratch=[
            pltpu.VMEM(blocks.shape, blocks.dtype),
            pltpu.SemaphoreType.DMA((blocks.shape[0],)),
        ],
    )
    return states


def places_in_order(count):
    quarter = count // 4
    first, second, third, fourth = (list(range(at, at + quarter)) for at in range(0, count, quarter))
    half = quarter // 2
    order = second + first[:half] + third[:half] + first[half:] + third[half:] + fourth
    return [count - 1 - place for place in order]


def last_first(count):
    return list(range(count - 1, -1, -1))


def exchange(pieces, axis):
    groups = [places_in_order(lax.axis_size(axis))]
    return lax.all_to_all(pieces, axis, 0, 0, axis_index_groups=groups)


def in_pieces(state, axis):
    count = lax.axis_size(axis)
    rows, cols = state.shape
    return state.reshape(count, rows // count, cols)


def shards(queries, keys, values, out_grad, gain):
    rows, width = queries.shape
    total_width = width * lax.axis_size("head")
    bf16, f32 = jnp.bfloat16, jnp.float32
    tokens, state = (rows, width), (width, HEAD_DIM)
    small = 2 * rows * width * HEAD_DIM
    large = 2 * rows * rows * width * 3 // 4
    gain_row = gain.reshape(1, width)
    flat = (width, rows)
    chunks = pltpu.SemaphoreType.DMA((width // COPY_COLS,))
    vm, hbm = pltpu.VMEM, pltpu.HBM
    rows_vm, flat_vm, state_vm = vm(tokens, bf16), vm(flat, bf16), vm(state, bf16)

    (own_kv,) = local_call(
        states_body,
        [],
        [hbm(state, bf16)],
        small,
        [keys, values],
        [rows_vm] * 2 + [state_vm] + [chunks] * 3,
    )
    kv_blocks = exchange(in_pieces(own_kv, "seq"), "seq")
    half = width // 2 // COPY_COLS * COPY_COLS
    early = width * 3 // 4 // COPY_COLS * COPY_COLS
    dma = pltpu.SemaphoreType.DMA

    def weights_of(cols):
        return (cols // HEAD_DIM * weight_rows(rows), BLOCK)

    half_vm, half_chunks = vm((rows, half), bf16), dma((half // COPY_COLS,))
    flipped, grad_flipped, local, first_weights = local_call(
        flip_body,
        [],
        [flat_vm] * 3 + [hbm(weights_of(half), bf16)],
        2 * large,
        [queries, keys, values, out_grad],
        [rows_vm, half_vm, half_vm, rows_vm, vm(weights_of(half), bf16)]
        + [chunks, half_chunks, half_chunks, chunks, dma((half // HEAD_DIM,))],
    )
    kv_blocks, flipped, grad_flipped, local, first_weights = lax.optimization_barrier(
        (kv_blocks, flipped, grad_flipped, local, first_weights)
    )
    kv_low = exchange(scan_blocks(kv_blocks, False), "seq").reshape(state)
    other = width - half
    other_vm, other_chunks = vm((rows, other), bf16), dma((other // COPY_COLS,))
    local, second_weights = local_call(
        local_body,
        [flipped, local],
        [flat_vm, hbm(weights_of(other), bf16)],
        large,
        [keys, values],
        [other_vm, other_vm, vm(weights_of(other), bf16)]
        + [other_chunks, other_chunks, dma((other // HEAD_DIM,))],
        {3: 0},
    )
    groups = lax.axis_size("head")
    attended, sums = local_call(
        sums_body,
        [gain_row, flipped, grad_flipped, local, kv_low],
        [flat_vm, vm((groups, 2, rows), f32)],
        small,
        aliases={3: 0},
    )
    sums = lax.all_to_all(sums, "head", 0, 0, axis_index_groups=[last_first(groups)])
    dout_flipped, own_grad = local_call(
        functools.partial(dout_body, total_width),
        [gain_row, flipped, grad_flipped, attended, sums],
        [flat_vm, hbm(state, bf16)],
        small,
        scratch=[state_vm, chunks],
        aliases={3: 0},
    )
    grad_blocks = exchange(in_pieces(own_grad, "seq"), "seq")
    early_vm, late_vm = vm((rows, early), bf16), vm((rows, width - early), bf16)
    query_grad, dout, early_part = local_call(
        query_body,
        [dout_flipped, kv_low],
        [hbm(tokens, bf16), rows_vm, early_vm],
        2 * large + small,
        [keys, values, first_weights, second_weights],
        [rows_vm] * 3 + [vm(weights_of(early), bf16)] + [chunks] * 3 + [dma((2,))],
    )
    grad_blocks, query_grad, dout, early_part = lax.optimization_barrier(
        (grad_blocks, query_grad, dout, early_part)
    )
    grad_low = exchange(scan_blocks(grad_blocks, True), "seq").reshape(state)
    key_part, late_part, value_kept = local_call(
        inner_body,
        [dout],
        [rows_vm, late_vm, rows_vm],
        3 * large,
        [queries, values, second_weights],
        [rows_vm, vm(weights_of(width - early), bf16)] + [chunks] * 2 + [dma((1,))],
        {3: 0},
    )
    key_grad, value_grad = local_call(
        final_body,
        [value_kept, key_part, early_part, late_part, grad_low],
        [hbm(tokens, bf16)] * 2,
        2 * small,
        [keys],
        [rows_vm] * 3 + [chunks] * 3,
    )
    return query_grad, key_grad, value_grad


def solution(mesh):
    return jax.shard_map(
        shards,
        mesh=mesh,
        in_specs=(
            P("seq", "head"),
            P("seq", "head"),
            P("seq", "head"),
            P("seq", "head"),
            P("head"),
        ),
        out_specs=(P("seq", "head"), P("seq", "head"), P("seq", "head")),
        check_vma=False,
    )
```

```python
import functools

import jax
import jax.numpy as jnp
from jax import lax
from jax.experimental import pallas as pl
from jax.experimental.pallas import tpu as pltpu
from jax.sharding import PartitionSpec as P

HEAD_DIM = 128
BLOCK = 256
COPY_COLS = 512
COPY_ROWS = 128
STATE_ROWS = 256
EPSILON = 1e-06
MIB = 1 << 20


def mm(a, b):
    return lax.dot_general(a, b, (((1,), (0,)), ((), ())), preferred_element_type=jnp.float32)


def mm_nt(a, b):
    return lax.dot_general(a, b, (((1,), (1,)), ((), ())), preferred_element_type=jnp.float32)


def mm_tn(a, b):
    return lax.dot_general(a, b, (((0,), (0,)), ((), ())), preferred_element_type=jnp.float32)


def pieces_of(ref, size):
    return [slice(at, at + size) for at in range(0, ref.shape[1], size)]


def masked(scores, diagonal, rows_first):
    shape = (BLOCK, BLOCK)
    rows = lax.broadcasted_iota(jnp.int32, shape, 0)
    cols = lax.broadcasted_iota(jnp.int32, shape, 1)
    keep = rows >= cols if rows_first else cols >= rows
    inside = slice(diagonal, diagonal + BLOCK)
    kept = jnp.where(keep, scores[:, inside], 0.0).astype(jnp.bfloat16)
    before = scores[:, :diagonal].astype(jnp.bfloat16)
    after = scores[:, inside.stop :].astype(jnp.bfloat16)
    parts = [part for part in (before, kept, after) if part.shape[1]]
    return jnp.concatenate(parts, axis=1) if len(parts) > 1 else kept


def column_copies(source, target, sems):
    copies = []
    for index, cols in enumerate(pieces_of(source, COPY_COLS)):
        copies.append(pltpu.make_async_copy(source.at[:, cols], target.at[:, cols], sems.at[index]))
    return copies


def row_copies(source, target, size, sems):
    copies = []
    for index in range(source.shape[0] // size):
        part = slice(index * size, (index + 1) * size)
        copies.append(pltpu.make_async_copy(source.at[part, :], target.at[part, :], sems.at[index]))
    return copies


def start_all(*groups):
    for parts in zip(*groups):
        for part in parts:
            part.start()


def wait_all(*groups):
    for group in groups:
        for part in group:
            part.wait()


def states_body(
    key_hbm, value_hbm, state_hbm, key_ref, value_ref, total_ref, state_ref,
    key_sems, value_sems, state_sems,
):
    keys = row_copies(key_hbm, key_ref, COPY_ROWS, key_sems)
    values = row_copies(value_hbm, value_ref, COPY_ROWS, value_sems)
    stores = row_copies(state_ref, state_hbm, STATE_ROWS, state_sems)
    start_all(keys, values)
    for index in range(len(keys)):
        keys[index].wait()
        values[index].wait()
        rows = slice(index * COPY_ROWS, (index + 1) * COPY_ROWS)
        for head in pieces_of(key_ref, HEAD_DIM):
            part = mm_tn(key_ref[rows, head], value_ref[rows, head])
            if index:
                part = part + total_ref[head, :]
            if index < len(keys) - 1:
                total_ref[head, :] = part
            else:
                state_ref[head, :] = part.astype(jnp.bfloat16)
                if head.stop % STATE_ROWS == 0:
                    stores[head.stop // STATE_ROWS - 1].start()
    wait_all(stores)


def weight_rows(rows):
    blocks = rows // BLOCK
    return blocks * (blocks + 1) // 2 * BLOCK


def local_part(key_ref, value_ref, own, flipped_ref, head, local_ref, weight_ref, row):
    for start in range(0, key_ref.shape[0], BLOCK):
        end = start + BLOCK
        parts = []
        for first in range(0, end, BLOCK):
            scores = mm(key_ref[first : first + BLOCK, own], flipped_ref[head, start:end])
            part = masked(scores, 0, False) if first == start else scores.astype(jnp.bfloat16)
            weight_ref[row : row + BLOCK, :] = part
            parts.append(part)
            row += BLOCK
        weights = jnp.concatenate(parts, axis=0) if len(parts) > 1 else parts[0]
        local = mm_tn(value_ref[:end, own], weights)
        local_ref[head, start:end] = local.astype(jnp.bfloat16)


def local_heads(first, key_ref, value_ref, loads, flipped_ref, local_ref, weight_ref, weight_hbm, sems):
    size = weight_rows(key_ref.shape[0])
    stores = []
    for index, step in enumerate(pieces_of(key_ref, COPY_COLS)):
        for load in loads:
            load[index].wait()
        for left in range(step.start, step.stop, HEAD_DIM):
            own = slice(left, left + HEAD_DIM)
            head = slice(first + left, first + left + HEAD_DIM)
            number = left // HEAD_DIM
            part = slice(number * size, (number + 1) * size)
            local_part(key_ref, value_ref, own, flipped_ref, head, local_ref, weight_ref, part.start)
            store = pltpu.make_async_copy(weight_ref.at[part, :], weight_hbm.at[part, :], sems.at[number])
            store.start()
            stores.append(store)
    return stores


def flip_body(
    query_hbm, key_hbm, value_hbm, grad_hbm, flipped_ref, grad_flipped_ref, local_ref, weight_hbm,
    query_ref, key_ref, value_ref, grad_ref, weight_ref,
    query_sems, key_sems, value_sems, grad_sems, weight_sems,
):
    part = slice(0, key_ref.shape[1])
    query_loads = column_copies(query_hbm, query_ref, query_sems)
    key_loads = column_copies(key_hbm.at[:, part], key_ref, key_sems)
    value_loads = column_copies(value_hbm.at[:, part], value_ref, value_sems)
    grad_loads = column_copies(grad_hbm, grad_ref, grad_sems)
    start_all(query_loads)
    start_all(key_loads, value_loads)
    start_all(grad_loads)
    for load, cols in zip(query_loads, pieces_of(query_ref, COPY_COLS)):
        load.wait()
        flipped_ref[cols, :] = query_ref[:, cols].T
    stores = local_heads(
        0, key_ref, value_ref, (key_loads, value_loads), flipped_ref, local_ref, weight_ref, weight_hbm, weight_sems
    )
    for load, cols in zip(grad_loads, pieces_of(grad_ref, COPY_COLS)):
        load.wait()
        grad_flipped_ref[cols, :] = grad_ref[:, cols].T
    wait_all(stores)


def local_body(
    key_hbm, value_hbm, flipped_ref, given_ref, local_ref, weight_hbm,
    key_ref, value_ref, weight_ref, key_sems, value_sems, weight_sems,
):
    first = local_ref.shape[0] - key_ref.shape[1]
    key_loads = column_copies(key_hbm.at[:, first:], key_ref, key_sems)
    value_loads = column_copies(value_hbm.at[:, first:], value_ref, value_sems)
    start_all(key_loads, value_loads)
    stores = local_heads(
        first, key_ref, value_ref, (key_loads, value_loads), flipped_ref, local_ref, weight_ref, weight_hbm, weight_sems
    )
    wait_all(stores)


def scan_body(reverse, block_ref, state_hbm, state_ref, sems):
    count = block_ref.shape[0]
    total = jnp.zeros(block_ref.shape[1:], jnp.float32)
    places = places_in_order(count)
    stores = []
    for place in range(count - 1, -1, -1) if reverse else range(count):
        rank = places.index(place)
        state_ref[rank] = total.astype(jnp.bfloat16)
        total = total + block_ref[rank].astype(jnp.float32)
        stores.append(pltpu.make_async_copy(state_ref.at[rank], state_hbm.at[rank], sems.at[rank]))
        stores[-1].start()
    wait_all(stores)


def heads_of(ref):
    return [slice(at, at + HEAD_DIM) for at in range(0, ref.shape[0], HEAD_DIM)]


def scaled_grad(gain_ref, grad_ref, head):
    gain = jnp.broadcast_to(gain_ref[:, head], (HEAD_DIM, HEAD_DIM)).T
    gain = jnp.concatenate([gain] * (grad_ref.shape[1] // HEAD_DIM), axis=1)
    return gain * grad_ref[head, :].astype(jnp.float32)


def fold(values):
    parts = [values[at : at + 8, :] for at in range(0, values.shape[0], 8)]
    while len(parts) > 1:
        parts = [sum(parts[at + 1 : at + 2], parts[at]) for at in range(0, len(parts), 2)]
    return parts[0]


def sums_body(gain_ref, flipped_ref, grad_ref, local_ref, state_ref, attended_ref, sums_ref):
    square = cross = jnp.zeros((8, local_ref.shape[1]), jnp.float32)
    for head in heads_of(local_ref):
        attended = mm_tn(state_ref[head, :], flipped_ref[head, :])
        attended = attended + attended_ref[head, :].astype(jnp.float32)
        attended_ref[head, :] = attended.astype(jnp.bfloat16)
        square += fold(attended * attended)
        cross += fold(scaled_grad(gain_ref, grad_ref, head) * attended)
    square = jnp.sum(square, axis=0, keepdims=True)
    cross = jnp.sum(cross, axis=0, keepdims=True)
    for group in range(sums_ref.shape[0]):
        sums_ref[group, 0:1, :] = square
        sums_ref[group, 1:2, :] = cross


def dout_body(
    width, gain_ref, flipped_ref, grad_ref, attended_ref, sums_ref, dout_ref, own_hbm, own_ref, sems
):
    stores = row_copies(own_ref, own_hbm, STATE_ROWS, sems)
    sums = sum(sums_ref[group] for group in range(sums_ref.shape[0]))
    inverse = 1.0 / jnp.sqrt(sums[0:1, :] / width + EPSILON)
    drop = sums[1:2, :] * (inverse * inverse * inverse) / width
    for head in heads_of(dout_ref):
        attended = dout_ref[head, :].astype(jnp.float32)
        dout = scaled_grad(gain_ref, grad_ref, head) * inverse - attended * drop
        dout = dout.astype(jnp.bfloat16)
        dout_ref[head, :] = dout
        own_ref[head, :] = mm_nt(flipped_ref[head, :], dout).astype(jnp.bfloat16)
        if head.stop % STATE_ROWS == 0:
            stores[head.stop // STATE_ROWS - 1].start()
    wait_all(stores)


def value_local(weight_ref, row, dout, target):
    blocks = dout.shape[0] // BLOCK
    for own in range(blocks):
        parts = []
        for other in range(own, blocks):
            start = row + (other * (other + 1) // 2 + own) * BLOCK
            parts.append(weight_ref[start : start + BLOCK, :])
        weights = jnp.concatenate(parts, axis=1) if len(parts) > 1 else parts[0]
        at = own * BLOCK
        target[at : at + BLOCK, :] = mm(weights, dout[at:, :]).astype(jnp.bfloat16)


def query_body(
    key_hbm, value_hbm, first_hbm, second_hbm, flipped_ref, state_ref, out_hbm, dout_ref, value_out,
    key_ref, value_ref, out_ref, weight_ref, key_sems, value_sems, out_sems, weight_sems,
):
    rows = dout_ref.shape[0]
    size = weight_rows(rows)
    key_copies = column_copies(key_hbm, key_ref, key_sems)
    value_copies = column_copies(value_hbm, value_ref, value_sems)
    there = first_hbm.shape[0]
    rest = weight_ref.shape[0] - there
    weight_copies = [
        pltpu.make_async_copy(first_hbm, weight_ref.at[:there, :], weight_sems.at[0]),
        pltpu.make_async_copy(second_hbm.at[:rest, :], weight_ref.at[there:, :], weight_sems.at[1]),
    ]
    start_all(key_copies, value_copies)
    start_all(weight_copies)
    for head in heads_of(flipped_ref):
        dout_ref[:, head] = flipped_ref[head, :].T
    stores = column_copies(out_ref, out_hbm, out_sems)
    for index, step in enumerate(pieces_of(out_ref, COPY_COLS)):
        key_copies[index].wait()
        value_copies[index].wait()
        for left in range(step.start, step.stop, HEAD_DIM):
            cols = slice(left, left + HEAD_DIM)
            for start in range(0, rows, BLOCK):
                end = start + BLOCK
                dout = dout_ref[start:end, cols]
                dscore = masked(mm_nt(dout, value_ref[:end, cols]), start, True)
                grad = mm(dscore, key_ref[:end, cols]) + mm_nt(dout, state_ref[cols, :])
                out_ref[start:end, cols] = grad.astype(jnp.bfloat16)
        stores[index].start()
    wait_all(weight_copies)
    for number, cols in enumerate(pieces_of(value_out, HEAD_DIM)):
        value_local(weight_ref, number * size, dout_ref[:, cols], value_out.at[:, cols])
    wait_all(stores)


def inner_body(
    query_hbm, value_hbm, weight_hbm, dout_ref, key_out, value_out, value_ref,
    query_ref, weight_ref, query_sems, value_sems, weight_sem,
):
    rows, width = key_out.shape
    size = weight_rows(rows)
    early = width - value_out.shape[1]
    query_copies = column_copies(query_hbm, query_ref, query_sems)
    value_copies = column_copies(value_hbm, value_ref, value_sems)
    skipped = weight_hbm.shape[0] - weight_ref.shape[0]
    weight_copy = pltpu.make_async_copy(weight_hbm.at[skipped:, :], weight_ref, weight_sem.at[0])
    start_all(query_copies, value_copies)
    weight_copy.start()
    for index, step in enumerate(pieces_of(key_out, COPY_COLS)):
        query_copies[index].wait()
        value_copies[index].wait()
        for left in range(step.start, step.stop, HEAD_DIM):
            if left == early:
                weight_copy.wait()
            cols = slice(left, left + HEAD_DIM)
            dout = key_out[:, cols]
            for start in range(0, rows, BLOCK):
                end = start + BLOCK
                scores = mm_nt(value_ref[start:end, cols], dout[start:, :])
                grad = mm(masked(scores, 0, False), query_ref[start:, cols])
                key_out[start:end, cols] = grad.astype(jnp.bfloat16)
            if left >= early:
                late = slice(left - early, left - early + HEAD_DIM)
                value_local(weight_ref, late.start // HEAD_DIM * size, dout, value_out.at[:, late])


def final_body(
    key_hbm, value_ref, key_part, early_part, late_part, state_ref, key_out_hbm, value_out_hbm,
    key_ref, key_out, value_out, in_sems, key_sems, value_sems,
):
    keys = column_copies(key_hbm, key_ref, in_sems)
    start_all(keys)
    key_stores = column_copies(key_out, key_out_hbm, key_sems)
    value_stores = column_copies(value_out, value_out_hbm, value_sems)
    for index, step in enumerate(pieces_of(key_out, COPY_COLS)):
        for left in range(step.start, step.stop, HEAD_DIM):
            cols = slice(left, left + HEAD_DIM)
            grad = key_part[:, cols].astype(jnp.float32) + mm_nt(value_ref[:, cols], state_ref[cols, :])
            key_out[:, cols] = grad.astype(jnp.bfloat16)
        key_stores[index].start()
    for index, step in enumerate(pieces_of(value_out, COPY_COLS)):
        keys[index].wait()
        for left in range(step.start, step.stop, HEAD_DIM):
            cols = slice(left, left + HEAD_DIM)
            early = early_part.shape[1]
            if left < early:
                part = early_part[:, cols]
            else:
                part = late_part[:, left - early : left - early + HEAD_DIM]
            grad = part.astype(jnp.float32) + mm(key_ref[:, cols], state_ref[cols, :])
            value_out[:, cols] = grad.astype(jnp.bfloat16)
        value_stores[index].start()
    wait_all(key_stores, value_stores)


def local_call(body, in_args, outs, flops, hbm_args=(), scratch=(), aliases=None):
    args = [pltpu.with_memory_space_constraint(a, pltpu.HBM) for a in hbm_args]
    args += [pltpu.with_memory_space_constraint(a, pltpu.VMEM) for a in in_args]
    specs = [pl.BlockSpec(memory_space=pltpu.HBM)] * len(hbm_args)
    specs += [pl.BlockSpec(memory_space=pltpu.VMEM)] * len(in_args)
    out_specs = []
    for out in outs:
        out_specs.append(pl.BlockSpec(memory_space=out.memory_space))
    moved = sum(a.size * a.dtype.itemsize for a in args)
    return pl.pallas_call(
        body,
        in_specs=specs,
        out_specs=out_specs,
        out_shape=outs,
        scratch_shapes=scratch,
        input_output_aliases=aliases or {},
        compiler_params=pltpu.CompilerParams(vmem_limit_bytes=16 * MIB),
        cost_estimate=pl.CostEstimate(flops=flops, bytes_accessed=moved, transcendentals=0),
    )(*args)


def scan_blocks(blocks, reverse):
    (states,) = local_call(
        functools.partial(scan_body, reverse),
        [blocks],
        [pltpu.HBM(blocks.shape, blocks.dtype)],
        blocks.size,
        scratch=[
            pltpu.VMEM(blocks.shape, blocks.dtype),
            pltpu.SemaphoreType.DMA((blocks.shape[0],)),
        ],
    )
    return states


def places_in_order(count):
    quarter = count // 4
    first, second, third, fourth = (list(range(at, at + quarter)) for at in range(0, count, quarter))
    half = quarter // 2
    order = second + first[:half] + third[:half] + first[half:] + third[half:] + fourth
    return [count - 1 - place for place in order]


def last_first(count):
    return list(range(count - 1, -1, -1))


def exchange(pieces, axis):
    groups = [places_in_order(lax.axis_size(axis))]
    return lax.all_to_all(pieces, axis, 0, 0, axis_index_groups=groups)


def in_pieces(state, axis):
    count = lax.axis_size(axis)
    rows, cols = state.shape
    return state.reshape(count, rows // count, cols)


def shards(queries, keys, values, out_grad, gain):
    rows, width = queries.shape
    total_width = width * lax.axis_size("head")
    bf16, f32 = jnp.bfloat16, jnp.float32
    tokens, state = (rows, width), (width, HEAD_DIM)
    small = 2 * rows * width * HEAD_DIM
    large = 2 * rows * rows * width * 3 // 4
    gain_row = gain.reshape(1, width)
    flat = (width, rows)
    dma = pltpu.SemaphoreType.DMA
    chunks, row_chunks = dma((width // COPY_COLS,)), dma((rows // COPY_ROWS,))
    state_chunks = dma((width // STATE_ROWS,))
    vm, hbm = pltpu.VMEM, pltpu.HBM
    rows_vm, flat_vm, state_vm = vm(tokens, bf16), vm(flat, bf16), vm(state, bf16)

    (own_kv,) = local_call(
        states_body,
        [],
        [hbm(state, bf16)],
        small,
        [keys, values],
        [rows_vm] * 2 + [vm(state, f32), state_vm] + [row_chunks] * 2 + [state_chunks],
    )
    kv_blocks = exchange(in_pieces(own_kv, "seq"), "seq")
    half = width // 2 // COPY_COLS * COPY_COLS
    early = width * 3 // 4 // HEAD_DIM * HEAD_DIM
    def weights_of(cols):
        return (cols // HEAD_DIM * weight_rows(rows), BLOCK)

    half_vm, half_chunks = vm((rows, half), bf16), dma((half // COPY_COLS,))
    flipped, grad_flipped, local, first_weights = local_call(
        flip_body,
        [],
        [flat_vm] * 3 + [hbm(weights_of(half), bf16)],
        2 * large,
        [queries, keys, values, out_grad],
        [rows_vm, half_vm, half_vm, rows_vm, vm(weights_of(half), bf16)]
        + [chunks, half_chunks, half_chunks, chunks, dma((half // HEAD_DIM,))],
    )
    kv_blocks, flipped, grad_flipped, local, first_weights = lax.optimization_barrier(
        (kv_blocks, flipped, grad_flipped, local, first_weights)
    )
    kv_low = exchange(scan_blocks(kv_blocks, False), "seq").reshape(state)
    other = width - half
    other_vm, other_chunks = vm((rows, other), bf16), dma((other // COPY_COLS,))
    local, second_weights = local_call(
        local_body,
        [flipped, local],
        [flat_vm, hbm(weights_of(other), bf16)],
        large,
        [keys, values],
        [other_vm, other_vm, vm(weights_of(other), bf16)]
        + [other_chunks, other_chunks, dma((other // HEAD_DIM,))],
        {3: 0},
    )
    groups = lax.axis_size("head")
    attended, sums = local_call(
        sums_body,
        [gain_row, flipped, grad_flipped, local, kv_low],
        [flat_vm, vm((groups, 2, rows), f32)],
        small,
        aliases={3: 0},
    )
    sums = lax.all_to_all(sums, "head", 0, 0, axis_index_groups=[last_first(groups)])
    dout_flipped, own_grad = local_call(
        functools.partial(dout_body, total_width),
        [gain_row, flipped, grad_flipped, attended, sums],
        [flat_vm, hbm(state, bf16)],
        small,
        scratch=[state_vm, state_chunks],
        aliases={3: 0},
    )
    grad_blocks = exchange(in_pieces(own_grad, "seq"), "seq")
    early_vm, late_vm = vm((rows, early), bf16), vm((rows, width - early), bf16)
    query_grad, dout, early_part = local_call(
        query_body,
        [dout_flipped, kv_low],
        [hbm(tokens, bf16), rows_vm, early_vm],
        2 * large + small,
        [keys, values, first_weights, second_weights],
        [rows_vm] * 3 + [vm(weights_of(early), bf16)] + [chunks] * 3 + [dma((2,))],
    )
    grad_blocks, query_grad, dout, early_part = lax.optimization_barrier(
        (grad_blocks, query_grad, dout, early_part)
    )
    grad_low = exchange(scan_blocks(grad_blocks, True), "seq").reshape(state)
    key_part, late_part, value_kept = local_call(
        inner_body,
        [dout],
        [rows_vm, late_vm, rows_vm],
        3 * large,
        [queries, values, second_weights],
        [rows_vm, vm(weights_of(width - early), bf16)] + [chunks] * 2 + [dma((1,))],
        {3: 0},
    )
    key_grad, value_grad = local_call(
        final_body,
        [value_kept, key_part, early_part, late_part, grad_low],
        [hbm(tokens, bf16)] * 2,
        2 * small,
        [keys],
        [rows_vm] * 3 + [chunks] * 3,
    )
    return query_grad, key_grad, value_grad


def solution(mesh):
    return jax.shard_map(
        shards,
        mesh=mesh,
        in_specs=(
            P("seq", "head"),
            P("seq", "head"),
            P("seq", "head"),
            P("seq", "head"),
            P("head"),
        ),
        out_specs=(P("seq", "head"), P("seq", "head"), P("seq", "head")),
        check_vma=False,
    )
```

```python
import functools

import jax
import jax.numpy as jnp
from jax import lax
from jax.experimental import pallas as pl
from jax.experimental.pallas import tpu as pltpu
from jax.sharding import PartitionSpec as P

HEAD_DIM = 128
BLOCK = 256
COPY_COLS = 512
COPY_ROWS = 128
STATE_ROWS = 256
EPSILON = 1e-06
MIB = 1 << 20


def mm(a, b):
    return lax.dot_general(a, b, (((1,), (0,)), ((), ())), preferred_element_type=jnp.float32)


def mm_nt(a, b):
    return lax.dot_general(a, b, (((1,), (1,)), ((), ())), preferred_element_type=jnp.float32)


def mm_tn(a, b):
    return lax.dot_general(a, b, (((0,), (0,)), ((), ())), preferred_element_type=jnp.float32)


def pieces_of(ref, size):
    return [slice(at, at + size) for at in range(0, ref.shape[1], size)]


def masked(scores, diagonal, rows_first):
    shape = (BLOCK, BLOCK)
    rows = lax.broadcasted_iota(jnp.int32, shape, 0)
    cols = lax.broadcasted_iota(jnp.int32, shape, 1)
    keep = rows >= cols if rows_first else cols >= rows
    inside = slice(diagonal, diagonal + BLOCK)
    kept = jnp.where(keep, scores[:, inside], 0.0).astype(jnp.bfloat16)
    before = scores[:, :diagonal].astype(jnp.bfloat16)
    after = scores[:, inside.stop :].astype(jnp.bfloat16)
    parts = [part for part in (before, kept, after) if part.shape[1]]
    return jnp.concatenate(parts, axis=1) if len(parts) > 1 else kept


def column_copies(source, target, sems):
    copies = []
    for index, cols in enumerate(pieces_of(source, COPY_COLS)):
        copies.append(pltpu.make_async_copy(source.at[:, cols], target.at[:, cols], sems.at[index]))
    return copies


def row_copies(source, target, size, sems):
    copies = []
    for index in range(source.shape[0] // size):
        part = slice(index * size, (index + 1) * size)
        copies.append(pltpu.make_async_copy(source.at[part, :], target.at[part, :], sems.at[index]))
    return copies


def start_all(*groups):
    for parts in zip(*groups):
        for part in parts:
            part.start()


def wait_all(*groups):
    for group in groups:
        for part in group:
            part.wait()


def states_body(
    key_hbm, value_hbm, state_hbm, key_ref, value_ref, total_ref, state_ref,
    key_sems, value_sems, state_sems,
):
    keys = row_copies(key_hbm, key_ref, COPY_ROWS, key_sems)
    values = row_copies(value_hbm, value_ref, COPY_ROWS, value_sems)
    stores = row_copies(state_ref, state_hbm, STATE_ROWS, state_sems)
    start_all(keys, values)
    for index in range(len(keys)):
        keys[index].wait()
        values[index].wait()
        rows = slice(index * COPY_ROWS, (index + 1) * COPY_ROWS)
        for head in pieces_of(key_ref, HEAD_DIM):
            part = mm_tn(key_ref[rows, head], value_ref[rows, head])
            if index:
                part = part + total_ref[head, :]
            if index < len(keys) - 1:
                total_ref[head, :] = part
            else:
                state_ref[head, :] = part.astype(jnp.bfloat16)
                if head.stop % STATE_ROWS == 0:
                    stores[head.stop // STATE_ROWS - 1].start()
    wait_all(stores)


def weight_rows(rows):
    blocks = rows // BLOCK
    return blocks * (blocks + 1) // 2 * BLOCK


def local_part(key_ref, value_ref, own, flipped_ref, head, local_ref, weight_ref, row):
    for start in range(0, key_ref.shape[0], BLOCK):
        end = start + BLOCK
        parts = []
        for first in range(0, end, BLOCK):
            scores = mm(key_ref[first : first + BLOCK, own], flipped_ref[head, start:end])
            part = masked(scores, 0, False) if first == start else scores.astype(jnp.bfloat16)
            weight_ref[row : row + BLOCK, :] = part
            parts.append(part)
            row += BLOCK
        weights = jnp.concatenate(parts, axis=0) if len(parts) > 1 else parts[0]
        local = mm_tn(value_ref[:end, own], weights)
        local_ref[head, start:end] = local.astype(jnp.bfloat16)


def local_heads(first, key_ref, value_ref, loads, flipped_ref, local_ref, weight_ref, weight_hbm, sems):
    size = weight_rows(key_ref.shape[0])
    stores = []
    for index, step in enumerate(pieces_of(key_ref, COPY_COLS)):
        for load in loads:
            load[index].wait()
        for left in range(step.start, step.stop, HEAD_DIM):
            own = slice(left, left + HEAD_DIM)
            head = slice(first + left, first + left + HEAD_DIM)
            number = left // HEAD_DIM
            part = slice(number * size, (number + 1) * size)
            local_part(key_ref, value_ref, own, flipped_ref, head, local_ref, weight_ref, part.start)
            store = pltpu.make_async_copy(weight_ref.at[part, :], weight_hbm.at[part, :], sems.at[number])
            store.start()
            stores.append(store)
    return stores


def flip_body(
    query_hbm, key_hbm, value_hbm, grad_hbm, flipped_ref, grad_flipped_ref, local_ref, weight_hbm,
    query_ref, key_ref, value_ref, grad_ref, weight_ref,
    query_sems, key_sems, value_sems, grad_sems, weight_sems,
):
    part = slice(0, key_ref.shape[1])
    query_loads = column_copies(query_hbm, query_ref, query_sems)
    key_loads = column_copies(key_hbm.at[:, part], key_ref, key_sems)
    value_loads = column_copies(value_hbm.at[:, part], value_ref, value_sems)
    grad_loads = column_copies(grad_hbm, grad_ref, grad_sems)
    start_all(query_loads)
    start_all(key_loads, value_loads)
    start_all(grad_loads)
    for load, cols in zip(query_loads, pieces_of(query_ref, COPY_COLS)):
        load.wait()
        flipped_ref[cols, :] = query_ref[:, cols].T
    stores = local_heads(
        0, key_ref, value_ref, (key_loads, value_loads), flipped_ref, local_ref, weight_ref, weight_hbm, weight_sems
    )
    for load, cols in zip(grad_loads, pieces_of(grad_ref, COPY_COLS)):
        load.wait()
        grad_flipped_ref[cols, :] = grad_ref[:, cols].T
    wait_all(stores)


def local_body(
    key_hbm, value_hbm, flipped_ref, given_ref, local_ref, weight_hbm,
    key_ref, value_ref, weight_ref, key_sems, value_sems, weight_sems,
):
    first = local_ref.shape[0] - key_ref.shape[1]
    key_loads = column_copies(key_hbm.at[:, first:], key_ref, key_sems)
    value_loads = column_copies(value_hbm.at[:, first:], value_ref, value_sems)
    start_all(key_loads, value_loads)
    stores = local_heads(
        first, key_ref, value_ref, (key_loads, value_loads), flipped_ref, local_ref, weight_ref, weight_hbm, weight_sems
    )
    wait_all(stores)


def scan_body(reverse, block_ref, state_hbm, state_ref, sems):
    count = block_ref.shape[0]
    total = jnp.zeros(block_ref.shape[1:], jnp.float32)
    places = places_in_order(count)
    stores = []
    for place in range(count - 1, -1, -1) if reverse else range(count):
        rank = places.index(place)
        state_ref[rank] = total.astype(jnp.bfloat16)
        total = total + block_ref[rank].astype(jnp.float32)
        stores.append(pltpu.make_async_copy(state_ref.at[rank], state_hbm.at[rank], sems.at[rank]))
        stores[-1].start()
    wait_all(stores)


def heads_of(ref):
    return [slice(at, at + HEAD_DIM) for at in range(0, ref.shape[0], HEAD_DIM)]


def scaled_grad(gain_ref, grad_ref, head):
    gain = jnp.broadcast_to(gain_ref[:, head], (HEAD_DIM, HEAD_DIM)).T
    gain = jnp.concatenate([gain] * (grad_ref.shape[1] // HEAD_DIM), axis=1)
    return gain * grad_ref[head, :].astype(jnp.float32)


def fold(values):
    parts = [values[at : at + 8, :] for at in range(0, values.shape[0], 8)]
    while len(parts) > 1:
        parts = [sum(parts[at + 1 : at + 2], parts[at]) for at in range(0, len(parts), 2)]
    return parts[0]


def sums_body(gain_ref, flipped_ref, grad_ref, local_ref, state_ref, attended_ref, sums_ref):
    square = cross = jnp.zeros((8, local_ref.shape[1]), jnp.float32)
    for head in heads_of(local_ref):
        attended = mm_tn(state_ref[head, :], flipped_ref[head, :])
        attended = attended + attended_ref[head, :].astype(jnp.float32)
        attended_ref[head, :] = attended.astype(jnp.bfloat16)
        square += fold(attended * attended)
        cross += fold(scaled_grad(gain_ref, grad_ref, head) * attended)
    square = jnp.sum(square, axis=0, keepdims=True)
    cross = jnp.sum(cross, axis=0, keepdims=True)
    for group in range(sums_ref.shape[0]):
        sums_ref[group, 0:1, :] = square
        sums_ref[group, 1:2, :] = cross


def dout_body(
    width, gain_ref, flipped_ref, grad_ref, attended_ref, sums_ref, dout_ref, own_hbm, own_ref, sems
):
    stores = row_copies(own_ref, own_hbm, STATE_ROWS, sems)
    sums = sum(sums_ref[group] for group in range(sums_ref.shape[0]))
    inverse = 1.0 / jnp.sqrt(sums[0:1, :] / width + EPSILON)
    drop = sums[1:2, :] * (inverse * inverse * inverse) / width
    for head in heads_of(dout_ref):
        attended = dout_ref[head, :].astype(jnp.float32)
        dout = scaled_grad(gain_ref, grad_ref, head) * inverse - attended * drop
        dout = dout.astype(jnp.bfloat16)
        dout_ref[head, :] = dout
        own_ref[head, :] = mm_nt(flipped_ref[head, :], dout).astype(jnp.bfloat16)
        if head.stop % STATE_ROWS == 0:
            stores[head.stop // STATE_ROWS - 1].start()
    wait_all(stores)


def value_local(weight_ref, row, dout, target):
    blocks = dout.shape[0] // BLOCK
    for own in range(blocks):
        parts = []
        for other in range(own, blocks):
            start = row + (other * (other + 1) // 2 + own) * BLOCK
            parts.append(weight_ref[start : start + BLOCK, :])
        weights = jnp.concatenate(parts, axis=1) if len(parts) > 1 else parts[0]
        at = own * BLOCK
        target[at : at + BLOCK, :] = mm(weights, dout[at:, :]).astype(jnp.bfloat16)


def query_body(
    key_hbm, value_hbm, first_hbm, second_hbm, flipped_ref, state_ref, out_hbm, dout_ref, value_out,
    key_ref, value_ref, out_ref, weight_ref, key_sems, value_sems, out_sems, weight_sems,
):
    rows = dout_ref.shape[0]
    size = weight_rows(rows)
    key_copies = column_copies(key_hbm, key_ref, key_sems)
    value_copies = column_copies(value_hbm, value_ref, value_sems)
    there = first_hbm.shape[0]
    rest = weight_ref.shape[0] - there
    weight_copies = [
        pltpu.make_async_copy(first_hbm, weight_ref.at[:there, :], weight_sems.at[0]),
        pltpu.make_async_copy(second_hbm.at[:rest, :], weight_ref.at[there:, :], weight_sems.at[1]),
    ]
    start_all(key_copies, value_copies)
    start_all(weight_copies)
    for head in heads_of(flipped_ref):
        dout_ref[:, head] = flipped_ref[head, :].T
    stores = column_copies(out_ref, out_hbm, out_sems)
    for index, step in enumerate(pieces_of(out_ref, COPY_COLS)):
        key_copies[index].wait()
        value_copies[index].wait()
        for left in range(step.start, step.stop, HEAD_DIM):
            cols = slice(left, left + HEAD_DIM)
            for start in range(0, rows, BLOCK):
                end = start + BLOCK
                dout = dout_ref[start:end, cols]
                dscore = masked(mm_nt(dout, value_ref[:end, cols]), start, True)
                grad = mm(dscore, key_ref[:end, cols]) + mm_nt(dout, state_ref[cols, :])
                out_ref[start:end, cols] = grad.astype(jnp.bfloat16)
        stores[index].start()
    wait_all(weight_copies)
    for number, cols in enumerate(pieces_of(value_out, HEAD_DIM)):
        value_local(weight_ref, number * size, dout_ref[:, cols], value_out.at[:, cols])
    wait_all(stores)


def inner_body(
    query_hbm, value_hbm, weight_hbm, dout_ref, key_out, value_out, value_ref,
    query_ref, weight_ref, query_sems, value_sems, weight_sem,
):
    rows, width = key_out.shape
    size = weight_rows(rows)
    early = width - value_out.shape[1]
    query_copies = column_copies(query_hbm, query_ref, query_sems)
    value_copies = column_copies(value_hbm, value_ref, value_sems)
    skipped = weight_hbm.shape[0] - weight_ref.shape[0]
    weight_copy = pltpu.make_async_copy(weight_hbm.at[skipped:, :], weight_ref, weight_sem.at[0])
    start_all(query_copies, value_copies)
    weight_copy.start()
    for index, step in enumerate(pieces_of(key_out, COPY_COLS)):
        query_copies[index].wait()
        value_copies[index].wait()
        for left in range(step.start, step.stop, HEAD_DIM):
            if left == early:
                weight_copy.wait()
            cols = slice(left, left + HEAD_DIM)
            dout = key_out[:, cols]
            for start in range(0, rows, BLOCK):
                end = start + BLOCK
                scores = mm_nt(value_ref[start:end, cols], dout[start:, :])
                grad = mm(masked(scores, 0, False), query_ref[start:, cols])
                key_out[start:end, cols] = grad.astype(jnp.bfloat16)
            if left >= early:
                late = slice(left - early, left - early + HEAD_DIM)
                value_local(weight_ref, late.start // HEAD_DIM * size, dout, value_out.at[:, late])


def final_body(
    key_hbm, value_ref, key_part, early_part, late_part, state_ref, key_out_hbm, value_out_hbm,
    key_ref, key_out, value_out, in_sems, key_sems, value_sems,
):
    keys = row_copies(key_hbm, key_ref, COPY_ROWS, in_sems)
    start_all(keys)
    key_stores = row_copies(key_out, key_out_hbm, COPY_ROWS, key_sems)
    value_stores = row_copies(value_out, value_out_hbm, COPY_ROWS, value_sems)
    early = early_part.shape[1]
    for index, store in enumerate(key_stores):
        rows = slice(index * COPY_ROWS, (index + 1) * COPY_ROWS)
        for cols in pieces_of(key_out, HEAD_DIM):
            part = key_part[rows, cols].astype(jnp.float32)
            grad = part + mm_nt(value_ref[rows, cols], state_ref[cols, :])
            key_out[rows, cols] = grad.astype(jnp.bfloat16)
        store.start()
    for index, store in enumerate(value_stores):
        rows = slice(index * COPY_ROWS, (index + 1) * COPY_ROWS)
        keys[index].wait()
        for cols in pieces_of(value_out, HEAD_DIM):
            if cols.start < early:
                part = early_part[rows, cols]
            else:
                part = late_part[rows, cols.start - early : cols.stop - early]
            grad = part.astype(jnp.float32) + mm(key_ref[rows, cols], state_ref[cols, :])
            value_out[rows, cols] = grad.astype(jnp.bfloat16)
        store.start()
    wait_all(key_stores, value_stores)


def local_call(body, in_args, outs, flops, hbm_args=(), scratch=(), aliases=None):
    args = [pltpu.with_memory_space_constraint(a, pltpu.HBM) for a in hbm_args]
    args += [pltpu.with_memory_space_constraint(a, pltpu.VMEM) for a in in_args]
    specs = [pl.BlockSpec(memory_space=pltpu.HBM)] * len(hbm_args)
    specs += [pl.BlockSpec(memory_space=pltpu.VMEM)] * len(in_args)
    out_specs = []
    for out in outs:
        out_specs.append(pl.BlockSpec(memory_space=out.memory_space))
    moved = sum(a.size * a.dtype.itemsize for a in args)
    return pl.pallas_call(
        body,
        in_specs=specs,
        out_specs=out_specs,
        out_shape=outs,
        scratch_shapes=scratch,
        input_output_aliases=aliases or {},
        compiler_params=pltpu.CompilerParams(vmem_limit_bytes=16 * MIB),
        cost_estimate=pl.CostEstimate(flops=flops, bytes_accessed=moved, transcendentals=0),
    )(*args)


def scan_blocks(blocks, reverse):
    (states,) = local_call(
        functools.partial(scan_body, reverse),
        [blocks],
        [pltpu.HBM(blocks.shape, blocks.dtype)],
        blocks.size,
        scratch=[
            pltpu.VMEM(blocks.shape, blocks.dtype),
            pltpu.SemaphoreType.DMA((blocks.shape[0],)),
        ],
    )
    return states


def places_in_order(count):
    quarter = count // 4
    first, second, third, fourth = (list(range(at, at + quarter)) for at in range(0, count, quarter))
    half = quarter // 2
    order = second + first[:half] + third[:half] + first[half:] + third[half:] + fourth
    return [(count - 1 - place) ^ 1 for place in order]


def last_first(count):
    return list(range(count - 1, -1, -1))


def exchange(pieces, axis):
    groups = [places_in_order(lax.axis_size(axis))]
    return lax.all_to_all(pieces, axis, 0, 0, axis_index_groups=groups)


def in_pieces(state, axis):
    count = lax.axis_size(axis)
    rows, cols = state.shape
    return state.reshape(count, rows // count, cols)


def shards(queries, keys, values, out_grad, gain):
    rows, width = queries.shape
    total_width = width * lax.axis_size("head")
    bf16, f32 = jnp.bfloat16, jnp.float32
    tokens, state = (rows, width), (width, HEAD_DIM)
    small = 2 * rows * width * HEAD_DIM
    large = 2 * rows * rows * width * 3 // 4
    gain_row = gain.reshape(1, width)
    flat = (width, rows)
    dma = pltpu.SemaphoreType.DMA
    chunks, row_chunks = dma((width // COPY_COLS,)), dma((rows // COPY_ROWS,))
    state_chunks = dma((width // STATE_ROWS,))
    vm, hbm = pltpu.VMEM, pltpu.HBM
    rows_vm, flat_vm, state_vm = vm(tokens, bf16), vm(flat, bf16), vm(state, bf16)

    (own_kv,) = local_call(
        states_body,
        [],
        [hbm(state, bf16)],
        small,
        [keys, values],
        [rows_vm] * 2 + [vm(state, f32), state_vm] + [row_chunks] * 2 + [state_chunks],
    )
    kv_blocks = exchange(in_pieces(own_kv, "seq"), "seq")
    half = width // 2 // COPY_COLS * COPY_COLS
    early = width * 3 // 4 // HEAD_DIM * HEAD_DIM
    def weights_of(cols):
        return (cols // HEAD_DIM * weight_rows(rows), BLOCK)

    half_vm, half_chunks = vm((rows, half), bf16), dma((half // COPY_COLS,))
    flipped, grad_flipped, local, first_weights = local_call(
        flip_body,
        [],
        [flat_vm] * 3 + [hbm(weights_of(half), bf16)],
        2 * large,
        [queries, keys, values, out_grad],
        [rows_vm, half_vm, half_vm, rows_vm, vm(weights_of(half), bf16)]
        + [chunks, half_chunks, half_chunks, chunks, dma((half // HEAD_DIM,))],
    )
    kv_blocks, flipped, grad_flipped, local, first_weights = lax.optimization_barrier(
        (kv_blocks, flipped, grad_flipped, local, first_weights)
    )
    kv_low = exchange(scan_blocks(kv_blocks, False), "seq").reshape(state)
    other = width - half
    other_vm, other_chunks = vm((rows, other), bf16), dma((other // COPY_COLS,))
    local, second_weights = local_call(
        local_body,
        [flipped, local],
        [flat_vm, hbm(weights_of(other), bf16)],
        large,
        [keys, values],
        [other_vm, other_vm, vm(weights_of(other), bf16)]
        + [other_chunks, other_chunks, dma((other // HEAD_DIM,))],
        {3: 0},
    )
    groups = lax.axis_size("head")
    attended, sums = local_call(
        sums_body,
        [gain_row, flipped, grad_flipped, local, kv_low],
        [flat_vm, vm((groups, 2, rows), f32)],
        small,
        aliases={3: 0},
    )
    sums = lax.all_to_all(sums, "head", 0, 0, axis_index_groups=[last_first(groups)])
    dout_flipped, own_grad = local_call(
        functools.partial(dout_body, total_width),
        [gain_row, flipped, grad_flipped, attended, sums],
        [flat_vm, hbm(state, bf16)],
        small,
        scratch=[state_vm, state_chunks],
        aliases={3: 0},
    )
    grad_blocks = exchange(in_pieces(own_grad, "seq"), "seq")
    early_vm, late_vm = vm((rows, early), bf16), vm((rows, width - early), bf16)
    query_grad, dout, early_part = local_call(
        query_body,
        [dout_flipped, kv_low],
        [hbm(tokens, bf16), rows_vm, early_vm],
        2 * large + small,
        [keys, values, first_weights, second_weights],
        [rows_vm] * 3 + [vm(weights_of(early), bf16)] + [chunks] * 3 + [dma((2,))],
    )
    grad_blocks, query_grad, dout, early_part = lax.optimization_barrier(
        (grad_blocks, query_grad, dout, early_part)
    )
    grad_low = exchange(scan_blocks(grad_blocks, True), "seq").reshape(state)
    key_part, late_part, value_kept = local_call(
        inner_body,
        [dout],
        [rows_vm, late_vm, rows_vm],
        3 * large,
        [queries, values, second_weights],
        [rows_vm, vm(weights_of(width - early), bf16)] + [chunks] * 2 + [dma((1,))],
        {3: 0},
    )
    key_grad, value_grad = local_call(
        final_body,
        [value_kept, key_part, early_part, late_part, grad_low],
        [hbm(tokens, bf16)] * 2,
        2 * small,
        [keys],
        [rows_vm] * 3 + [row_chunks] * 3,
    )
    return query_grad, key_grad, value_grad


def solution(mesh):
    return jax.shard_map(
        shards,
        mesh=mesh,
        in_specs=(
            P("seq", "head"),
            P("seq", "head"),
            P("seq", "head"),
            P("seq", "head"),
            P("head"),
        ),
        out_specs=(P("seq", "head"), P("seq", "head"), P("seq", "head")),
        check_vma=False,
    )
```

```python
import functools

import jax
import jax.numpy as jnp
from jax import lax
from jax.experimental import pallas as pl
from jax.experimental.pallas import tpu as pltpu
from jax.sharding import PartitionSpec as P

HEAD_DIM = 128
BLOCK = 256
COPY_COLS = 512
COPY_ROWS = 128
STATE_ROWS = 256
EPSILON = 1e-06
MIB = 1 << 20


def mm(a, b):
    return lax.dot_general(a, b, (((1,), (0,)), ((), ())), preferred_element_type=jnp.float32)


def mm_nt(a, b):
    return lax.dot_general(a, b, (((1,), (1,)), ((), ())), preferred_element_type=jnp.float32)


def mm_tn(a, b):
    return lax.dot_general(a, b, (((0,), (0,)), ((), ())), preferred_element_type=jnp.float32)


def pieces_of(ref, size):
    return [slice(at, at + size) for at in range(0, ref.shape[1], size)]


def masked(scores, diagonal, rows_first):
    shape = (BLOCK, BLOCK)
    rows = lax.broadcasted_iota(jnp.int32, shape, 0)
    cols = lax.broadcasted_iota(jnp.int32, shape, 1)
    keep = rows >= cols if rows_first else cols >= rows
    inside = slice(diagonal, diagonal + BLOCK)
    kept = jnp.where(keep, scores[:, inside], 0.0).astype(jnp.bfloat16)
    before = scores[:, :diagonal].astype(jnp.bfloat16)
    after = scores[:, inside.stop :].astype(jnp.bfloat16)
    parts = [part for part in (before, kept, after) if part.shape[1]]
    return jnp.concatenate(parts, axis=1) if len(parts) > 1 else kept


def column_copies(source, target, sems):
    copies = []
    for index, cols in enumerate(pieces_of(source, COPY_COLS)):
        copies.append(pltpu.make_async_copy(source.at[:, cols], target.at[:, cols], sems.at[index]))
    return copies


def row_copies(source, target, size, sems):
    copies = []
    for index in range(source.shape[0] // size):
        part = slice(index * size, (index + 1) * size)
        copies.append(pltpu.make_async_copy(source.at[part, :], target.at[part, :], sems.at[index]))
    return copies


def start_all(*groups):
    for parts in zip(*groups):
        for part in parts:
            part.start()


def wait_all(*groups):
    for group in groups:
        for part in group:
            part.wait()


def states_body(
    key_hbm, value_hbm, state_hbm, key_ref, value_ref, total_ref, state_ref,
    key_sems, value_sems, state_sems,
):
    keys = row_copies(key_hbm, key_ref, COPY_ROWS, key_sems)
    values = row_copies(value_hbm, value_ref, COPY_ROWS, value_sems)
    stores = row_copies(state_ref, state_hbm, STATE_ROWS, state_sems)
    start_all(keys, values)
    for index in range(len(keys)):
        keys[index].wait()
        values[index].wait()
        rows = slice(index * COPY_ROWS, (index + 1) * COPY_ROWS)
        for head in pieces_of(key_ref, HEAD_DIM):
            part = mm_tn(key_ref[rows, head], value_ref[rows, head])
            if index:
                part = part + total_ref[head, :]
            if index < len(keys) - 1:
                total_ref[head, :] = part
            else:
                state_ref[head, :] = part.astype(jnp.bfloat16)
                if head.stop % STATE_ROWS == 0:
                    stores[head.stop // STATE_ROWS - 1].start()
    wait_all(stores)


def weight_rows(rows):
    blocks = rows // BLOCK
    return blocks * (blocks + 1) // 2 * BLOCK


def local_part(key_ref, value_ref, own, flipped_ref, head, local_ref, weight_ref, row):
    for start in range(0, key_ref.shape[0], BLOCK):
        end = start + BLOCK
        parts = []
        for first in range(0, end, BLOCK):
            scores = mm(key_ref[first : first + BLOCK, own], flipped_ref[head, start:end])
            part = masked(scores, 0, False) if first == start else scores.astype(jnp.bfloat16)
            weight_ref[row : row + BLOCK, :] = part
            parts.append(part)
            row += BLOCK
        weights = jnp.concatenate(parts, axis=0) if len(parts) > 1 else parts[0]
        local = mm_tn(value_ref[:end, own], weights)
        local_ref[head, start:end] = local.astype(jnp.bfloat16)


def local_heads(first, key_ref, value_ref, loads, flipped_ref, local_ref, weight_ref, weight_hbm, sems):
    size = weight_rows(key_ref.shape[0])
    stores = []
    for index, step in enumerate(pieces_of(key_ref, COPY_COLS)):
        for load in loads:
            load[index].wait()
        for left in range(step.start, step.stop, HEAD_DIM):
            own = slice(left, left + HEAD_DIM)
            head = slice(first + left, first + left + HEAD_DIM)
            number = left // HEAD_DIM
            part = slice(number * size, (number + 1) * size)
            local_part(key_ref, value_ref, own, flipped_ref, head, local_ref, weight_ref, part.start)
            store = pltpu.make_async_copy(weight_ref.at[part, :], weight_hbm.at[part, :], sems.at[number])
            store.start()
            stores.append(store)
    return stores


def flip_body(
    query_hbm, key_hbm, value_hbm, grad_hbm, flipped_ref, grad_flipped_ref, local_ref, weight_hbm,
    query_ref, key_ref, value_ref, grad_ref, weight_ref,
    query_sems, key_sems, value_sems, grad_sems, weight_sems,
):
    part = slice(0, key_ref.shape[1])
    query_loads = column_copies(query_hbm, query_ref, query_sems)
    key_loads = column_copies(key_hbm.at[:, part], key_ref, key_sems)
    value_loads = column_copies(value_hbm.at[:, part], value_ref, value_sems)
    grad_loads = column_copies(grad_hbm, grad_ref, grad_sems)
    start_all(query_loads)
    start_all(key_loads, value_loads)
    start_all(grad_loads)
    for load, cols in zip(query_loads, pieces_of(query_ref, COPY_COLS)):
        load.wait()
        flipped_ref[cols, :] = query_ref[:, cols].T
    stores = local_heads(
        0, key_ref, value_ref, (key_loads, value_loads), flipped_ref, local_ref, weight_ref, weight_hbm, weight_sems
    )
    for load, cols in zip(grad_loads, pieces_of(grad_ref, COPY_COLS)):
        load.wait()
        grad_flipped_ref[cols, :] = grad_ref[:, cols].T
    wait_all(stores)


def local_body(
    key_hbm, value_hbm, flipped_ref, given_ref, local_ref, weight_hbm,
    key_ref, value_ref, weight_ref, key_sems, value_sems, weight_sems,
):
    first = local_ref.shape[0] - key_ref.shape[1]
    key_loads = column_copies(key_hbm.at[:, first:], key_ref, key_sems)
    value_loads = column_copies(value_hbm.at[:, first:], value_ref, value_sems)
    start_all(key_loads, value_loads)
    stores = local_heads(
        first, key_ref, value_ref, (key_loads, value_loads), flipped_ref, local_ref, weight_ref, weight_hbm, weight_sems
    )
    wait_all(stores)


def scan_body(reverse, block_ref, state_hbm, state_ref, sems):
    count = block_ref.shape[0]
    total = jnp.zeros(block_ref.shape[1:], jnp.float32)
    owners, back = owner_order(count), return_order(count)
    stores = []
    for place in range(count - 1, -1, -1) if reverse else range(count):
        rank = back.index(place)
        state_ref[rank] = total.astype(jnp.bfloat16)
        total = total + block_ref[owners.index(place)].astype(jnp.float32)
        stores.append(pltpu.make_async_copy(state_ref.at[rank], state_hbm.at[rank], sems.at[rank]))
        stores[-1].start()
    wait_all(stores)


def heads_of(ref):
    return [slice(at, at + HEAD_DIM) for at in range(0, ref.shape[0], HEAD_DIM)]


def scaled_grad(gain_ref, grad_ref, head):
    gain = jnp.broadcast_to(gain_ref[:, head], (HEAD_DIM, HEAD_DIM)).T
    gain = jnp.concatenate([gain] * (grad_ref.shape[1] // HEAD_DIM), axis=1)
    return gain * grad_ref[head, :].astype(jnp.float32)


def fold(values):
    parts = [values[at : at + 8, :] for at in range(0, values.shape[0], 8)]
    while len(parts) > 1:
        parts = [sum(parts[at + 1 : at + 2], parts[at]) for at in range(0, len(parts), 2)]
    return parts[0]


def sums_body(table, gain_ref, flipped_ref, grad_ref, local_ref, state_ref, attended_ref, sums_ref):
    square = cross = jnp.zeros((8, local_ref.shape[1]), jnp.float32)
    for head in heads_of(local_ref):
        attended = mm_tn(state_of(state_ref, head, table), flipped_ref[head, :])
        attended = attended + attended_ref[head, :].astype(jnp.float32)
        attended_ref[head, :] = attended.astype(jnp.bfloat16)
        square += fold(attended * attended)
        cross += fold(scaled_grad(gain_ref, grad_ref, head) * attended)
    square = jnp.sum(square, axis=0, keepdims=True)
    cross = jnp.sum(cross, axis=0, keepdims=True)
    for group in range(sums_ref.shape[0]):
        sums_ref[group, 0:1, :] = square
        sums_ref[group, 1:2, :] = cross


def dout_body(
    width, gain_ref, flipped_ref, grad_ref, attended_ref, sums_ref, dout_ref, own_hbm, own_ref, sems
):
    stores = row_copies(own_ref, own_hbm, STATE_ROWS, sems)
    sums = sum(sums_ref[group] for group in range(sums_ref.shape[0]))
    inverse = 1.0 / jnp.sqrt(sums[0:1, :] / width + EPSILON)
    drop = sums[1:2, :] * (inverse * inverse * inverse) / width
    for head in heads_of(dout_ref):
        attended = dout_ref[head, :].astype(jnp.float32)
        dout = scaled_grad(gain_ref, grad_ref, head) * inverse - attended * drop
        dout = dout.astype(jnp.bfloat16)
        dout_ref[head, :] = dout
        own_ref[head, :] = mm_nt(flipped_ref[head, :], dout).astype(jnp.bfloat16)
        if head.stop % STATE_ROWS == 0:
            stores[head.stop // STATE_ROWS - 1].start()
    wait_all(stores)


def value_local(weight_ref, row, dout, target):
    blocks = dout.shape[0] // BLOCK
    for own in range(blocks):
        parts = []
        for other in range(own, blocks):
            start = row + (other * (other + 1) // 2 + own) * BLOCK
            parts.append(weight_ref[start : start + BLOCK, :])
        weights = jnp.concatenate(parts, axis=1) if len(parts) > 1 else parts[0]
        at = own * BLOCK
        target[at : at + BLOCK, :] = mm(weights, dout[at:, :]).astype(jnp.bfloat16)


def query_body(
    table, key_hbm, value_hbm, first_hbm, second_hbm, flipped_ref, state_ref, out_hbm, dout_ref, value_out,
    key_ref, value_ref, out_ref, weight_ref, key_sems, value_sems, out_sems, weight_sems,
):
    rows = dout_ref.shape[0]
    size = weight_rows(rows)
    key_copies = column_copies(key_hbm, key_ref, key_sems)
    value_copies = column_copies(value_hbm, value_ref, value_sems)
    there = first_hbm.shape[0]
    rest = weight_ref.shape[0] - there
    weight_copies = [
        pltpu.make_async_copy(first_hbm, weight_ref.at[:there, :], weight_sems.at[0]),
        pltpu.make_async_copy(second_hbm.at[:rest, :], weight_ref.at[there:, :], weight_sems.at[1]),
    ]
    start_all(key_copies, value_copies)
    start_all(weight_copies)
    for head in heads_of(flipped_ref):
        dout_ref[:, head] = flipped_ref[head, :].T
    stores = column_copies(out_ref, out_hbm, out_sems)
    for index, step in enumerate(pieces_of(out_ref, COPY_COLS)):
        key_copies[index].wait()
        value_copies[index].wait()
        for left in range(step.start, step.stop, HEAD_DIM):
            cols = slice(left, left + HEAD_DIM)
            state = state_of(state_ref, cols, table)
            for start in range(0, rows, BLOCK):
                end = start + BLOCK
                dout = dout_ref[start:end, cols]
                dscore = masked(mm_nt(dout, value_ref[:end, cols]), start, True)
                grad = mm(dscore, key_ref[:end, cols]) + mm_nt(dout, state)
                out_ref[start:end, cols] = grad.astype(jnp.bfloat16)
        stores[index].start()
    wait_all(weight_copies)
    for number, cols in enumerate(pieces_of(value_out, HEAD_DIM)):
        value_local(weight_ref, number * size, dout_ref[:, cols], value_out.at[:, cols])
    wait_all(stores)


def inner_body(
    query_hbm, value_hbm, weight_hbm, dout_ref, key_out, value_out, value_ref,
    query_ref, weight_ref, query_sems, value_sems, weight_sem,
):
    rows, width = key_out.shape
    size = weight_rows(rows)
    early = width - value_out.shape[1]
    query_copies = column_copies(query_hbm, query_ref, query_sems)
    value_copies = column_copies(value_hbm, value_ref, value_sems)
    skipped = weight_hbm.shape[0] - weight_ref.shape[0]
    weight_copy = pltpu.make_async_copy(weight_hbm.at[skipped:, :], weight_ref, weight_sem.at[0])
    start_all(query_copies, value_copies)
    weight_copy.start()
    for index, step in enumerate(pieces_of(key_out, COPY_COLS)):
        query_copies[index].wait()
        value_copies[index].wait()
        for left in range(step.start, step.stop, HEAD_DIM):
            if left == early:
                weight_copy.wait()
            cols = slice(left, left + HEAD_DIM)
            dout = key_out[:, cols]
            for start in range(0, rows, BLOCK):
                end = start + BLOCK
                scores = mm_nt(value_ref[start:end, cols], dout[start:, :])
                grad = mm(masked(scores, 0, False), query_ref[start:, cols])
                key_out[start:end, cols] = grad.astype(jnp.bfloat16)
            if left >= early:
                late = slice(left - early, left - early + HEAD_DIM)
                value_local(weight_ref, late.start // HEAD_DIM * size, dout, value_out.at[:, late])


def final_body(
    table, key_hbm, value_ref, key_part, early_part, late_part, state_ref, key_out_hbm, value_out_hbm,
    key_ref, key_out, value_out, in_sems, key_sems, value_sems,
):
    keys = column_copies(key_hbm, key_ref, in_sems)
    start_all(keys)
    key_stores = column_copies(key_out, key_out_hbm, key_sems)
    value_stores = column_copies(value_out, value_out_hbm, value_sems)
    for index, step in enumerate(pieces_of(key_out, COPY_COLS)):
        for left in range(step.start, step.stop, HEAD_DIM):
            cols = slice(left, left + HEAD_DIM)
            grad = key_part[:, cols].astype(jnp.float32) + mm_nt(value_ref[:, cols], state_of(state_ref, cols, table))
            key_out[:, cols] = grad.astype(jnp.bfloat16)
        key_stores[index].start()
    for index, step in enumerate(pieces_of(value_out, COPY_COLS)):
        keys[index].wait()
        for left in range(step.start, step.stop, HEAD_DIM):
            cols = slice(left, left + HEAD_DIM)
            early = early_part.shape[1]
            if left < early:
                part = early_part[:, cols]
            else:
                part = late_part[:, left - early : left - early + HEAD_DIM]
            grad = part.astype(jnp.float32) + mm(key_ref[:, cols], state_of(state_ref, cols, table))
            value_out[:, cols] = grad.astype(jnp.bfloat16)
        value_stores[index].start()
    wait_all(key_stores, value_stores)


def local_call(body, in_args, outs, flops, hbm_args=(), scratch=(), aliases=None):
    args = [pltpu.with_memory_space_constraint(a, pltpu.HBM) for a in hbm_args]
    args += [pltpu.with_memory_space_constraint(a, pltpu.VMEM) for a in in_args]
    specs = [pl.BlockSpec(memory_space=pltpu.HBM)] * len(hbm_args)
    specs += [pl.BlockSpec(memory_space=pltpu.VMEM)] * len(in_args)
    out_specs = []
    for out in outs:
        out_specs.append(pl.BlockSpec(memory_space=out.memory_space))
    moved = sum(a.size * a.dtype.itemsize for a in args)
    return pl.pallas_call(
        body,
        in_specs=specs,
        out_specs=out_specs,
        out_shape=outs,
        scratch_shapes=scratch,
        input_output_aliases=aliases or {},
        compiler_params=pltpu.CompilerParams(vmem_limit_bytes=16 * MIB),
        cost_estimate=pl.CostEstimate(flops=flops, bytes_accessed=moved, transcendentals=0),
    )(*args)


def scan_blocks(blocks, reverse):
    (states,) = local_call(
        functools.partial(scan_body, reverse),
        [blocks],
        [pltpu.HBM(blocks.shape, blocks.dtype)],
        blocks.size,
        scratch=[
            pltpu.VMEM(blocks.shape, blocks.dtype),
            pltpu.SemaphoreType.DMA((blocks.shape[0],)),
        ],
    )
    return states


def owner_order(count):
    quarter = count // 4
    first, second, third, fourth = (list(range(at, at + quarter)) for at in range(0, count, quarter))
    half = quarter // 2
    order = second + first[:half] + third[:half] + first[half:] + third[half:] + fourth
    return [count - 1 - place for place in order]


def return_order(count):
    return [place ^ 1 for place in owner_order(count)]


def piece_table(count):
    back = return_order(count)
    return [back.index(place) for place in owner_order(count)]


def state_of(state_ref, head, table):
    size = state_ref.shape[0] // len(table)
    if size >= HEAD_DIM:
        at = table[head.start // size] * size + head.start % size
        return state_ref[at : at + HEAD_DIM, :]
    pieces = table[head.start // size : head.stop // size]
    return jnp.concatenate([state_ref[at * size : (at + 1) * size, :] for at in pieces], axis=0)


def last_first(count):
    return list(range(count - 1, -1, -1))


def exchange(pieces, axis, order):
    return lax.all_to_all(pieces, axis, 0, 0, axis_index_groups=[order(lax.axis_size(axis))])


def in_pieces(state, axis):
    count = lax.axis_size(axis)
    rows, cols = state.shape
    return state.reshape(count, rows // count, cols)


def shards(queries, keys, values, out_grad, gain):
    rows, width = queries.shape
    total_width = width * lax.axis_size("head")
    bf16, f32 = jnp.bfloat16, jnp.float32
    tokens, state = (rows, width), (width, HEAD_DIM)
    small = 2 * rows * width * HEAD_DIM
    large = 2 * rows * rows * width * 3 // 4
    gain_row = gain.reshape(1, width)
    table = piece_table(lax.axis_size("seq"))
    flat = (width, rows)
    dma = pltpu.SemaphoreType.DMA
    chunks, row_chunks = dma((width // COPY_COLS,)), dma((rows // COPY_ROWS,))
    state_chunks = dma((width // STATE_ROWS,))
    vm, hbm = pltpu.VMEM, pltpu.HBM
    rows_vm, flat_vm, state_vm = vm(tokens, bf16), vm(flat, bf16), vm(state, bf16)

    (own_kv,) = local_call(
        states_body,
        [],
        [hbm(state, bf16)],
        small,
        [keys, values],
        [rows_vm] * 2 + [vm(state, f32), state_vm] + [row_chunks] * 2 + [state_chunks],
    )
    kv_blocks = exchange(in_pieces(own_kv, "seq"), "seq", owner_order)
    half = width // 2 // COPY_COLS * COPY_COLS
    early = width * 3 // 4 // HEAD_DIM * HEAD_DIM
    def weights_of(cols):
        return (cols // HEAD_DIM * weight_rows(rows), BLOCK)

    half_vm, half_chunks = vm((rows, half), bf16), dma((half // COPY_COLS,))
    flipped, grad_flipped, local, first_weights = local_call(
        flip_body,
        [],
        [flat_vm] * 3 + [hbm(weights_of(half), bf16)],
        2 * large,
        [queries, keys, values, out_grad],
        [rows_vm, half_vm, half_vm, rows_vm, vm(weights_of(half), bf16)]
        + [chunks, half_chunks, half_chunks, chunks, dma((half // HEAD_DIM,))],
    )
    kv_blocks, flipped, grad_flipped, local, first_weights = lax.optimization_barrier(
        (kv_blocks, flipped, grad_flipped, local, first_weights)
    )
    kv_low = exchange(scan_blocks(kv_blocks, False), "seq", return_order).reshape(state)
    other = width - half
    other_vm, other_chunks = vm((rows, other), bf16), dma((other // COPY_COLS,))
    local, second_weights = local_call(
        local_body,
        [flipped, local],
        [flat_vm, hbm(weights_of(other), bf16)],
        large,
        [keys, values],
        [other_vm, other_vm, vm(weights_of(other), bf16)]
        + [other_chunks, other_chunks, dma((other // HEAD_DIM,))],
        {3: 0},
    )
    groups = lax.axis_size("head")
    attended, sums = local_call(
        functools.partial(sums_body, table),
        [gain_row, flipped, grad_flipped, local, kv_low],
        [flat_vm, vm((groups, 2, rows), f32)],
        small,
        aliases={3: 0},
    )
    sums = lax.all_to_all(sums, "head", 0, 0, axis_index_groups=[last_first(groups)])
    dout_flipped, own_grad = local_call(
        functools.partial(dout_body, total_width),
        [gain_row, flipped, grad_flipped, attended, sums],
        [flat_vm, hbm(state, bf16)],
        small,
        scratch=[state_vm, state_chunks],
        aliases={3: 0},
    )
    grad_blocks = exchange(in_pieces(own_grad, "seq"), "seq", owner_order)
    early_vm, late_vm = vm((rows, early), bf16), vm((rows, width - early), bf16)
    query_grad, dout, early_part = local_call(
        functools.partial(query_body, table),
        [dout_flipped, kv_low],
        [hbm(tokens, bf16), rows_vm, early_vm],
        2 * large + small,
        [keys, values, first_weights, second_weights],
        [rows_vm] * 3 + [vm(weights_of(early), bf16)] + [chunks] * 3 + [dma((2,))],
    )
    grad_blocks, query_grad, dout, early_part = lax.optimization_barrier(
        (grad_blocks, query_grad, dout, early_part)
    )
    grad_low = exchange(scan_blocks(grad_blocks, True), "seq", return_order).reshape(state)
    key_part, late_part, value_kept = local_call(
        inner_body,
        [dout],
        [rows_vm, late_vm, rows_vm],
        3 * large,
        [queries, values, second_weights],
        [rows_vm, vm(weights_of(width - early), bf16)] + [chunks] * 2 + [dma((1,))],
        {3: 0},
    )
    key_grad, value_grad = local_call(
        functools.partial(final_body, table),
        [value_kept, key_part, early_part, late_part, grad_low],
        [hbm(tokens, bf16)] * 2,
        2 * small,
        [keys],
        [rows_vm] * 3 + [chunks] * 3,
    )
    return query_grad, key_grad, value_grad


def solution(mesh):
    return jax.shard_map(
        shards,
        mesh=mesh,
        in_specs=(
            P("seq", "head"),
            P("seq", "head"),
            P("seq", "head"),
            P("seq", "head"),
            P("head"),
        ),
        out_specs=(P("seq", "head"), P("seq", "head"), P("seq", "head")),
        check_vma=False,
    )
```

```python
import functools

import jax
import jax.numpy as jnp
from jax import lax
from jax.experimental import pallas as pl
from jax.experimental.pallas import tpu as pltpu
from jax.sharding import PartitionSpec as P

HEAD_DIM = 128
BLOCK = 256
COPY_COLS = 512
COPY_ROWS = 128
STATE_ROWS = 256
EPSILON = 1e-06
MIB = 1 << 20


def mm(a, b):
    return lax.dot_general(a, b, (((1,), (0,)), ((), ())), preferred_element_type=jnp.float32)


def mm_nt(a, b):
    return lax.dot_general(a, b, (((1,), (1,)), ((), ())), preferred_element_type=jnp.float32)


def mm_tn(a, b):
    return lax.dot_general(a, b, (((0,), (0,)), ((), ())), preferred_element_type=jnp.float32)


def pieces_of(ref, size):
    return [slice(at, at + size) for at in range(0, ref.shape[1], size)]


def masked(scores, diagonal, rows_first):
    shape = (BLOCK, BLOCK)
    rows = lax.broadcasted_iota(jnp.int32, shape, 0)
    cols = lax.broadcasted_iota(jnp.int32, shape, 1)
    keep = rows >= cols if rows_first else cols >= rows
    inside = slice(diagonal, diagonal + BLOCK)
    kept = jnp.where(keep, scores[:, inside], 0.0).astype(jnp.bfloat16)
    before = scores[:, :diagonal].astype(jnp.bfloat16)
    after = scores[:, inside.stop :].astype(jnp.bfloat16)
    parts = [part for part in (before, kept, after) if part.shape[1]]
    return jnp.concatenate(parts, axis=1) if len(parts) > 1 else kept


def column_copies(source, target, sems):
    copies = []
    for index, cols in enumerate(pieces_of(source, COPY_COLS)):
        copies.append(pltpu.make_async_copy(source.at[:, cols], target.at[:, cols], sems.at[index]))
    return copies


def row_copies(source, target, size, sems):
    copies = []
    for index in range(source.shape[0] // size):
        part = slice(index * size, (index + 1) * size)
        copies.append(pltpu.make_async_copy(source.at[part, :], target.at[part, :], sems.at[index]))
    return copies


def start_all(*groups):
    for parts in zip(*groups):
        for part in parts:
            part.start()


def wait_all(*groups):
    for group in groups:
        for part in group:
            part.wait()


def states_body(
    key_hbm, value_hbm, state_hbm, key_ref, value_ref, total_ref, state_ref,
    key_sems, value_sems, state_sems,
):
    keys = row_copies(key_hbm, key_ref, COPY_ROWS, key_sems)
    values = row_copies(value_hbm, value_ref, COPY_ROWS, value_sems)
    stores = row_copies(state_ref, state_hbm, STATE_ROWS, state_sems)
    start_all(keys, values)
    for index in range(len(keys)):
        keys[index].wait()
        values[index].wait()
        rows = slice(index * COPY_ROWS, (index + 1) * COPY_ROWS)
        for head in pieces_of(key_ref, HEAD_DIM):
            part = mm_tn(key_ref[rows, head], value_ref[rows, head])
            if index:
                part = part + total_ref[head, :]
            if index < len(keys) - 1:
                total_ref[head, :] = part
            else:
                state_ref[head, :] = part.astype(jnp.bfloat16)
                if head.stop % STATE_ROWS == 0:
                    stores[head.stop // STATE_ROWS - 1].start()
    wait_all(stores)


def weight_rows(rows):
    blocks = rows // BLOCK
    return blocks * (blocks + 1) // 2 * BLOCK


def local_part(key_ref, value_ref, own, flipped_ref, head, local_ref, weight_ref, row):
    for start in range(0, key_ref.shape[0], BLOCK):
        end = start + BLOCK
        parts = []
        for first in range(0, end, BLOCK):
            scores = mm(key_ref[first : first + BLOCK, own], flipped_ref[head, start:end])
            part = masked(scores, 0, False) if first == start else scores.astype(jnp.bfloat16)
            weight_ref[row : row + BLOCK, :] = part
            parts.append(part)
            row += BLOCK
        weights = jnp.concatenate(parts, axis=0) if len(parts) > 1 else parts[0]
        local = mm_tn(value_ref[:end, own], weights)
        local_ref[head, start:end] = local.astype(jnp.bfloat16)


def local_heads(first, key_ref, value_ref, loads, flipped_ref, local_ref, weight_ref, weight_hbm, sems):
    size = weight_rows(key_ref.shape[0])
    stores = []
    for index, step in enumerate(pieces_of(key_ref, COPY_COLS)):
        for load in loads:
            load[index].wait()
        for left in range(step.start, step.stop, HEAD_DIM):
            own = slice(left, left + HEAD_DIM)
            head = slice(first + left, first + left + HEAD_DIM)
            number = left // HEAD_DIM
            part = slice(number * size, (number + 1) * size)
            local_part(key_ref, value_ref, own, flipped_ref, head, local_ref, weight_ref, part.start)
            store = pltpu.make_async_copy(weight_ref.at[part, :], weight_hbm.at[part, :], sems.at[number])
            store.start()
            stores.append(store)
    return stores


def flip_body(
    query_hbm, key_hbm, value_hbm, grad_hbm, flipped_ref, grad_flipped_ref, local_ref, weight_hbm,
    query_ref, key_ref, value_ref, grad_ref, weight_ref,
    query_sems, key_sems, value_sems, grad_sems, weight_sems,
):
    part = slice(0, key_ref.shape[1])
    query_loads = column_copies(query_hbm, query_ref, query_sems)
    key_loads = column_copies(key_hbm.at[:, part], key_ref, key_sems)
    value_loads = column_copies(value_hbm.at[:, part], value_ref, value_sems)
    grad_loads = column_copies(grad_hbm, grad_ref, grad_sems)
    start_all(query_loads)
    start_all(key_loads, value_loads)
    start_all(grad_loads)
    for load, cols in zip(query_loads, pieces_of(query_ref, COPY_COLS)):
        load.wait()
        flipped_ref[cols, :] = query_ref[:, cols].T
    stores = local_heads(
        0, key_ref, value_ref, (key_loads, value_loads), flipped_ref, local_ref, weight_ref, weight_hbm, weight_sems
    )
    for load, cols in zip(grad_loads, pieces_of(grad_ref, COPY_COLS)):
        load.wait()
        grad_flipped_ref[cols, :] = grad_ref[:, cols].T
    wait_all(stores)


def local_body(
    key_hbm, value_hbm, flipped_ref, given_ref, local_ref, weight_hbm,
    key_ref, value_ref, weight_ref, key_sems, value_sems, weight_sems,
):
    first = local_ref.shape[0] - key_ref.shape[1]
    key_loads = column_copies(key_hbm.at[:, first:], key_ref, key_sems)
    value_loads = column_copies(value_hbm.at[:, first:], value_ref, value_sems)
    start_all(key_loads, value_loads)
    stores = local_heads(
        first, key_ref, value_ref, (key_loads, value_loads), flipped_ref, local_ref, weight_ref, weight_hbm, weight_sems
    )
    wait_all(stores)


def scan_body(reverse, block_ref, state_hbm, state_ref, sems):
    count = block_ref.shape[0]
    total = jnp.zeros(block_ref.shape[1:], jnp.float32)
    places = places_in_order(count)
    stores = []
    for place in range(count - 1, -1, -1) if reverse else range(count):
        rank = places.index(place)
        state_ref[rank] = total.astype(jnp.bfloat16)
        total = total + block_ref[rank].astype(jnp.float32)
        stores.append(pltpu.make_async_copy(state_ref.at[rank], state_hbm.at[rank], sems.at[rank]))
        stores[-1].start()
    wait_all(stores)


def heads_of(ref):
    return [slice(at, at + HEAD_DIM) for at in range(0, ref.shape[0], HEAD_DIM)]


def scaled_grad(gain_ref, grad_ref, head):
    gain = jnp.broadcast_to(gain_ref[:, head], (HEAD_DIM, HEAD_DIM)).T
    gain = jnp.concatenate([gain] * (grad_ref.shape[1] // HEAD_DIM), axis=1)
    return gain * grad_ref[head, :].astype(jnp.float32)


def fold(values):
    parts = [values[at : at + 8, :] for at in range(0, values.shape[0], 8)]
    while len(parts) > 1:
        parts = [sum(parts[at + 1 : at + 2], parts[at]) for at in range(0, len(parts), 2)]
    return parts[0]


def sums_body(gain_ref, flipped_ref, grad_ref, local_ref, state_ref, attended_ref, sums_ref):
    square = cross = jnp.zeros((8, local_ref.shape[1]), jnp.float32)
    for head in heads_of(local_ref):
        attended = mm_tn(state_ref[head, :], flipped_ref[head, :])
        attended = attended + attended_ref[head, :].astype(jnp.float32)
        attended_ref[head, :] = attended.astype(jnp.bfloat16)
        square += fold(attended * attended)
        cross += fold(scaled_grad(gain_ref, grad_ref, head) * attended)
    square = jnp.sum(square, axis=0, keepdims=True)
    cross = jnp.sum(cross, axis=0, keepdims=True)
    for group in range(sums_ref.shape[0]):
        sums_ref[group, 0:1, :] = square
        sums_ref[group, 1:2, :] = cross


def query_part(dout, key_ref, value_ref, own, state, out_ref):
    for start in range(0, dout.shape[0], BLOCK):
        end = start + BLOCK
        block = dout[start:end, :]
        dscore = masked(mm_nt(block, value_ref[:end, own]), start, True)
        grad = mm(dscore, key_ref[:end, own]) + mm_nt(block, state)
        out_ref[start:end, own] = grad.astype(jnp.bfloat16)


def on_odd_place():
    return lax.axis_index("head") % 2 == 1


def dout_body(
    width, key_hbm, value_hbm, gain_ref, flipped_ref, grad_ref, attended_ref, sums_ref, state_ref,
    dout_ref, own_hbm, out_hbm, own_ref, key_ref, value_ref, out_ref, own_sems, sems,
):
    odd = on_odd_place()
    part = slice(0, key_ref.shape[1])
    stores = row_copies(own_ref, own_hbm, STATE_ROWS, own_sems)
    key_copy = pltpu.make_async_copy(key_hbm.at[:, part], key_ref, sems.at[0])
    value_copy = pltpu.make_async_copy(value_hbm.at[:, part], value_ref, sems.at[1])
    out_copy = pltpu.make_async_copy(out_ref, out_hbm.at[:, part], sems.at[2])

    @pl.when(odd)
    def _():
        key_copy.start()
        value_copy.start()

    sums = sum(sums_ref[group] for group in range(sums_ref.shape[0]))
    inverse = 1.0 / jnp.sqrt(sums[0:1, :] / width + EPSILON)
    drop = sums[1:2, :] * (inverse * inverse * inverse) / width
    for head in heads_of(dout_ref):
        attended = dout_ref[head, :].astype(jnp.float32)
        dout = scaled_grad(gain_ref, grad_ref, head) * inverse - attended * drop
        dout = dout.astype(jnp.bfloat16)
        dout_ref[head, :] = dout
        own_ref[head, :] = mm_nt(flipped_ref[head, :], dout).astype(jnp.bfloat16)
        if head.stop % STATE_ROWS == 0:
            stores[head.stop // STATE_ROWS - 1].start()

    @pl.when(odd)
    def _():
        key_copy.wait()
        value_copy.wait()
        for own in pieces_of(key_ref, HEAD_DIM):
            query_part(dout_ref[own, :].T, key_ref, value_ref, own, state_ref[own, :], out_ref)
        out_copy.start()
        out_copy.wait()

    wait_all(stores)


def value_local(weight_ref, row, dout, target):
    blocks = dout.shape[0] // BLOCK
    for own in range(blocks):
        parts = []
        for other in range(own, blocks):
            start = row + (other * (other + 1) // 2 + own) * BLOCK
            parts.append(weight_ref[start : start + BLOCK, :])
        weights = jnp.concatenate(parts, axis=1) if len(parts) > 1 else parts[0]
        at = own * BLOCK
        target[at : at + BLOCK, :] = mm(weights, dout[at:, :]).astype(jnp.bfloat16)


def query_body(
    key_hbm, value_hbm, first_hbm, second_hbm, given_hbm, flipped_ref, state_ref,
    out_hbm, dout_ref, value_out,
    key_ref, value_ref, out_ref, weight_ref, key_sems, value_sems, out_sems, weight_sems,
):
    even = jnp.logical_not(on_odd_place())
    size = weight_rows(dout_ref.shape[0])
    key_copies = column_copies(key_hbm, key_ref, key_sems)
    value_copies = column_copies(value_hbm, value_ref, value_sems)
    there = first_hbm.shape[0]
    rest = weight_ref.shape[0] - there
    weight_copies = [
        pltpu.make_async_copy(first_hbm, weight_ref.at[:there, :], weight_sems.at[0]),
        pltpu.make_async_copy(second_hbm.at[:rest, :], weight_ref.at[there:, :], weight_sems.at[1]),
    ]

    @pl.when(even)
    def _():
        key_copies[0].start()
        value_copies[0].start()

    start_all(key_copies[1:], value_copies[1:])
    start_all(weight_copies)
    for head in heads_of(flipped_ref):
        dout_ref[:, head] = flipped_ref[head, :].T
    stores = column_copies(out_ref, out_hbm, out_sems)

    def one(index, step):
        key_copies[index].wait()
        value_copies[index].wait()
        for left in range(step.start, step.stop, HEAD_DIM):
            cols = slice(left, left + HEAD_DIM)
            query_part(dout_ref[:, cols], key_ref, value_ref, cols, state_ref[cols, :], out_ref)
        stores[index].start()

    for index, step in enumerate(pieces_of(out_ref, COPY_COLS)):
        if index:
            one(index, step)
        else:
            pl.when(even)(functools.partial(one, index, step))
    wait_all(weight_copies)
    for number, cols in enumerate(pieces_of(value_out, HEAD_DIM)):
        value_local(weight_ref, number * size, dout_ref[:, cols], value_out.at[:, cols])
    pl.when(even)(stores[0].wait)
    wait_all(stores[1:])


def inner_body(
    query_hbm, value_hbm, weight_hbm, dout_ref, key_out, value_out, value_ref,
    query_ref, weight_ref, query_sems, value_sems, weight_sem,
):
    rows, width = key_out.shape
    size = weight_rows(rows)
    early = width - value_out.shape[1]
    query_copies = column_copies(query_hbm, query_ref, query_sems)
    value_copies = column_copies(value_hbm, value_ref, value_sems)
    skipped = weight_hbm.shape[0] - weight_ref.shape[0]
    weight_copy = pltpu.make_async_copy(weight_hbm.at[skipped:, :], weight_ref, weight_sem.at[0])
    start_all(query_copies, value_copies)
    weight_copy.start()
    for index, step in enumerate(pieces_of(key_out, COPY_COLS)):
        query_copies[index].wait()
        value_copies[index].wait()
        for left in range(step.start, step.stop, HEAD_DIM):
            if left == early:
                weight_copy.wait()
            cols = slice(left, left + HEAD_DIM)
            dout = key_out[:, cols]
            for start in range(0, rows, BLOCK):
                end = start + BLOCK
                scores = mm_nt(value_ref[start:end, cols], dout[start:, :])
                grad = mm(masked(scores, 0, False), query_ref[start:, cols])
                key_out[start:end, cols] = grad.astype(jnp.bfloat16)
            if left >= early:
                late = slice(left - early, left - early + HEAD_DIM)
                value_local(weight_ref, late.start // HEAD_DIM * size, dout, value_out.at[:, late])


def final_body(
    key_hbm, value_ref, key_part, early_part, late_part, state_ref, key_out_hbm, value_out_hbm,
    key_ref, key_out, value_out, in_sems, key_sems, value_sems,
):
    keys = column_copies(key_hbm, key_ref, in_sems)
    start_all(keys)
    key_stores = column_copies(key_out, key_out_hbm, key_sems)
    value_stores = column_copies(value_out, value_out_hbm, value_sems)
    for index, step in enumerate(pieces_of(key_out, COPY_COLS)):
        for left in range(step.start, step.stop, HEAD_DIM):
            cols = slice(left, left + HEAD_DIM)
            grad = key_part[:, cols].astype(jnp.float32) + mm_nt(value_ref[:, cols], state_ref[cols, :])
            key_out[:, cols] = grad.astype(jnp.bfloat16)
        key_stores[index].start()
    for index, step in enumerate(pieces_of(value_out, COPY_COLS)):
        keys[index].wait()
        for left in range(step.start, step.stop, HEAD_DIM):
            cols = slice(left, left + HEAD_DIM)
            early = early_part.shape[1]
            if left < early:
                part = early_part[:, cols]
            else:
                part = late_part[:, left - early : left - early + HEAD_DIM]
            grad = part.astype(jnp.float32) + mm(key_ref[:, cols], state_ref[cols, :])
            value_out[:, cols] = grad.astype(jnp.bfloat16)
        value_stores[index].start()
    wait_all(key_stores, value_stores)


def local_call(body, in_args, outs, flops, hbm_args=(), scratch=(), aliases=None):
    args = [pltpu.with_memory_space_constraint(a, pltpu.HBM) for a in hbm_args]
    args += [pltpu.with_memory_space_constraint(a, pltpu.VMEM) for a in in_args]
    specs = [pl.BlockSpec(memory_space=pltpu.HBM)] * len(hbm_args)
    specs += [pl.BlockSpec(memory_space=pltpu.VMEM)] * len(in_args)
    out_specs = []
    for out in outs:
        out_specs.append(pl.BlockSpec(memory_space=out.memory_space))
    moved = sum(a.size * a.dtype.itemsize for a in args)
    return pl.pallas_call(
        body,
        in_specs=specs,
        out_specs=out_specs,
        out_shape=outs,
        scratch_shapes=scratch,
        input_output_aliases=aliases or {},
        compiler_params=pltpu.CompilerParams(vmem_limit_bytes=16 * MIB),
        cost_estimate=pl.CostEstimate(flops=flops, bytes_accessed=moved, transcendentals=0),
    )(*args)


def scan_blocks(blocks, reverse):
    (states,) = local_call(
        functools.partial(scan_body, reverse),
        [blocks],
        [pltpu.HBM(blocks.shape, blocks.dtype)],
        blocks.size,
        scratch=[
            pltpu.VMEM(blocks.shape, blocks.dtype),
            pltpu.SemaphoreType.DMA((blocks.shape[0],)),
        ],
    )
    return states


def places_in_order(count):
    quarter = count // 4
    first, second, third, fourth = (list(range(at, at + quarter)) for at in range(0, count, quarter))
    half = quarter // 2
    order = second + first[:half] + third[:half] + first[half:] + third[half:] + fourth
    return [(count - 1 - place) ^ 1 for place in order]


def last_first(count):
    return list(range(count - 1, -1, -1))


def exchange(pieces, axis):
    groups = [places_in_order(lax.axis_size(axis))]
    return lax.all_to_all(pieces, axis, 0, 0, axis_index_groups=groups)


def in_pieces(state, axis):
    count = lax.axis_size(axis)
    rows, cols = state.shape
    return state.reshape(count, rows // count, cols)


def shards(queries, keys, values, out_grad, gain):
    rows, width = queries.shape
    total_width = width * lax.axis_size("head")
    bf16, f32 = jnp.bfloat16, jnp.float32
    tokens, state = (rows, width), (width, HEAD_DIM)
    small = 2 * rows * width * HEAD_DIM
    large = 2 * rows * rows * width * 3 // 4
    gain_row = gain.reshape(1, width)
    flat = (width, rows)
    dma = pltpu.SemaphoreType.DMA
    chunks, row_chunks = dma((width // COPY_COLS,)), dma((rows // COPY_ROWS,))
    state_chunks = dma((width // STATE_ROWS,))
    vm, hbm = pltpu.VMEM, pltpu.HBM
    rows_vm, flat_vm, state_vm = vm(tokens, bf16), vm(flat, bf16), vm(state, bf16)

    (own_kv,) = local_call(
        states_body,
        [],
        [hbm(state, bf16)],
        small,
        [keys, values],
        [rows_vm] * 2 + [vm(state, f32), state_vm] + [row_chunks] * 2 + [state_chunks],
    )
    kv_blocks = exchange(in_pieces(own_kv, "seq"), "seq")
    half = width // 2 // COPY_COLS * COPY_COLS
    early = width * 3 // 4 // HEAD_DIM * HEAD_DIM
    def weights_of(cols):
        return (cols // HEAD_DIM * weight_rows(rows), BLOCK)

    half_vm, half_chunks = vm((rows, half), bf16), dma((half // COPY_COLS,))
    flipped, grad_flipped, local, first_weights = local_call(
        flip_body,
        [],
        [flat_vm] * 3 + [hbm(weights_of(half), bf16)],
        2 * large,
        [queries, keys, values, out_grad],
        [rows_vm, half_vm, half_vm, rows_vm, vm(weights_of(half), bf16)]
        + [chunks, half_chunks, half_chunks, chunks, dma((half // HEAD_DIM,))],
    )
    kv_blocks, flipped, grad_flipped, local, first_weights = lax.optimization_barrier(
        (kv_blocks, flipped, grad_flipped, local, first_weights)
    )
    kv_low = exchange(scan_blocks(kv_blocks, False), "seq").reshape(state)
    other = width - half
    other_vm, other_chunks = vm((rows, other), bf16), dma((other // COPY_COLS,))
    local, second_weights = local_call(
        local_body,
        [flipped, local],
        [flat_vm, hbm(weights_of(other), bf16)],
        large,
        [keys, values],
        [other_vm, other_vm, vm(weights_of(other), bf16)]
        + [other_chunks, other_chunks, dma((other // HEAD_DIM,))],
        {3: 0},
    )
    groups = lax.axis_size("head")
    attended, sums = local_call(
        sums_body,
        [gain_row, flipped, grad_flipped, local, kv_low],
        [flat_vm, vm((groups, 2, rows), f32)],
        small,
        aliases={3: 0},
    )
    sums = lax.all_to_all(sums, "head", 0, 0, axis_index_groups=[last_first(groups)])
    part_vm = vm((rows, COPY_COLS), bf16)
    dout_flipped, own_grad, query_grad = local_call(
        functools.partial(dout_body, total_width),
        [gain_row, flipped, grad_flipped, attended, sums, kv_low],
        [flat_vm, hbm(state, bf16), hbm(tokens, bf16)],
        2 * small,
        [keys, values],
        [state_vm] + [part_vm] * 3 + [state_chunks, dma((3,))],
        {5: 0},
    )
    grad_blocks = exchange(in_pieces(own_grad, "seq"), "seq")
    early_vm, late_vm = vm((rows, early), bf16), vm((rows, width - early), bf16)
    query_grad, dout, early_part = local_call(
        query_body,
        [dout_flipped, kv_low],
        [hbm(tokens, bf16), rows_vm, early_vm],
        2 * large + small,
        [keys, values, first_weights, second_weights, query_grad],
        [rows_vm] * 3 + [vm(weights_of(early), bf16)] + [chunks] * 3 + [dma((2,))],
        {4: 0},
    )
    grad_blocks, query_grad, dout, early_part = lax.optimization_barrier(
        (grad_blocks, query_grad, dout, early_part)
    )
    grad_low = exchange(scan_blocks(grad_blocks, True), "seq").reshape(state)
    key_part, late_part, value_kept = local_call(
        inner_body,
        [dout],
        [rows_vm, late_vm, rows_vm],
        3 * large,
        [queries, values, second_weights],
        [rows_vm, vm(weights_of(width - early), bf16)] + [chunks] * 2 + [dma((1,))],
        {3: 0},
    )
    key_grad, value_grad = local_call(
        final_body,
        [value_kept, key_part, early_part, late_part, grad_low],
        [hbm(tokens, bf16)] * 2,
        2 * small,
        [keys],
        [rows_vm] * 3 + [chunks] * 3,
    )
    return query_grad, key_grad, value_grad


def solution(mesh):
    return jax.shard_map(
        shards,
        mesh=mesh,
        in_specs=(
            P("seq", "head"),
            P("seq", "head"),
            P("seq", "head"),
            P("seq", "head"),
            P("head"),
        ),
        out_specs=(P("seq", "head"), P("seq", "head"), P("seq", "head")),
        check_vma=False,
    )
```

```python
import functools

import jax
import jax.numpy as jnp
from jax import lax
from jax.experimental import pallas as pl
from jax.experimental.pallas import tpu as pltpu
from jax.sharding import PartitionSpec as P

HEAD_DIM = 128
BLOCK = 256
COPY_COLS = 512
COPY_ROWS = 128
STATE_ROWS = 256
EPSILON = 1e-06
MIB = 1 << 20


def mm(a, b):
    return lax.dot_general(a, b, (((1,), (0,)), ((), ())), preferred_element_type=jnp.float32)


def mm_nt(a, b):
    return lax.dot_general(a, b, (((1,), (1,)), ((), ())), preferred_element_type=jnp.float32)


def mm_tn(a, b):
    return lax.dot_general(a, b, (((0,), (0,)), ((), ())), preferred_element_type=jnp.float32)


def pieces_of(ref, size):
    return [slice(at, at + size) for at in range(0, ref.shape[1], size)]


def masked(scores, diagonal, rows_first):
    shape = (BLOCK, BLOCK)
    rows = lax.broadcasted_iota(jnp.int32, shape, 0)
    cols = lax.broadcasted_iota(jnp.int32, shape, 1)
    keep = rows >= cols if rows_first else cols >= rows
    inside = slice(diagonal, diagonal + BLOCK)
    kept = jnp.where(keep, scores[:, inside], 0.0).astype(jnp.bfloat16)
    before = scores[:, :diagonal].astype(jnp.bfloat16)
    after = scores[:, inside.stop :].astype(jnp.bfloat16)
    parts = [part for part in (before, kept, after) if part.shape[1]]
    return jnp.concatenate(parts, axis=1) if len(parts) > 1 else kept


def column_copies(source, target, sems):
    copies = []
    for index, cols in enumerate(pieces_of(source, COPY_COLS)):
        copies.append(pltpu.make_async_copy(source.at[:, cols], target.at[:, cols], sems.at[index]))
    return copies


def row_copies(source, target, size, sems):
    copies = []
    for index in range(source.shape[0] // size):
        part = slice(index * size, (index + 1) * size)
        copies.append(pltpu.make_async_copy(source.at[part, :], target.at[part, :], sems.at[index]))
    return copies


def start_all(*groups):
    for parts in zip(*groups):
        for part in parts:
            part.start()


def wait_all(*groups):
    for group in groups:
        for part in group:
            part.wait()


def states_body(
    key_hbm, value_hbm, state_hbm, key_ref, value_ref, total_ref, state_ref,
    key_sems, value_sems, state_sems,
):
    keys = row_copies(key_hbm, key_ref, COPY_ROWS, key_sems)
    values = row_copies(value_hbm, value_ref, COPY_ROWS, value_sems)
    stores = row_copies(state_ref, state_hbm, STATE_ROWS, state_sems)
    start_all(keys, values)
    for index in range(len(keys)):
        keys[index].wait()
        values[index].wait()
        rows = slice(index * COPY_ROWS, (index + 1) * COPY_ROWS)
        for head in pieces_of(key_ref, HEAD_DIM):
            part = mm_tn(key_ref[rows, head], value_ref[rows, head])
            if index:
                part = part + total_ref[head, :]
            if index < len(keys) - 1:
                total_ref[head, :] = part
            else:
                state_ref[head, :] = part.astype(jnp.bfloat16)
                if head.stop % STATE_ROWS == 0:
                    stores[head.stop // STATE_ROWS - 1].start()
    wait_all(stores)


def weight_rows(rows):
    blocks = rows // BLOCK
    return blocks * (blocks + 1) // 2 * BLOCK


def local_part(key_ref, value_ref, own, flipped_ref, head, local_ref, weight_ref, row):
    for start in range(0, key_ref.shape[0], BLOCK):
        end = start + BLOCK
        parts = []
        for first in range(0, end, BLOCK):
            scores = mm(key_ref[first : first + BLOCK, own], flipped_ref[head, start:end])
            part = masked(scores, 0, False) if first == start else scores.astype(jnp.bfloat16)
            weight_ref[row : row + BLOCK, :] = part
            parts.append(part)
            row += BLOCK
        weights = jnp.concatenate(parts, axis=0) if len(parts) > 1 else parts[0]
        local = mm_tn(value_ref[:end, own], weights)
        local_ref[head, start:end] = local.astype(jnp.bfloat16)


def local_heads(first, key_ref, value_ref, loads, flipped_ref, local_ref, weight_ref, weight_hbm, sems):
    size = weight_rows(key_ref.shape[0])
    stores = []
    for index, step in enumerate(pieces_of(key_ref, COPY_COLS)):
        for load in loads:
            load[index].wait()
        for left in range(step.start, step.stop, HEAD_DIM):
            own = slice(left, left + HEAD_DIM)
            head = slice(first + left, first + left + HEAD_DIM)
            number = left // HEAD_DIM
            part = slice(number * size, (number + 1) * size)
            local_part(key_ref, value_ref, own, flipped_ref, head, local_ref, weight_ref, part.start)
            store = pltpu.make_async_copy(weight_ref.at[part, :], weight_hbm.at[part, :], sems.at[number])
            store.start()
            stores.append(store)
    return stores


def flip_body(
    query_hbm, key_hbm, value_hbm, grad_hbm, flipped_ref, grad_flipped_ref, local_ref, weight_hbm,
    query_ref, key_ref, value_ref, grad_ref, weight_ref,
    query_sems, key_sems, value_sems, grad_sems, weight_sems,
):
    part = slice(0, key_ref.shape[1])
    query_loads = column_copies(query_hbm, query_ref, query_sems)
    key_loads = column_copies(key_hbm.at[:, part], key_ref, key_sems)
    value_loads = column_copies(value_hbm.at[:, part], value_ref, value_sems)
    grad_loads = column_copies(grad_hbm, grad_ref, grad_sems)
    start_all(query_loads)
    start_all(key_loads, value_loads)
    start_all(grad_loads)
    for load, cols in zip(query_loads, pieces_of(query_ref, COPY_COLS)):
        load.wait()
        flipped_ref[cols, :] = query_ref[:, cols].T
    stores = local_heads(
        0, key_ref, value_ref, (key_loads, value_loads), flipped_ref, local_ref, weight_ref, weight_hbm, weight_sems
    )
    for load, cols in zip(grad_loads, pieces_of(grad_ref, COPY_COLS)):
        load.wait()
        grad_flipped_ref[cols, :] = grad_ref[:, cols].T
    wait_all(stores)


def local_body(
    key_hbm, value_hbm, flipped_ref, given_ref, local_ref, weight_hbm,
    key_ref, value_ref, weight_ref, key_sems, value_sems, weight_sems,
):
    first = local_ref.shape[0] - key_ref.shape[1]
    key_loads = column_copies(key_hbm.at[:, first:], key_ref, key_sems)
    value_loads = column_copies(value_hbm.at[:, first:], value_ref, value_sems)
    start_all(key_loads, value_loads)
    stores = local_heads(
        first, key_ref, value_ref, (key_loads, value_loads), flipped_ref, local_ref, weight_ref, weight_hbm, weight_sems
    )
    wait_all(stores)


def on_odd_place():
    return lax.axis_index("head") % 2 == 1


def scan_ranks(reverse, block_ref, state_hbm, state_ref, sems):
    count = block_ref.shape[0]
    total = jnp.zeros(block_ref.shape[1:], jnp.float32)
    places = places_in_order(count)
    stores = []
    for place in range(count - 1, -1, -1) if reverse else range(count):
        rank = places.index(place)
        state_ref[rank] = total.astype(jnp.bfloat16)
        total = total + block_ref[rank].astype(jnp.float32)
        stores.append(pltpu.make_async_copy(state_ref.at[rank], state_hbm.at[rank], sems.at[rank]))
        stores[-1].start()
    wait_all(stores)


def scan_body(reverse, block_ref, state_hbm, state_ref, sems):
    odd = on_odd_place()

    @pl.when(odd)
    def _():
        scan_ranks(not reverse, block_ref, state_hbm, state_ref, sems)

    @pl.when(jnp.logical_not(odd))
    def _():
        scan_ranks(reverse, block_ref, state_hbm, state_ref, sems)


def heads_of(ref):
    return [slice(at, at + HEAD_DIM) for at in range(0, ref.shape[0], HEAD_DIM)]


def scaled_grad(gain_ref, grad_ref, head):
    gain = jnp.broadcast_to(gain_ref[:, head], (HEAD_DIM, HEAD_DIM)).T
    gain = jnp.concatenate([gain] * (grad_ref.shape[1] // HEAD_DIM), axis=1)
    return gain * grad_ref[head, :].astype(jnp.float32)


def fold(values):
    parts = [values[at : at + 8, :] for at in range(0, values.shape[0], 8)]
    while len(parts) > 1:
        parts = [sum(parts[at + 1 : at + 2], parts[at]) for at in range(0, len(parts), 2)]
    return parts[0]


def sums_body(gain_ref, flipped_ref, grad_ref, local_ref, state_ref, attended_ref, sums_ref):
    square = cross = jnp.zeros((8, local_ref.shape[1]), jnp.float32)
    for head in heads_of(local_ref):
        attended = mm_tn(state_ref[head, :], flipped_ref[head, :])
        attended = attended + attended_ref[head, :].astype(jnp.float32)
        attended_ref[head, :] = attended.astype(jnp.bfloat16)
        square += fold(attended * attended)
        cross += fold(scaled_grad(gain_ref, grad_ref, head) * attended)
    square = jnp.sum(square, axis=0, keepdims=True)
    cross = jnp.sum(cross, axis=0, keepdims=True)
    for group in range(sums_ref.shape[0]):
        sums_ref[group, 0:1, :] = square
        sums_ref[group, 1:2, :] = cross


def dout_body(
    width, gain_ref, flipped_ref, grad_ref, attended_ref, sums_ref, dout_ref, own_hbm, own_ref, sems
):
    stores = row_copies(own_ref, own_hbm, STATE_ROWS, sems)
    sums = sum(sums_ref[group] for group in range(sums_ref.shape[0]))
    inverse = 1.0 / jnp.sqrt(sums[0:1, :] / width + EPSILON)
    drop = sums[1:2, :] * (inverse * inverse * inverse) / width
    for head in heads_of(dout_ref):
        attended = dout_ref[head, :].astype(jnp.float32)
        dout = scaled_grad(gain_ref, grad_ref, head) * inverse - attended * drop
        dout = dout.astype(jnp.bfloat16)
        dout_ref[head, :] = dout
        own_ref[head, :] = mm_nt(flipped_ref[head, :], dout).astype(jnp.bfloat16)
        if head.stop % STATE_ROWS == 0:
            stores[head.stop // STATE_ROWS - 1].start()
    wait_all(stores)


def value_local(weight_ref, row, dout, target):
    blocks = dout.shape[0] // BLOCK
    for own in range(blocks):
        parts = []
        for other in range(own, blocks):
            start = row + (other * (other + 1) // 2 + own) * BLOCK
            parts.append(weight_ref[start : start + BLOCK, :])
        weights = jnp.concatenate(parts, axis=1) if len(parts) > 1 else parts[0]
        at = own * BLOCK
        target[at : at + BLOCK, :] = mm(weights, dout[at:, :]).astype(jnp.bfloat16)


def query_body(
    key_hbm, value_hbm, first_hbm, second_hbm, flipped_ref, state_ref, out_hbm, dout_ref, value_out,
    key_ref, value_ref, out_ref, weight_ref, key_sems, value_sems, out_sems, weight_sems,
):
    rows = dout_ref.shape[0]
    size = weight_rows(rows)
    key_copies = column_copies(key_hbm, key_ref, key_sems)
    value_copies = column_copies(value_hbm, value_ref, value_sems)
    there = first_hbm.shape[0]
    rest = weight_ref.shape[0] - there
    weight_copies = [
        pltpu.make_async_copy(first_hbm, weight_ref.at[:there, :], weight_sems.at[0]),
        pltpu.make_async_copy(second_hbm.at[:rest, :], weight_ref.at[there:, :], weight_sems.at[1]),
    ]
    start_all(key_copies, value_copies)
    start_all(weight_copies)
    for head in heads_of(flipped_ref):
        dout_ref[:, head] = flipped_ref[head, :].T
    stores = column_copies(out_ref, out_hbm, out_sems)
    for index, step in enumerate(pieces_of(out_ref, COPY_COLS)):
        key_copies[index].wait()
        value_copies[index].wait()
        for left in range(step.start, step.stop, HEAD_DIM):
            cols = slice(left, left + HEAD_DIM)
            for start in range(0, rows, BLOCK):
                end = start + BLOCK
                dout = dout_ref[start:end, cols]
                dscore = masked(mm_nt(dout, value_ref[:end, cols]), start, True)
                grad = mm(dscore, key_ref[:end, cols]) + mm_nt(dout, state_ref[cols, :])
                out_ref[start:end, cols] = grad.astype(jnp.bfloat16)
        stores[index].start()
    wait_all(weight_copies)
    for number, cols in enumerate(pieces_of(value_out, HEAD_DIM)):
        value_local(weight_ref, number * size, dout_ref[:, cols], value_out.at[:, cols])
    wait_all(stores)


def inner_body(
    query_hbm, value_hbm, weight_hbm, dout_ref, key_out, value_out, value_ref,
    query_ref, weight_ref, query_sems, value_sems, weight_sem,
):
    rows, width = key_out.shape
    size = weight_rows(rows)
    early = width - value_out.shape[1]
    query_copies = column_copies(query_hbm, query_ref, query_sems)
    value_copies = column_copies(value_hbm, value_ref, value_sems)
    skipped = weight_hbm.shape[0] - weight_ref.shape[0]
    weight_copy = pltpu.make_async_copy(weight_hbm.at[skipped:, :], weight_ref, weight_sem.at[0])
    start_all(query_copies, value_copies)
    weight_copy.start()
    for index, step in enumerate(pieces_of(key_out, COPY_COLS)):
        query_copies[index].wait()
        value_copies[index].wait()
        for left in range(step.start, step.stop, HEAD_DIM):
            if left == early:
                weight_copy.wait()
            cols = slice(left, left + HEAD_DIM)
            dout = key_out[:, cols]
            for start in range(0, rows, BLOCK):
                end = start + BLOCK
                scores = mm_nt(value_ref[start:end, cols], dout[start:, :])
                grad = mm(masked(scores, 0, False), query_ref[start:, cols])
                key_out[start:end, cols] = grad.astype(jnp.bfloat16)
            if left >= early:
                late = slice(left - early, left - early + HEAD_DIM)
                value_local(weight_ref, late.start // HEAD_DIM * size, dout, value_out.at[:, late])


def final_body(
    key_hbm, value_ref, key_part, early_part, late_part, state_ref, key_out_hbm, value_out_hbm,
    key_ref, key_out, value_out, in_sems, key_sems, value_sems,
):
    keys = column_copies(key_hbm, key_ref, in_sems)
    start_all(keys)
    key_stores = column_copies(key_out, key_out_hbm, key_sems)
    value_stores = column_copies(value_out, value_out_hbm, value_sems)
    for index, step in enumerate(pieces_of(key_out, COPY_COLS)):
        for left in range(step.start, step.stop, HEAD_DIM):
            cols = slice(left, left + HEAD_DIM)
            grad = key_part[:, cols].astype(jnp.float32) + mm_nt(value_ref[:, cols], state_ref[cols, :])
            key_out[:, cols] = grad.astype(jnp.bfloat16)
        key_stores[index].start()
    for index, step in enumerate(pieces_of(value_out, COPY_COLS)):
        keys[index].wait()
        for left in range(step.start, step.stop, HEAD_DIM):
            cols = slice(left, left + HEAD_DIM)
            early = early_part.shape[1]
            if left < early:
                part = early_part[:, cols]
            else:
                part = late_part[:, left - early : left - early + HEAD_DIM]
            grad = part.astype(jnp.float32) + mm(key_ref[:, cols], state_ref[cols, :])
            value_out[:, cols] = grad.astype(jnp.bfloat16)
        value_stores[index].start()
    wait_all(key_stores, value_stores)


def local_call(body, in_args, outs, flops, hbm_args=(), scratch=(), aliases=None):
    args = [pltpu.with_memory_space_constraint(a, pltpu.HBM) for a in hbm_args]
    args += [pltpu.with_memory_space_constraint(a, pltpu.VMEM) for a in in_args]
    specs = [pl.BlockSpec(memory_space=pltpu.HBM)] * len(hbm_args)
    specs += [pl.BlockSpec(memory_space=pltpu.VMEM)] * len(in_args)
    out_specs = []
    for out in outs:
        out_specs.append(pl.BlockSpec(memory_space=out.memory_space))
    moved = sum(a.size * a.dtype.itemsize for a in args)
    return pl.pallas_call(
        body,
        in_specs=specs,
        out_specs=out_specs,
        out_shape=outs,
        scratch_shapes=scratch,
        input_output_aliases=aliases or {},
        compiler_params=pltpu.CompilerParams(vmem_limit_bytes=16 * MIB),
        cost_estimate=pl.CostEstimate(flops=flops, bytes_accessed=moved, transcendentals=0),
    )(*args)


def scan_blocks(blocks, reverse):
    (states,) = local_call(
        functools.partial(scan_body, reverse),
        [blocks],
        [pltpu.HBM(blocks.shape, blocks.dtype)],
        blocks.size,
        scratch=[
            pltpu.VMEM(blocks.shape, blocks.dtype),
            pltpu.SemaphoreType.DMA((blocks.shape[0],)),
        ],
    )
    return states


def places_in_order(count):
    quarter = count // 4
    first, second, third, fourth = (list(range(at, at + quarter)) for at in range(0, count, quarter))
    half = quarter // 2
    order = second + first[:half] + third[:half] + first[half:] + third[half:] + fourth
    return [count - 1 - place for place in order]


def last_first(count):
    return list(range(count - 1, -1, -1))


def exchange(pieces):
    count, heads = lax.axis_size("seq"), lax.axis_size("head")
    groups = []
    for head in range(heads):
        places = places_in_order(count)
        if head % 2:
            places = [count - 1 - place for place in places]
        groups.append([place * heads + head for place in places])
    return lax.all_to_all(pieces, ("seq", "head"), 0, 0, axis_index_groups=groups)


def in_pieces(state, axis):
    count = lax.axis_size(axis)
    rows, cols = state.shape
    return state.reshape(count, rows // count, cols)


def shards(queries, keys, values, out_grad, gain):
    rows, width = queries.shape
    total_width = width * lax.axis_size("head")
    bf16, f32 = jnp.bfloat16, jnp.float32
    tokens, state = (rows, width), (width, HEAD_DIM)
    small = 2 * rows * width * HEAD_DIM
    large = 2 * rows * rows * width * 3 // 4
    gain_row = gain.reshape(1, width)
    flat = (width, rows)
    dma = pltpu.SemaphoreType.DMA
    chunks, row_chunks = dma((width // COPY_COLS,)), dma((rows // COPY_ROWS,))
    state_chunks = dma((width // STATE_ROWS,))
    vm, hbm = pltpu.VMEM, pltpu.HBM
    rows_vm, flat_vm, state_vm = vm(tokens, bf16), vm(flat, bf16), vm(state, bf16)

    (own_kv,) = local_call(
        states_body,
        [],
        [hbm(state, bf16)],
        small,
        [keys, values],
        [rows_vm] * 2 + [vm(state, f32), state_vm] + [row_chunks] * 2 + [state_chunks],
    )
    kv_blocks = exchange(in_pieces(own_kv, "seq"))
    half = width // 2 // COPY_COLS * COPY_COLS
    early = width * 3 // 4 // HEAD_DIM * HEAD_DIM
    def weights_of(cols):
        return (cols // HEAD_DIM * weight_rows(rows), BLOCK)

    half_vm, half_chunks = vm((rows, half), bf16), dma((half // COPY_COLS,))
    flipped, grad_flipped, local, first_weights = local_call(
        flip_body,
        [],
        [flat_vm] * 3 + [hbm(weights_of(half), bf16)],
        2 * large,
        [queries, keys, values, out_grad],
        [rows_vm, half_vm, half_vm, rows_vm, vm(weights_of(half), bf16)]
        + [chunks, half_chunks, half_chunks, chunks, dma((half // HEAD_DIM,))],
    )
    kv_blocks, flipped, grad_flipped, local, first_weights = lax.optimization_barrier(
        (kv_blocks, flipped, grad_flipped, local, first_weights)
    )
    kv_low = exchange(scan_blocks(kv_blocks, False)).reshape(state)
    other = width - half
    other_vm, other_chunks = vm((rows, other), bf16), dma((other // COPY_COLS,))
    local, second_weights = local_call(
        local_body,
        [flipped, local],
        [flat_vm, hbm(weights_of(other), bf16)],
        large,
        [keys, values],
        [other_vm, other_vm, vm(weights_of(other), bf16)]
        + [other_chunks, other_chunks, dma((other // HEAD_DIM,))],
        {3: 0},
    )
    groups = lax.axis_size("head")
    attended, sums = local_call(
        sums_body,
        [gain_row, flipped, grad_flipped, local, kv_low],
        [flat_vm, vm((groups, 2, rows), f32)],
        small,
        aliases={3: 0},
    )
    sums = lax.all_to_all(sums, "head", 0, 0, axis_index_groups=[last_first(groups)])
    dout_flipped, own_grad = local_call(
        functools.partial(dout_body, total_width),
        [gain_row, flipped, grad_flipped, attended, sums],
        [flat_vm, hbm(state, bf16)],
        small,
        scratch=[state_vm, state_chunks],
        aliases={3: 0},
    )
    grad_blocks = exchange(in_pieces(own_grad, "seq"))
    early_vm, late_vm = vm((rows, early), bf16), vm((rows, width - early), bf16)
    query_grad, dout, early_part = local_call(
        query_body,
        [dout_flipped, kv_low],
        [hbm(tokens, bf16), rows_vm, early_vm],
        2 * large + small,
        [keys, values, first_weights, second_weights],
        [rows_vm] * 3 + [vm(weights_of(early), bf16)] + [chunks] * 3 + [dma((2,))],
    )
    grad_blocks, query_grad, dout, early_part = lax.optimization_barrier(
        (grad_blocks, query_grad, dout, early_part)
    )
    grad_low = exchange(scan_blocks(grad_blocks, True)).reshape(state)
    key_part, late_part, value_kept = local_call(
        inner_body,
        [dout],
        [rows_vm, late_vm, rows_vm],
        3 * large,
        [queries, values, second_weights],
        [rows_vm, vm(weights_of(width - early), bf16)] + [chunks] * 2 + [dma((1,))],
        {3: 0},
    )
    key_grad, value_grad = local_call(
        final_body,
        [value_kept, key_part, early_part, late_part, grad_low],
        [hbm(tokens, bf16)] * 2,
        2 * small,
        [keys],
        [rows_vm] * 3 + [chunks] * 3,
    )
    return query_grad, key_grad, value_grad


def solution(mesh):
    return jax.shard_map(
        shards,
        mesh=mesh,
        in_specs=(
            P("seq", "head"),
            P("seq", "head"),
            P("seq", "head"),
            P("seq", "head"),
            P("head"),
        ),
        out_specs=(P("seq", "head"), P("seq", "head"), P("seq", "head")),
        check_vma=False,
    )
```

```python
import functools

import jax
import jax.numpy as jnp
from jax import lax
from jax.experimental import pallas as pl
from jax.experimental.pallas import tpu as pltpu
from jax.sharding import PartitionSpec as P

HEAD_DIM = 128
BLOCK = 256
COPY_COLS = 512
COPY_ROWS = 128
STATE_ROWS = 256
EPSILON = 1e-06
MIB = 1 << 20


def mm(a, b):
    return lax.dot_general(a, b, (((1,), (0,)), ((), ())), preferred_element_type=jnp.float32)


def mm_nt(a, b):
    return lax.dot_general(a, b, (((1,), (1,)), ((), ())), preferred_element_type=jnp.float32)


def mm_tn(a, b):
    return lax.dot_general(a, b, (((0,), (0,)), ((), ())), preferred_element_type=jnp.float32)


def pieces_of(ref, size):
    return [slice(at, at + size) for at in range(0, ref.shape[1], size)]


def masked(scores, diagonal, rows_first):
    shape = (BLOCK, BLOCK)
    rows = lax.broadcasted_iota(jnp.int32, shape, 0)
    cols = lax.broadcasted_iota(jnp.int32, shape, 1)
    keep = rows >= cols if rows_first else cols >= rows
    inside = slice(diagonal, diagonal + BLOCK)
    kept = jnp.where(keep, scores[:, inside], 0.0).astype(jnp.bfloat16)
    before = scores[:, :diagonal].astype(jnp.bfloat16)
    after = scores[:, inside.stop :].astype(jnp.bfloat16)
    parts = [part for part in (before, kept, after) if part.shape[1]]
    return jnp.concatenate(parts, axis=1) if len(parts) > 1 else kept


def column_copies(source, target, sems):
    copies = []
    for index, cols in enumerate(pieces_of(source, COPY_COLS)):
        copies.append(pltpu.make_async_copy(source.at[:, cols], target.at[:, cols], sems.at[index]))
    return copies


def row_copies(source, target, size, sems):
    copies = []
    for index in range(source.shape[0] // size):
        part = slice(index * size, (index + 1) * size)
        copies.append(pltpu.make_async_copy(source.at[part, :], target.at[part, :], sems.at[index]))
    return copies


def start_all(*groups):
    for parts in zip(*groups):
        for part in parts:
            part.start()


def wait_all(*groups):
    for group in groups:
        for part in group:
            part.wait()


def states_body(
    key_hbm, value_hbm, state_hbm, key_ref, value_ref, total_ref, state_ref,
    key_sems, value_sems, state_sems,
):
    keys = row_copies(key_hbm, key_ref, COPY_ROWS, key_sems)
    values = row_copies(value_hbm, value_ref, COPY_ROWS, value_sems)
    stores = row_copies(state_ref, state_hbm, STATE_ROWS, state_sems)
    start_all(keys, values)
    for index in range(len(keys)):
        keys[index].wait()
        values[index].wait()
        rows = slice(index * COPY_ROWS, (index + 1) * COPY_ROWS)
        for head in pieces_of(key_ref, HEAD_DIM):
            part = mm_tn(key_ref[rows, head], value_ref[rows, head])
            if index:
                part = part + total_ref[head, :]
            if index < len(keys) - 1:
                total_ref[head, :] = part
            else:
                state_ref[head, :] = part.astype(jnp.bfloat16)
                if head.stop % STATE_ROWS == 0:
                    stores[head.stop // STATE_ROWS - 1].start()
    wait_all(stores)


def weight_rows(rows):
    blocks = rows // BLOCK
    return blocks * (blocks + 1) // 2 * BLOCK


def local_part(key_ref, value_ref, own, flipped_ref, head, local_ref, weight_ref, row):
    for start in range(0, key_ref.shape[0], BLOCK):
        end = start + BLOCK
        parts = []
        for first in range(0, end, BLOCK):
            scores = mm(key_ref[first : first + BLOCK, own], flipped_ref[head, start:end])
            part = masked(scores, 0, False) if first == start else scores.astype(jnp.bfloat16)
            weight_ref[row : row + BLOCK, :] = part
            parts.append(part)
            row += BLOCK
        weights = jnp.concatenate(parts, axis=0) if len(parts) > 1 else parts[0]
        local = mm_tn(value_ref[:end, own], weights)
        local_ref[head, start:end] = local.astype(jnp.bfloat16)


def local_heads(first, key_ref, value_ref, loads, flipped_ref, local_ref, weight_ref, weight_hbm, sems):
    size = weight_rows(key_ref.shape[0])
    stores = []
    for index, step in enumerate(pieces_of(key_ref, COPY_COLS)):
        for load in loads:
            load[index].wait()
        for left in range(step.start, step.stop, HEAD_DIM):
            own = slice(left, left + HEAD_DIM)
            head = slice(first + left, first + left + HEAD_DIM)
            number = left // HEAD_DIM
            part = slice(number * size, (number + 1) * size)
            local_part(key_ref, value_ref, own, flipped_ref, head, local_ref, weight_ref, part.start)
            store = pltpu.make_async_copy(weight_ref.at[part, :], weight_hbm.at[part, :], sems.at[number])
            store.start()
            stores.append(store)
    return stores


def flip_body(
    query_hbm, key_hbm, value_hbm, grad_hbm, flipped_ref, grad_flipped_ref, local_ref, weight_hbm,
    query_ref, key_ref, value_ref, grad_ref, weight_ref,
    query_sems, key_sems, value_sems, grad_sems, weight_sems,
):
    part = slice(0, key_ref.shape[1])
    query_loads = column_copies(query_hbm, query_ref, query_sems)
    key_loads = column_copies(key_hbm.at[:, part], key_ref, key_sems)
    value_loads = column_copies(value_hbm.at[:, part], value_ref, value_sems)
    grad_loads = column_copies(grad_hbm, grad_ref, grad_sems)
    start_all(query_loads)
    start_all(key_loads, value_loads)
    start_all(grad_loads)
    for load, cols in zip(query_loads, pieces_of(query_ref, COPY_COLS)):
        load.wait()
        flipped_ref[cols, :] = query_ref[:, cols].T
    stores = local_heads(
        0, key_ref, value_ref, (key_loads, value_loads), flipped_ref, local_ref, weight_ref, weight_hbm, weight_sems
    )
    for load, cols in zip(grad_loads, pieces_of(grad_ref, COPY_COLS)):
        load.wait()
        grad_flipped_ref[cols, :] = grad_ref[:, cols].T
    wait_all(stores)


def local_body(
    key_hbm, value_hbm, flipped_ref, given_ref, local_ref, weight_hbm,
    key_ref, value_ref, weight_ref, key_sems, value_sems, weight_sems,
):
    first = local_ref.shape[0] - key_ref.shape[1]
    key_loads = column_copies(key_hbm.at[:, first:], key_ref, key_sems)
    value_loads = column_copies(value_hbm.at[:, first:], value_ref, value_sems)
    start_all(key_loads, value_loads)
    stores = local_heads(
        first, key_ref, value_ref, (key_loads, value_loads), flipped_ref, local_ref, weight_ref, weight_hbm, weight_sems
    )
    wait_all(stores)


def scan_body(reverse, block_ref, state_hbm, state_ref, sems):
    count = block_ref.shape[0]
    total = jnp.zeros(block_ref.shape[1:], jnp.float32)
    places = places_in_order(count, 0 if reverse else 1)
    stores = []
    for place in range(count - 1, -1, -1) if reverse else range(count):
        rank = places.index(place)
        state_ref[rank] = total.astype(jnp.bfloat16)
        total = total + block_ref[rank].astype(jnp.float32)
        stores.append(pltpu.make_async_copy(state_ref.at[rank], state_hbm.at[rank], sems.at[rank]))
        stores[-1].start()
    wait_all(stores)


def heads_of(ref):
    return [slice(at, at + HEAD_DIM) for at in range(0, ref.shape[0], HEAD_DIM)]


def scaled_grad(gain_ref, grad_ref, head):
    gain = jnp.broadcast_to(gain_ref[:, head], (HEAD_DIM, HEAD_DIM)).T
    gain = jnp.concatenate([gain] * (grad_ref.shape[1] // HEAD_DIM), axis=1)
    return gain * grad_ref[head, :].astype(jnp.float32)


def fold(values):
    parts = [values[at : at + 8, :] for at in range(0, values.shape[0], 8)]
    while len(parts) > 1:
        parts = [sum(parts[at + 1 : at + 2], parts[at]) for at in range(0, len(parts), 2)]
    return parts[0]


def sums_body(gain_ref, flipped_ref, grad_ref, local_ref, state_ref, attended_ref, sums_ref):
    square = cross = jnp.zeros((8, local_ref.shape[1]), jnp.float32)
    for head in heads_of(local_ref):
        attended = mm_tn(state_ref[head, :], flipped_ref[head, :])
        attended = attended + attended_ref[head, :].astype(jnp.float32)
        attended_ref[head, :] = attended.astype(jnp.bfloat16)
        square += fold(attended * attended)
        cross += fold(scaled_grad(gain_ref, grad_ref, head) * attended)
    square = jnp.sum(square, axis=0, keepdims=True)
    cross = jnp.sum(cross, axis=0, keepdims=True)
    for group in range(sums_ref.shape[0]):
        sums_ref[group, 0:1, :] = square
        sums_ref[group, 1:2, :] = cross


def dout_body(
    width, gain_ref, flipped_ref, grad_ref, attended_ref, sums_ref, dout_ref, own_hbm, own_ref, sems
):
    stores = row_copies(own_ref, own_hbm, STATE_ROWS, sems)
    sums = sum(sums_ref[group] for group in range(sums_ref.shape[0]))
    inverse = 1.0 / jnp.sqrt(sums[0:1, :] / width + EPSILON)
    drop = sums[1:2, :] * (inverse * inverse * inverse) / width
    for head in heads_of(dout_ref):
        attended = dout_ref[head, :].astype(jnp.float32)
        dout = scaled_grad(gain_ref, grad_ref, head) * inverse - attended * drop
        dout = dout.astype(jnp.bfloat16)
        dout_ref[head, :] = dout
        own_ref[head, :] = mm_nt(flipped_ref[head, :], dout).astype(jnp.bfloat16)
        if head.stop % STATE_ROWS == 0:
            stores[head.stop // STATE_ROWS - 1].start()
    wait_all(stores)


def value_local(weight_ref, row, dout, target):
    blocks = dout.shape[0] // BLOCK
    for own in range(blocks):
        parts = []
        for other in range(own, blocks):
            start = row + (other * (other + 1) // 2 + own) * BLOCK
            parts.append(weight_ref[start : start + BLOCK, :])
        weights = jnp.concatenate(parts, axis=1) if len(parts) > 1 else parts[0]
        at = own * BLOCK
        target[at : at + BLOCK, :] = mm(weights, dout[at:, :]).astype(jnp.bfloat16)


def query_body(
    key_hbm, value_hbm, first_hbm, second_hbm, flipped_ref, state_ref, out_hbm, dout_ref, value_out,
    key_ref, value_ref, out_ref, weight_ref, key_sems, value_sems, out_sems, weight_sems,
):
    rows = dout_ref.shape[0]
    size = weight_rows(rows)
    key_copies = column_copies(key_hbm, key_ref, key_sems)
    value_copies = column_copies(value_hbm, value_ref, value_sems)
    there = first_hbm.shape[0]
    rest = weight_ref.shape[0] - there
    weight_copies = [
        pltpu.make_async_copy(first_hbm, weight_ref.at[:there, :], weight_sems.at[0]),
        pltpu.make_async_copy(second_hbm.at[:rest, :], weight_ref.at[there:, :], weight_sems.at[1]),
    ]
    start_all(key_copies, value_copies)
    start_all(weight_copies)
    for head in heads_of(flipped_ref):
        dout_ref[:, head] = flipped_ref[head, :].T
    stores = column_copies(out_ref, out_hbm, out_sems)
    for index, step in enumerate(pieces_of(out_ref, COPY_COLS)):
        key_copies[index].wait()
        value_copies[index].wait()
        for left in range(step.start, step.stop, HEAD_DIM):
            cols = slice(left, left + HEAD_DIM)
            for start in range(0, rows, BLOCK):
                end = start + BLOCK
                dout = dout_ref[start:end, cols]
                dscore = masked(mm_nt(dout, value_ref[:end, cols]), start, True)
                grad = mm(dscore, key_ref[:end, cols]) + mm_nt(dout, state_ref[cols, :])
                out_ref[start:end, cols] = grad.astype(jnp.bfloat16)
        stores[index].start()
    wait_all(weight_copies)
    for number, cols in enumerate(pieces_of(value_out, HEAD_DIM)):
        value_local(weight_ref, number * size, dout_ref[:, cols], value_out.at[:, cols])
    wait_all(stores)


def inner_body(
    query_hbm, value_hbm, weight_hbm, dout_ref, key_out, value_out, value_ref,
    query_ref, weight_ref, query_sems, value_sems, weight_sem,
):
    rows, width = key_out.shape
    size = weight_rows(rows)
    early = width - value_out.shape[1]
    query_copies = column_copies(query_hbm, query_ref, query_sems)
    value_copies = column_copies(value_hbm, value_ref, value_sems)
    skipped = weight_hbm.shape[0] - weight_ref.shape[0]
    weight_copy = pltpu.make_async_copy(weight_hbm.at[skipped:, :], weight_ref, weight_sem.at[0])
    start_all(query_copies, value_copies)
    weight_copy.start()
    for index, step in enumerate(pieces_of(key_out, COPY_COLS)):
        query_copies[index].wait()
        value_copies[index].wait()
        for left in range(step.start, step.stop, HEAD_DIM):
            if left == early:
                weight_copy.wait()
            cols = slice(left, left + HEAD_DIM)
            dout = key_out[:, cols]
            for start in range(0, rows, BLOCK):
                end = start + BLOCK
                scores = mm_nt(value_ref[start:end, cols], dout[start:, :])
                grad = mm(masked(scores, 0, False), query_ref[start:, cols])
                key_out[start:end, cols] = grad.astype(jnp.bfloat16)
            if left >= early:
                late = slice(left - early, left - early + HEAD_DIM)
                value_local(weight_ref, late.start // HEAD_DIM * size, dout, value_out.at[:, late])


def final_body(
    key_hbm, value_ref, key_part, early_part, late_part, state_ref, key_out_hbm, value_out_hbm,
    key_ref, key_out, value_out, in_sems, key_sems, value_sems,
):
    key_copy = pltpu.make_async_copy(key_hbm, key_ref, in_sems.at[0])
    key_copy.start()
    key_stores = column_copies(key_out, key_out_hbm, key_sems)
    value_stores = column_copies(value_out, value_out_hbm, value_sems)
    for index, step in enumerate(pieces_of(key_out, COPY_COLS)):
        for left in range(step.start, step.stop, HEAD_DIM):
            cols = slice(left, left + HEAD_DIM)
            grad = key_part[:, cols].astype(jnp.float32) + mm_nt(value_ref[:, cols], state_ref[cols, :])
            key_out[:, cols] = grad.astype(jnp.bfloat16)
        key_stores[index].start()
    key_copy.wait()
    for index, step in enumerate(pieces_of(value_out, COPY_COLS)):
        for left in range(step.start, step.stop, HEAD_DIM):
            cols = slice(left, left + HEAD_DIM)
            early = early_part.shape[1]
            if left < early:
                part = early_part[:, cols]
            else:
                part = late_part[:, left - early : left - early + HEAD_DIM]
            grad = part.astype(jnp.float32) + mm(key_ref[:, cols], state_ref[cols, :])
            value_out[:, cols] = grad.astype(jnp.bfloat16)
        value_stores[index].start()
    wait_all(key_stores, value_stores)


def local_call(body, in_args, outs, flops, hbm_args=(), scratch=(), aliases=None):
    args = [pltpu.with_memory_space_constraint(a, pltpu.HBM) for a in hbm_args]
    args += [pltpu.with_memory_space_constraint(a, pltpu.VMEM) for a in in_args]
    specs = [pl.BlockSpec(memory_space=pltpu.HBM)] * len(hbm_args)
    specs += [pl.BlockSpec(memory_space=pltpu.VMEM)] * len(in_args)
    out_specs = []
    for out in outs:
        out_specs.append(pl.BlockSpec(memory_space=out.memory_space))
    moved = sum(a.size * a.dtype.itemsize for a in args)
    return pl.pallas_call(
        body,
        in_specs=specs,
        out_specs=out_specs,
        out_shape=outs,
        scratch_shapes=scratch,
        input_output_aliases=aliases or {},
        compiler_params=pltpu.CompilerParams(vmem_limit_bytes=16 * MIB),
        cost_estimate=pl.CostEstimate(flops=flops, bytes_accessed=moved, transcendentals=0),
    )(*args)


def scan_blocks(blocks, reverse):
    (states,) = local_call(
        functools.partial(scan_body, reverse),
        [blocks],
        [pltpu.HBM(blocks.shape, blocks.dtype)],
        blocks.size,
        scratch=[
            pltpu.VMEM(blocks.shape, blocks.dtype),
            pltpu.SemaphoreType.DMA((blocks.shape[0],)),
        ],
    )
    return states


def places_in_order(count, flip):
    quarter = count // 4
    first, second, third, fourth = (list(range(at, at + quarter)) for at in range(0, count, quarter))
    half = quarter // 2
    order = second + first[:half] + third[:half] + first[half:] + third[half:] + fourth
    return [(count - 1 - place) ^ flip for place in order]


def last_first(count):
    return list(range(count - 1, -1, -1))


def exchange(pieces, axis, flip):
    groups = [places_in_order(lax.axis_size(axis), flip)]
    return lax.all_to_all(pieces, axis, 0, 0, axis_index_groups=groups)


def in_pieces(state, axis):
    count = lax.axis_size(axis)
    rows, cols = state.shape
    return state.reshape(count, rows // count, cols)


def shards(queries, keys, values, out_grad, gain):
    rows, width = queries.shape
    total_width = width * lax.axis_size("head")
    bf16, f32 = jnp.bfloat16, jnp.float32
    tokens, state = (rows, width), (width, HEAD_DIM)
    small = 2 * rows * width * HEAD_DIM
    large = 2 * rows * rows * width * 3 // 4
    gain_row = gain.reshape(1, width)
    flat = (width, rows)
    dma = pltpu.SemaphoreType.DMA
    chunks, row_chunks = dma((width // COPY_COLS,)), dma((rows // COPY_ROWS,))
    state_chunks = dma((width // STATE_ROWS,))
    vm, hbm = pltpu.VMEM, pltpu.HBM
    rows_vm, flat_vm, state_vm = vm(tokens, bf16), vm(flat, bf16), vm(state, bf16)

    (own_kv,) = local_call(
        states_body,
        [],
        [hbm(state, bf16)],
        small,
        [keys, values],
        [rows_vm] * 2 + [vm(state, f32), state_vm] + [row_chunks] * 2 + [state_chunks],
    )
    kv_blocks = exchange(in_pieces(own_kv, "seq"), "seq", 1)
    half = width // 2 // COPY_COLS * COPY_COLS
    early = width * 3 // 4 // HEAD_DIM * HEAD_DIM
    def weights_of(cols):
        return (cols // HEAD_DIM * weight_rows(rows), BLOCK)

    half_vm, half_chunks = vm((rows, half), bf16), dma((half // COPY_COLS,))
    flipped, grad_flipped, local, first_weights = local_call(
        flip_body,
        [],
        [flat_vm] * 3 + [hbm(weights_of(half), bf16)],
        2 * large,
        [queries, keys, values, out_grad],
        [rows_vm, half_vm, half_vm, rows_vm, vm(weights_of(half), bf16)]
        + [chunks, half_chunks, half_chunks, chunks, dma((half // HEAD_DIM,))],
    )
    kv_blocks, flipped, grad_flipped, local, first_weights = lax.optimization_barrier(
        (kv_blocks, flipped, grad_flipped, local, first_weights)
    )
    kv_low = exchange(scan_blocks(kv_blocks, False), "seq", 1).reshape(state)
    other = width - half
    other_vm, other_chunks = vm((rows, other), bf16), dma((other // COPY_COLS,))
    local, second_weights = local_call(
        local_body,
        [flipped, local],
        [flat_vm, hbm(weights_of(other), bf16)],
        large,
        [keys, values],
        [other_vm, other_vm, vm(weights_of(other), bf16)]
        + [other_chunks, other_chunks, dma((other // HEAD_DIM,))],
        {3: 0},
    )
    groups = lax.axis_size("head")
    attended, sums = local_call(
        sums_body,
        [gain_row, flipped, grad_flipped, local, kv_low],
        [flat_vm, vm((groups, 2, rows), f32)],
        small,
        aliases={3: 0},
    )
    sums = lax.all_to_all(sums, "head", 0, 0, axis_index_groups=[last_first(groups)])
    dout_flipped, own_grad = local_call(
        functools.partial(dout_body, total_width),
        [gain_row, flipped, grad_flipped, attended, sums],
        [flat_vm, hbm(state, bf16)],
        small,
        scratch=[state_vm, state_chunks],
        aliases={3: 0},
    )
    grad_blocks = exchange(in_pieces(own_grad, "seq"), "seq", 0)
    early_vm, late_vm = vm((rows, early), bf16), vm((rows, width - early), bf16)
    query_grad, dout, early_part = local_call(
        query_body,
        [dout_flipped, kv_low],
        [hbm(tokens, bf16), rows_vm, early_vm],
        2 * large + small,
        [keys, values, first_weights, second_weights],
        [rows_vm] * 3 + [vm(weights_of(early), bf16)] + [chunks] * 3 + [dma((2,))],
    )
    grad_blocks, query_grad, dout, early_part = lax.optimization_barrier(
        (grad_blocks, query_grad, dout, early_part)
    )
    grad_low = exchange(scan_blocks(grad_blocks, True), "seq", 0).reshape(state)
    key_part, late_part, value_kept = local_call(
        inner_body,
        [dout],
        [rows_vm, late_vm, rows_vm],
        3 * large,
        [queries, values, second_weights],
        [rows_vm, vm(weights_of(width - early), bf16)] + [chunks] * 2 + [dma((1,))],
        {3: 0},
    )
    key_grad, value_grad = local_call(
        final_body,
        [value_kept, key_part, early_part, late_part, grad_low],
        [hbm(tokens, bf16)] * 2,
        2 * small,
        [keys],
        [rows_vm] * 3 + [dma((1,))] + [chunks] * 2,
    )
    return query_grad, key_grad, value_grad


def solution(mesh):
    return jax.shard_map(
        shards,
        mesh=mesh,
        in_specs=(
            P("seq", "head"),
            P("seq", "head"),
            P("seq", "head"),
            P("seq", "head"),
            P("head"),
        ),
        out_specs=(P("seq", "head"), P("seq", "head"), P("seq", "head")),
        check_vma=False,
    )
```

```python
import functools

import jax
import jax.numpy as jnp
from jax import lax
from jax.experimental import pallas as pl
from jax.experimental.pallas import tpu as pltpu
from jax.sharding import PartitionSpec as P

HEAD_DIM = 128
BLOCK = 256
COPY_COLS = 512
COPY_ROWS = 128
STATE_ROWS = 256
EPSILON = 1e-06
MIB = 1 << 20


def mm(a, b):
    return lax.dot_general(a, b, (((1,), (0,)), ((), ())), preferred_element_type=jnp.float32)


def mm_nt(a, b):
    return lax.dot_general(a, b, (((1,), (1,)), ((), ())), preferred_element_type=jnp.float32)


def mm_tn(a, b):
    return lax.dot_general(a, b, (((0,), (0,)), ((), ())), preferred_element_type=jnp.float32)


def pieces_of(ref, size):
    return [slice(at, at + size) for at in range(0, ref.shape[1], size)]


def masked(scores, diagonal, rows_first):
    shape = (BLOCK, BLOCK)
    rows = lax.broadcasted_iota(jnp.int32, shape, 0)
    cols = lax.broadcasted_iota(jnp.int32, shape, 1)
    keep = rows >= cols if rows_first else cols >= rows
    inside = slice(diagonal, diagonal + BLOCK)
    kept = jnp.where(keep, scores[:, inside], 0.0).astype(jnp.bfloat16)
    before = scores[:, :diagonal].astype(jnp.bfloat16)
    after = scores[:, inside.stop :].astype(jnp.bfloat16)
    parts = [part for part in (before, kept, after) if part.shape[1]]
    return jnp.concatenate(parts, axis=1) if len(parts) > 1 else kept


def column_copies(source, target, sems):
    copies = []
    for index, cols in enumerate(pieces_of(source, COPY_COLS)):
        copies.append(pltpu.make_async_copy(source.at[:, cols], target.at[:, cols], sems.at[index]))
    return copies


def row_copies(source, target, size, sems):
    copies = []
    for index in range(source.shape[0] // size):
        part = slice(index * size, (index + 1) * size)
        copies.append(pltpu.make_async_copy(source.at[part, :], target.at[part, :], sems.at[index]))
    return copies


def start_all(*groups):
    for parts in zip(*groups):
        for part in parts:
            part.start()


def wait_all(*groups):
    for group in groups:
        for part in group:
            part.wait()


def states_body(
    key_hbm, value_hbm, state_hbm, key_ref, value_ref, total_ref, state_ref,
    key_sems, value_sems, state_sems,
):
    keys = row_copies(key_hbm, key_ref, COPY_ROWS, key_sems)
    values = row_copies(value_hbm, value_ref, COPY_ROWS, value_sems)
    stores = row_copies(state_ref, state_hbm, STATE_ROWS, state_sems)
    start_all(keys, values)
    for index in range(len(keys)):
        keys[index].wait()
        values[index].wait()
        rows = slice(index * COPY_ROWS, (index + 1) * COPY_ROWS)
        for head in pieces_of(key_ref, HEAD_DIM):
            part = mm_tn(key_ref[rows, head], value_ref[rows, head])
            if index:
                part = part + total_ref[head, :]
            if index < len(keys) - 1:
                total_ref[head, :] = part
            else:
                state_ref[head, :] = part.astype(jnp.bfloat16)
                if head.stop % STATE_ROWS == 0:
                    stores[head.stop // STATE_ROWS - 1].start()
    wait_all(stores)


def weight_rows(rows):
    blocks = rows // BLOCK
    return blocks * (blocks + 1) // 2 * BLOCK


def local_part(key_ref, value_ref, own, flipped_ref, head, local_ref, weight_ref, row):
    for start in range(0, key_ref.shape[0], BLOCK):
        end = start + BLOCK
        parts = []
        for first in range(0, end, BLOCK):
            scores = mm(key_ref[first : first + BLOCK, own], flipped_ref[head, start:end])
            part = masked(scores, 0, False) if first == start else scores.astype(jnp.bfloat16)
            weight_ref[row : row + BLOCK, :] = part
            parts.append(part)
            row += BLOCK
        weights = jnp.concatenate(parts, axis=0) if len(parts) > 1 else parts[0]
        local = mm_tn(value_ref[:end, own], weights)
        local_ref[head, start:end] = local.astype(jnp.bfloat16)


def local_heads(first, key_ref, value_ref, loads, flipped_ref, local_ref, weight_ref, weight_hbm, sems):
    size = weight_rows(key_ref.shape[0])
    stores = []
    for index, step in enumerate(pieces_of(key_ref, COPY_COLS)):
        for load in loads:
            load[index].wait()
        for left in range(step.start, step.stop, HEAD_DIM):
            own = slice(left, left + HEAD_DIM)
            head = slice(first + left, first + left + HEAD_DIM)
            number = left // HEAD_DIM
            part = slice(number * size, (number + 1) * size)
            local_part(key_ref, value_ref, own, flipped_ref, head, local_ref, weight_ref, part.start)
            store = pltpu.make_async_copy(weight_ref.at[part, :], weight_hbm.at[part, :], sems.at[number])
            store.start()
            stores.append(store)
    return stores


def flip_body(
    query_hbm, key_hbm, value_hbm, grad_hbm, flipped_ref, grad_flipped_ref, local_ref, weight_hbm,
    query_ref, key_ref, value_ref, grad_ref, weight_ref,
    query_sems, key_sems, value_sems, grad_sems, weight_sems,
):
    part = slice(0, key_ref.shape[1])
    query_loads = column_copies(query_hbm, query_ref, query_sems)
    key_loads = column_copies(key_hbm.at[:, part], key_ref, key_sems)
    value_loads = column_copies(value_hbm.at[:, part], value_ref, value_sems)
    grad_loads = column_copies(grad_hbm, grad_ref, grad_sems)
    start_all(query_loads)
    start_all(key_loads, value_loads)
    start_all(grad_loads)
    for load, cols in zip(query_loads, pieces_of(query_ref, COPY_COLS)):
        load.wait()
        flipped_ref[cols, :] = query_ref[:, cols].T
    stores = local_heads(
        0, key_ref, value_ref, (key_loads, value_loads), flipped_ref, local_ref, weight_ref, weight_hbm, weight_sems
    )
    for load, cols in zip(grad_loads, pieces_of(grad_ref, COPY_COLS)):
        load.wait()
        grad_flipped_ref[cols, :] = grad_ref[:, cols].T
    wait_all(stores)


def local_body(
    key_hbm, value_hbm, flipped_ref, given_ref, local_ref, weight_hbm,
    key_ref, value_ref, weight_ref, key_sems, value_sems, weight_sems,
):
    first = local_ref.shape[0] - key_ref.shape[1]
    key_loads = column_copies(key_hbm.at[:, first:], key_ref, key_sems)
    value_loads = column_copies(value_hbm.at[:, first:], value_ref, value_sems)
    start_all(key_loads, value_loads)
    stores = local_heads(
        first, key_ref, value_ref, (key_loads, value_loads), flipped_ref, local_ref, weight_ref, weight_hbm, weight_sems
    )
    wait_all(stores)


def scan_body(reverse, block_ref, state_hbm, state_ref, sems):
    count = block_ref.shape[0]
    total = jnp.zeros(block_ref.shape[1:], jnp.float32)
    places = places_in_order(count, 0 if reverse else 1)
    stores = []
    for place in range(count - 1, -1, -1) if reverse else range(count):
        rank = places.index(place)
        state_ref[rank] = total.astype(jnp.bfloat16)
        total = total + block_ref[rank].astype(jnp.float32)
        stores.append(pltpu.make_async_copy(state_ref.at[rank], state_hbm.at[rank], sems.at[rank]))
        stores[-1].start()
    wait_all(stores)


def heads_of(ref):
    return [slice(at, at + HEAD_DIM) for at in range(0, ref.shape[0], HEAD_DIM)]


def scaled_grad(gain_ref, grad_ref, head):
    gain = jnp.broadcast_to(gain_ref[:, head], (HEAD_DIM, HEAD_DIM)).T
    gain = jnp.concatenate([gain] * (grad_ref.shape[1] // HEAD_DIM), axis=1)
    return gain * grad_ref[head, :].astype(jnp.float32)


def fold(values):
    parts = [values[at : at + 8, :] for at in range(0, values.shape[0], 8)]
    while len(parts) > 1:
        parts = [sum(parts[at + 1 : at + 2], parts[at]) for at in range(0, len(parts), 2)]
    return parts[0]


def sums_body(gain_ref, flipped_ref, grad_ref, local_ref, state_ref, attended_ref, sums_ref):
    square = cross = jnp.zeros((8, local_ref.shape[1]), jnp.float32)
    for head in heads_of(local_ref):
        attended = mm_tn(state_ref[head, :], flipped_ref[head, :])
        attended = attended + attended_ref[head, :].astype(jnp.float32)
        attended_ref[head, :] = attended.astype(jnp.bfloat16)
        square += fold(attended * attended)
        cross += fold(scaled_grad(gain_ref, grad_ref, head) * attended)
    square = jnp.sum(square, axis=0, keepdims=True)
    cross = jnp.sum(cross, axis=0, keepdims=True)
    sums_ref[0:1, :] = square
    sums_ref[1:2, :] = cross


def dout_body(width, groups, gain_ref, flipped_ref, grad_ref, attended_ref, *refs):
    dout_ref, own_hbm, own_ref, sems = refs[groups:]
    stores = row_copies(own_ref, own_hbm, STATE_ROWS, sems)
    sums = sum(ref[...] for ref in refs[:groups])
    inverse = 1.0 / jnp.sqrt(sums[0:1, :] / width + EPSILON)
    drop = sums[1:2, :] * (inverse * inverse * inverse) / width
    for head in heads_of(dout_ref):
        attended = dout_ref[head, :].astype(jnp.float32)
        dout = scaled_grad(gain_ref, grad_ref, head) * inverse - attended * drop
        dout = dout.astype(jnp.bfloat16)
        dout_ref[head, :] = dout
        own_ref[head, :] = mm_nt(flipped_ref[head, :], dout).astype(jnp.bfloat16)
        if head.stop % STATE_ROWS == 0:
            stores[head.stop // STATE_ROWS - 1].start()
    wait_all(stores)


def value_local(weight_ref, row, dout, target):
    blocks = dout.shape[0] // BLOCK
    for own in range(blocks):
        parts = []
        for other in range(own, blocks):
            start = row + (other * (other + 1) // 2 + own) * BLOCK
            parts.append(weight_ref[start : start + BLOCK, :])
        weights = jnp.concatenate(parts, axis=1) if len(parts) > 1 else parts[0]
        at = own * BLOCK
        target[at : at + BLOCK, :] = mm(weights, dout[at:, :]).astype(jnp.bfloat16)


def query_body(
    key_hbm, value_hbm, first_hbm, second_hbm, flipped_ref, state_ref, out_hbm, dout_ref, value_out,
    key_ref, value_ref, out_ref, weight_ref, key_sems, value_sems, out_sems, weight_sems,
):
    rows = dout_ref.shape[0]
    size = weight_rows(rows)
    key_copies = column_copies(key_hbm, key_ref, key_sems)
    value_copies = column_copies(value_hbm, value_ref, value_sems)
    there = first_hbm.shape[0]
    rest = weight_ref.shape[0] - there
    weight_copies = [
        pltpu.make_async_copy(first_hbm, weight_ref.at[:there, :], weight_sems.at[0]),
        pltpu.make_async_copy(second_hbm.at[:rest, :], weight_ref.at[there:, :], weight_sems.at[1]),
    ]
    start_all(key_copies, value_copies)
    start_all(weight_copies)
    for head in heads_of(flipped_ref):
        dout_ref[:, head] = flipped_ref[head, :].T
    stores = column_copies(out_ref, out_hbm, out_sems)
    for index, step in enumerate(pieces_of(out_ref, COPY_COLS)):
        key_copies[index].wait()
        value_copies[index].wait()
        for left in range(step.start, step.stop, HEAD_DIM):
            cols = slice(left, left + HEAD_DIM)
            for start in range(0, rows, BLOCK):
                end = start + BLOCK
                dout = dout_ref[start:end, cols]
                dscore = masked(mm_nt(dout, value_ref[:end, cols]), start, True)
                grad = mm(dscore, key_ref[:end, cols]) + mm_nt(dout, state_ref[cols, :])
                out_ref[start:end, cols] = grad.astype(jnp.bfloat16)
        stores[index].start()
    wait_all(weight_copies)
    for number, cols in enumerate(pieces_of(value_out, HEAD_DIM)):
        value_local(weight_ref, number * size, dout_ref[:, cols], value_out.at[:, cols])
    wait_all(stores)


def inner_body(
    query_hbm, value_hbm, weight_hbm, dout_ref, key_out, value_out, value_ref,
    query_ref, weight_ref, query_sems, value_sems, weight_sem,
):
    rows, width = key_out.shape
    size = weight_rows(rows)
    early = width - value_out.shape[1]
    query_copies = column_copies(query_hbm, query_ref, query_sems)
    value_copies = column_copies(value_hbm, value_ref, value_sems)
    skipped = weight_hbm.shape[0] - weight_ref.shape[0]
    weight_copy = pltpu.make_async_copy(weight_hbm.at[skipped:, :], weight_ref, weight_sem.at[0])
    start_all(query_copies, value_copies)
    weight_copy.start()
    for index, step in enumerate(pieces_of(key_out, COPY_COLS)):
        query_copies[index].wait()
        value_copies[index].wait()
        for left in range(step.start, step.stop, HEAD_DIM):
            if left == early:
                weight_copy.wait()
            cols = slice(left, left + HEAD_DIM)
            dout = key_out[:, cols]
            for start in range(0, rows, BLOCK):
                end = start + BLOCK
                scores = mm_nt(value_ref[start:end, cols], dout[start:, :])
                grad = mm(masked(scores, 0, False), query_ref[start:, cols])
                key_out[start:end, cols] = grad.astype(jnp.bfloat16)
            if left >= early:
                late = slice(left - early, left - early + HEAD_DIM)
                value_local(weight_ref, late.start // HEAD_DIM * size, dout, value_out.at[:, late])


def final_body(
    key_hbm, value_ref, key_part, early_part, late_part, state_ref, key_out_hbm, value_out_hbm,
    key_ref, key_out, value_out, in_sems, key_sems, value_sems,
):
    key_copy = pltpu.make_async_copy(key_hbm, key_ref, in_sems.at[0])
    key_copy.start()
    key_stores = column_copies(key_out, key_out_hbm, key_sems)
    value_stores = column_copies(value_out, value_out_hbm, value_sems)
    for index, step in enumerate(pieces_of(key_out, COPY_COLS)):
        for left in range(step.start, step.stop, HEAD_DIM):
            cols = slice(left, left + HEAD_DIM)
            grad = key_part[:, cols].astype(jnp.float32) + mm_nt(value_ref[:, cols], state_ref[cols, :])
            key_out[:, cols] = grad.astype(jnp.bfloat16)
        key_stores[index].start()
    key_copy.wait()
    for index, step in enumerate(pieces_of(value_out, COPY_COLS)):
        for left in range(step.start, step.stop, HEAD_DIM):
            cols = slice(left, left + HEAD_DIM)
            early = early_part.shape[1]
            if left < early:
                part = early_part[:, cols]
            else:
                part = late_part[:, left - early : left - early + HEAD_DIM]
            grad = part.astype(jnp.float32) + mm(key_ref[:, cols], state_ref[cols, :])
            value_out[:, cols] = grad.astype(jnp.bfloat16)
        value_stores[index].start()
    wait_all(key_stores, value_stores)


def local_call(body, in_args, outs, flops, hbm_args=(), scratch=(), aliases=None):
    args = [pltpu.with_memory_space_constraint(a, pltpu.HBM) for a in hbm_args]
    args += [pltpu.with_memory_space_constraint(a, pltpu.VMEM) for a in in_args]
    specs = [pl.BlockSpec(memory_space=pltpu.HBM)] * len(hbm_args)
    specs += [pl.BlockSpec(memory_space=pltpu.VMEM)] * len(in_args)
    out_specs = []
    for out in outs:
        out_specs.append(pl.BlockSpec(memory_space=out.memory_space))
    moved = sum(a.size * a.dtype.itemsize for a in args)
    return pl.pallas_call(
        body,
        in_specs=specs,
        out_specs=out_specs,
        out_shape=outs,
        scratch_shapes=scratch,
        input_output_aliases=aliases or {},
        compiler_params=pltpu.CompilerParams(vmem_limit_bytes=16 * MIB),
        cost_estimate=pl.CostEstimate(flops=flops, bytes_accessed=moved, transcendentals=0),
    )(*args)


def scan_blocks(blocks, reverse):
    (states,) = local_call(
        functools.partial(scan_body, reverse),
        [blocks],
        [pltpu.HBM(blocks.shape, blocks.dtype)],
        blocks.size,
        scratch=[
            pltpu.VMEM(blocks.shape, blocks.dtype),
            pltpu.SemaphoreType.DMA((blocks.shape[0],)),
        ],
    )
    return states


def places_in_order(count, flip):
    quarter = count // 4
    first, second, third, fourth = (list(range(at, at + quarter)) for at in range(0, count, quarter))
    half = quarter // 2
    order = second + first[:half] + third[:half] + first[half:] + third[half:] + fourth
    return [(count - 1 - place) ^ flip for place in order]


def from_all(part, axis):
    count = lax.axis_size(axis)
    parts = [part]
    for shift in range(1, count):
        pairs = [(place, (place + shift) % count) for place in range(count)]
        parts.append(lax.ppermute(part, axis, pairs))
    return parts


def exchange(pieces, axis, flip):
    groups = [places_in_order(lax.axis_size(axis), flip)]
    return lax.all_to_all(pieces, axis, 0, 0, axis_index_groups=groups)


def in_pieces(state, axis):
    count = lax.axis_size(axis)
    rows, cols = state.shape
    return state.reshape(count, rows // count, cols)


def shards(queries, keys, values, out_grad, gain):
    rows, width = queries.shape
    total_width = width * lax.axis_size("head")
    bf16, f32 = jnp.bfloat16, jnp.float32
    tokens, state = (rows, width), (width, HEAD_DIM)
    small = 2 * rows * width * HEAD_DIM
    large = 2 * rows * rows * width * 3 // 4
    gain_row = gain.reshape(1, width)
    flat = (width, rows)
    dma = pltpu.SemaphoreType.DMA
    chunks, row_chunks = dma((width // COPY_COLS,)), dma((rows // COPY_ROWS,))
    state_chunks = dma((width // STATE_ROWS,))
    vm, hbm = pltpu.VMEM, pltpu.HBM
    rows_vm, flat_vm, state_vm = vm(tokens, bf16), vm(flat, bf16), vm(state, bf16)

    (own_kv,) = local_call(
        states_body,
        [],
        [hbm(state, bf16)],
        small,
        [keys, values],
        [rows_vm] * 2 + [vm(state, f32), state_vm] + [row_chunks] * 2 + [state_chunks],
    )
    kv_blocks = exchange(in_pieces(own_kv, "seq"), "seq", 1)
    half = width // 2 // COPY_COLS * COPY_COLS
    early = width * 3 // 4 // HEAD_DIM * HEAD_DIM
    def weights_of(cols):
        return (cols // HEAD_DIM * weight_rows(rows), BLOCK)

    half_vm, half_chunks = vm((rows, half), bf16), dma((half // COPY_COLS,))
    flipped, grad_flipped, local, first_weights = local_call(
        flip_body,
        [],
        [flat_vm] * 3 + [hbm(weights_of(half), bf16)],
        2 * large,
        [queries, keys, values, out_grad],
        [rows_vm, half_vm, half_vm, rows_vm, vm(weights_of(half), bf16)]
        + [chunks, half_chunks, half_chunks, chunks, dma((half // HEAD_DIM,))],
    )
    kv_blocks, flipped, grad_flipped, local, first_weights = lax.optimization_barrier(
        (kv_blocks, flipped, grad_flipped, local, first_weights)
    )
    kv_low = exchange(scan_blocks(kv_blocks, False), "seq", 1).reshape(state)
    other = width - half
    other_vm, other_chunks = vm((rows, other), bf16), dma((other // COPY_COLS,))
    local, second_weights = local_call(
        local_body,
        [flipped, local],
        [flat_vm, hbm(weights_of(other), bf16)],
        large,
        [keys, values],
        [other_vm, other_vm, vm(weights_of(other), bf16)]
        + [other_chunks, other_chunks, dma((other // HEAD_DIM,))],
        {3: 0},
    )
    groups = lax.axis_size("head")
    attended, sums = local_call(
        sums_body,
        [gain_row, flipped, grad_flipped, local, kv_low],
        [flat_vm, vm((2, rows), f32)],
        small,
        aliases={3: 0},
    )
    sums = from_all(sums, "head")
    dout_flipped, own_grad = local_call(
        functools.partial(dout_body, total_width, groups),
        [gain_row, flipped, grad_flipped, attended] + sums,
        [flat_vm, hbm(state, bf16)],
        small,
        scratch=[state_vm, state_chunks],
        aliases={3: 0},
    )
    grad_blocks = exchange(in_pieces(own_grad, "seq"), "seq", 0)
    early_vm, late_vm = vm((rows, early), bf16), vm((rows, width - early), bf16)
    query_grad, dout, early_part = local_call(
        query_body,
        [dout_flipped, kv_low],
        [hbm(tokens, bf16), rows_vm, early_vm],
        2 * large + small,
        [keys, values, first_weights, second_weights],
        [rows_vm] * 3 + [vm(weights_of(early), bf16)] + [chunks] * 3 + [dma((2,))],
    )
    grad_blocks, query_grad, dout, early_part = lax.optimization_barrier(
        (grad_blocks, query_grad, dout, early_part)
    )
    grad_low = exchange(scan_blocks(grad_blocks, True), "seq", 0).reshape(state)
    key_part, late_part, value_kept = local_call(
        inner_body,
        [dout],
        [rows_vm, late_vm, rows_vm],
        3 * large,
        [queries, values, second_weights],
        [rows_vm, vm(weights_of(width - early), bf16)] + [chunks] * 2 + [dma((1,))],
        {3: 0},
    )
    key_grad, value_grad = local_call(
        final_body,
        [value_kept, key_part, early_part, late_part, grad_low],
        [hbm(tokens, bf16)] * 2,
        2 * small,
        [keys],
        [rows_vm] * 3 + [dma((1,))] + [chunks] * 2,
    )
    return query_grad, key_grad, value_grad


def solution(mesh):
    return jax.shard_map(
        shards,
        mesh=mesh,
        in_specs=(
            P("seq", "head"),
            P("seq", "head"),
            P("seq", "head"),
            P("seq", "head"),
            P("head"),
        ),
        out_specs=(P("seq", "head"), P("seq", "head"), P("seq", "head")),
        check_vma=False,
    )
```

```python
import functools

import jax
import jax.numpy as jnp
from jax import lax
from jax.experimental import pallas as pl
from jax.experimental.pallas import tpu as pltpu
from jax.sharding import PartitionSpec as P

HEAD_DIM = 128
BLOCK = 256
COPY_COLS = 512
COPY_ROWS = 128
STATE_ROWS = 256
EPSILON = 1e-06
MIB = 1 << 20


def mm(a, b):
    return lax.dot_general(a, b, (((1,), (0,)), ((), ())), preferred_element_type=jnp.float32)


def mm_nt(a, b):
    return lax.dot_general(a, b, (((1,), (1,)), ((), ())), preferred_element_type=jnp.float32)


def mm_tn(a, b):
    return lax.dot_general(a, b, (((0,), (0,)), ((), ())), preferred_element_type=jnp.float32)


def pieces_of(ref, size):
    return [slice(at, at + size) for at in range(0, ref.shape[1], size)]


def masked(scores, diagonal, rows_first):
    shape = (BLOCK, BLOCK)
    rows = lax.broadcasted_iota(jnp.int32, shape, 0)
    cols = lax.broadcasted_iota(jnp.int32, shape, 1)
    keep = rows >= cols if rows_first else cols >= rows
    inside = slice(diagonal, diagonal + BLOCK)
    kept = jnp.where(keep, scores[:, inside], 0.0).astype(jnp.bfloat16)
    before = scores[:, :diagonal].astype(jnp.bfloat16)
    after = scores[:, inside.stop :].astype(jnp.bfloat16)
    parts = [part for part in (before, kept, after) if part.shape[1]]
    return jnp.concatenate(parts, axis=1) if len(parts) > 1 else kept


def column_copies(source, target, sems):
    copies = []
    for index, cols in enumerate(pieces_of(source, COPY_COLS)):
        copies.append(pltpu.make_async_copy(source.at[:, cols], target.at[:, cols], sems.at[index]))
    return copies


def row_copies(source, target, size, sems):
    copies = []
    for index in range(source.shape[0] // size):
        part = slice(index * size, (index + 1) * size)
        copies.append(pltpu.make_async_copy(source.at[part, :], target.at[part, :], sems.at[index]))
    return copies


def start_all(*groups):
    for parts in zip(*groups):
        for part in parts:
            part.start()


def wait_all(*groups):
    for group in groups:
        for part in group:
            part.wait()


def states_body(
    key_hbm, value_hbm, state_hbm, key_ref, value_ref, total_ref, state_ref,
    key_sems, value_sems, state_sems,
):
    keys = row_copies(key_hbm, key_ref, COPY_ROWS, key_sems)
    values = row_copies(value_hbm, value_ref, COPY_ROWS, value_sems)
    stores = row_copies(state_ref, state_hbm, STATE_ROWS, state_sems)
    start_all(keys, values)
    for index in range(len(keys)):
        keys[index].wait()
        values[index].wait()
        rows = slice(index * COPY_ROWS, (index + 1) * COPY_ROWS)
        for head in pieces_of(key_ref, HEAD_DIM):
            part = mm_tn(key_ref[rows, head], value_ref[rows, head])
            if index:
                part = part + total_ref[head, :]
            if index < len(keys) - 1:
                total_ref[head, :] = part
            else:
                state_ref[head, :] = part.astype(jnp.bfloat16)
                if head.stop % STATE_ROWS == 0:
                    stores[head.stop // STATE_ROWS - 1].start()
    wait_all(stores)


def weight_rows(rows):
    blocks = rows // BLOCK
    return blocks * (blocks + 1) // 2 * BLOCK


def local_part(key_ref, value_ref, own, flipped_ref, head, local_ref, weight_ref, row):
    for start in range(0, key_ref.shape[0], BLOCK):
        end = start + BLOCK
        parts = []
        for first in range(0, end, BLOCK):
            scores = mm(key_ref[first : first + BLOCK, own], flipped_ref[head, start:end])
            part = masked(scores, 0, False) if first == start else scores.astype(jnp.bfloat16)
            weight_ref[row : row + BLOCK, :] = part
            parts.append(part)
            row += BLOCK
        weights = jnp.concatenate(parts, axis=0) if len(parts) > 1 else parts[0]
        local = mm_tn(value_ref[:end, own], weights)
        local_ref[head, start:end] = local.astype(jnp.bfloat16)


def local_heads(first, key_ref, value_ref, loads, flipped_ref, local_ref, weight_ref, weight_hbm, sems):
    size = weight_rows(key_ref.shape[0])
    stores = []
    for index, step in enumerate(pieces_of(key_ref, COPY_COLS)):
        for load in loads:
            load[index].wait()
        for left in range(step.start, step.stop, HEAD_DIM):
            own = slice(left, left + HEAD_DIM)
            head = slice(first + left, first + left + HEAD_DIM)
            number = left // HEAD_DIM
            part = slice(number * size, (number + 1) * size)
            local_part(key_ref, value_ref, own, flipped_ref, head, local_ref, weight_ref, part.start)
            store = pltpu.make_async_copy(weight_ref.at[part, :], weight_hbm.at[part, :], sems.at[number])
            store.start()
            stores.append(store)
    return stores


def flip_body(
    query_hbm, key_hbm, value_hbm, grad_hbm, flipped_ref, grad_flipped_ref, local_ref, weight_hbm,
    query_ref, key_ref, value_ref, grad_ref, weight_ref,
    query_sems, key_sems, value_sems, grad_sems, weight_sems,
):
    part = slice(0, key_ref.shape[1])
    query_loads = column_copies(query_hbm, query_ref, query_sems)
    key_loads = column_copies(key_hbm.at[:, part], key_ref, key_sems)
    value_loads = column_copies(value_hbm.at[:, part], value_ref, value_sems)
    grad_loads = column_copies(grad_hbm, grad_ref, grad_sems)
    start_all(query_loads)
    start_all(key_loads, value_loads)
    start_all(grad_loads)
    for load, cols in zip(query_loads, pieces_of(query_ref, COPY_COLS)):
        load.wait()
        flipped_ref[cols, :] = query_ref[:, cols].T
    stores = local_heads(
        0, key_ref, value_ref, (key_loads, value_loads), flipped_ref, local_ref, weight_ref, weight_hbm, weight_sems
    )
    for load, cols in zip(grad_loads, pieces_of(grad_ref, COPY_COLS)):
        load.wait()
        grad_flipped_ref[cols, :] = grad_ref[:, cols].T
    wait_all(stores)


def local_body(
    key_hbm, value_hbm, flipped_ref, given_ref, local_ref, weight_hbm,
    key_ref, value_ref, weight_ref, key_sems, value_sems, weight_sems,
):
    first = local_ref.shape[0] - key_ref.shape[1]
    key_loads = column_copies(key_hbm.at[:, first:], key_ref, key_sems)
    value_loads = column_copies(value_hbm.at[:, first:], value_ref, value_sems)
    start_all(key_loads, value_loads)
    stores = local_heads(
        first, key_ref, value_ref, (key_loads, value_loads), flipped_ref, local_ref, weight_ref, weight_hbm, weight_sems
    )
    wait_all(stores)


def scan_body(reverse, block_ref, state_hbm, state_ref, sems):
    count = block_ref.shape[0]
    total = jnp.zeros(block_ref.shape[1:], jnp.float32)
    places = places_in_order(count, 0 if reverse else 1)
    stores = []
    for place in range(count - 1, -1, -1) if reverse else range(count):
        rank = places.index(place)
        state_ref[rank] = total.astype(jnp.bfloat16)
        total = total + block_ref[rank].astype(jnp.float32)
        stores.append(pltpu.make_async_copy(state_ref.at[rank], state_hbm.at[rank], sems.at[rank]))
        stores[-1].start()
    wait_all(stores)


def heads_of(ref):
    return [slice(at, at + HEAD_DIM) for at in range(0, ref.shape[0], HEAD_DIM)]


def scaled_grad(gain_ref, grad_ref, head):
    gain = jnp.broadcast_to(gain_ref[:, head], (HEAD_DIM, HEAD_DIM)).T
    gain = jnp.concatenate([gain] * (grad_ref.shape[1] // HEAD_DIM), axis=1)
    return gain * grad_ref[head, :].astype(jnp.float32)


def fold(values):
    parts = [values[at : at + 8, :] for at in range(0, values.shape[0], 8)]
    while len(parts) > 1:
        parts = [sum(parts[at + 1 : at + 2], parts[at]) for at in range(0, len(parts), 2)]
    return parts[0]


def sums_body(gain_ref, flipped_ref, grad_ref, local_ref, state_ref, attended_ref, sums_ref):
    square = cross = jnp.zeros((8, local_ref.shape[1]), jnp.float32)
    for head in heads_of(local_ref):
        attended = mm_tn(state_ref[head, :], flipped_ref[head, :])
        attended = attended + attended_ref[head, :].astype(jnp.float32)
        attended_ref[head, :] = attended.astype(jnp.bfloat16)
        square += fold(attended * attended)
        cross += fold(scaled_grad(gain_ref, grad_ref, head) * attended)
    square = jnp.sum(square, axis=0, keepdims=True)
    cross = jnp.sum(cross, axis=0, keepdims=True)
    sums_ref[0:1, :] = square
    sums_ref[1:2, :] = cross


def dout_body(width, groups, gain_ref, flipped_ref, grad_ref, attended_ref, *refs):
    dout_ref, own_hbm, own_ref, sems = refs[groups:]
    stores = row_copies(own_ref, own_hbm, STATE_ROWS, sems)
    sums = sum(ref[...] for ref in refs[:groups])
    inverse = 1.0 / jnp.sqrt(sums[0:1, :] / width + EPSILON)
    drop = sums[1:2, :] * (inverse * inverse * inverse) / width
    for head in heads_of(dout_ref):
        attended = dout_ref[head, :].astype(jnp.float32)
        dout = scaled_grad(gain_ref, grad_ref, head) * inverse - attended * drop
        dout = dout.astype(jnp.bfloat16)
        dout_ref[head, :] = dout
        own_ref[head, :] = mm_nt(flipped_ref[head, :], dout).astype(jnp.bfloat16)
        if head.stop % STATE_ROWS == 0:
            stores[head.stop // STATE_ROWS - 1].start()
    wait_all(stores)


def value_local(weight_ref, row, dout, target):
    blocks = dout.shape[0] // BLOCK
    for own in range(blocks):
        parts = []
        for other in range(own, blocks):
            start = row + (other * (other + 1) // 2 + own) * BLOCK
            parts.append(weight_ref[start : start + BLOCK, :])
        weights = jnp.concatenate(parts, axis=1) if len(parts) > 1 else parts[0]
        at = own * BLOCK
        target[at : at + BLOCK, :] = mm(weights, dout[at:, :]).astype(jnp.bfloat16)


def query_body(
    key_hbm, value_hbm, first_hbm, second_hbm, flipped_ref, state_ref, out_hbm, dout_ref, value_out,
    key_ref, value_ref, out_ref, weight_ref, key_sems, value_sems, out_sems, weight_sems,
):
    rows = dout_ref.shape[0]
    size = weight_rows(rows)
    key_copies = column_copies(key_hbm, key_ref, key_sems)
    value_copies = column_copies(value_hbm, value_ref, value_sems)
    there = first_hbm.shape[0]
    rest = weight_ref.shape[0] - there
    weight_copies = [
        pltpu.make_async_copy(first_hbm, weight_ref.at[:there, :], weight_sems.at[0]),
        pltpu.make_async_copy(second_hbm.at[:rest, :], weight_ref.at[there:, :], weight_sems.at[1]),
    ]
    start_all(key_copies, value_copies)
    start_all(weight_copies)
    for head in heads_of(flipped_ref):
        dout_ref[:, head] = flipped_ref[head, :].T
    stores = column_copies(out_ref, out_hbm, out_sems)
    for index, step in enumerate(pieces_of(out_ref, COPY_COLS)):
        key_copies[index].wait()
        value_copies[index].wait()
        for left in range(step.start, step.stop, HEAD_DIM):
            cols = slice(left, left + HEAD_DIM)
            for start in range(0, rows, BLOCK):
                end = start + BLOCK
                dout = dout_ref[start:end, cols]
                dscore = masked(mm_nt(dout, value_ref[:end, cols]), start, True)
                grad = mm(dscore, key_ref[:end, cols]) + mm_nt(dout, state_ref[cols, :])
                out_ref[start:end, cols] = grad.astype(jnp.bfloat16)
        stores[index].start()
    wait_all(weight_copies)
    for number, cols in enumerate(pieces_of(value_out, HEAD_DIM)):
        value_local(weight_ref, number * size, dout_ref[:, cols], value_out.at[:, cols])
    wait_all(stores)


def inner_body(
    query_hbm, value_hbm, weight_hbm, dout_ref, key_out, value_out, value_ref,
    query_ref, weight_ref, query_sems, value_sems, weight_sem,
):
    rows, width = key_out.shape
    size = weight_rows(rows)
    early = width - value_out.shape[1]
    query_copies = column_copies(query_hbm, query_ref, query_sems)
    value_copies = column_copies(value_hbm, value_ref, value_sems)
    skipped = weight_hbm.shape[0] - weight_ref.shape[0]
    weight_copy = pltpu.make_async_copy(weight_hbm.at[skipped:, :], weight_ref, weight_sem.at[0])
    start_all(query_copies, value_copies)
    weight_copy.start()
    for index, step in enumerate(pieces_of(key_out, COPY_COLS)):
        query_copies[index].wait()
        value_copies[index].wait()
        for left in range(step.start, step.stop, HEAD_DIM):
            if left == early:
                weight_copy.wait()
            cols = slice(left, left + HEAD_DIM)
            dout = key_out[:, cols]
            for start in range(0, rows, BLOCK):
                end = start + BLOCK
                scores = mm_nt(value_ref[start:end, cols], dout[start:, :])
                grad = mm(masked(scores, 0, False), query_ref[start:, cols])
                key_out[start:end, cols] = grad.astype(jnp.bfloat16)
            if left >= early:
                late = slice(left - early, left - early + HEAD_DIM)
                value_local(weight_ref, late.start // HEAD_DIM * size, dout, value_out.at[:, late])


def final_body(
    key_hbm, value_ref, key_part, early_part, late_part, state_ref, key_out_hbm, value_out_hbm,
    key_ref, key_out, value_out, in_sems, key_sems, value_sems,
):
    key_copy = pltpu.make_async_copy(key_hbm, key_ref, in_sems.at[0])
    key_copy.start()
    key_stores = column_copies(key_out, key_out_hbm, key_sems)
    value_stores = column_copies(value_out, value_out_hbm, value_sems)
    for index, step in enumerate(pieces_of(key_out, COPY_COLS)):
        for left in range(step.start, step.stop, HEAD_DIM):
            cols = slice(left, left + HEAD_DIM)
            grad = key_part[:, cols].astype(jnp.float32) + mm_nt(value_ref[:, cols], state_ref[cols, :])
            key_out[:, cols] = grad.astype(jnp.bfloat16)
        key_stores[index].start()
    key_copy.wait()
    for index, step in enumerate(pieces_of(value_out, COPY_COLS)):
        for left in range(step.start, step.stop, HEAD_DIM):
            cols = slice(left, left + HEAD_DIM)
            early = early_part.shape[1]
            if left < early:
                part = early_part[:, cols]
            else:
                part = late_part[:, left - early : left - early + HEAD_DIM]
            grad = part.astype(jnp.float32) + mm(key_ref[:, cols], state_ref[cols, :])
            value_out[:, cols] = grad.astype(jnp.bfloat16)
        value_stores[index].start()
    wait_all(key_stores, value_stores)


def local_call(body, in_args, outs, flops, hbm_args=(), scratch=(), aliases=None):
    args = [pltpu.with_memory_space_constraint(a, pltpu.HBM) for a in hbm_args]
    args += [pltpu.with_memory_space_constraint(a, pltpu.VMEM) for a in in_args]
    specs = [pl.BlockSpec(memory_space=pltpu.HBM)] * len(hbm_args)
    specs += [pl.BlockSpec(memory_space=pltpu.VMEM)] * len(in_args)
    out_specs = []
    for out in outs:
        out_specs.append(pl.BlockSpec(memory_space=out.memory_space))
    moved = sum(a.size * a.dtype.itemsize for a in args)
    return pl.pallas_call(
        body,
        in_specs=specs,
        out_specs=out_specs,
        out_shape=outs,
        scratch_shapes=scratch,
        input_output_aliases=aliases or {},
        compiler_params=pltpu.CompilerParams(vmem_limit_bytes=16 * MIB),
        cost_estimate=pl.CostEstimate(flops=flops, bytes_accessed=moved, transcendentals=0),
    )(*args)


def scan_blocks(blocks, reverse):
    (states,) = local_call(
        functools.partial(scan_body, reverse),
        [blocks],
        [pltpu.HBM(blocks.shape, blocks.dtype)],
        blocks.size,
        scratch=[
            pltpu.VMEM(blocks.shape, blocks.dtype),
            pltpu.SemaphoreType.DMA((blocks.shape[0],)),
        ],
    )
    return states


def places_in_order(count, flip):
    quarter = count // 4
    first, second, third, fourth = (list(range(at, at + quarter)) for at in range(0, count, quarter))
    half = quarter // 2
    order = second + first[:half] + third[:half] + first[half:] + third[half:] + fourth
    return [(count - 1 - place) ^ flip for place in order]


def from_all(part, axis):
    count = lax.axis_size(axis)
    parts = [part]
    paired = count & (count - 1) == 0
    for shift in range(1, count):
        pairs = [(place, place ^ shift if paired else (place + shift) % count) for place in range(count)]
        parts.append(lax.ppermute(part, axis, pairs))
    return parts


def exchange(pieces, axis, flip):
    groups = [places_in_order(lax.axis_size(axis), flip)]
    return lax.all_to_all(pieces, axis, 0, 0, axis_index_groups=groups)


def in_pieces(state, axis):
    count = lax.axis_size(axis)
    rows, cols = state.shape
    return state.reshape(count, rows // count, cols)


def shards(queries, keys, values, out_grad, gain):
    rows, width = queries.shape
    total_width = width * lax.axis_size("head")
    bf16, f32 = jnp.bfloat16, jnp.float32
    tokens, state = (rows, width), (width, HEAD_DIM)
    small = 2 * rows * width * HEAD_DIM
    large = 2 * rows * rows * width * 3 // 4
    gain_row = gain.reshape(1, width)
    flat = (width, rows)
    dma = pltpu.SemaphoreType.DMA
    chunks, row_chunks = dma((width // COPY_COLS,)), dma((rows // COPY_ROWS,))
    state_chunks = dma((width // STATE_ROWS,))
    vm, hbm = pltpu.VMEM, pltpu.HBM
    rows_vm, flat_vm, state_vm = vm(tokens, bf16), vm(flat, bf16), vm(state, bf16)

    (own_kv,) = local_call(
        states_body,
        [],
        [hbm(state, bf16)],
        small,
        [keys, values],
        [rows_vm] * 2 + [vm(state, f32), state_vm] + [row_chunks] * 2 + [state_chunks],
    )
    kv_blocks = exchange(in_pieces(own_kv, "seq"), "seq", 1)
    half = width // 2 // COPY_COLS * COPY_COLS
    early = width * 3 // 4 // HEAD_DIM * HEAD_DIM
    def weights_of(cols):
        return (cols // HEAD_DIM * weight_rows(rows), BLOCK)

    half_vm, half_chunks = vm((rows, half), bf16), dma((half // COPY_COLS,))
    flipped, grad_flipped, local, first_weights = local_call(
        flip_body,
        [],
        [flat_vm] * 3 + [hbm(weights_of(half), bf16)],
        2 * large,
        [queries, keys, values, out_grad],
        [rows_vm, half_vm, half_vm, rows_vm, vm(weights_of(half), bf16)]
        + [chunks, half_chunks, half_chunks, chunks, dma((half // HEAD_DIM,))],
    )
    kv_blocks, flipped, grad_flipped, local, first_weights = lax.optimization_barrier(
        (kv_blocks, flipped, grad_flipped, local, first_weights)
    )
    kv_low = exchange(scan_blocks(kv_blocks, False), "seq", 1).reshape(state)
    other = width - half
    other_vm, other_chunks = vm((rows, other), bf16), dma((other // COPY_COLS,))
    local, second_weights = local_call(
        local_body,
        [flipped, local],
        [flat_vm, hbm(weights_of(other), bf16)],
        large,
        [keys, values],
        [other_vm, other_vm, vm(weights_of(other), bf16)]
        + [other_chunks, other_chunks, dma((other // HEAD_DIM,))],
        {3: 0},
    )
    groups = lax.axis_size("head")
    attended, sums = local_call(
        sums_body,
        [gain_row, flipped, grad_flipped, local, kv_low],
        [flat_vm, vm((2, rows), f32)],
        small,
        aliases={3: 0},
    )
    sums = from_all(sums, "head")
    dout_flipped, own_grad = local_call(
        functools.partial(dout_body, total_width, groups),
        [gain_row, flipped, grad_flipped, attended] + sums,
        [flat_vm, hbm(state, bf16)],
        small,
        scratch=[state_vm, state_chunks],
        aliases={3: 0},
    )
    grad_blocks = exchange(in_pieces(own_grad, "seq"), "seq", 0)
    early_vm, late_vm = vm((rows, early), bf16), vm((rows, width - early), bf16)
    query_grad, dout, early_part = local_call(
        query_body,
        [dout_flipped, kv_low],
        [hbm(tokens, bf16), rows_vm, early_vm],
        2 * large + small,
        [keys, values, first_weights, second_weights],
        [rows_vm] * 3 + [vm(weights_of(early), bf16)] + [chunks] * 3 + [dma((2,))],
    )
    grad_blocks, query_grad, dout, early_part = lax.optimization_barrier(
        (grad_blocks, query_grad, dout, early_part)
    )
    grad_low = exchange(scan_blocks(grad_blocks, True), "seq", 0).reshape(state)
    key_part, late_part, value_kept = local_call(
        inner_body,
        [dout],
        [rows_vm, late_vm, rows_vm],
        3 * large,
        [queries, values, second_weights],
        [rows_vm, vm(weights_of(width - early), bf16)] + [chunks] * 2 + [dma((1,))],
        {3: 0},
    )
    key_grad, value_grad = local_call(
        final_body,
        [value_kept, key_part, early_part, late_part, grad_low],
        [hbm(tokens, bf16)] * 2,
        2 * small,
        [keys],
        [rows_vm] * 3 + [dma((1,))] + [chunks] * 2,
    )
    return query_grad, key_grad, value_grad


def solution(mesh):
    return jax.shard_map(
        shards,
        mesh=mesh,
        in_specs=(
            P("seq", "head"),
            P("seq", "head"),
            P("seq", "head"),
            P("seq", "head"),
            P("head"),
        ),
        out_specs=(P("seq", "head"), P("seq", "head"), P("seq", "head")),
        check_vma=False,
    )
```

```python
import functools

import jax
import jax.numpy as jnp
from jax import lax
from jax.experimental import pallas as pl
from jax.experimental.pallas import tpu as pltpu
from jax.sharding import PartitionSpec as P

HEAD_DIM = 128
BLOCK = 256
COPY_COLS = 512
COPY_ROWS = 128
STATE_ROWS = 256
EPSILON = 1e-06
MIB = 1 << 20


def mm(a, b):
    return lax.dot_general(a, b, (((1,), (0,)), ((), ())), preferred_element_type=jnp.float32)


def mm_nt(a, b):
    return lax.dot_general(a, b, (((1,), (1,)), ((), ())), preferred_element_type=jnp.float32)


def mm_tn(a, b):
    return lax.dot_general(a, b, (((0,), (0,)), ((), ())), preferred_element_type=jnp.float32)


def pieces_of(ref, size):
    return [slice(at, at + size) for at in range(0, ref.shape[1], size)]


def masked(scores, diagonal, rows_first):
    shape = (BLOCK, BLOCK)
    rows = lax.broadcasted_iota(jnp.int32, shape, 0)
    cols = lax.broadcasted_iota(jnp.int32, shape, 1)
    keep = rows >= cols if rows_first else cols >= rows
    inside = slice(diagonal, diagonal + BLOCK)
    kept = jnp.where(keep, scores[:, inside], 0.0).astype(jnp.bfloat16)
    before = scores[:, :diagonal].astype(jnp.bfloat16)
    after = scores[:, inside.stop :].astype(jnp.bfloat16)
    parts = [part for part in (before, kept, after) if part.shape[1]]
    return jnp.concatenate(parts, axis=1) if len(parts) > 1 else kept


def column_copies(source, target, sems):
    copies = []
    for index, cols in enumerate(pieces_of(source, COPY_COLS)):
        copies.append(pltpu.make_async_copy(source.at[:, cols], target.at[:, cols], sems.at[index]))
    return copies


def row_copies(source, target, size, sems):
    copies = []
    for index in range(source.shape[0] // size):
        part = slice(index * size, (index + 1) * size)
        copies.append(pltpu.make_async_copy(source.at[part, :], target.at[part, :], sems.at[index]))
    return copies


def start_all(*groups):
    for parts in zip(*groups):
        for part in parts:
            part.start()


def wait_all(*groups):
    for group in groups:
        for part in group:
            part.wait()


def states_body(
    key_hbm, value_hbm, state_hbm, key_ref, value_ref, total_ref, state_ref,
    key_sems, value_sems, state_sems,
):
    keys = row_copies(key_hbm, key_ref, COPY_ROWS, key_sems)
    values = row_copies(value_hbm, value_ref, COPY_ROWS, value_sems)
    stores = row_copies(state_ref, state_hbm, STATE_ROWS, state_sems)
    start_all(keys, values)
    for index in range(len(keys)):
        keys[index].wait()
        values[index].wait()
        rows = slice(index * COPY_ROWS, (index + 1) * COPY_ROWS)
        for head in pieces_of(key_ref, HEAD_DIM):
            part = mm_tn(key_ref[rows, head], value_ref[rows, head])
            if index:
                part = part + total_ref[head, :]
            if index < len(keys) - 1:
                total_ref[head, :] = part
            else:
                state_ref[head, :] = part.astype(jnp.bfloat16)
                if head.stop % STATE_ROWS == 0:
                    stores[head.stop // STATE_ROWS - 1].start()
    wait_all(stores)


def weight_rows(rows):
    blocks = rows // BLOCK
    return blocks * (blocks + 1) // 2 * BLOCK


def local_part(key_ref, value_ref, own, flipped_ref, head, local_ref, weight_ref, row):
    for start in range(0, key_ref.shape[0], BLOCK):
        end = start + BLOCK
        parts = []
        for first in range(0, end, BLOCK):
            scores = mm(key_ref[first : first + BLOCK, own], flipped_ref[head, start:end])
            part = masked(scores, 0, False) if first == start else scores.astype(jnp.bfloat16)
            weight_ref[row : row + BLOCK, :] = part
            parts.append(part)
            row += BLOCK
        weights = jnp.concatenate(parts, axis=0) if len(parts) > 1 else parts[0]
        local = mm_tn(value_ref[:end, own], weights)
        local_ref[head, start:end] = local.astype(jnp.bfloat16)


def local_heads(first, key_ref, value_ref, loads, flipped_ref, local_ref, weight_ref, weight_hbm, sems):
    size = weight_rows(key_ref.shape[0])
    stores = []
    for index, step in enumerate(pieces_of(key_ref, COPY_COLS)):
        for load in loads:
            load[index].wait()
        for left in range(step.start, step.stop, HEAD_DIM):
            own = slice(left, left + HEAD_DIM)
            head = slice(first + left, first + left + HEAD_DIM)
            number = left // HEAD_DIM
            part = slice(number * size, (number + 1) * size)
            local_part(key_ref, value_ref, own, flipped_ref, head, local_ref, weight_ref, part.start)
            store = pltpu.make_async_copy(weight_ref.at[part, :], weight_hbm.at[part, :], sems.at[number])
            store.start()
            stores.append(store)
    return stores


def flip_body(
    query_hbm, key_hbm, value_hbm, grad_hbm, flipped_ref, grad_flipped_ref, local_ref, weight_hbm,
    query_ref, key_ref, value_ref, grad_ref, weight_ref,
    query_sems, key_sems, value_sems, grad_sems, weight_sems,
):
    part = slice(0, key_ref.shape[1])
    query_loads = column_copies(query_hbm, query_ref, query_sems)
    key_loads = column_copies(key_hbm.at[:, part], key_ref, key_sems)
    value_loads = column_copies(value_hbm.at[:, part], value_ref, value_sems)
    grad_loads = column_copies(grad_hbm, grad_ref, grad_sems)
    start_all(query_loads)
    start_all(key_loads, value_loads)
    start_all(grad_loads)
    for load, cols in zip(query_loads, pieces_of(query_ref, COPY_COLS)):
        load.wait()
        flipped_ref[cols, :] = query_ref[:, cols].T
    stores = local_heads(
        0, key_ref, value_ref, (key_loads, value_loads), flipped_ref, local_ref, weight_ref, weight_hbm, weight_sems
    )
    for load, cols in zip(grad_loads, pieces_of(grad_ref, COPY_COLS)):
        load.wait()
        grad_flipped_ref[cols, :] = grad_ref[:, cols].T
    wait_all(stores)


def local_body(
    key_hbm, value_hbm, flipped_ref, given_ref, local_ref, weight_hbm,
    key_ref, value_ref, weight_ref, key_sems, value_sems, weight_sems,
):
    first = local_ref.shape[0] - key_ref.shape[1]
    key_loads = column_copies(key_hbm.at[:, first:], key_ref, key_sems)
    value_loads = column_copies(value_hbm.at[:, first:], value_ref, value_sems)
    start_all(key_loads, value_loads)
    stores = local_heads(
        first, key_ref, value_ref, (key_loads, value_loads), flipped_ref, local_ref, weight_ref, weight_hbm, weight_sems
    )
    wait_all(stores)


def scan_body(reverse, block_ref, state_hbm, state_ref, sems):
    count = block_ref.shape[0]
    total = jnp.zeros(block_ref.shape[1:], jnp.float32)
    places = places_in_order(count, 0 if reverse else 1)
    stores = []
    for place in range(count - 1, -1, -1) if reverse else range(count):
        rank = places.index(place)
        state_ref[rank] = total.astype(jnp.bfloat16)
        total = total + block_ref[rank].astype(jnp.float32)
        stores.append(pltpu.make_async_copy(state_ref.at[rank], state_hbm.at[rank], sems.at[rank]))
        stores[-1].start()
    wait_all(stores)


def heads_of(ref):
    return [slice(at, at + HEAD_DIM) for at in range(0, ref.shape[0], HEAD_DIM)]


def scaled_grad(gain_ref, grad_ref, head):
    gain = jnp.broadcast_to(gain_ref[:, head], (HEAD_DIM, HEAD_DIM)).T
    gain = jnp.concatenate([gain] * (grad_ref.shape[1] // HEAD_DIM), axis=1)
    return gain * grad_ref[head, :].astype(jnp.float32)


def fold(values):
    parts = [values[at : at + 8, :] for at in range(0, values.shape[0], 8)]
    while len(parts) > 1:
        parts = [sum(parts[at + 1 : at + 2], parts[at]) for at in range(0, len(parts), 2)]
    return parts[0]


def sums_body(gain_ref, flipped_ref, grad_ref, local_ref, state_ref, attended_ref, sums_ref):
    square = cross = jnp.zeros((8, local_ref.shape[1]), jnp.float32)
    for head in heads_of(local_ref):
        attended = mm_tn(state_ref[head, :], flipped_ref[head, :])
        attended = attended + attended_ref[head, :].astype(jnp.float32)
        attended_ref[head, :] = attended.astype(jnp.bfloat16)
        square += fold(attended * attended)
        cross += fold(scaled_grad(gain_ref, grad_ref, head) * attended)
    square = jnp.sum(square, axis=0, keepdims=True)
    cross = jnp.sum(cross, axis=0, keepdims=True)
    sums_ref[0:1, :] = square
    sums_ref[1:2, :] = cross


def dout_body(width, groups, gain_ref, flipped_ref, grad_ref, attended_ref, *refs):
    dout_ref, own_hbm, own_ref, sems = refs[groups:]
    stores = row_copies(own_ref, own_hbm, STATE_ROWS, sems)
    sums = sum(ref[...] for ref in refs[:groups])
    inverse = 1.0 / jnp.sqrt(sums[0:1, :] / width + EPSILON)
    drop = sums[1:2, :] * (inverse * inverse * inverse) / width
    for head in heads_of(dout_ref):
        attended = dout_ref[head, :].astype(jnp.float32)
        dout = scaled_grad(gain_ref, grad_ref, head) * inverse - attended * drop
        dout = dout.astype(jnp.bfloat16)
        dout_ref[head, :] = dout
        own_ref[head, :] = mm_nt(flipped_ref[head, :], dout).astype(jnp.bfloat16)
        if head.stop % STATE_ROWS == 0:
            stores[head.stop // STATE_ROWS - 1].start()
    wait_all(stores)


def value_local(weight_ref, row, dout, target):
    blocks = dout.shape[0] // BLOCK
    for own in range(blocks):
        parts = []
        for other in range(own, blocks):
            start = row + (other * (other + 1) // 2 + own) * BLOCK
            parts.append(weight_ref[start : start + BLOCK, :])
        weights = jnp.concatenate(parts, axis=1) if len(parts) > 1 else parts[0]
        at = own * BLOCK
        target[at : at + BLOCK, :] = mm(weights, dout[at:, :]).astype(jnp.bfloat16)


def query_body(
    key_hbm, value_hbm, first_hbm, second_hbm, flipped_ref, state_ref, out_hbm, dout_ref, value_out,
    key_ref, value_ref, out_ref, weight_ref, key_sems, value_sems, out_sems, weight_sems,
):
    rows = dout_ref.shape[0]
    size = weight_rows(rows)
    key_copies = column_copies(key_hbm, key_ref, key_sems)
    value_copies = column_copies(value_hbm, value_ref, value_sems)
    there = first_hbm.shape[0]
    rest = weight_ref.shape[0] - there
    weight_copies = [
        pltpu.make_async_copy(first_hbm, weight_ref.at[:there, :], weight_sems.at[0]),
        pltpu.make_async_copy(second_hbm.at[:rest, :], weight_ref.at[there:, :], weight_sems.at[1]),
    ]
    start_all(key_copies, value_copies)
    start_all(weight_copies)
    for head in heads_of(flipped_ref):
        dout_ref[:, head] = flipped_ref[head, :].T
    stores = column_copies(out_ref, out_hbm, out_sems)
    for index, step in enumerate(pieces_of(out_ref, COPY_COLS)):
        key_copies[index].wait()
        value_copies[index].wait()
        for left in range(step.start, step.stop, HEAD_DIM):
            cols = slice(left, left + HEAD_DIM)
            for start in range(0, rows, BLOCK):
                end = start + BLOCK
                dout = dout_ref[start:end, cols]
                dscore = masked(mm_nt(dout, value_ref[:end, cols]), start, True)
                grad = mm(dscore, key_ref[:end, cols]) + mm_nt(dout, state_ref[cols, :])
                out_ref[start:end, cols] = grad.astype(jnp.bfloat16)
        stores[index].start()
    wait_all(weight_copies)
    for number, cols in enumerate(pieces_of(value_out, HEAD_DIM)):
        value_local(weight_ref, number * size, dout_ref[:, cols], value_out.at[:, cols])
    wait_all(stores)


def inner_body(
    query_hbm, value_hbm, weight_hbm, dout_ref, key_out, value_out, value_ref,
    query_ref, weight_ref, query_sems, value_sems, weight_sem,
):
    rows, width = key_out.shape
    size = weight_rows(rows)
    early = width - value_out.shape[1]
    query_copies = column_copies(query_hbm, query_ref, query_sems)
    value_copies = column_copies(value_hbm, value_ref, value_sems)
    skipped = weight_hbm.shape[0] - weight_ref.shape[0]
    weight_copy = pltpu.make_async_copy(weight_hbm.at[skipped:, :], weight_ref, weight_sem.at[0])
    start_all(query_copies, value_copies)
    weight_copy.start()
    for index, step in enumerate(pieces_of(key_out, COPY_COLS)):
        query_copies[index].wait()
        value_copies[index].wait()
        for left in range(step.start, step.stop, HEAD_DIM):
            if left == early:
                weight_copy.wait()
            cols = slice(left, left + HEAD_DIM)
            dout = key_out[:, cols]
            for start in range(0, rows, BLOCK):
                end = start + BLOCK
                scores = mm_nt(value_ref[start:end, cols], dout[start:, :])
                grad = mm(masked(scores, 0, False), query_ref[start:, cols])
                key_out[start:end, cols] = grad.astype(jnp.bfloat16)
            if left >= early:
                late = slice(left - early, left - early + HEAD_DIM)
                value_local(weight_ref, late.start // HEAD_DIM * size, dout, value_out.at[:, late])


def final_body(
    key_hbm, value_ref, key_part, early_part, late_part, state_ref, key_out_hbm, value_out_hbm,
    key_ref, key_out, value_out, in_sems, key_sems, value_sems,
):
    key_copy = pltpu.make_async_copy(key_hbm, key_ref, in_sems.at[0])
    key_copy.start()
    key_stores = column_copies(key_out, key_out_hbm, key_sems)
    value_stores = column_copies(value_out, value_out_hbm, value_sems)
    for index, step in enumerate(pieces_of(key_out, COPY_COLS)):
        for left in range(step.start, step.stop, HEAD_DIM):
            cols = slice(left, left + HEAD_DIM)
            grad = key_part[:, cols].astype(jnp.float32) + mm_nt(value_ref[:, cols], state_ref[cols, :])
            key_out[:, cols] = grad.astype(jnp.bfloat16)
        key_stores[index].start()
    key_copy.wait()
    for index, step in enumerate(pieces_of(value_out, COPY_COLS)):
        for left in range(step.start, step.stop, HEAD_DIM):
            cols = slice(left, left + HEAD_DIM)
            early = early_part.shape[1]
            if left < early:
                part = early_part[:, cols]
            else:
                part = late_part[:, left - early : left - early + HEAD_DIM]
            grad = part.astype(jnp.float32) + mm(key_ref[:, cols], state_ref[cols, :])
            value_out[:, cols] = grad.astype(jnp.bfloat16)
        value_stores[index].start()
    wait_all(key_stores, value_stores)


def local_call(body, in_args, outs, flops, hbm_args=(), scratch=(), aliases=None):
    args = [pltpu.with_memory_space_constraint(a, pltpu.HBM) for a in hbm_args]
    args += [pltpu.with_memory_space_constraint(a, pltpu.VMEM) for a in in_args]
    specs = [pl.BlockSpec(memory_space=pltpu.HBM)] * len(hbm_args)
    specs += [pl.BlockSpec(memory_space=pltpu.VMEM)] * len(in_args)
    out_specs = []
    for out in outs:
        out_specs.append(pl.BlockSpec(memory_space=out.memory_space))
    moved = sum(a.size * a.dtype.itemsize for a in args)
    return pl.pallas_call(
        body,
        in_specs=specs,
        out_specs=out_specs,
        out_shape=outs,
        scratch_shapes=scratch,
        input_output_aliases=aliases or {},
        compiler_params=pltpu.CompilerParams(vmem_limit_bytes=16 * MIB),
        cost_estimate=pl.CostEstimate(flops=flops, bytes_accessed=moved, transcendentals=0),
    )(*args)


def scan_blocks(blocks, reverse):
    (states,) = local_call(
        functools.partial(scan_body, reverse),
        [blocks],
        [pltpu.HBM(blocks.shape, blocks.dtype)],
        blocks.size,
        scratch=[
            pltpu.VMEM(blocks.shape, blocks.dtype),
            pltpu.SemaphoreType.DMA((blocks.shape[0],)),
        ],
    )
    return states


def places_in_order(count, flip):
    quarter = count // 4
    first, second, third, fourth = (list(range(at, at + quarter)) for at in range(0, count, quarter))
    half = quarter // 2
    order = second + first[:half] + third[:half] + first[half:] + third[half:] + fourth
    return [(count - 1 - place) ^ flip for place in order]


def from_all(part, axis):
    count = lax.axis_size(axis)
    parts = [part]
    paired = count & (count - 1) == 0
    for shift in sorted(range(1, count), key=lambda shift: shift % 2):
        pairs = [(place, place ^ shift if paired else (place + shift) % count) for place in range(count)]
        parts.append(lax.ppermute(part, axis, pairs))
    return parts


def exchange(pieces, axis, flip):
    groups = [places_in_order(lax.axis_size(axis), flip)]
    return lax.all_to_all(pieces, axis, 0, 0, axis_index_groups=groups)


def in_pieces(state, axis):
    count = lax.axis_size(axis)
    rows, cols = state.shape
    return state.reshape(count, rows // count, cols)


def shards(queries, keys, values, out_grad, gain):
    rows, width = queries.shape
    total_width = width * lax.axis_size("head")
    bf16, f32 = jnp.bfloat16, jnp.float32
    tokens, state = (rows, width), (width, HEAD_DIM)
    small = 2 * rows * width * HEAD_DIM
    large = 2 * rows * rows * width * 3 // 4
    gain_row = gain.reshape(1, width)
    flat = (width, rows)
    dma = pltpu.SemaphoreType.DMA
    chunks, row_chunks = dma((width // COPY_COLS,)), dma((rows // COPY_ROWS,))
    state_chunks = dma((width // STATE_ROWS,))
    vm, hbm = pltpu.VMEM, pltpu.HBM
    rows_vm, flat_vm, state_vm = vm(tokens, bf16), vm(flat, bf16), vm(state, bf16)

    (own_kv,) = local_call(
        states_body,
        [],
        [hbm(state, bf16)],
        small,
        [keys, values],
        [rows_vm] * 2 + [vm(state, f32), state_vm] + [row_chunks] * 2 + [state_chunks],
    )
    kv_blocks = exchange(in_pieces(own_kv, "seq"), "seq", 1)
    half = width // 2 // COPY_COLS * COPY_COLS
    early = width * 3 // 4 // HEAD_DIM * HEAD_DIM
    def weights_of(cols):
        return (cols // HEAD_DIM * weight_rows(rows), BLOCK)

    half_vm, half_chunks = vm((rows, half), bf16), dma((half // COPY_COLS,))
    flipped, grad_flipped, local, first_weights = local_call(
        flip_body,
        [],
        [flat_vm] * 3 + [hbm(weights_of(half), bf16)],
        2 * large,
        [queries, keys, values, out_grad],
        [rows_vm, half_vm, half_vm, rows_vm, vm(weights_of(half), bf16)]
        + [chunks, half_chunks, half_chunks, chunks, dma((half // HEAD_DIM,))],
    )
    kv_blocks, flipped, grad_flipped, local, first_weights = lax.optimization_barrier(
        (kv_blocks, flipped, grad_flipped, local, first_weights)
    )
    kv_low = exchange(scan_blocks(kv_blocks, False), "seq", 1).reshape(state)
    other = width - half
    other_vm, other_chunks = vm((rows, other), bf16), dma((other // COPY_COLS,))
    local, second_weights = local_call(
        local_body,
        [flipped, local],
        [flat_vm, hbm(weights_of(other), bf16)],
        large,
        [keys, values],
        [other_vm, other_vm, vm(weights_of(other), bf16)]
        + [other_chunks, other_chunks, dma((other // HEAD_DIM,))],
        {3: 0},
    )
    groups = lax.axis_size("head")
    attended, sums = local_call(
        sums_body,
        [gain_row, flipped, grad_flipped, local, kv_low],
        [flat_vm, vm((2, rows), f32)],
        small,
        aliases={3: 0},
    )
    sums = from_all(sums, "head")
    dout_flipped, own_grad = local_call(
        functools.partial(dout_body, total_width, groups),
        [gain_row, flipped, grad_flipped, attended] + sums,
        [flat_vm, hbm(state, bf16)],
        small,
        scratch=[state_vm, state_chunks],
        aliases={3: 0},
    )
    grad_blocks = exchange(in_pieces(own_grad, "seq"), "seq", 0)
    early_vm, late_vm = vm((rows, early), bf16), vm((rows, width - early), bf16)
    query_grad, dout, early_part = local_call(
        query_body,
        [dout_flipped, kv_low],
        [hbm(tokens, bf16), rows_vm, early_vm],
        2 * large + small,
        [keys, values, first_weights, second_weights],
        [rows_vm] * 3 + [vm(weights_of(early), bf16)] + [chunks] * 3 + [dma((2,))],
    )
    grad_blocks, query_grad, dout, early_part = lax.optimization_barrier(
        (grad_blocks, query_grad, dout, early_part)
    )
    grad_low = exchange(scan_blocks(grad_blocks, True), "seq", 0).reshape(state)
    key_part, late_part, value_kept = local_call(
        inner_body,
        [dout],
        [rows_vm, late_vm, rows_vm],
        3 * large,
        [queries, values, second_weights],
        [rows_vm, vm(weights_of(width - early), bf16)] + [chunks] * 2 + [dma((1,))],
        {3: 0},
    )
    key_grad, value_grad = local_call(
        final_body,
        [value_kept, key_part, early_part, late_part, grad_low],
        [hbm(tokens, bf16)] * 2,
        2 * small,
        [keys],
        [rows_vm] * 3 + [dma((1,))] + [chunks] * 2,
    )
    return query_grad, key_grad, value_grad


def solution(mesh):
    return jax.shard_map(
        shards,
        mesh=mesh,
        in_specs=(
            P("seq", "head"),
            P("seq", "head"),
            P("seq", "head"),
            P("seq", "head"),
            P("head"),
        ),
        out_specs=(P("seq", "head"), P("seq", "head"), P("seq", "head")),
        check_vma=False,
    )
```

```python
import functools

import jax
import jax.numpy as jnp
from jax import lax
from jax.experimental import pallas as pl
from jax.experimental.pallas import tpu as pltpu
from jax.sharding import PartitionSpec as P

HEAD_DIM = 128
BLOCK = 256
COPY_COLS = 512
COPY_ROWS = 128
STATE_ROWS = 256
EPSILON = 1e-06
MIB = 1 << 20


def mm(a, b):
    return lax.dot_general(a, b, (((1,), (0,)), ((), ())), preferred_element_type=jnp.float32)


def mm_nt(a, b):
    return lax.dot_general(a, b, (((1,), (1,)), ((), ())), preferred_element_type=jnp.float32)


def mm_tn(a, b):
    return lax.dot_general(a, b, (((0,), (0,)), ((), ())), preferred_element_type=jnp.float32)


def pieces_of(ref, size):
    return [slice(at, at + size) for at in range(0, ref.shape[1], size)]


def masked(scores, diagonal, rows_first):
    shape = (BLOCK, BLOCK)
    rows = lax.broadcasted_iota(jnp.int32, shape, 0)
    cols = lax.broadcasted_iota(jnp.int32, shape, 1)
    keep = rows >= cols if rows_first else cols >= rows
    inside = slice(diagonal, diagonal + BLOCK)
    kept = jnp.where(keep, scores[:, inside], 0.0).astype(jnp.bfloat16)
    before = scores[:, :diagonal].astype(jnp.bfloat16)
    after = scores[:, inside.stop :].astype(jnp.bfloat16)
    parts = [part for part in (before, kept, after) if part.shape[1]]
    return jnp.concatenate(parts, axis=1) if len(parts) > 1 else kept


def column_copies(source, target, sems):
    copies = []
    for index, cols in enumerate(pieces_of(source, COPY_COLS)):
        copies.append(pltpu.make_async_copy(source.at[:, cols], target.at[:, cols], sems.at[index]))
    return copies


def row_copies(source, target, size, sems):
    copies = []
    for index in range(source.shape[0] // size):
        part = slice(index * size, (index + 1) * size)
        copies.append(pltpu.make_async_copy(source.at[part, :], target.at[part, :], sems.at[index]))
    return copies


def start_all(*groups):
    for parts in zip(*groups):
        for part in parts:
            part.start()


def wait_all(*groups):
    for group in groups:
        for part in group:
            part.wait()


def states_body(
    key_hbm, value_hbm, state_hbm, key_ref, value_ref, total_ref, state_ref,
    key_sems, value_sems, state_sems,
):
    keys = row_copies(key_hbm, key_ref, COPY_ROWS, key_sems)
    values = row_copies(value_hbm, value_ref, COPY_ROWS, value_sems)
    stores = row_copies(state_ref, state_hbm, STATE_ROWS, state_sems)
    start_all(keys, values)
    for index in range(len(keys)):
        keys[index].wait()
        values[index].wait()
        rows = slice(index * COPY_ROWS, (index + 1) * COPY_ROWS)
        for head in pieces_of(key_ref, HEAD_DIM):
            part = mm_tn(key_ref[rows, head], value_ref[rows, head])
            if index:
                part = part + total_ref[head, :]
            if index < len(keys) - 1:
                total_ref[head, :] = part
            else:
                state_ref[head, :] = part.astype(jnp.bfloat16)
                if head.stop % STATE_ROWS == 0:
                    stores[head.stop // STATE_ROWS - 1].start()
    wait_all(stores)


def weight_rows(rows):
    blocks = rows // BLOCK
    return blocks * (blocks + 1) // 2 * BLOCK


def local_part(key_ref, value_ref, own, flipped_ref, head, local_ref, weight_ref, row):
    for start in range(0, key_ref.shape[0], BLOCK):
        end = start + BLOCK
        parts = []
        for first in range(0, end, BLOCK):
            scores = mm(key_ref[first : first + BLOCK, own], flipped_ref[head, start:end])
            part = masked(scores, 0, False) if first == start else scores.astype(jnp.bfloat16)
            weight_ref[row : row + BLOCK, :] = part
            parts.append(part)
            row += BLOCK
        weights = jnp.concatenate(parts, axis=0) if len(parts) > 1 else parts[0]
        local = mm_tn(value_ref[:end, own], weights)
        local_ref[head, start:end] = local.astype(jnp.bfloat16)


def local_heads(first, key_ref, value_ref, loads, flipped_ref, local_ref, weight_ref, weight_hbm, sems):
    size = weight_rows(key_ref.shape[0])
    stores = []
    for index, step in enumerate(pieces_of(key_ref, COPY_COLS)):
        for load in loads:
            load[index].wait()
        for left in range(step.start, step.stop, HEAD_DIM):
            own = slice(left, left + HEAD_DIM)
            head = slice(first + left, first + left + HEAD_DIM)
            number = left // HEAD_DIM
            part = slice(number * size, (number + 1) * size)
            local_part(key_ref, value_ref, own, flipped_ref, head, local_ref, weight_ref, part.start)
            store = pltpu.make_async_copy(weight_ref.at[part, :], weight_hbm.at[part, :], sems.at[number])
            store.start()
            stores.append(store)
    return stores


def flip_body(
    query_hbm, key_hbm, value_hbm, grad_hbm, flipped_ref, grad_flipped_ref, local_ref, weight_hbm,
    query_ref, key_ref, value_ref, grad_ref, weight_ref,
    query_sems, key_sems, value_sems, grad_sems, weight_sems,
):
    part = slice(0, key_ref.shape[1])
    query_loads = column_copies(query_hbm, query_ref, query_sems)
    key_loads = column_copies(key_hbm.at[:, part], key_ref, key_sems)
    value_loads = column_copies(value_hbm.at[:, part], value_ref, value_sems)
    grad_loads = column_copies(grad_hbm, grad_ref, grad_sems)
    start_all(query_loads)
    start_all(key_loads, value_loads)
    start_all(grad_loads)
    for load, cols in zip(query_loads, pieces_of(query_ref, COPY_COLS)):
        load.wait()
        flipped_ref[cols, :] = query_ref[:, cols].T
    stores = local_heads(
        0, key_ref, value_ref, (key_loads, value_loads), flipped_ref, local_ref, weight_ref, weight_hbm, weight_sems
    )
    for load, cols in zip(grad_loads, pieces_of(grad_ref, COPY_COLS)):
        load.wait()
        grad_flipped_ref[cols, :] = grad_ref[:, cols].T
    wait_all(stores)


def local_body(
    key_hbm, value_hbm, flipped_ref, given_ref, local_ref, weight_hbm,
    key_ref, value_ref, weight_ref, key_sems, value_sems, weight_sems,
):
    first = local_ref.shape[0] - key_ref.shape[1]
    key_loads = column_copies(key_hbm.at[:, first:], key_ref, key_sems)
    value_loads = column_copies(value_hbm.at[:, first:], value_ref, value_sems)
    start_all(key_loads, value_loads)
    stores = local_heads(
        first, key_ref, value_ref, (key_loads, value_loads), flipped_ref, local_ref, weight_ref, weight_hbm, weight_sems
    )
    wait_all(stores)


def scan_body(reverse, block_ref, state_hbm, state_ref, sems):
    count = block_ref.shape[0]
    total = jnp.zeros(block_ref.shape[1:], jnp.float32)
    places = places_in_order(count, 0 if reverse else 1)
    stores = []
    for place in range(count - 1, -1, -1) if reverse else range(count):
        rank = places.index(place)
        state_ref[rank] = total.astype(jnp.bfloat16)
        total = total + block_ref[rank].astype(jnp.float32)
        stores.append(pltpu.make_async_copy(state_ref.at[rank], state_hbm.at[rank], sems.at[rank]))
        stores[-1].start()
    wait_all(stores)


def heads_of(ref):
    return [slice(at, at + HEAD_DIM) for at in range(0, ref.shape[0], HEAD_DIM)]


def scaled_grad(gain_ref, grad_ref, head):
    gain = jnp.broadcast_to(gain_ref[:, head], (HEAD_DIM, HEAD_DIM)).T
    gain = jnp.concatenate([gain] * (grad_ref.shape[1] // HEAD_DIM), axis=1)
    return gain * grad_ref[head, :].astype(jnp.float32)


def fold(values):
    parts = [values[at : at + 8, :] for at in range(0, values.shape[0], 8)]
    while len(parts) > 1:
        parts = [sum(parts[at + 1 : at + 2], parts[at]) for at in range(0, len(parts), 2)]
    return parts[0]


def sums_body(gain_ref, flipped_ref, grad_ref, local_ref, state_ref, attended_ref, sums_ref):
    square = cross = jnp.zeros((8, local_ref.shape[1]), jnp.float32)
    for head in heads_of(local_ref):
        attended = mm_tn(state_ref[head, :], flipped_ref[head, :])
        attended = attended + attended_ref[head, :].astype(jnp.float32)
        attended_ref[head, :] = attended.astype(jnp.bfloat16)
        square += fold(attended * attended)
        cross += fold(scaled_grad(gain_ref, grad_ref, head) * attended)
    square = jnp.sum(square, axis=0, keepdims=True)
    cross = jnp.sum(cross, axis=0, keepdims=True)
    sums_ref[0:1, :] = square
    sums_ref[1:2, :] = cross


def dout_body(width, groups, gain_ref, flipped_ref, grad_ref, attended_ref, *refs):
    dout_ref, own_hbm, own_ref, sems = refs[groups:]
    stores = row_copies(own_ref, own_hbm, STATE_ROWS, sems)
    sums = sum(ref[...] for ref in refs[:groups])
    inverse = 1.0 / jnp.sqrt(sums[0:1, :] / width + EPSILON)
    drop = sums[1:2, :] * (inverse * inverse * inverse) / width
    for head in heads_of(dout_ref):
        attended = dout_ref[head, :].astype(jnp.float32)
        dout = scaled_grad(gain_ref, grad_ref, head) * inverse - attended * drop
        dout = dout.astype(jnp.bfloat16)
        dout_ref[head, :] = dout
        own_ref[head, :] = mm_nt(flipped_ref[head, :], dout).astype(jnp.bfloat16)
        if head.stop % STATE_ROWS == 0:
            stores[head.stop // STATE_ROWS - 1].start()
    wait_all(stores)


def value_local(weight_ref, row, dout, target):
    blocks = dout.shape[0] // BLOCK
    for own in range(blocks):
        parts = []
        for other in range(own, blocks):
            start = row + (other * (other + 1) // 2 + own) * BLOCK
            parts.append(weight_ref[start : start + BLOCK, :])
        weights = jnp.concatenate(parts, axis=1) if len(parts) > 1 else parts[0]
        at = own * BLOCK
        target[at : at + BLOCK, :] = mm(weights, dout[at:, :]).astype(jnp.bfloat16)


def query_body(
    key_hbm, value_hbm, first_hbm, second_hbm, flipped_ref, state_ref, out_hbm, dout_ref, value_out,
    key_ref, value_ref, out_ref, weight_ref, key_sems, value_sems, out_sems, weight_sems,
):
    rows = dout_ref.shape[0]
    size = weight_rows(rows)
    key_copies = column_copies(key_hbm, key_ref, key_sems)
    value_copies = column_copies(value_hbm, value_ref, value_sems)
    there = first_hbm.shape[0]
    rest = weight_ref.shape[0] - there
    weight_copies = [
        pltpu.make_async_copy(first_hbm, weight_ref.at[:there, :], weight_sems.at[0]),
        pltpu.make_async_copy(second_hbm.at[:rest, :], weight_ref.at[there:, :], weight_sems.at[1]),
    ]
    start_all(key_copies, value_copies)
    start_all(weight_copies)
    for head in heads_of(flipped_ref):
        dout_ref[:, head] = flipped_ref[head, :].T
    stores = column_copies(out_ref, out_hbm, out_sems)
    for index, step in enumerate(pieces_of(out_ref, COPY_COLS)):
        key_copies[index].wait()
        value_copies[index].wait()
        for left in range(step.start, step.stop, HEAD_DIM):
            cols = slice(left, left + HEAD_DIM)
            for start in range(0, rows, BLOCK):
                end = start + BLOCK
                dout = dout_ref[start:end, cols]
                dscore = masked(mm_nt(dout, value_ref[:end, cols]), start, True)
                grad = mm(dscore, key_ref[:end, cols]) + mm_nt(dout, state_ref[cols, :])
                out_ref[start:end, cols] = grad.astype(jnp.bfloat16)
        stores[index].start()
    wait_all(weight_copies)
    for number, cols in enumerate(pieces_of(value_out, HEAD_DIM)):
        value_local(weight_ref, number * size, dout_ref[:, cols], value_out.at[:, cols])
    wait_all(stores)


def inner_body(
    query_hbm, value_hbm, weight_hbm, dout_ref, key_out, value_out, value_ref,
    query_ref, weight_ref, query_sems, value_sems, weight_sem,
):
    rows, width = key_out.shape
    size = weight_rows(rows)
    early = width - value_out.shape[1]
    query_copies = column_copies(query_hbm, query_ref, query_sems)
    value_copies = column_copies(value_hbm, value_ref, value_sems)
    skipped = weight_hbm.shape[0] - weight_ref.shape[0]
    weight_copy = pltpu.make_async_copy(weight_hbm.at[skipped:, :], weight_ref, weight_sem.at[0])
    start_all(query_copies, value_copies)
    weight_copy.start()
    for index, step in enumerate(pieces_of(key_out, COPY_COLS)):
        query_copies[index].wait()
        value_copies[index].wait()
        for left in range(step.start, step.stop, HEAD_DIM):
            if left == early:
                weight_copy.wait()
            cols = slice(left, left + HEAD_DIM)
            dout = key_out[:, cols]
            for start in range(0, rows, BLOCK):
                end = start + BLOCK
                scores = mm_nt(value_ref[start:end, cols], dout[start:, :])
                grad = mm(masked(scores, 0, False), query_ref[start:, cols])
                key_out[start:end, cols] = grad.astype(jnp.bfloat16)
            if left >= early:
                late = slice(left - early, left - early + HEAD_DIM)
                value_local(weight_ref, late.start // HEAD_DIM * size, dout, value_out.at[:, late])


def final_body(
    key_hbm, value_ref, key_part, early_part, late_part, state_ref, key_out_hbm, value_out_hbm,
    key_ref, key_out, value_out, in_sems, key_sems, value_sems,
):
    key_copy = pltpu.make_async_copy(key_hbm, key_ref, in_sems.at[0])
    key_copy.start()
    key_stores = column_copies(key_out, key_out_hbm, key_sems)
    value_stores = column_copies(value_out, value_out_hbm, value_sems)
    for index, step in enumerate(pieces_of(key_out, COPY_COLS)):
        for left in range(step.start, step.stop, HEAD_DIM):
            cols = slice(left, left + HEAD_DIM)
            grad = key_part[:, cols].astype(jnp.float32) + mm_nt(value_ref[:, cols], state_ref[cols, :])
            key_out[:, cols] = grad.astype(jnp.bfloat16)
        key_stores[index].start()
    key_copy.wait()
    for index, step in enumerate(pieces_of(value_out, COPY_COLS)):
        for left in range(step.start, step.stop, HEAD_DIM):
            cols = slice(left, left + HEAD_DIM)
            early = early_part.shape[1]
            if left < early:
                part = early_part[:, cols]
            else:
                part = late_part[:, left - early : left - early + HEAD_DIM]
            grad = part.astype(jnp.float32) + mm(key_ref[:, cols], state_ref[cols, :])
            value_out[:, cols] = grad.astype(jnp.bfloat16)
        value_stores[index].start()
    wait_all(key_stores, value_stores)


def local_call(body, in_args, outs, flops, hbm_args=(), scratch=(), aliases=None):
    args = [pltpu.with_memory_space_constraint(a, pltpu.HBM) for a in hbm_args]
    args += [pltpu.with_memory_space_constraint(a, pltpu.VMEM) for a in in_args]
    specs = [pl.BlockSpec(memory_space=pltpu.HBM)] * len(hbm_args)
    specs += [pl.BlockSpec(memory_space=pltpu.VMEM)] * len(in_args)
    out_specs = []
    for out in outs:
        out_specs.append(pl.BlockSpec(memory_space=out.memory_space))
    moved = sum(a.size * a.dtype.itemsize for a in args)
    return pl.pallas_call(
        body,
        in_specs=specs,
        out_specs=out_specs,
        out_shape=outs,
        scratch_shapes=scratch,
        input_output_aliases=aliases or {},
        compiler_params=pltpu.CompilerParams(vmem_limit_bytes=16 * MIB),
        cost_estimate=pl.CostEstimate(flops=flops, bytes_accessed=moved, transcendentals=0),
    )(*args)


def scan_blocks(blocks, reverse):
    (states,) = local_call(
        functools.partial(scan_body, reverse),
        [blocks],
        [pltpu.HBM(blocks.shape, blocks.dtype)],
        blocks.size,
        scratch=[
            pltpu.VMEM(blocks.shape, blocks.dtype),
            pltpu.SemaphoreType.DMA((blocks.shape[0],)),
        ],
    )
    return states


def places_in_order(count, flip):
    quarter = count // 4
    first, second, third, fourth = (list(range(at, at + quarter)) for at in range(0, count, quarter))
    half = quarter // 2
    order = second + first[:half] + third[:half] + first[half:] + third[half:] + fourth
    return [(count - 1 - place) ^ flip for place in order]


def from_all(part, axis):
    count = lax.axis_size(axis)
    parts = [part]
    for shift in range(count - 1, 0, -1):
        pairs = [(place, (place + shift) % count) for place in range(count)]
        parts.append(lax.ppermute(part, axis, pairs))
    return parts


def exchange(pieces, axis, flip):
    groups = [places_in_order(lax.axis_size(axis), flip)]
    return lax.all_to_all(pieces, axis, 0, 0, axis_index_groups=groups)


def in_pieces(state, axis):
    count = lax.axis_size(axis)
    rows, cols = state.shape
    return state.reshape(count, rows // count, cols)


def shards(queries, keys, values, out_grad, gain):
    rows, width = queries.shape
    total_width = width * lax.axis_size("head")
    bf16, f32 = jnp.bfloat16, jnp.float32
    tokens, state = (rows, width), (width, HEAD_DIM)
    small = 2 * rows * width * HEAD_DIM
    large = 2 * rows * rows * width * 3 // 4
    gain_row = gain.reshape(1, width)
    flat = (width, rows)
    dma = pltpu.SemaphoreType.DMA
    chunks, row_chunks = dma((width // COPY_COLS,)), dma((rows // COPY_ROWS,))
    state_chunks = dma((width // STATE_ROWS,))
    vm, hbm = pltpu.VMEM, pltpu.HBM
    rows_vm, flat_vm, state_vm = vm(tokens, bf16), vm(flat, bf16), vm(state, bf16)

    (own_kv,) = local_call(
        states_body,
        [],
        [hbm(state, bf16)],
        small,
        [keys, values],
        [rows_vm] * 2 + [vm(state, f32), state_vm] + [row_chunks] * 2 + [state_chunks],
    )
    kv_blocks = exchange(in_pieces(own_kv, "seq"), "seq", 1)
    half = width // 2 // COPY_COLS * COPY_COLS
    early = width * 3 // 4 // HEAD_DIM * HEAD_DIM
    def weights_of(cols):
        return (cols // HEAD_DIM * weight_rows(rows), BLOCK)

    half_vm, half_chunks = vm((rows, half), bf16), dma((half // COPY_COLS,))
    flipped, grad_flipped, local, first_weights = local_call(
        flip_body,
        [],
        [flat_vm] * 3 + [hbm(weights_of(half), bf16)],
        2 * large,
        [queries, keys, values, out_grad],
        [rows_vm, half_vm, half_vm, rows_vm, vm(weights_of(half), bf16)]
        + [chunks, half_chunks, half_chunks, chunks, dma((half // HEAD_DIM,))],
    )
    kv_blocks, flipped, grad_flipped, local, first_weights = lax.optimization_barrier(
        (kv_blocks, flipped, grad_flipped, local, first_weights)
    )
    kv_low = exchange(scan_blocks(kv_blocks, False), "seq", 1).reshape(state)
    other = width - half
    other_vm, other_chunks = vm((rows, other), bf16), dma((other // COPY_COLS,))
    local, second_weights = local_call(
        local_body,
        [flipped, local],
        [flat_vm, hbm(weights_of(other), bf16)],
        large,
        [keys, values],
        [other_vm, other_vm, vm(weights_of(other), bf16)]
        + [other_chunks, other_chunks, dma((other // HEAD_DIM,))],
        {3: 0},
    )
    groups = lax.axis_size("head")
    attended, sums = local_call(
        sums_body,
        [gain_row, flipped, grad_flipped, local, kv_low],
        [flat_vm, vm((2, rows), f32)],
        small,
        aliases={3: 0},
    )
    sums = from_all(sums, "head")
    dout_flipped, own_grad = local_call(
        functools.partial(dout_body, total_width, groups),
        [gain_row, flipped, grad_flipped, attended] + sums,
        [flat_vm, hbm(state, bf16)],
        small,
        scratch=[state_vm, state_chunks],
        aliases={3: 0},
    )
    grad_blocks = exchange(in_pieces(own_grad, "seq"), "seq", 0)
    early_vm, late_vm = vm((rows, early), bf16), vm((rows, width - early), bf16)
    query_grad, dout, early_part = local_call(
        query_body,
        [dout_flipped, kv_low],
        [hbm(tokens, bf16), rows_vm, early_vm],
        2 * large + small,
        [keys, values, first_weights, second_weights],
        [rows_vm] * 3 + [vm(weights_of(early), bf16)] + [chunks] * 3 + [dma((2,))],
    )
    grad_blocks, query_grad, dout, early_part = lax.optimization_barrier(
        (grad_blocks, query_grad, dout, early_part)
    )
    grad_low = exchange(scan_blocks(grad_blocks, True), "seq", 0).reshape(state)
    key_part, late_part, value_kept = local_call(
        inner_body,
        [dout],
        [rows_vm, late_vm, rows_vm],
        3 * large,
        [queries, values, second_weights],
        [rows_vm, vm(weights_of(width - early), bf16)] + [chunks] * 2 + [dma((1,))],
        {3: 0},
    )
    key_grad, value_grad = local_call(
        final_body,
        [value_kept, key_part, early_part, late_part, grad_low],
        [hbm(tokens, bf16)] * 2,
        2 * small,
        [keys],
        [rows_vm] * 3 + [dma((1,))] + [chunks] * 2,
    )
    return query_grad, key_grad, value_grad


def solution(mesh):
    return jax.shard_map(
        shards,
        mesh=mesh,
        in_specs=(
            P("seq", "head"),
            P("seq", "head"),
            P("seq", "head"),
            P("seq", "head"),
            P("head"),
        ),
        out_specs=(P("seq", "head"), P("seq", "head"), P("seq", "head")),
        check_vma=False,
    )
```
